32 devices in a mesh: gx: 4 (over y, x), gy: 4 (over z), gz: 2 (over core).
Axes of the slice: x: 2, y: 2, z: 4, core: 2. Of those that a mesh axis runs over, the one named last changes fastest.
Arguments:
- tokens: bfloat16 [32, 8192, 128], P(('gx', 'gy', 'gz')), may hold values from -150 to 150
- task_id: int32 [32], P(('gx', 'gy', 'gz')), may hold values from 0 to 17
- valid_count: int32 [32], P(('gx', 'gy', 'gz')), may hold values from 2028 to 8115, as said below
- cross_params: bfloat16 [3029248], P(('gx', 'gy', 'gz')), may hold values from -50 to 50
- latent_params: bfloat16 [3150848], P(('gx', 'gy', 'gz')), may hold values from -50 to 50
- out_grad: bfloat16 [32, 512, 512], P(('gx', 'gy', 'gz')), may hold values from -6 to 6
Outputs:
- latents_out: bfloat16 [32, 512, 512], P(('gx', 'gy', 'gz'))
- token_grad: float32 [32, 8192, 128], P(('gx', 'gy', 'gz'))
- cross_grad: float32 [3029248], P(('gx', 'gy', 'gz'))
- latent_grad: float32 [3150848], P(('gx', 'gy', 'gz'))
The draws below stay inside these ranges and needn't reach their ends.
Inputs may be any that keep to these rules, and one draw needn't show every extreme that they name: `valid_count`: patches at places below a scene's count are valid; some scene has all 8115 valid and some has 2028.
All inputs are finite; a program needn't handle non-finite values.
Results may differ from the reference program's by a relative error of at most 0.015.
Values may be sent and summed in bfloat16 or wider, within the bound.
No kernel may reach another device: no remote copies, remote signals or barrier semaphores. Data moves between devices by JAX's collectives and lax.ppermute only.
A program may use at most 256 MiB of HBM per device.

```python
import math
import jax
import jax.numpy as jnp
import numpy as np
from jax import lax

D = 512
FF = 2048
C = 128
LAT = 512
HEADS = 8
HEAD = 64
NTASK = 18
TOK = 8192
PATCH = 8115
SCENES = 32
PCROSS = 3029248
PLAT = 3150848


def cross_layout_drawn():
    return [('latents', (LAT, D)), ('task_table', (NTASK, D)), ('query_gain', (D,)), ('query_bias', (D,)), ('context_gain', (C,)), ('context_bias', (C,)), ('query_weight', (D, D)), ('key_weight', (C, D)), ('value_weight', (C, D)), ('output_weight', (D, D)), ('output_bias', (D,)), ('feed_gain', (D,)), ('feed_bias', (D,)), ('up_weight', (D, FF)), ('up_bias', (FF,)), ('down_weight', (FF, D)), ('down_bias', (D,))]


def latent_layout_drawn():
    return [('attend_gain', (D,)), ('attend_bias', (D,)), ('joint_weight', (D, 3 * D)), ('merge_weight', (D, D)), ('merge_bias', (D,)), ('feed_gain', (D,)), ('feed_bias', (D,)), ('up_weight', (D, FF)), ('up_bias', (FF,)), ('down_weight', (FF, D)), ('down_bias', (D,))]


def flat_draw(key, layout, settings, total_length):
    pieces = []
    used = 0
    for index, (name, shape) in enumerate(layout):
        extent = 1
        for length in shape:
            extent = extent * length
        scale, shift = settings[name]
        noise = jnp.clip(jax.random.normal(jax.random.fold_in(key, index), shape, jnp.float32), -5.0, 5.0)
        if name == 'latents':
            row_key = jax.random.fold_in(key, 500)
            column_key = jax.random.fold_in(key, 501)
            rows = jnp.exp(jax.random.uniform(row_key, (shape[0], 1), jnp.float32, math.log(0.3), math.log(3.0)))
            columns = jnp.exp(jax.random.uniform(column_key, (1, shape[1]), jnp.float32, 0.0, math.log(3.0)))
            noise = noise * rows * columns
        pieces.append((shift + scale * noise).reshape(extent))
        used = used + extent
    tail = jax.random.normal(jax.random.fold_in(key, 999), (total_length - used,), jnp.float32) * 0.02
    pieces.append(tail)
    return jnp.concatenate(pieces).astype(jnp.bfloat16)


def feed_settings():
    return {'feed_gain': (0.15, 1.0), 'feed_bias': (0.3, 0.0), 'up_weight': (D ** (-0.5), 0.0), 'up_bias': (0.3, 0.0), 'down_weight': (2.0 * FF ** (-0.5), 0.0), 'down_bias': (0.3, 0.0)}


def draw_cross_params(key, part):
    key = jax.random.fold_in(key, 11)
    settings = feed_settings()
    settings['latents'] = (1.0, 0.0)
    settings['task_table'] = (0.5, 0.0)
    settings['query_gain'] = (0.15, 1.0)
    settings['query_bias'] = (0.3, 0.0)
    settings['context_gain'] = (0.15, 1.0)
    settings['context_bias'] = (0.3, 0.0)
    settings['query_weight'] = ((2.0 / D) ** 0.5, 0.0)
    settings['key_weight'] = ((2.0 / C) ** 0.5, 0.0)
    settings['value_weight'] = (C ** (-0.5), 0.0)
    settings['output_weight'] = (10.0 * D ** (-0.5), 0.0)
    settings['output_bias'] = (0.3, 0.0)
    return flat_draw(key, cross_layout_drawn(), settings, PCROSS)


def draw_latent_params(key, part):
    key = jax.random.fold_in(key, 12)
    settings = feed_settings()
    settings['attend_gain'] = (0.15, 1.0)
    settings['attend_bias'] = (0.3, 0.0)
    settings['joint_weight'] = ((2.0 / D) ** 0.5, 0.0)
    settings['merge_weight'] = (3.0 * D ** (-0.5), 0.0)
    settings['merge_bias'] = (0.3, 0.0)
    return flat_draw(key, latent_layout_drawn(), settings, PLAT)


def draw_tokens(key, part):
    key = jax.random.fold_in(key, 13)
    base_key, row_key, column_key = jax.random.split(key, 3)
    base = jax.random.normal(base_key, (SCENES, TOK, C), jnp.float32)
    base = jnp.clip(base, -5.0, 5.0)
    rows = jnp.exp(jax.random.uniform(row_key, (SCENES, TOK, 1), jnp.float32, 0.0, math.log(10.0)))
    columns = jnp.exp(jax.random.uniform(column_key, (1, 1, C), jnp.float32, 0.0, math.log(3.0)))
    return (base * rows * columns).astype(jnp.bfloat16)


def draw_valid_count(key, part):
    key = jax.random.fold_in(key, 14)
    count_key, order_key = jax.random.split(key)
    counts = jax.random.randint(count_key, (SCENES,), PATCH // 4, PATCH + 1)
    order = jax.random.permutation(order_key, SCENES)
    counts = counts.at[order[0]].set(PATCH).at[order[1]].set(PATCH // 4)
    return counts.astype(jnp.int32)


def with_ends(values, rng, least, high):
    index_at = [jax.random.randint(jax.random.fold_in(rng, axis), (), 0, length) for axis, length in enumerate(values.shape)]
    longest = values.shape.index(max(values.shape))
    beside = index_at[:longest] + [(index_at[longest] + 1) % values.shape[longest]] + index_at[longest + 1:]
    return values.at[tuple(index_at)].set(least).at[tuple(beside)].set(high)


def level_of(rng, shape, cuts, least, high):
    level, own = 1.0, jax.random.fold_in(rng, 6)
    for axis_at, shards_of in cuts:
        draws = jnp.exp(jax.random.uniform(jax.random.fold_in(own, axis_at), (shards_of,), jnp.float32, least / len(cuts), high / len(cuts)))
        level = level * jnp.repeat(draws, shape[axis_at] // shards_of).reshape([-1 if axis == axis_at else 1 for axis in range(len(shape))])
    return level


def rank_table(amount, slope):
    loads = [(1 << 20) // math.isqrt(grade ** slope) + 1 for grade in range(1, amount + 1)]
    deviation = 1 + sum(loads) // (1 << 30)
    return np.cumsum(np.array([max(1, weight // deviation) for weight in loads]))


def skewed_ids(own_key, dims, count, slope):
    grid = rank_table(count, slope)
    pick = jax.random.randint(jax.random.fold_in(own_key, 1), dims, 0, int(grid[count - 1]))
    grade = jnp.searchsorted(jnp.asarray(grid, jnp.int32), pick, side="right")
    return jax.random.permutation(jax.random.fold_in(own_key, 2), count)[grade].astype(jnp.int32)


def bell_draw(key, shape, deviation, most, cuts=(), dtype=jnp.bfloat16):
    values = deviation * jax.random.normal(key, shape, jnp.float32)
    if cuts:
        values = values * level_of(key, shape, cuts, -0.22, 0.18)
    return jnp.clip(values, -most, most).astype(dtype)


def setup_inputs(seed: int = 0) -> dict:
    arg_keys = jax.random.split(jax.random.key(seed), 7)
    return {
        "tokens": draw_tokens(jax.random.fold_in(arg_keys[6], 71), 0),
        "task_id": with_ends(skewed_ids(arg_keys[1], (SCENES,), NTASK, 2), jax.random.fold_in(arg_keys[1], 3), 0, NTASK - 1).astype(jnp.int32),
        "valid_count": draw_valid_count(jax.random.fold_in(arg_keys[6], 71), 0),
        "cross_params": draw_cross_params(jax.random.fold_in(arg_keys[6], 71), 0),
        "latent_params": draw_latent_params(jax.random.fold_in(arg_keys[6], 71), 0),
        "out_grad": bell_draw(arg_keys[5], (SCENES, LAT, D), 1.0, 6.0, ((0, 32),)),
    }


epsilon = 1e-05
highest = lax.Precision.HIGHEST

@jax.custom_vjp
def low(v):
    return lax.optimization_barrier(v.astype(jnp.bfloat16)).astype(jnp.float32)

@jax.custom_vjp
def low_back(v):
    return v

def low_keep(v):
    return (low(v), None)

def low_pass(kept, grad):
    return (grad,)

def back_keep(v):
    return (v, None)

def back_low(kept, grad):
    return (low(grad),)
low.defvjp(low_keep, low_pass)
low_back.defvjp(back_keep, back_low)

def cross_layout():
    return [('latents', (LAT, D)), ('task_table', (NTASK, D)), ('query_gain', (D,)), ('query_bias', (D,)), ('context_gain', (C,)), ('context_bias', (C,)), ('query_weight', (D, D)), ('key_weight', (C, D)), ('value_weight', (C, D)), ('output_weight', (D, D)), ('output_bias', (D,)), ('feed_gain', (D,)), ('feed_bias', (D,)), ('up_weight', (D, FF)), ('up_bias', (FF,)), ('down_weight', (FF, D)), ('down_bias', (D,))]

def latent_layout():
    return [('attend_gain', (D,)), ('attend_bias', (D,)), ('joint_weight', (D, 3 * D)), ('merge_weight', (D, D)), ('merge_bias', (D,)), ('feed_gain', (D,)), ('feed_bias', (D,)), ('up_weight', (D, FF)), ('up_bias', (FF,)), ('down_weight', (FF, D)), ('down_bias', (D,))]

def unpack(flat, layout):
    pieces = {}
    offset = 0
    for name, shape in layout:
        extent = 1
        for length in shape:
            extent = extent * length
        pieces[name] = flat[offset:offset + extent].reshape(shape)
        offset = offset + extent
    return pieces

def layer_norm(value, gain, bias):
    centred = value - lax.optimization_barrier(jnp.mean(value, axis=-1, keepdims=True))
    spread = lax.optimization_barrier(jnp.mean(centred * centred, axis=-1, keepdims=True))
    return centred * lax.rsqrt(spread + epsilon) * gain + bias

def matmul(left, right):
    return jnp.dot(left, right, precision=highest)

def feed_forward(hidden, params):
    normed = low(layer_norm(hidden, params['feed_gain'], params['feed_bias']))
    inner = low_back(matmul(normed, params['up_weight']) + params['up_bias'])
    active = low(jax.nn.gelu(inner, approximate=False))
    return hidden + low_back(matmul(active, params['down_weight']) + params['down_bias'])

def cross_layer(tokens, task, count, params):
    chosen = (jnp.arange(NTASK) == task).astype(jnp.float32)
    start = params['latents'] + lax.optimization_barrier(jnp.sum(chosen[:, None] * params['task_table'], axis=0))
    normed = low(layer_norm(start, params['query_gain'], params['query_bias']))
    context = low(layer_norm(tokens, params['context_gain'], params['context_bias']))
    query = low(low_back(matmul(normed, params['query_weight'])))
    keys = low(low_back(matmul(context, params['key_weight'])))
    values = low(low_back(matmul(context, params['value_weight'])))
    scores = low_back(matmul(query, keys.T) * D ** (-0.5))
    place = jnp.arange(TOK)
    valid = (place < count) | (place >= PATCH)
    scores = jnp.where(valid[None, :], scores, -1e+30)
    weights = jax.nn.softmax(scores, axis=-1)
    mixed = low(low_back(matmul(low(weights), values)))
    hidden = start + low_back(matmul(mixed, params['output_weight']) + params['output_bias'])
    return feed_forward(hidden, params)

def latent_layer(hidden, params):
    normed = low(layer_norm(hidden, params['attend_gain'], params['attend_bias']))
    joint = low(low_back(matmul(normed, params['joint_weight'])))
    split = joint.reshape(LAT, 3, HEADS, HEAD)
    scores = low_back(jnp.einsum('qhd,khd->hqk', split[:, 0], split[:, 1], precision=highest) * HEAD ** (-0.5))
    weights = jax.nn.softmax(scores, axis=-1)
    mixed = jnp.einsum('hqk,khd->qhd', low(weights), split[:, 2], precision=highest).reshape(LAT, D)
    mixed = low(low_back(mixed))
    after = hidden + low_back(matmul(mixed, params['merge_weight']) + params['merge_bias'])
    return feed_forward(after, params)

def forward(tokens, cross_flat, latent_flat, task, count):
    first = cross_layer(tokens, task, count, unpack(cross_flat, cross_layout()))
    return latent_layer(first, unpack(latent_flat, latent_layout()))

def reference(tokens, task_id, valid_count, cross_params, latent_params, out_grad):
    cross_flat = cross_params.astype(jnp.float32)
    latent_flat = latent_params.astype(jnp.float32)

    def scene_step(totals, items):
        scene_tokens, task, count, cotangent = items

        def local(scene, cross_part, latent_part):
            return forward(scene, cross_part, latent_part, task, count)
        result, backward = jax.vjp(local, scene_tokens.astype(jnp.float32), cross_flat, latent_flat)
        scene_grad, cross_part_grad, latent_part_grad = backward(cotangent.astype(jnp.float32))
        return ((totals[0] + cross_part_grad, totals[1] + latent_part_grad), (result.astype(jnp.bfloat16), scene_grad))
    init = (jnp.zeros_like(cross_flat), jnp.zeros_like(latent_flat))
    (cross_total, latent_total), (latents_out, token_grad) = lax.scan(scene_step, init, (tokens, task_id, valid_count, out_grad))
    return (latents_out, token_grad, cross_total, latent_total)
```

```python
import functools
import math
import types

import jax
import jax.numpy as jnp
from jax import lax
from jax.experimental import pallas as pl
from jax.experimental.pallas import tpu as pltpu
from jax.sharding import PartitionSpec as P

D = 512
FF = 2048
C = 128
LAT = 512
HEADS = 8
HEAD = 64
NTASK = 18
LANG = 77
LANES = 128
TILE = 16
UNIT = TILE * LANES
BLOCK = 1024
AXES = ("gx", "gy", "gz")

epsilon = 1e-05
negative = -1e30
LOG2E = math.log2(math.e)
bf16 = jnp.bfloat16
f32 = jnp.float32
VMEM_LIMIT = 60 * 1024 * 1024


def layout_of(**shapes):
    table = {}
    row = 0
    for name, dims in shapes.items():
        table[name] = (row, dims)
        row += math.prod(dims) // LANES
    return types.SimpleNamespace(**table), row


CROSS, CROSS_ROWS = layout_of(
    latents=(LAT, D),
    task_table=(NTASK, D),
    query_gain=(D,),
    query_bias=(D,),
    context_gain=(C,),
    context_bias=(C,),
    query_weight=(D, D),
    key_weight=(C, D),
    value_weight=(C, D),
    output_weight=(D, D),
    output_bias=(D,),
    feed_gain=(D,),
    feed_bias=(D,),
    up_weight=(D, FF),
    up_bias=(FF,),
    down_weight=(FF, D),
    down_bias=(D,),
)
LATENT, LATENT_ROWS = layout_of(
    attend_gain=(D,),
    attend_bias=(D,),
    joint_weight=(D, 3 * D),
    merge_weight=(D, D),
    merge_bias=(D,),
    feed_gain=(D,),
    feed_bias=(D,),
    up_weight=(D, FF),
    up_bias=(FF,),
    down_weight=(FF, D),
    down_bias=(D,),
)


def vectors_of(table):
    return [place for place in vars(table).values() if len(place[1]) == 1]


class Windows:
    def __init__(self, total, devices):
        self.total = total
        self.devices = devices
        self.shard = total // devices
        starts = [self.shard * d for d in range(devices)]
        self.first = [s // UNIT * TILE for s in starts]
        self.phase = [s % UNIT for s in starts]
        self.rows = max(-(-(p + self.shard) // UNIT) * TILE for p in self.phase)
        self.padded = max(f + self.rows for f in self.first)
        self.full = -(-total // UNIT) * TILE
        self.shard_rows = -(-self.shard // (8 * LANES)) * 8


def dot(left, right):
    return jnp.dot(left, right, preferred_element_type=f32)


def dot_nt(left, right):
    return lax.dot_general(left, right, (((1,), (1,)), ((), ())), preferred_element_type=f32)


def dot_tn(left, right):
    return lax.dot_general(left, right, (((0,), (0,)), ((), ())), preferred_element_type=f32)


def split(value, axis):
    high = value.astype(bf16)
    low = (value - high.astype(f32)).astype(bf16)
    return jnp.concatenate([high, low], axis=axis)


def normalise(value):
    centred = value - jnp.mean(value, axis=-1, keepdims=True)
    rstd = lax.rsqrt(jnp.mean(centred * centred, axis=-1, keepdims=True) + epsilon)
    return centred * rstd, rstd


def normalise_back(grad, unit, rstd, gain):
    inner = grad * gain
    return rstd * (
        inner
        - jnp.mean(inner, axis=-1, keepdims=True)
        - unit * jnp.mean(inner * unit, axis=-1, keepdims=True)
    )


def column_sum(value):
    return jnp.sum(value, axis=0, keepdims=True)


def vmem_specs(count):
    return [pl.BlockSpec(memory_space=pltpu.VMEM)] * count


def shape(dims, dtype):
    return jax.ShapeDtypeStruct(dims, dtype)


def call(kernel, name, outs, inputs, scratch=(), smem=0, flops=0, moved=0):
    specs = [pl.BlockSpec(memory_space=pltpu.SMEM)] * smem + vmem_specs(len(inputs) - smem)
    return pl.pallas_call(
        kernel,
        name=name,
        out_shape=outs,
        in_specs=specs,
        out_specs=jax.tree.map(lambda _: pl.BlockSpec(memory_space=pltpu.VMEM), outs),
        scratch_shapes=list(scratch),
        compiler_params=pltpu.CompilerParams(vmem_limit_bytes=VMEM_LIMIT),
        cost_estimate=pl.CostEstimate(flops=flops, bytes_accessed=moved, transcendentals=0),
    )(*inputs)


def place_kernel(shift_ref, shard_ref, out_ref):
    rows = shard_ref.shape[0]
    down, across = shift_ref[0] // LANES, shift_ref[0] % LANES
    value = shard_ref[...].astype(f32)
    turned = pltpu.roll(value, across, axis=1)
    above = pltpu.roll(turned, 1, axis=0)
    lane = lax.broadcasted_iota(jnp.int32, (rows, LANES), 1)
    out_ref[...] = pltpu.roll(jnp.where(lane < across, above, turned), down, axis=0).astype(bf16)


def place(shard, windows, index):
    rows = windows.rows
    padded = jnp.pad(shard, (0, rows * LANES - windows.shard)).reshape(rows, LANES)
    shift = (windows.shard * index) % UNIT
    return call(place_kernel, "place", shape((rows, LANES), bf16), [shift.reshape(1), padded], smem=1)


def extract_kernel(shift_ref, window_ref, out_ref):
    rows = window_ref.shape[0]
    down, across = shift_ref[0] // LANES, shift_ref[0] % LANES
    value = window_ref[...].astype(f32)
    turned = pltpu.roll(value, lax.rem(LANES - across, LANES), axis=1)
    below = pltpu.roll(turned, rows - 1, axis=0)
    lane = lax.broadcasted_iota(jnp.int32, (rows, LANES), 1)
    merged = pltpu.roll(
        jnp.where(lane < LANES - across, turned, below), lax.rem(rows - down, rows), axis=0
    )
    out_ref[...] = merged[: out_ref.shape[0]]


def extract(window, windows, index):
    shift = (windows.shard * index) % UNIT
    rows = min(windows.shard_rows, windows.rows)
    found = call(
        extract_kernel, "extract", shape((rows, LANES), f32), [shift.reshape(1), window], smem=1
    )
    return found.reshape(-1)[: windows.shard]


def assemble(gathered_ref, flat_ref, windows):
    rows = windows.rows
    for d in range(windows.devices):
        first = windows.first[d]
        last = windows.first[d + 1] if d + 1 < windows.devices else windows.full - TILE
        block = gathered_ref[d * rows : d * rows + last + TILE - first, :].astype(f32)
        if windows.phase[d]:
            flat_ref[first : first + TILE, :] += block[:TILE]
            flat_ref[first + TILE : last + TILE, :] = block[TILE:]
        else:
            flat_ref[first : last + TILE, :] = block


def relay(flat_ref, place, out_ref):
    first, (rows, columns) = place
    chunks = columns // LANES
    step = 64

    def body(index, carry):
        begin = pl.multiple_of(index * step, step)
        for chunk in range(chunks):
            part = flat_ref[pl.ds(first + begin * chunks + chunk, step, stride=chunks), :]
            out_ref[pl.ds(begin, step), chunk * LANES : (chunk + 1) * LANES] = part.astype(out_ref.dtype)
        return carry

    lax.fori_loop(0, rows // step, body, 0)


def relay_vectors(flat_ref, table, out_ref):
    for index, (first, dims) in enumerate(vectors_of(table)):
        for chunk in range(dims[0] // LANES):
            out_ref[index : index + 1, chunk * LANES : (chunk + 1) * LANES] = flat_ref[
                first + chunk : first + chunk + 1, :
            ]


def unpack_cross_kernel(windows, task_ref, gathered_ref, vectors_ref, start_ref, query_ref, key_ref,
                        value_ref, output_ref, up_ref, down_ref, flat_ref):
    assemble(gathered_ref, flat_ref, windows)
    relay_vectors(flat_ref, CROSS, vectors_ref)
    chunks = D // LANES
    first, unused = CROSS.task_table
    base = first + task_ref[0] * chunks
    relay(flat_ref, CROSS.latents, start_ref)
    for chunk in range(chunks):
        row = flat_ref[pl.ds(base + chunk, 1), :]
        start_ref[:, chunk * LANES : (chunk + 1) * LANES] += row
    relay(flat_ref, CROSS.query_weight, query_ref)
    relay(flat_ref, CROSS.key_weight, key_ref)
    relay(flat_ref, CROSS.value_weight, value_ref)
    relay(flat_ref, CROSS.output_weight, output_ref)
    relay(flat_ref, CROSS.up_weight, up_ref)
    relay(flat_ref, CROSS.down_weight, down_ref)


def unpack_cross(gathered, task, windows):
    outs = [
        shape((16, FF), f32), shape((LAT, D), f32), shape((D, D), bf16), shape((C, D), bf16),
        shape((C, D), bf16), shape((D, D), bf16), shape((D, FF), bf16), shape((FF, D), bf16),
    ]
    return call(
        functools.partial(unpack_cross_kernel, windows), "unpack_cross", outs, [task, gathered],
        scratch=[pltpu.VMEM((windows.full, LANES), f32)], smem=1,
    )


def unpack_latent_kernel(windows, gathered_ref, vectors_ref, joint_ref, merge_ref, up_ref, down_ref,
                         flat_ref):
    assemble(gathered_ref, flat_ref, windows)
    relay_vectors(flat_ref, LATENT, vectors_ref)
    relay(flat_ref, LATENT.joint_weight, joint_ref)
    relay(flat_ref, LATENT.merge_weight, merge_ref)
    relay(flat_ref, LATENT.up_weight, up_ref)
    relay(flat_ref, LATENT.down_weight, down_ref)


def unpack_latent(gathered, windows):
    outs = [
        shape((8, FF), f32), shape((D, 3 * D), bf16), shape((D, D), bf16), shape((D, FF), bf16),
        shape((FF, D), bf16),
    ]
    return call(
        functools.partial(unpack_latent_kernel, windows), "unpack_latent", outs, [gathered],
        scratch=[pltpu.VMEM((windows.full, LANES), f32)],
    )


def put(flat_ref, first, columns, row, value, column=0):
    chunks = columns // LANES
    rows = value.shape[0]
    for chunk in range(value.shape[1] // LANES):
        begin = first + row * chunks + column // LANES + chunk
        flat_ref[pl.ds(begin, rows, stride=chunks), :] = value[:, chunk * LANES : (chunk + 1) * LANES]


def put_vector(flat_ref, first, value, column=0):
    for chunk in range(value.shape[1] // LANES):
        row = first + column // LANES + chunk
        flat_ref[row : row + 1, :] = value[:, chunk * LANES : (chunk + 1) * LANES]


def to_windows(flat_ref, out_ref, windows):
    rows = windows.rows
    for d in range(windows.devices):
        first = windows.first[d]
        out_ref[d * rows : (d + 1) * rows, :] = flat_ref[first : first + rows, :].astype(bf16)


def clear_tail(flat_ref, used):
    total = flat_ref.shape[0]
    flat_ref[used:total, :] = jnp.zeros((total - used, LANES), f32)


def gelu_and_slope(value):
    half = 0.5 + 0.5 * lax.erf(value * math.sqrt(0.5))
    density = jnp.exp2(value * value * (-0.5 * LOG2E)) * (1.0 / math.sqrt(2.0 * math.pi))
    return value * half, half + value * density


def feed_forward(hidden, gain, bias, up_ref, up_bias, down_ref, down_bias, normed_ref, active_ref, slope_ref):
    unit, rstd = normalise(hidden)
    normed_ref[...] = (unit * gain + bias).astype(bf16)
    step = 256
    for begin in range(0, FF, step):
        inner = dot(normed_ref[...], up_ref[:, begin : begin + step]) + up_bias[:, begin : begin + step]
        active, slope = gelu_and_slope(inner)
        active_ref[:, begin : begin + step] = active.astype(bf16)
        slope_ref[:, begin : begin + step] = slope.astype(bf16)
    return hidden + (dot(active_ref[...], down_ref[...]) + down_bias)


def feed_backward(grad, hidden, gain, up_ref, down_ref, normed_ref, active_ref, slope_ref, flat_ref, table):
    unit, rstd = normalise(hidden)
    branch = grad.astype(bf16)
    put_vector(flat_ref, table.down_bias[0], column_sum(branch.astype(f32)))
    step = 256
    total = None
    normed = normed_ref[...]
    for begin in range(0, FF, step):
        put(flat_ref, table.down_weight[0], D, begin, dot_tn(active_ref[:, begin : begin + step], branch))
        active_grad = dot_nt(branch, down_ref[begin : begin + step, :])
        inner = (active_grad * slope_ref[:, begin : begin + step].astype(f32)).astype(bf16)
        slope_ref[:, begin : begin + step] = inner
        put_vector(flat_ref, table.up_bias[0], column_sum(inner.astype(f32)), begin)
        put(flat_ref, table.up_weight[0], FF, 0, dot_tn(normed, inner), begin)
    normed_grad = dot_nt(slope_ref[...], up_ref[...])
    put_vector(flat_ref, table.feed_gain[0], column_sum(normed_grad * unit))
    put_vector(flat_ref, table.feed_bias[0], column_sum(normed_grad))
    return grad + normalise_back(normed_grad, unit, rstd, gain)


def vector(vectors_ref, table, place):
    index = vectors_of(table).index(place)
    return vectors_ref[index : index + 1, : place[1][0]]


def block_kinds(count, begin, block, total):
    language = total - LANG
    end = begin + block
    some = (begin < count) | (end > language)
    full = (end <= count) | (count >= language) | (begin >= language)
    return some, full


def masked(scores, count, begin, total):
    place = begin + lax.broadcasted_iota(jnp.int32, (scores.shape[0], 1), 0)
    valid = (place < count) | (place >= total - LANG)
    return jnp.where(valid, scores, negative)


def cross_forward_kernel(count_ref, tokens_ref, start_ref, vectors_ref, wq_ref, wk_ref, wv_ref, wo_ref,
                         up_ref, down_ref,
                         normedq_ref, query_ref, keyed_ref, mixture_ref, lse_ref, hidden_ref, normed_ref,
                         active_ref, slope_ref, out_ref,
                         scores_ref, acc_ref, max_ref, sum_ref):
    total = tokens_ref.shape[0]
    count = count_ref[0]
    start = start_ref[...]
    unit, rstd = normalise(start)
    normedq_ref[...] = (
        unit * vector(vectors_ref, CROSS, CROSS.query_gain) + vector(vectors_ref, CROSS, CROSS.query_bias)
    ).astype(bf16)
    query_ref[...] = dot(normedq_ref[...], wq_ref[...]).astype(bf16)
    keyed_ref[...] = dot_nt(query_ref[...], wk_ref[...]) * D ** (-0.5)
    keyed = split(keyed_ref[...] * LOG2E, 1)
    gain = vector(vectors_ref, CROSS, CROSS.context_gain)
    bias = vector(vectors_ref, CROSS, CROSS.context_bias)
    max_ref[...] = jnp.full(max_ref.shape, negative, f32)
    sum_ref[...] = jnp.zeros(sum_ref.shape, f32)
    acc_ref[...] = jnp.zeros(acc_ref.shape, f32)
    block = scores_ref.shape[0]

    def visit(index, carry):
        begin = pl.multiple_of(index * block, block)
        some, full = block_kinds(count, begin, block, total)

        @pl.when(some)
        def _():
            unit, rstd = normalise(tokens_ref[pl.ds(begin, block), :].astype(f32))
            context = (unit * gain + bias).astype(bf16)
            scores_ref[...] = dot_nt(jnp.concatenate([context, context], axis=1), keyed)

            @pl.when(jnp.logical_not(full))
            def _():
                scores_ref[...] = masked(scores_ref[...], count, begin, total)

            old = max_ref[...]
            newest = jnp.maximum(old, jnp.max(scores_ref[...], axis=0, keepdims=True))
            weights = jnp.exp2(scores_ref[...] - newest)
            fade = jnp.exp2(old - newest)
            max_ref[...] = newest
            sum_ref[...] = sum_ref[...] * fade + column_sum(weights)
            acc_ref[...] = acc_ref[...] * fade + dot_tn(context, weights.astype(bf16))

        return carry

    lax.fori_loop(0, total // block, visit, 0)
    totals = sum_ref[...]
    lse_ref[...] = max_ref[...] + jnp.log2(totals)
    mixture_ref[...] = acc_ref[...] * (1.0 / totals)
    values = jnp.concatenate([wv_ref[...], wv_ref[...]], axis=0)
    attended = dot_tn(split(mixture_ref[...], 0), values)
    hidden_ref[...] = start + (
        dot(attended.astype(bf16), wo_ref[...]) + vector(vectors_ref, CROSS, CROSS.output_bias)
    )
    out_ref[...] = feed_forward(
        hidden_ref[...], vector(vectors_ref, CROSS, CROSS.feed_gain), vector(vectors_ref, CROSS, CROSS.feed_bias),
        up_ref, vector(vectors_ref, CROSS, CROSS.up_bias), down_ref, vector(vectors_ref, CROSS, CROSS.down_bias),
        normed_ref, active_ref, slope_ref,
    )


def cross_forward(count, tokens, start, vectors, wq, wk, wv, wo, up, down):
    block = min(BLOCK, tokens.shape[0])
    outs = [
        shape((LAT, D), bf16), shape((LAT, D), bf16), shape((LAT, C), f32), shape((C, LAT), f32),
        shape((1, LAT), f32), shape((LAT, D), f32), shape((LAT, D), bf16), shape((LAT, FF), bf16),
        shape((LAT, FF), bf16), shape((LAT, D), f32),
    ]
    scratch = [
        pltpu.VMEM((block, LAT), f32), pltpu.VMEM((C, LAT), f32), pltpu.VMEM((1, LAT), f32),
        pltpu.VMEM((1, LAT), f32),
    ]
    return call(
        cross_forward_kernel, "cross_forward", outs,
        [count, tokens, start, vectors, wq, wk, wv, wo, up, down], scratch=scratch, smem=1,
        flops=15_000_000_000, moved=16_000_000,
    )


def pair_mask(value, side):
    lane = lax.broadcasted_iota(jnp.int32, (1, LANES), 1)
    keep = (lane < HEAD) if side == 0 else (lane >= HEAD)
    return jnp.where(keep, value, jnp.zeros_like(value))


def latent_kernel(windows, hidden_ref, cotangent_ref, vectors_ref, joint_w_ref, merge_ref, up_ref, down_ref,
                  out_ref, grad_ref, windows_ref,
                  flat_ref, probs_ref, joint_ref, mixed_ref, after_ref, normedl_ref, normed_ref, active_ref,
                  slope_ref, query_grad_ref, joint_grad_ref):
    gain = vector(vectors_ref, LATENT, LATENT.attend_gain)
    unit, rstd = normalise(hidden_ref[...])
    normedl_ref[...] = (unit * gain + vector(vectors_ref, LATENT, LATENT.attend_bias)).astype(bf16)
    joint_ref[...] = dot(normedl_ref[...], joint_w_ref[...]).astype(bf16)
    scale = HEAD ** (-0.5)
    for pair in range(HEADS // 2):
        lanes = slice(pair * LANES, (pair + 1) * LANES)
        query = joint_ref[:, lanes]
        keys = joint_ref[:, D + pair * LANES : D + (pair + 1) * LANES]
        values = joint_ref[:, 2 * D + pair * LANES : 2 * D + (pair + 1) * LANES]
        mixed = None
        for side in range(2):
            scores = dot_nt(pair_mask(keys, side), query) * (scale * LOG2E)
            weights = jnp.exp2(scores - jnp.max(scores, axis=0, keepdims=True))
            weights = weights * (1.0 / column_sum(weights))
            probs_ref[2 * pair + side] = weights
            part = dot_tn(pair_mask(values, side), weights.astype(bf16))
            mixed = part if mixed is None else mixed + part
        mixed_ref[lanes, :] = mixed.astype(bf16)
    after_ref[...] = hidden_ref[...] + (
        dot_tn(mixed_ref[...], merge_ref[...]) + vector(vectors_ref, LATENT, LATENT.merge_bias)
    )
    feed_gain = vector(vectors_ref, LATENT, LATENT.feed_gain)
    out_ref[...] = feed_forward(
        after_ref[...], feed_gain, vector(vectors_ref, LATENT, LATENT.feed_bias), up_ref,
        vector(vectors_ref, LATENT, LATENT.up_bias), down_ref, vector(vectors_ref, LATENT, LATENT.down_bias),
        normed_ref, active_ref, slope_ref,
    ).astype(bf16)

    clear_tail(flat_ref, LATENT_ROWS)
    after_grad = feed_backward(
        cotangent_ref[...].astype(f32), after_ref[...], feed_gain, up_ref, down_ref, normed_ref, active_ref,
        slope_ref, flat_ref, LATENT,
    )
    branch = after_grad.astype(bf16)
    put(flat_ref, LATENT.merge_weight[0], D, 0, dot(mixed_ref[...], branch))
    put_vector(flat_ref, LATENT.merge_bias[0], column_sum(branch.astype(f32)))
    mixed_grad = dot_nt(branch, merge_ref[...]).astype(bf16)
    for pair in range(HEADS // 2):
        lanes = slice(pair * LANES, (pair + 1) * LANES)
        query = joint_ref[:, lanes]
        keys = joint_ref[:, D + pair * LANES : D + (pair + 1) * LANES]
        values = joint_ref[:, 2 * D + pair * LANES : 2 * D + (pair + 1) * LANES]
        grads = mixed_grad[:, lanes]
        query_part = key_part = value_part = None
        for side in range(2):
            probs = probs_ref[2 * pair + side]
            part = dot(probs.astype(bf16), pair_mask(grads, side))
            value_part = part if side == 0 else value_part + part
            probs_grad = dot_nt(pair_mask(values, side), grads)
            delta = column_sum(probs * probs_grad)
            scores_grad = (probs * (probs_grad - delta)).astype(bf16)
            part = dot(scores_grad, pair_mask(query, side))
            key_part = part if side == 0 else key_part + part
            part = dot_tn(pair_mask(keys, side), scores_grad)
            query_part = part if side == 0 else query_part + part
        query_grad_ref[lanes, :] = query_part * scale
        joint_grad_ref[:, D + pair * LANES : D + (pair + 1) * LANES] = (key_part * scale).astype(bf16)
        joint_grad_ref[:, 2 * D + pair * LANES : 2 * D + (pair + 1) * LANES] = value_part.astype(bf16)
    joint_grad_ref[:, :D] = query_grad_ref[...].T.astype(bf16)
    put(flat_ref, LATENT.joint_weight[0], 3 * D, 0, dot_tn(normedl_ref[...], joint_grad_ref[...]))
    normed_grad = dot_nt(joint_grad_ref[...], joint_w_ref[...])
    put_vector(flat_ref, LATENT.attend_gain[0], column_sum(normed_grad * unit))
    put_vector(flat_ref, LATENT.attend_bias[0], column_sum(normed_grad))
    grad_ref[...] = after_grad + normalise_back(normed_grad, unit, rstd, gain)
    to_windows(flat_ref, windows_ref, windows)


def latent_layer(hidden, cotangent, vectors, joint, merge, up, down, windows):
    outs = [
        shape((LAT, D), bf16), shape((LAT, D), f32),
        shape((windows.devices * windows.rows, LANES), bf16),
    ]
    scratch = [
        pltpu.VMEM((windows.padded, LANES), f32), pltpu.VMEM((HEADS, LAT, LAT), f32),
        pltpu.VMEM((LAT, 3 * D), bf16), pltpu.VMEM((D, LAT), bf16), pltpu.VMEM((LAT, D), f32),
        pltpu.VMEM((LAT, D), bf16), pltpu.VMEM((LAT, D), bf16), pltpu.VMEM((LAT, FF), bf16),
        pltpu.VMEM((LAT, FF), bf16), pltpu.VMEM((D, LAT), f32), pltpu.VMEM((LAT, 3 * D), bf16),
    ]
    return call(
        functools.partial(latent_kernel, windows), "latent_layer", outs,
        [hidden, cotangent, vectors, joint, merge, up, down], scratch=scratch,
        flops=20_000_000_000, moved=16_000_000,
    )


def cross_backward_kernel(windows, count_ref, task_ref, tokens_ref, grad_ref, start_ref, vectors_ref, wq_ref,
                          wk_ref, wv_ref, wo_ref, up_ref, down_ref, normedq_ref, query_ref, keyed_ref,
                          mixture_ref, lse_ref, hidden_ref, normed_ref, active_ref, saved_slope_ref,
                          token_grad_ref, windows_ref,
                          flat_ref, slope_ref, scores_ref, acc_ref, gains_ref):
    total = tokens_ref.shape[0]
    count = count_ref[0]
    clear_tail(flat_ref, CROSS_ROWS)
    slope_ref[...] = saved_slope_ref[...]
    hidden_grad = feed_backward(
        grad_ref[...], hidden_ref[...], vector(vectors_ref, CROSS, CROSS.feed_gain), up_ref, down_ref, normed_ref,
        active_ref, slope_ref, flat_ref, CROSS,
    )
    branch = hidden_grad.astype(bf16)
    values = jnp.concatenate([wv_ref[...], wv_ref[...]], axis=0)
    mixture = split(mixture_ref[...], 0)
    attended = dot_tn(mixture, values)
    put(flat_ref, CROSS.output_weight[0], D, 0, dot_tn(attended.astype(bf16), branch))
    put_vector(flat_ref, CROSS.output_bias[0], column_sum(branch.astype(f32)))
    attended_grad = dot_nt(branch, wo_ref[...]).astype(bf16)
    both = dot(mixture, attended_grad)
    put(flat_ref, CROSS.value_weight[0], D, 0, both[:C] + both[C:])
    valued = split(dot_nt(attended_grad, wv_ref[...]), 1)
    delta = column_sum((attended_grad.astype(f32) * attended).T)
    lse = lse_ref[...]
    keyed = split(keyed_ref[...] * LOG2E, 1)
    paired = split(keyed_ref[...], 1)
    gain = vector(vectors_ref, CROSS, CROSS.context_gain)
    bias = vector(vectors_ref, CROSS, CROSS.context_bias)
    acc_ref[...] = jnp.zeros(acc_ref.shape, f32)
    gains_ref[...] = jnp.zeros(gains_ref.shape, f32)
    block = scores_ref.shape[0]

    def visit(index, carry):
        begin = pl.multiple_of(index * block, block)
        some, full = block_kinds(count, begin, block, total)

        @pl.when(some)
        def _():
            unit, rstd = normalise(tokens_ref[pl.ds(begin, block), :].astype(f32))
            context = (unit * gain + bias).astype(bf16)
            twice = jnp.concatenate([context, context], axis=1)
            scores_ref[...] = dot_nt(twice, keyed)

            @pl.when(jnp.logical_not(full))
            def _():
                scores_ref[...] = masked(scores_ref[...], count, begin, total)

            probs = jnp.exp2(scores_ref[...] - lse)
            probs_grad = dot_nt(twice, valued)
            scores_grad = (probs * (probs_grad - delta)).astype(bf16)
            acc_ref[...] += dot_tn(context, scores_grad)
            wide = dot(probs.astype(bf16), valued) + dot(scores_grad, paired)
            context_grad = wide[:, :C] + wide[:, C:]
            gains_ref[0:1, :] += column_sum(context_grad * unit)
            gains_ref[1:2, :] += column_sum(context_grad)
            token_grad_ref[pl.ds(begin, block), :] = normalise_back(context_grad, unit, rstd, gain)

        @pl.when(jnp.logical_not(some))
        def _():
            token_grad_ref[pl.ds(begin, block), :] = jnp.zeros((block, C), f32)

        return carry

    lax.fori_loop(0, total // block, visit, 0)
    put_vector(flat_ref, CROSS.context_gain[0], gains_ref[0:1, :])
    put_vector(flat_ref, CROSS.context_bias[0], gains_ref[1:2, :])
    pulled = split(acc_ref[...] * D ** (-0.5), 0)
    both = dot(pulled, query_ref[...])
    put(flat_ref, CROSS.key_weight[0], D, 0, both[:C] + both[C:])
    query_grad = dot_tn(pulled, jnp.concatenate([wk_ref[...], wk_ref[...]], axis=0)).astype(bf16)
    put(flat_ref, CROSS.query_weight[0], D, 0, dot_tn(normedq_ref[...], query_grad))
    normed_grad = dot_nt(query_grad, wq_ref[...])
    unit, rstd = normalise(start_ref[...])
    put_vector(flat_ref, CROSS.query_gain[0], column_sum(normed_grad * unit))
    put_vector(flat_ref, CROSS.query_bias[0], column_sum(normed_grad))
    start_grad = hidden_grad + normalise_back(normed_grad, unit, rstd, vector(vectors_ref, CROSS, CROSS.query_gain))
    put(flat_ref, CROSS.latents[0], D, 0, start_grad)
    first, unused = CROSS.task_table
    chunks = D // LANES
    flat_ref[first : first + NTASK * chunks, :] = jnp.zeros((NTASK * chunks, LANES), f32)
    sums = column_sum(start_grad)
    base = first + task_ref[0] * chunks
    for chunk in range(chunks):
        flat_ref[pl.ds(base + chunk, 1), :] = sums[:, chunk * LANES : (chunk + 1) * LANES]
    to_windows(flat_ref, windows_ref, windows)


def cross_backward(count, task, tokens, grad, start, vectors, wq, wk, wv, wo, up, down, saved, windows):
    block = min(BLOCK, tokens.shape[0])
    outs = [
        shape(tokens.shape, f32),
        shape((windows.devices * windows.rows, LANES), bf16),
    ]
    scratch = [
        pltpu.VMEM((windows.padded, LANES), f32), pltpu.VMEM((LAT, FF), bf16), pltpu.VMEM((block, LAT), f32),
        pltpu.VMEM((C, LAT), f32), pltpu.VMEM((8, C), f32),
    ]
    return call(
        functools.partial(cross_backward_kernel, windows), "cross_backward", outs,
        [count, task, tokens, grad, start, vectors, wq, wk, wv, wo, up, down, *saved], scratch=scratch,
        smem=2, flops=25_000_000_000, moved=24_000_000,
    )


def body(tokens, task_id, valid_count, cross_params, latent_params, out_grad):
    devices = lax.axis_size(AXES)
    index = lax.axis_index(AXES)
    cross_windows = Windows(cross_params.shape[0] * devices, devices)
    latent_windows = Windows(latent_params.shape[0] * devices, devices)
    cross_all = lax.all_gather(place(cross_params, cross_windows, index), AXES, axis=0, tiled=True)
    latent_all = lax.all_gather(place(latent_params, latent_windows, index), AXES, axis=0, tiled=True)
    vectors, start, wq, wk, wv, wo, up, down = unpack_cross(cross_all, task_id, cross_windows)
    *saved, first = cross_forward(valid_count, tokens[0], start, vectors, wq, wk, wv, wo, up, down)
    latent_weights = unpack_latent(latent_all, latent_windows)
    latents_out, first_grad, latent_grads = latent_layer(first, out_grad[0], *latent_weights, latent_windows)
    latent_window = lax.psum_scatter(latent_grads, AXES, scatter_dimension=0, tiled=True)
    token_grad, cross_grads = cross_backward(
        valid_count, task_id, tokens[0], first_grad, start, vectors, wq, wk, wv, wo, up, down, saved,
        cross_windows,
    )
    cross_window = lax.psum_scatter(cross_grads, AXES, scatter_dimension=0, tiled=True)
    return (
        latents_out[None],
        token_grad[None],
        extract(cross_window, cross_windows, index),
        extract(latent_window, latent_windows, index),
    )


def solution(mesh):
    return jax.shard_map(
        body,
        mesh=mesh,
        in_specs=(
            P(AXES, None, None),
            P(AXES),
            P(AXES),
            P(AXES),
            P(AXES),
            P(AXES, None, None),
        ),
        out_specs=(
            P(AXES, None, None),
            P(AXES, None, None),
            P(AXES),
            P(AXES),
        ),
        check_vma=False,
    )
```

```python
import functools
import math
import types

import jax
import jax.numpy as jnp
from jax import lax
from jax.experimental import pallas as pl
from jax.experimental.pallas import tpu as pltpu
from jax.sharding import PartitionSpec as P

D = 512
FF = 2048
C = 128
LAT = 512
HEADS = 8
HEAD = 64
NTASK = 18
LANG = 77
LANES = 128
TILE = 16
UNIT = TILE * LANES
BLOCK = 1024
AXES = ("gx", "gy", "gz")

epsilon = 1e-05
negative = -1e30
LOG2E = math.log2(math.e)
bf16 = jnp.bfloat16
f32 = jnp.float32
VMEM_LIMIT = 60 * 1024 * 1024


def layout_of(**shapes):
    table = {}
    row = 0
    for name, dims in shapes.items():
        table[name] = (row, dims)
        row += math.prod(dims) // LANES
    return types.SimpleNamespace(**table), row


CROSS, CROSS_ROWS = layout_of(
    latents=(LAT, D),
    task_table=(NTASK, D),
    query_gain=(D,),
    query_bias=(D,),
    context_gain=(C,),
    context_bias=(C,),
    query_weight=(D, D),
    key_weight=(C, D),
    value_weight=(C, D),
    output_weight=(D, D),
    output_bias=(D,),
    feed_gain=(D,),
    feed_bias=(D,),
    up_weight=(D, FF),
    up_bias=(FF,),
    down_weight=(FF, D),
    down_bias=(D,),
)
LATENT, LATENT_ROWS = layout_of(
    attend_gain=(D,),
    attend_bias=(D,),
    joint_weight=(D, 3 * D),
    merge_weight=(D, D),
    merge_bias=(D,),
    feed_gain=(D,),
    feed_bias=(D,),
    up_weight=(D, FF),
    up_bias=(FF,),
    down_weight=(FF, D),
    down_bias=(D,),
)


def vectors_of(table):
    return [place for place in vars(table).values() if len(place[1]) == 1]


class Windows:
    def __init__(self, total, devices):
        self.total = total
        self.devices = devices
        self.shard = total // devices
        starts = [self.shard * d for d in range(devices)]
        self.first = [s // UNIT * TILE for s in starts]
        self.phase = [s % UNIT for s in starts]
        self.rows = max(-(-(p + self.shard) // UNIT) * TILE for p in self.phase)
        self.padded = max(f + self.rows for f in self.first)
        self.full = -(-total // UNIT) * TILE
        self.shard_rows = -(-self.shard // (8 * LANES)) * 8

    def outs(self, parts):
        return [shape((self.devices // parts * self.rows, LANES), bf16)] * parts

    def firsts(self, owners):
        return self.shard * owners // UNIT * TILE


def dot(left, right):
    return jnp.dot(left, right, preferred_element_type=f32)


def dot_nt(left, right):
    return lax.dot_general(left, right, (((1,), (1,)), ((), ())), preferred_element_type=f32)


def dot_tn(left, right):
    return lax.dot_general(left, right, (((0,), (0,)), ((), ())), preferred_element_type=f32)


def split(value, axis):
    high = value.astype(bf16)
    low = (value - high.astype(f32)).astype(bf16)
    return jnp.concatenate([high, low], axis=axis)


def normalise(value):
    centred = value - jnp.mean(value, axis=-1, keepdims=True)
    rstd = lax.rsqrt(jnp.mean(centred * centred, axis=-1, keepdims=True) + epsilon)
    return centred * rstd, rstd


def normalise_back(grad, unit, rstd, gain):
    inner = grad * gain
    return rstd * (
        inner
        - jnp.mean(inner, axis=-1, keepdims=True)
        - unit * jnp.mean(inner * unit, axis=-1, keepdims=True)
    )


def column_sum(value):
    return jnp.sum(value, axis=0, keepdims=True)


def vmem_specs(count):
    return [pl.BlockSpec(memory_space=pltpu.VMEM)] * count


def shape(dims, dtype):
    return jax.ShapeDtypeStruct(dims, dtype)


def call(kernel, name, outs, inputs, scratch=(), smem=0, flops=0, moved=0):
    specs = [pl.BlockSpec(memory_space=pltpu.SMEM)] * smem + vmem_specs(len(inputs) - smem)
    return pl.pallas_call(
        kernel,
        name=name,
        out_shape=outs,
        in_specs=specs,
        out_specs=jax.tree.map(lambda _: pl.BlockSpec(memory_space=pltpu.VMEM), outs),
        scratch_shapes=list(scratch),
        compiler_params=pltpu.CompilerParams(vmem_limit_bytes=VMEM_LIMIT),
        cost_estimate=pl.CostEstimate(flops=flops, bytes_accessed=moved, transcendentals=0),
    )(*inputs)


def shifted(value, shift):
    down, across = shift // LANES, shift % LANES
    turned = pltpu.roll(value, across, axis=1)
    above = pltpu.roll(turned, 1, axis=0)
    lane = lax.broadcasted_iota(jnp.int32, value.shape, 1)
    return pltpu.roll(jnp.where(lane < across, above, turned), down, axis=0)


def place_kernel(shifts_ref, shards_ref, *out_refs):
    begin = 0
    for number, out_ref in enumerate(out_refs):
        rows = out_ref.shape[0]
        value = shards_ref[begin : begin + rows, :].astype(f32)
        out_ref[...] = shifted(value, shifts_ref[number]).astype(bf16)
        begin += rows


def place(shards, windows, index):
    padded = [
        jnp.pad(shard, (0, w.rows * LANES - w.shard)) for shard, w in zip(shards, windows)
    ]
    together = jnp.concatenate(padded).reshape(-1, LANES)
    shifts = jnp.stack([(w.shard * index) % UNIT for w in windows])
    outs = [shape((w.rows, LANES), bf16) for w in windows]
    return call(place_kernel, "place", outs, [shifts, together], smem=1)


def extract_kernel(count, shift_ref, *refs):
    out_ref = refs[count]
    rows = refs[0].shape[0]
    down, across = shift_ref[0] // LANES, shift_ref[0] % LANES
    value = refs[0][...].astype(f32)
    for ref in refs[1:count]:
        value += ref[...].astype(f32)
    turned = pltpu.roll(value, lax.rem(LANES - across, LANES), axis=1)
    below = pltpu.roll(turned, rows - 1, axis=0)
    lane = lax.broadcasted_iota(jnp.int32, (rows, LANES), 1)
    merged = pltpu.roll(
        jnp.where(lane < LANES - across, turned, below), lax.rem(rows - down, rows), axis=0
    )
    out_ref[...] = merged[: out_ref.shape[0]]


def extract(parts, windows, grid):
    shift = (windows.shard * grid.index) % UNIT
    rows = min(windows.shard_rows, windows.rows)
    found = call(
        functools.partial(extract_kernel, len(parts)), "extract", shape((rows, LANES), f32),
        [shift.reshape(1), *parts], smem=1,
    )
    return found.reshape(-1)[: windows.shard]


class Grid:
    def __init__(self):
        self.nx, self.ny, self.nz = (lax.axis_size(axis) for axis in AXES)
        self.nl = 2 if self.nx % 2 == 0 else 1
        self.nh = self.nx // self.nl
        self.index = lax.axis_index(AXES)

    def order(self):
        return [
            (c, h, l, y)
            for c in range(self.nz)
            for h in range(self.nh)
            for l in range(self.nl)
            for y in range(self.ny)
        ]

    def owners(self, places):
        gx, gy, gz = (lax.axis_index(axis) for axis in AXES)
        c, h, l, y = (jnp.array(column, jnp.int32) for column in zip(*places))
        high = (gx // self.nl + h) % self.nh
        low = (gx % self.nl + l) % self.nl
        return ((high * self.nl + low) * self.ny + (gy + y) % self.ny) * self.nz + (gz + c) % self.nz

    def along_core(self, value, step):
        return lax.ppermute(value, AXES[2], [(i, (i + step) % self.nz) for i in range(self.nz)])

    def along_depth(self, value, step):
        return lax.ppermute(value, AXES[1], [(i, (i + step) % self.ny) for i in range(self.ny)])

    def along_low(self, value, step):
        nl = self.nl
        return lax.ppermute(
            value, AXES[0], [(i, i // nl * nl + (i + step) % nl) for i in range(self.nx)]
        )

    def along_high(self, value, step):
        nl = self.nl
        return lax.ppermute(value, AXES[0], [(i, (i + step * nl) % self.nx) for i in range(self.nx)])


def combine_kernel(rows, groups, picks, *refs):
    inputs = refs[: sum(groups)]
    outputs = refs[len(inputs) : len(inputs) + len(picks)]
    buffers = refs[len(inputs) + len(picks) : -2]
    held, results = buffers[: len(inputs)], buffers[len(inputs) :]
    in_sem, out_sem = refs[-2:]
    starts = [sum(groups[:g]) for g in range(len(groups))]
    jobs = [
        (g, block, o, slot) for o, pick in enumerate(picks) for slot, (g, block) in enumerate(pick)
    ]
    loads = []
    for number, (g, block, o, slot) in enumerate(jobs):
        part = pl.ds(block * rows, rows)
        copies = [
            pltpu.make_async_copy(inputs[i].at[part], held[i].at[part], in_sem.at[number, i - starts[g]])
            for i in range(starts[g], starts[g] + groups[g])
        ]
        for copy in copies:
            copy.start()
        loads.append(copies)
    stores = []
    for number, (g, block, o, slot) in enumerate(jobs):
        for copy in loads[number]:
            copy.wait()
        part, target = pl.ds(block * rows, rows), pl.ds(slot * rows, rows)
        total = held[starts[g]][part, :].astype(f32)
        for i in range(starts[g] + 1, starts[g] + groups[g]):
            total += held[i][part, :].astype(f32)
        results[o][target, :] = total.astype(bf16)
        copy = pltpu.make_async_copy(results[o].at[target], outputs[o].at[target], out_sem.at[number])
        copy.start()
        stores.append(copy)
    for copy in stores:
        copy.wait()


def combine(name, rows, groups, picks):
    inputs = [value for group in groups for value in group]
    outs = [shape((len(pick) * rows, LANES), bf16) for pick in picks]
    jobs = sum(len(pick) for pick in picks)
    anywhere = pl.BlockSpec(memory_space=pl.ANY)
    moved = 2 * LANES * rows * jobs * (1 + len(groups[0]))
    return pl.pallas_call(
        functools.partial(combine_kernel, rows, tuple(len(group) for group in groups), picks),
        name=name,
        out_shape=outs,
        in_specs=[anywhere] * len(inputs),
        out_specs=[anywhere] * len(outs),
        scratch_shapes=[pltpu.VMEM(value.shape, bf16) for value in inputs + outs]
        + [
            pltpu.SemaphoreType.DMA((jobs, max(len(group) for group in groups))),
            pltpu.SemaphoreType.DMA((jobs,)),
        ],
        compiler_params=pltpu.CompilerParams(vmem_limit_bytes=VMEM_LIMIT),
        cost_estimate=pl.CostEstimate(flops=moved, bytes_accessed=moved, transcendentals=0),
    )(*inputs)


def reduce_core(parts, grid):
    return [parts[0]] + [grid.along_core(parts[c], c) for c in range(1, grid.nz)]


def reduce_plane_first(group, rows, grid):
    nh, nl, ny = grid.nh, grid.nl, grid.ny
    half = ny // 2
    place = lambda h, l, y: (0, (h * nl + l) * ny + y)
    picks = [[place(h, l, y) for h in range(nh) for y in range(half)] for l in range(nl)]
    picks += [[place(h, l, y) for l in range(nl) for y in range(half, ny)] for h in range(nh)]
    outs = combine("plane_first", rows, [group], picks)
    lows, highs = outs[:nl], outs[nl:]
    lows = [lows[0]] + [grid.along_low(lows[l], l) for l in range(1, nl)]
    highs = [highs[0]] + [grid.along_high(highs[h], h) for h in range(1, nh)]
    return lows, highs


def reduce_plane_second(lows, highs, rows, grid):
    nh, nl, ny = grid.nh, grid.nl, grid.ny
    half = ny // 2
    rest = ny - half
    picks = [[(0, h * half + y) for y in range(half)] for h in range(nh)]
    picks += [[(1, l * rest + y) for y in range(rest)] for l in range(nl)]
    outs = combine("plane_second", rows, [lows, highs], picks)
    first, second = outs[:nh], outs[nh:]
    first = [first[0]] + [grid.along_high(first[h], h) for h in range(1, nh)]
    second = [second[0]] + [grid.along_low(second[l], l) for l in range(1, nl)]
    return first, second


def reduce_depth(first, second, rows, grid):
    half = grid.ny // 2
    picks = [[(0, y)] for y in range(half)] + [[(1, y)] for y in range(grid.ny - half)]
    outs = combine("depth", rows, [first, second], picks)
    return [outs[0]] + [grid.along_depth(outs[y], y) for y in range(1, grid.ny)]


def gather_depth(window, grid):
    return [window] + [grid.along_depth(window, -y) for y in range(1, grid.ny)]


def gather_plane_first(column, grid):
    half = grid.ny // 2
    first, second = jnp.concatenate(column[:half]), jnp.concatenate(column[half:])
    lows = [first] + [grid.along_low(first, -l) for l in range(1, grid.nl)]
    highs = [second] + [grid.along_high(second, -h) for h in range(1, grid.nh)]
    return lows, highs


def gather_plane_second(lows, highs, grid):
    first, second = jnp.concatenate(lows), jnp.concatenate(highs)
    return (
        [first] + [grid.along_high(first, -h) for h in range(1, grid.nh)],
        [second] + [grid.along_low(second, -l) for l in range(1, grid.nl)],
    )


def gather_core(first, second, grid):
    pieces = first + second
    return [pieces] + [[grid.along_core(piece, -c) for piece in pieces] for c in range(1, grid.nz)]


def gather_places(grid):
    half = grid.ny // 2
    places = []
    for c in range(grid.nz):
        for h in range(grid.nh):
            places += [(c, h, l, y) for l in range(grid.nl) for y in range(half)]
        for l in range(grid.nl):
            places += [(c, h, l, y) for h in range(grid.nh) for y in range(half, grid.ny)]
    return places


def after(value, *others):
    return lax.optimization_barrier((value, *others))[0]


def assemble(firsts_ref, gathered_refs, flat_ref, windows):
    rows = windows.rows
    inner = max(windows.shard // UNIT - 1, 0) * TILE
    after = TILE + inner

    def clear(place, carry):
        first = pl.multiple_of(firsts_ref[place], TILE)
        flat_ref[pl.ds(first, TILE), :] = jnp.zeros((TILE, LANES), f32)
        flat_ref[pl.ds(first + after, rows - after), :] = jnp.zeros((rows - after, LANES), f32)
        return carry

    lax.fori_loop(0, windows.devices, clear, 0)
    place = 0
    for gathered_ref in gathered_refs:
        blocks = gathered_ref.shape[0] // rows

        def visit(block, carry, gathered_ref=gathered_ref, place=place):
            first = pl.multiple_of(firsts_ref[place + block], TILE)
            value = gathered_ref[pl.ds(pl.multiple_of(block * rows, TILE), rows), :].astype(f32)
            flat_ref[pl.ds(first, TILE), :] += value[:TILE]
            if inner:
                flat_ref[pl.ds(first + TILE, inner), :] = value[TILE:after]
            flat_ref[pl.ds(first + after, rows - after), :] += value[after:]
            return carry

        lax.fori_loop(0, blocks, visit, 0)
        place += blocks


def relay(flat_ref, place, out_ref):
    first, (rows, columns) = place
    chunks = columns // LANES
    step = 64

    def body(index, carry):
        begin = pl.multiple_of(index * step, step)
        for chunk in range(chunks):
            part = flat_ref[pl.ds(first + begin * chunks + chunk, step, stride=chunks), :]
            out_ref[pl.ds(begin, step), chunk * LANES : (chunk + 1) * LANES] = part.astype(out_ref.dtype)
        return carry

    lax.fori_loop(0, rows // step, body, 0)


def relay_vectors(flat_ref, table, out_ref):
    for index, (first, dims) in enumerate(vectors_of(table)):
        for chunk in range(dims[0] // LANES):
            out_ref[index : index + 1, chunk * LANES : (chunk + 1) * LANES] = flat_ref[
                first + chunk : first + chunk + 1, :
            ]


def unpack_cross_kernel(windows, count, firsts_ref, task_ref, *refs):
    vectors_ref, start_ref, query_ref, key_ref, value_ref, output_ref, up_ref, down_ref, flat_ref = refs[count:]
    assemble(firsts_ref, refs[:count], flat_ref, windows)
    relay_vectors(flat_ref, CROSS, vectors_ref)
    chunks = D // LANES
    first, unused = CROSS.task_table
    base = first + task_ref[0] * chunks
    relay(flat_ref, CROSS.latents, start_ref)
    for chunk in range(chunks):
        row = flat_ref[pl.ds(base + chunk, 1), :]
        start_ref[:, chunk * LANES : (chunk + 1) * LANES] += row
    relay(flat_ref, CROSS.query_weight, query_ref)
    relay(flat_ref, CROSS.key_weight, key_ref)
    relay(flat_ref, CROSS.value_weight, value_ref)
    relay(flat_ref, CROSS.output_weight, output_ref)
    relay(flat_ref, CROSS.up_weight, up_ref)
    relay(flat_ref, CROSS.down_weight, down_ref)


def unpack_cross(firsts, gathered, task, windows):
    outs = [
        shape((16, FF), f32), shape((LAT, D), f32), shape((D, D), bf16), shape((C, D), bf16),
        shape((C, D), bf16), shape((D, D), bf16), shape((D, FF), bf16), shape((FF, D), bf16),
    ]
    return call(
        functools.partial(unpack_cross_kernel, windows, len(gathered)), "unpack_cross", outs,
        [firsts, task, *gathered], scratch=[pltpu.VMEM((windows.padded, LANES), f32)], smem=2,
    )


def unpack_latent_kernel(windows, count, firsts_ref, *refs):
    vectors_ref, joint_ref, merge_ref, up_ref, down_ref, flat_ref = refs[count:]
    assemble(firsts_ref, refs[:count], flat_ref, windows)
    relay_vectors(flat_ref, LATENT, vectors_ref)
    relay(flat_ref, LATENT.joint_weight, joint_ref)
    relay(flat_ref, LATENT.merge_weight, merge_ref)
    relay(flat_ref, LATENT.up_weight, up_ref)
    relay(flat_ref, LATENT.down_weight, down_ref)


def unpack_latent(firsts, gathered, windows):
    outs = [
        shape((8, FF), f32), shape((D, 3 * D), bf16), shape((D, D), bf16), shape((D, FF), bf16),
        shape((FF, D), bf16),
    ]
    return call(
        functools.partial(unpack_latent_kernel, windows, len(gathered)), "unpack_latent", outs,
        [firsts, *gathered], scratch=[pltpu.VMEM((windows.padded, LANES), f32)], smem=1,
    )


def put(flat_ref, first, columns, row, value, column=0):
    chunks = columns // LANES
    rows = value.shape[0]
    for chunk in range(value.shape[1] // LANES):
        begin = first + row * chunks + column // LANES + chunk
        flat_ref[pl.ds(begin, rows, stride=chunks), :] = value[:, chunk * LANES : (chunk + 1) * LANES]


def put_vector(flat_ref, first, value, column=0):
    for chunk in range(value.shape[1] // LANES):
        row = first + column // LANES + chunk
        flat_ref[row : row + 1, :] = value[:, chunk * LANES : (chunk + 1) * LANES]


def to_windows(flat_ref, firsts_ref, out_refs, windows):
    rows = windows.rows
    each = windows.devices // len(out_refs)
    for part, out_ref in enumerate(out_refs):

        def visit(place, carry):
            first = pl.multiple_of(firsts_ref[part * each + place], TILE)
            slot = pl.multiple_of(place * rows, TILE)
            out_ref[pl.ds(slot, rows), :] = flat_ref[pl.ds(first, rows), :].astype(bf16)
            return carry

        lax.fori_loop(0, each, visit, 0)


def clear_tail(flat_ref, used):
    total = flat_ref.shape[0]
    flat_ref[used:total, :] = jnp.zeros((total - used, LANES), f32)


def gelu_and_slope(value):
    half = 0.5 + 0.5 * lax.erf(value * math.sqrt(0.5))
    density = jnp.exp2(value * value * (-0.5 * LOG2E)) * (1.0 / math.sqrt(2.0 * math.pi))
    return value * half, half + value * density


def feed_forward(hidden, gain, bias, up_ref, up_bias, down_ref, down_bias, normed_ref, active_ref, slope_ref):
    unit, rstd = normalise(hidden)
    normed_ref[...] = (unit * gain + bias).astype(bf16)
    step = 256
    for begin in range(0, FF, step):
        inner = dot(normed_ref[...], up_ref[:, begin : begin + step]) + up_bias[:, begin : begin + step]
        active, slope = gelu_and_slope(inner)
        active_ref[:, begin : begin + step] = active.astype(bf16)
        slope_ref[:, begin : begin + step] = slope.astype(bf16)
    return hidden + (dot(active_ref[...], down_ref[...]) + down_bias)


def feed_backward(grad, hidden, gain, up_ref, down_ref, normed_ref, active_ref, slope_ref, flat_ref, table,
                  base=0):
    unit, rstd = normalise(hidden)
    branch = grad.astype(bf16)
    put_vector(flat_ref, table.down_bias[0] - base, column_sum(branch.astype(f32)))
    step = 256
    total = None
    normed = normed_ref[...]
    for begin in range(0, FF, step):
        put(flat_ref, table.down_weight[0] - base, D, begin, dot_tn(active_ref[:, begin : begin + step], branch))
        active_grad = dot_nt(branch, down_ref[begin : begin + step, :])
        inner = (active_grad * slope_ref[:, begin : begin + step].astype(f32)).astype(bf16)
        slope_ref[:, begin : begin + step] = inner
        put_vector(flat_ref, table.up_bias[0] - base, column_sum(inner.astype(f32)), begin)
        put(flat_ref, table.up_weight[0] - base, FF, 0, dot_tn(normed, inner), begin)
    normed_grad = dot_nt(slope_ref[...], up_ref[...])
    put_vector(flat_ref, table.feed_gain[0] - base, column_sum(normed_grad * unit))
    put_vector(flat_ref, table.feed_bias[0] - base, column_sum(normed_grad))
    return grad + normalise_back(normed_grad, unit, rstd, gain)


def vector(vectors_ref, table, place):
    index = vectors_of(table).index(place)
    return vectors_ref[index : index + 1, : place[1][0]]


def block_kinds(count, begin, block, total):
    language = total - LANG
    end = begin + block
    some = (begin < count) | (end > language)
    full = (end <= count) | (count >= language) | (begin >= language)
    return some, full


def masked(scores, count, begin, total):
    place = begin + lax.broadcasted_iota(jnp.int32, (scores.shape[0], 1), 0)
    valid = (place < count) | (place >= total - LANG)
    return jnp.where(valid, scores, negative)


def cross_forward_kernel(count_ref, tokens_ref, start_ref, vectors_ref, wq_ref, wk_ref, wv_ref, wo_ref,
                         up_ref, down_ref,
                         normedq_ref, query_ref, keyed_ref, mixture_ref, lse_ref, hidden_ref, normed_ref,
                         active_ref, slope_ref, out_ref,
                         scores_ref, acc_ref, max_ref, sum_ref):
    total = tokens_ref.shape[0]
    count = count_ref[0]
    start = start_ref[...]
    unit, rstd = normalise(start)
    normedq_ref[...] = (
        unit * vector(vectors_ref, CROSS, CROSS.query_gain) + vector(vectors_ref, CROSS, CROSS.query_bias)
    ).astype(bf16)
    query_ref[...] = dot(normedq_ref[...], wq_ref[...]).astype(bf16)
    keyed_ref[...] = dot_nt(query_ref[...], wk_ref[...]) * D ** (-0.5)
    keyed = split(keyed_ref[...] * LOG2E, 1)
    gain = vector(vectors_ref, CROSS, CROSS.context_gain)
    bias = vector(vectors_ref, CROSS, CROSS.context_bias)
    max_ref[...] = jnp.full(max_ref.shape, negative, f32)
    sum_ref[...] = jnp.zeros(sum_ref.shape, f32)
    acc_ref[...] = jnp.zeros(acc_ref.shape, f32)
    block = scores_ref.shape[0]

    def visit(index, carry):
        begin = pl.multiple_of(index * block, block)
        some, full = block_kinds(count, begin, block, total)

        @pl.when(some)
        def _():
            unit, rstd = normalise(tokens_ref[pl.ds(begin, block), :].astype(f32))
            context = (unit * gain + bias).astype(bf16)
            scores_ref[...] = dot_nt(jnp.concatenate([context, context], axis=1), keyed)

            @pl.when(jnp.logical_not(full))
            def _():
                scores_ref[...] = masked(scores_ref[...], count, begin, total)

            old = max_ref[...]
            newest = jnp.maximum(old, jnp.max(scores_ref[...], axis=0, keepdims=True))
            weights = jnp.exp2(scores_ref[...] - newest)
            fade = jnp.exp2(old - newest)
            max_ref[...] = newest
            sum_ref[...] = sum_ref[...] * fade + column_sum(weights)
            acc_ref[...] = acc_ref[...] * fade + dot_tn(context, weights.astype(bf16))

        return carry

    lax.fori_loop(0, total // block, visit, 0)
    totals = sum_ref[...]
    lse_ref[...] = max_ref[...] + jnp.log2(totals)
    mixture_ref[...] = acc_ref[...] * (1.0 / totals)
    values = jnp.concatenate([wv_ref[...], wv_ref[...]], axis=0)
    attended = dot_tn(split(mixture_ref[...], 0), values)
    hidden_ref[...] = start + (
        dot(attended.astype(bf16), wo_ref[...]) + vector(vectors_ref, CROSS, CROSS.output_bias)
    )
    out_ref[...] = feed_forward(
        hidden_ref[...], vector(vectors_ref, CROSS, CROSS.feed_gain), vector(vectors_ref, CROSS, CROSS.feed_bias),
        up_ref, vector(vectors_ref, CROSS, CROSS.up_bias), down_ref, vector(vectors_ref, CROSS, CROSS.down_bias),
        normed_ref, active_ref, slope_ref,
    )


def cross_forward(count, tokens, start, vectors, wq, wk, wv, wo, up, down):
    block = min(BLOCK, tokens.shape[0])
    outs = [
        shape((LAT, D), bf16), shape((LAT, D), bf16), shape((LAT, C), f32), shape((C, LAT), f32),
        shape((1, LAT), f32), shape((LAT, D), f32), shape((LAT, D), bf16), shape((LAT, FF), bf16),
        shape((LAT, FF), bf16), shape((LAT, D), f32),
    ]
    scratch = [
        pltpu.VMEM((block, LAT), f32), pltpu.VMEM((C, LAT), f32), pltpu.VMEM((1, LAT), f32),
        pltpu.VMEM((1, LAT), f32),
    ]
    return call(
        cross_forward_kernel, "cross_forward", outs,
        [count, tokens, start, vectors, wq, wk, wv, wo, up, down], scratch=scratch, smem=1,
        flops=15_000_000_000, moved=16_000_000,
    )


def pair_mask(value, side):
    lane = lax.broadcasted_iota(jnp.int32, (1, LANES), 1)
    keep = (lane < HEAD) if side == 0 else (lane >= HEAD)
    return jnp.where(keep, value, jnp.zeros_like(value))


def latent_kernel(windows, parts, firsts_ref, hidden_ref, cotangent_ref, vectors_ref, joint_w_ref, merge_ref,
                  up_ref, down_ref, out_ref, grad_ref, *rest):
    windows_refs, rest = rest[:parts], rest[parts:]
    (flat_ref, probs_ref, joint_ref, mixed_ref, after_ref, normedl_ref, normed_ref, active_ref, slope_ref, query_grad_ref, joint_grad_ref) = rest
    gain = vector(vectors_ref, LATENT, LATENT.attend_gain)
    unit, rstd = normalise(hidden_ref[...])
    normedl_ref[...] = (unit * gain + vector(vectors_ref, LATENT, LATENT.attend_bias)).astype(bf16)
    joint_ref[...] = dot(normedl_ref[...], joint_w_ref[...]).astype(bf16)
    scale = HEAD ** (-0.5)
    for pair in range(HEADS // 2):
        lanes = slice(pair * LANES, (pair + 1) * LANES)
        query = joint_ref[:, lanes]
        keys = joint_ref[:, D + pair * LANES : D + (pair + 1) * LANES]
        values = joint_ref[:, 2 * D + pair * LANES : 2 * D + (pair + 1) * LANES]
        mixed = None
        for side in range(2):
            scores = dot_nt(pair_mask(keys, side), query) * (scale * LOG2E)
            weights = jnp.exp2(scores - jnp.max(scores, axis=0, keepdims=True))
            weights = weights * (1.0 / column_sum(weights))
            probs_ref[2 * pair + side] = weights
            part = dot_tn(pair_mask(values, side), weights.astype(bf16))
            mixed = part if mixed is None else mixed + part
        mixed_ref[lanes, :] = mixed.astype(bf16)
    after_ref[...] = hidden_ref[...] + (
        dot_tn(mixed_ref[...], merge_ref[...]) + vector(vectors_ref, LATENT, LATENT.merge_bias)
    )
    feed_gain = vector(vectors_ref, LATENT, LATENT.feed_gain)
    out_ref[...] = feed_forward(
        after_ref[...], feed_gain, vector(vectors_ref, LATENT, LATENT.feed_bias), up_ref,
        vector(vectors_ref, LATENT, LATENT.up_bias), down_ref, vector(vectors_ref, LATENT, LATENT.down_bias),
        normed_ref, active_ref, slope_ref,
    ).astype(bf16)

    clear_tail(flat_ref, LATENT_ROWS)
    after_grad = feed_backward(
        cotangent_ref[...].astype(f32), after_ref[...], feed_gain, up_ref, down_ref, normed_ref, active_ref,
        slope_ref, flat_ref, LATENT,
    )
    branch = after_grad.astype(bf16)
    put(flat_ref, LATENT.merge_weight[0], D, 0, dot(mixed_ref[...], branch))
    put_vector(flat_ref, LATENT.merge_bias[0], column_sum(branch.astype(f32)))
    mixed_grad = dot_nt(branch, merge_ref[...]).astype(bf16)
    for pair in range(HEADS // 2):
        lanes = slice(pair * LANES, (pair + 1) * LANES)
        query = joint_ref[:, lanes]
        keys = joint_ref[:, D + pair * LANES : D + (pair + 1) * LANES]
        values = joint_ref[:, 2 * D + pair * LANES : 2 * D + (pair + 1) * LANES]
        grads = mixed_grad[:, lanes]
        query_part = key_part = value_part = None
        for side in range(2):
            probs = probs_ref[2 * pair + side]
            part = dot(probs.astype(bf16), pair_mask(grads, side))
            value_part = part if side == 0 else value_part + part
            probs_grad = dot_nt(pair_mask(values, side), grads)
            delta = column_sum(probs * probs_grad)
            scores_grad = (probs * (probs_grad - delta)).astype(bf16)
            part = dot(scores_grad, pair_mask(query, side))
            key_part = part if side == 0 else key_part + part
            part = dot_tn(pair_mask(keys, side), scores_grad)
            query_part = part if side == 0 else query_part + part
        query_grad_ref[lanes, :] = query_part * scale
        joint_grad_ref[:, D + pair * LANES : D + (pair + 1) * LANES] = (key_part * scale).astype(bf16)
        joint_grad_ref[:, 2 * D + pair * LANES : 2 * D + (pair + 1) * LANES] = value_part.astype(bf16)
    joint_grad_ref[:, :D] = query_grad_ref[...].T.astype(bf16)
    put(flat_ref, LATENT.joint_weight[0], 3 * D, 0, dot_tn(normedl_ref[...], joint_grad_ref[...]))
    normed_grad = dot_nt(joint_grad_ref[...], joint_w_ref[...])
    put_vector(flat_ref, LATENT.attend_gain[0], column_sum(normed_grad * unit))
    put_vector(flat_ref, LATENT.attend_bias[0], column_sum(normed_grad))
    grad_ref[...] = after_grad + normalise_back(normed_grad, unit, rstd, gain)
    to_windows(flat_ref, firsts_ref, windows_refs, windows)


def latent_layer(firsts, hidden, cotangent, vectors, joint, merge, up, down, windows, grid):
    outs = [shape((LAT, D), bf16), shape((LAT, D), f32)] + windows.outs(grid.nz)
    scratch = [
        pltpu.VMEM((windows.padded, LANES), f32), pltpu.VMEM((HEADS, LAT, LAT), f32),
        pltpu.VMEM((LAT, 3 * D), bf16), pltpu.VMEM((D, LAT), bf16), pltpu.VMEM((LAT, D), f32),
        pltpu.VMEM((LAT, D), bf16), pltpu.VMEM((LAT, D), bf16), pltpu.VMEM((LAT, FF), bf16),
        pltpu.VMEM((LAT, FF), bf16), pltpu.VMEM((D, LAT), f32), pltpu.VMEM((LAT, 3 * D), bf16),
    ]
    return call(
        functools.partial(latent_kernel, windows, grid.nz), "latent_layer", outs,
        [firsts, hidden, cotangent, vectors, joint, merge, up, down], scratch=scratch, smem=1,
        flops=20_000_000_000, moved=16_000_000,
    )


SPLIT = CROSS.value_weight[0] // TILE * TILE


def cross_feed_kernel(grad_ref, vectors_ref, wv_ref, wo_ref, up_ref, down_ref, mixture_ref, hidden_ref,
                      normed_ref, active_ref, saved_slope_ref,
                      hidden_grad_ref, valued_ref, delta_ref, out_ref, flat_ref, slope_ref):
    flat_ref[:TILE, :] = jnp.zeros((TILE, LANES), f32)
    clear_tail(flat_ref, CROSS_ROWS - SPLIT)
    slope_ref[...] = saved_slope_ref[...]
    hidden_grad = feed_backward(
        grad_ref[...], hidden_ref[...], vector(vectors_ref, CROSS, CROSS.feed_gain), up_ref, down_ref, normed_ref,
        active_ref, slope_ref, flat_ref, CROSS, SPLIT,
    )
    hidden_grad_ref[...] = hidden_grad
    branch = hidden_grad.astype(bf16)
    values = jnp.concatenate([wv_ref[...], wv_ref[...]], axis=0)
    mixture = split(mixture_ref[...], 0)
    attended = dot_tn(mixture, values)
    put(flat_ref, CROSS.output_weight[0] - SPLIT, D, 0, dot_tn(attended.astype(bf16), branch))
    put_vector(flat_ref, CROSS.output_bias[0] - SPLIT, column_sum(branch.astype(f32)))
    attended_grad = dot_nt(branch, wo_ref[...]).astype(bf16)
    both = dot(mixture, attended_grad)
    put(flat_ref, CROSS.value_weight[0] - SPLIT, D, 0, both[:C] + both[C:])
    valued_ref[...] = split(dot_nt(attended_grad, wv_ref[...]), 1)
    delta_ref[...] = column_sum((attended_grad.astype(f32) * attended).T)
    out_ref[...] = flat_ref[...].astype(bf16)


def cross_feed(grad, vectors, wv, wo, up, down, mixture, hidden, normed, active, slope, windows):
    rows = windows.padded - SPLIT
    outs = [
        shape((LAT, D), f32), shape((LAT, 2 * C), bf16), shape((1, LAT), f32), shape((rows, LANES), bf16),
    ]
    return call(
        cross_feed_kernel, "cross_feed", outs,
        [grad, vectors, wv, wo, up, down, mixture, hidden, normed, active, slope],
        scratch=[pltpu.VMEM((rows, LANES), f32), pltpu.VMEM((LAT, FF), bf16)],
        flops=8_000_000_000, moved=24_000_000,
    )


def cross_attend_kernel(windows, parts, firsts_ref, count_ref, task_ref, tokens_ref, hidden_grad_ref, valued_ref,
                        delta_ref, later_ref, start_ref, vectors_ref, wq_ref, wk_ref, normedq_ref, query_ref,
                        keyed_ref, lse_ref, token_grad_ref, *rest):
    windows_refs = rest[:parts]
    flat_ref, scores_ref, acc_ref, gains_ref = rest[parts:]
    total = tokens_ref.shape[0]
    count = count_ref[0]
    flat_ref[SPLIT:, :] = later_ref[...].astype(f32)
    lse, delta = lse_ref[...], delta_ref[...]
    valued = valued_ref[...]
    keyed = split(keyed_ref[...] * LOG2E, 1)
    paired = split(keyed_ref[...], 1)
    gain = vector(vectors_ref, CROSS, CROSS.context_gain)
    bias = vector(vectors_ref, CROSS, CROSS.context_bias)
    acc_ref[...] = jnp.zeros(acc_ref.shape, f32)
    gains_ref[...] = jnp.zeros(gains_ref.shape, f32)
    block = scores_ref.shape[0]

    def visit(index, carry):
        begin = pl.multiple_of(index * block, block)
        some, full = block_kinds(count, begin, block, total)

        @pl.when(some)
        def _():
            unit, rstd = normalise(tokens_ref[pl.ds(begin, block), :].astype(f32))
            context = (unit * gain + bias).astype(bf16)
            twice = jnp.concatenate([context, context], axis=1)
            scores_ref[...] = dot_nt(twice, keyed)

            @pl.when(jnp.logical_not(full))
            def _():
                scores_ref[...] = masked(scores_ref[...], count, begin, total)

            probs = jnp.exp2(scores_ref[...] - lse)
            probs_grad = dot_nt(twice, valued)
            scores_grad = (probs * (probs_grad - delta)).astype(bf16)
            acc_ref[...] += dot_tn(context, scores_grad)
            wide = dot(probs.astype(bf16), valued) + dot(scores_grad, paired)
            context_grad = wide[:, :C] + wide[:, C:]
            gains_ref[0:1, :] += column_sum(context_grad * unit)
            gains_ref[1:2, :] += column_sum(context_grad)
            token_grad_ref[pl.ds(begin, block), :] = normalise_back(context_grad, unit, rstd, gain)

        @pl.when(jnp.logical_not(some))
        def _():
            token_grad_ref[pl.ds(begin, block), :] = jnp.zeros((block, C), f32)

        return carry

    lax.fori_loop(0, total // block, visit, 0)
    put_vector(flat_ref, CROSS.context_gain[0], gains_ref[0:1, :])
    put_vector(flat_ref, CROSS.context_bias[0], gains_ref[1:2, :])
    pulled = split(acc_ref[...] * D ** (-0.5), 0)
    both = dot(pulled, query_ref[...])
    put(flat_ref, CROSS.key_weight[0], D, 0, both[:C] + both[C:])
    query_grad = dot_tn(pulled, jnp.concatenate([wk_ref[...], wk_ref[...]], axis=0)).astype(bf16)
    put(flat_ref, CROSS.query_weight[0], D, 0, dot_tn(normedq_ref[...], query_grad))
    normed_grad = dot_nt(query_grad, wq_ref[...])
    unit, rstd = normalise(start_ref[...])
    put_vector(flat_ref, CROSS.query_gain[0], column_sum(normed_grad * unit))
    put_vector(flat_ref, CROSS.query_bias[0], column_sum(normed_grad))
    gain = vector(vectors_ref, CROSS, CROSS.query_gain)
    start_grad = hidden_grad_ref[...] + normalise_back(normed_grad, unit, rstd, gain)
    put(flat_ref, CROSS.latents[0], D, 0, start_grad)
    first, unused = CROSS.task_table
    chunks = D // LANES
    flat_ref[first : first + NTASK * chunks, :] = jnp.zeros((NTASK * chunks, LANES), f32)
    sums = column_sum(start_grad)
    base = first + task_ref[0] * chunks
    for chunk in range(chunks):
        flat_ref[pl.ds(base + chunk, 1), :] = sums[:, chunk * LANES : (chunk + 1) * LANES]
    to_windows(flat_ref, firsts_ref, windows_refs, windows)


def cross_attend(firsts, count, task, tokens, hidden_grad, valued, delta, later, start, vectors, wq, wk, normedq,
                 query, keyed, lse, windows, grid):
    block = min(BLOCK, tokens.shape[0])
    outs = [shape(tokens.shape, f32)] + windows.outs(grid.nz)
    scratch = [
        pltpu.VMEM((windows.padded, LANES), f32), pltpu.VMEM((block, LAT), f32), pltpu.VMEM((C, LAT), f32),
        pltpu.VMEM((8, C), f32),
    ]
    return call(
        functools.partial(cross_attend_kernel, windows, grid.nz), "cross_attend", outs,
        [firsts, count, task, tokens, hidden_grad, valued, delta, later, start, vectors, wq, wk, normedq, query,
         keyed, lse],
        scratch=scratch, smem=3, flops=20_000_000_000, moved=24_000_000,
    )


def body(tokens, task_id, valid_count, cross_params, latent_params, out_grad):
    grid = Grid()
    devices = grid.nx * grid.ny * grid.nz
    cw = Windows(cross_params.shape[0] * devices, devices)
    lw = Windows(latent_params.shape[0] * devices, devices)
    gathered_from = grid.owners(gather_places(grid))
    scattered_to = grid.owners(grid.order())
    tokens = tokens[0]

    cross_window, latent_window = place([cross_params, latent_params], [cw, lw], grid.index)
    cross_column = gather_depth(cross_window, grid)
    latent_window = after(latent_window, *cross_column[1:])
    latent_column = gather_depth(latent_window, grid)
    pieces = gather_plane_second(*gather_plane_first(cross_column, grid), grid)
    cross_all = sum(gather_core(*pieces, grid), [])
    latent_column = [after(value, pieces[0][-1], pieces[1][-1]) for value in latent_column]
    lows, highs = gather_plane_first(latent_column, grid)
    vectors, start, wq, wk, wv, wo, up, down = unpack_cross(cw.firsts(gathered_from), cross_all, task_id, cw)
    first, second = gather_plane_second(lows, highs, grid)
    start = after(start, first[0], second[0])
    normedq, query, keyed, mixture, lse, hidden, normed, active, slope, result = cross_forward(
        valid_count, tokens, start, vectors, wq, wk, wv, wo, up, down
    )
    latent_all = sum(gather_core(first, second, grid), [])
    latent_weights = unpack_latent(lw.firsts(gathered_from), latent_all, lw)
    latents_out, result_grad, *latent_parts = latent_layer(
        lw.firsts(scattered_to), result, out_grad[0], *latent_weights, lw, grid
    )

    group = reduce_core(latent_parts, grid)
    hidden_grad, valued, delta, later = cross_feed(
        result_grad, vectors, wv, wo, up, down, mixture, hidden, normed, active, slope, cw
    )
    lows, highs = reduce_plane_first(group, lw.rows, grid)
    valued = after(valued, lows[0])
    token_grad, *cross_parts = cross_attend(
        cw.firsts(scattered_to), valid_count, task_id, tokens, hidden_grad, valued, delta, later, start, vectors,
        wq, wk, normedq, query, keyed, lse, cw, grid,
    )
    group = reduce_core(cross_parts, grid)
    lows, highs = reduce_plane_second(lows, highs, lw.rows, grid)
    latent_column = reduce_depth(lows, highs, lw.rows, grid)
    lows, highs = reduce_plane_first(group, cw.rows, grid)
    lows, highs = reduce_plane_second(lows, highs, cw.rows, grid)
    cross_column = reduce_depth(lows, highs, cw.rows, grid)
    return (
        latents_out[None],
        token_grad[None],
        extract(cross_column, cw, grid),
        extract(latent_column, lw, grid),
    )


def solution(mesh):
    return jax.shard_map(
        body,
        mesh=mesh,
        in_specs=(
            P(AXES, None, None),
            P(AXES),
            P(AXES),
            P(AXES),
            P(AXES),
            P(AXES, None, None),
        ),
        out_specs=(
            P(AXES, None, None),
            P(AXES, None, None),
            P(AXES),
            P(AXES),
        ),
        check_vma=False,
    )
```

```python
import functools
import math
import types

import jax
import jax.numpy as jnp
from jax import lax
from jax.experimental import pallas as pl
from jax.experimental.pallas import tpu as pltpu
from jax.sharding import PartitionSpec as P

D = 512
FF = 2048
C = 128
LAT = 512
HEADS = 8
HEAD = 64
NTASK = 18
LANG = 77
LANES = 128
TILE = 16
UNIT = TILE * LANES
BLOCK = 1024
AXES = ("gx", "gy", "gz")

epsilon = 1e-05
negative = -1e30
LOG2E = math.log2(math.e)
bf16 = jnp.bfloat16
f32 = jnp.float32
VMEM_LIMIT = 60 * 1024 * 1024


def layout_of(**shapes):
    table = {}
    row = 0
    for name, dims in shapes.items():
        table[name] = (row, dims)
        row += math.prod(dims) // LANES
    return types.SimpleNamespace(**table), row


CROSS, CROSS_ROWS = layout_of(
    latents=(LAT, D),
    task_table=(NTASK, D),
    query_gain=(D,),
    query_bias=(D,),
    context_gain=(C,),
    context_bias=(C,),
    query_weight=(D, D),
    key_weight=(C, D),
    value_weight=(C, D),
    output_weight=(D, D),
    output_bias=(D,),
    feed_gain=(D,),
    feed_bias=(D,),
    up_weight=(D, FF),
    up_bias=(FF,),
    down_weight=(FF, D),
    down_bias=(D,),
)
LATENT, LATENT_ROWS = layout_of(
    attend_gain=(D,),
    attend_bias=(D,),
    joint_weight=(D, 3 * D),
    merge_weight=(D, D),
    merge_bias=(D,),
    feed_gain=(D,),
    feed_bias=(D,),
    up_weight=(D, FF),
    up_bias=(FF,),
    down_weight=(FF, D),
    down_bias=(D,),
)


def vectors_of(table):
    return [place for place in vars(table).values() if len(place[1]) == 1]


class Windows:
    def __init__(self, total, devices):
        self.total = total
        self.devices = devices
        self.shard = total // devices
        starts = [self.shard * d for d in range(devices)]
        self.first = [s // UNIT * TILE for s in starts]
        self.phase = [s % UNIT for s in starts]
        self.rows = max(-(-(p + self.shard) // UNIT) * TILE for p in self.phase)
        self.padded = max(f + self.rows for f in self.first)
        self.full = -(-total // UNIT) * TILE
        self.shard_rows = -(-self.shard // (8 * LANES)) * 8

    def outs(self, parts):
        return [shape((self.devices // parts * self.rows, LANES), bf16)] * parts

    def firsts(self, owners):
        return self.shard * owners // UNIT * TILE

    def quarter(self, parts):
        return -(-self.rows // (parts * TILE)) * TILE


def dot(left, right):
    return jnp.dot(left, right, preferred_element_type=f32)


def dot_nt(left, right):
    return lax.dot_general(left, right, (((1,), (1,)), ((), ())), preferred_element_type=f32)


def dot_tn(left, right):
    return lax.dot_general(left, right, (((0,), (0,)), ((), ())), preferred_element_type=f32)


def split(value, axis):
    high = value.astype(bf16)
    low = (value - high.astype(f32)).astype(bf16)
    return jnp.concatenate([high, low], axis=axis)


def normalise(value):
    centred = value - jnp.mean(value, axis=-1, keepdims=True)
    rstd = lax.rsqrt(jnp.mean(centred * centred, axis=-1, keepdims=True) + epsilon)
    return centred * rstd, rstd


def normalise_back(grad, unit, rstd, gain):
    inner = grad * gain
    return rstd * (
        inner
        - jnp.mean(inner, axis=-1, keepdims=True)
        - unit * jnp.mean(inner * unit, axis=-1, keepdims=True)
    )


def column_sum(value):
    return jnp.sum(value, axis=0, keepdims=True)


def vmem_specs(count):
    return [pl.BlockSpec(memory_space=pltpu.VMEM)] * count


def shape(dims, dtype):
    return jax.ShapeDtypeStruct(dims, dtype)


def bytes_of(value):
    return math.prod(value.shape) * jnp.dtype(value.dtype).itemsize


def vmem_limit(*values):
    return min(sum(map(bytes_of, values)) + 16 * 2**20, VMEM_LIMIT)


def call(kernel, name, outs, inputs, scratch=(), smem=0, flops=0, moved=0, alone=True):
    specs = [pl.BlockSpec(memory_space=pltpu.SMEM)] * smem + vmem_specs(len(inputs) - smem)
    limit = VMEM_LIMIT if alone else vmem_limit(*inputs, *jax.tree.leaves(outs), *scratch)
    return pl.pallas_call(
        kernel,
        name=name,
        out_shape=outs,
        in_specs=specs,
        out_specs=jax.tree.map(lambda _: pl.BlockSpec(memory_space=pltpu.VMEM), outs),
        scratch_shapes=list(scratch),
        compiler_params=pltpu.CompilerParams(vmem_limit_bytes=limit),
        cost_estimate=pl.CostEstimate(flops=flops, bytes_accessed=moved, transcendentals=0),
    )(*inputs)


def shifted(value, shift):
    down, across = shift // LANES, shift % LANES
    turned = pltpu.roll(value, across, axis=1)
    above = pltpu.roll(turned, 1, axis=0)
    lane = lax.broadcasted_iota(jnp.int32, value.shape, 1)
    return pltpu.roll(jnp.where(lane < across, above, turned), down, axis=0)


def place_kernel(shifts_ref, shards_ref, *out_refs):
    begin = 0
    for number, out_ref in enumerate(out_refs):
        rows = out_ref.shape[0]
        value = shards_ref[begin : begin + rows, :].astype(f32)
        out_ref[...] = shifted(value, shifts_ref[number]).astype(bf16)
        begin += rows


def place(shards, windows, index):
    padded = [
        jnp.pad(shard, (0, w.rows * LANES - w.shard)) for shard, w in zip(shards, windows)
    ]
    together = jnp.concatenate(padded).reshape(-1, LANES)
    shifts = jnp.stack([(w.shard * index) % UNIT for w in windows])
    outs = [shape((w.rows, LANES), bf16) for w in windows]
    return call(place_kernel, "place", outs, [shifts, together], smem=1, alone=False)


def extract_kernel(count, shift_ref, *refs):
    out_ref, total_ref = refs[-2:]
    rows = total_ref.shape[0]
    value = refs[0][:rows, :].astype(f32)
    for ref in refs[1:count]:
        value += ref[:rows, :].astype(f32)
    total_ref[...] = value
    begin = 0
    for ref in refs[count:-2]:
        size = min(ref.shape[0], rows - begin)
        if size > 0:
            total_ref[begin : begin + size, :] += ref[:size, :].astype(f32)
        begin += ref.shape[0]
    down, across = shift_ref[0] // LANES, shift_ref[0] % LANES
    turned = pltpu.roll(total_ref[...], lax.rem(LANES - across, LANES), axis=1)
    below = pltpu.roll(turned, rows - 1, axis=0)
    lane = lax.broadcasted_iota(jnp.int32, (rows, LANES), 1)
    merged = pltpu.roll(
        jnp.where(lane < LANES - across, turned, below), lax.rem(rows - down, rows), axis=0
    )
    out_ref[...] = merged[: out_ref.shape[0]]


def extract(parts, quarters, windows, grid):
    shift = (windows.shard * grid.index) % UNIT
    rows = min(windows.shard_rows, windows.rows)
    found = call(
        functools.partial(extract_kernel, len(parts)), "extract", shape((rows, LANES), f32),
        [shift.reshape(1), *parts, *quarters], scratch=[pltpu.VMEM((windows.rows, LANES), f32)], smem=1,
        alone=False,
    )
    return found.reshape(-1)[: windows.shard]


class Grid:
    def __init__(self):
        self.nx, self.ny, self.nz = (lax.axis_size(axis) for axis in AXES)
        self.nl = 2 if self.nx % 2 == 0 else 1
        self.nh = self.nx // self.nl
        self.index = lax.axis_index(AXES)

    def order(self):
        return [
            (c, h, l, y)
            for c in range(self.nz)
            for h in range(self.nh)
            for l in range(self.nl)
            for y in range(self.ny)
        ]

    def owners(self, places):
        gx, gy, gz = (lax.axis_index(axis) for axis in AXES)
        c, h, l, y = (jnp.array(column, jnp.int32) for column in zip(*places))
        high = (gx // self.nl + h) % self.nh
        low = (gx % self.nl + l) % self.nl
        return ((high * self.nl + low) * self.ny + (gy + y) % self.ny) * self.nz + (gz + c) % self.nz

    def along_core(self, value, step):
        return lax.ppermute(value, AXES[2], [(i, (i + step) % self.nz) for i in range(self.nz)])

    def along_depth(self, value, step):
        return lax.ppermute(value, AXES[1], [(i, (i + step) % self.ny) for i in range(self.ny)])

    def along_low(self, value, step):
        nl = self.nl
        return lax.ppermute(
            value, AXES[0], [(i, i // nl * nl + (i + step) % nl) for i in range(self.nx)]
        )

    def along_high(self, value, step):
        nl = self.nl
        return lax.ppermute(value, AXES[0], [(i, (i + step * nl) % self.nx) for i in range(self.nx)])


def combine_kernel(groups, picks, *refs):
    starts = [sum(len(bases) for rows, bases in groups[:g]) for g in range(len(groups))]
    outputs = refs[sum(len(bases) for rows, bases in groups) :]
    for output, pick in zip(outputs, picks):
        row = 0
        for g, block in pick:
            rows, bases = groups[g]
            total = None
            for i, base in enumerate(bases):
                begin = base + block * rows
                part = refs[starts[g] + i][begin : begin + rows, :].astype(f32)
                total = part if total is None else total + part
            output[row : row + rows, :] = total.astype(bf16)
            row += rows


def combine(name, groups, picks):
    inputs = [array for rows, sources in groups for array, base in sources]
    kinds = tuple((rows, tuple(base for array, base in sources)) for rows, sources in groups)
    sizes = [sum(groups[g][0] for g, block in pick) for pick in picks]
    outs = [shape((size, LANES), bf16) for size in sizes]
    moved = 6 * LANES * sum(sizes)
    return call(
        functools.partial(combine_kernel, kinds, picks), name, outs, inputs, flops=moved, moved=moved, alone=False
    )


def reduce_core(parts, grid):
    return [(parts[0], 0)] + [(grid.along_core(parts[c], c), 0) for c in range(1, grid.nz)]


def first_picks(grid, g):
    nh, nl, ny = grid.nh, grid.nl, grid.ny
    half = ny // 2
    block = lambda h, l, y: (g, (h * nl + l) * ny + y)
    lows = [[block(h, l, y) for h in range(nh) for y in range(half)] for l in range(nl)]
    highs = [[block(h, l, y) for l in range(nl) for y in range(half, ny)] for h in range(nh)]
    return lows, highs


def halves(grid):
    return [grid.ny // 2, grid.ny - grid.ny // 2]


def half_order(grid):
    half = grid.ny // 2
    places = []
    for c in range(grid.nz):
        for depths in (range(half), range(half, grid.ny)):
            places += [(c, h, l, y) for h in range(grid.nh) for l in range(grid.nl) for y in depths]
    return places


def half_first_picks(grid, first_group, second_group):
    nh, nl = grid.nh, grid.nl
    half, rest = halves(grid)
    lows = [[(first_group, (h * nl + l) * half + y) for h in range(nh) for y in range(half)] for l in range(nl)]
    highs = [[(second_group, (h * nl + l) * rest + y) for l in range(nl) for y in range(rest)] for h in range(nh)]
    return lows, highs


def second_picks(grid, low_group, high_group):
    half = grid.ny // 2
    rest = grid.ny - half
    highs = [[(low_group, h * half + y) for y in range(half)] for h in range(grid.nh)]
    lows = [[(high_group, l * rest + y) for y in range(rest)] for l in range(grid.nl)]
    return highs, lows


def depth_picks(grid, first_group, second_group):
    half = grid.ny // 2
    return [(first_group, y) for y in range(half)] + [(second_group, y) for y in range(grid.ny - half)]


def send_low(arrays, grid):
    return [grid.along_low(array, l + 1) for l, array in enumerate(arrays)]


def send_high(arrays, grid):
    return [grid.along_high(array, h + 1) for h, array in enumerate(arrays)]


def send_depth(arrays, grid):
    return [grid.along_depth(array, y + 1) for y, array in enumerate(arrays)]


def at(arrays, base=0):
    return [(array, base) for array in arrays]


def reduce_first(group, rows, grid):
    lows, highs = first_picks(grid, 0)
    outs = combine("plane_first", [(rows, group)], lows + highs)
    keep_low, keep_high = outs[0], outs[grid.nl]
    return (
        at([keep_low] + send_low(outs[1 : grid.nl], grid)),
        at([keep_high] + send_high(outs[grid.nl + 1 :], grid)),
    )


def reduce_second(lows, highs, rows, grid):
    to_high, to_low = second_picks(grid, 0, 1)
    outs = combine("plane_second", [(rows, lows), (rows, highs)], to_high + to_low)
    keep_first, keep_second = outs[0], outs[grid.nh]
    return (
        at([keep_first] + send_high(outs[1 : grid.nh], grid)),
        at([keep_second] + send_low(outs[grid.nh + 1 :], grid)),
    )


def reduce_depth(first, second, rows, grid):
    outs = combine("depth", [(rows, first), (rows, second)], [[pick] for pick in depth_picks(grid, 0, 1)])
    return [outs[0]] + send_depth(outs[1:], grid)


def reduce_second_and_first(lows, highs, rows, small_groups, small_rows, grid):
    to_high, to_low = second_picks(grid, 0, 1)
    small_low, small_high = half_first_picks(grid, 2, 3)
    nh, nl, half = grid.nh, grid.nl, grid.ny // 2
    picks = [to_high[0], to_low[0], small_low[0], small_high[0]]
    picks += [to_high[h] + small_high[h] for h in range(1, nh)]
    picks += [to_low[l] + small_low[l] for l in range(1, nl)]
    outs = combine("second_and_first", [(rows, lows), (rows, highs)] + [(small_rows, group) for group in small_groups], picks)
    keep_first, keep_second, keep_low, keep_high = outs[:4]
    high = send_high(outs[4 : 3 + nh], grid)
    low = send_low(outs[3 + nh :], grid)
    first, second = at([keep_first]) + at(high), at([keep_second]) + at(low)
    lows = at([keep_low]) + at(low, (grid.ny - half) * rows)
    highs = at([keep_high]) + at(high, half * rows)
    return first, second, lows, highs


def reduce_depth_both(first, second, rows, small_first, small_second, small_rows, grid):
    groups = [(rows, first), (rows, second), (small_rows, small_first), (small_rows, small_second)]
    picks = [list(pair) for pair in zip(depth_picks(grid, 0, 1), depth_picks(grid, 2, 3))]
    outs = combine("depth_both", groups, picks)
    return [outs[0]] + send_depth(outs[1:], grid)


def quarter_owners(grid):
    gx, gy, gz = (lax.axis_index(axis) for axis in AXES)
    c, h, l, y = (jnp.array(column, jnp.int32) for column in zip(*half_order(grid)))
    quarter = (gx // grid.nl + h) % grid.nh * grid.nl + (gx % grid.nl + l) % grid.nl
    return (gy + y) % grid.ny * grid.nz + (gz + c) % grid.nz, quarter


def collect_quarters(parts, base, rows, grid):
    (own,) = combine("quarter", [(rows, at(parts, base))], [[(0, 0)]])
    zero = jnp.zeros_like(own)
    first = jnp.where(lax.axis_index(AXES[0]) == 0, own, zero)
    return [first] + [lax.ppermute(own, AXES[0], [(x, 0)]) for x in range(1, grid.nx)]


def gather_depth(window, grid):
    return [window] + [grid.along_depth(window, -y) for y in range(1, grid.ny)]


def gather_plane_first(column, grid):
    half = grid.ny // 2
    first, second = jnp.concatenate(column[:half]), jnp.concatenate(column[half:])
    lows = [first] + [grid.along_low(first, -l) for l in range(1, grid.nl)]
    highs = [second] + [grid.along_high(second, -h) for h in range(1, grid.nh)]
    return lows, highs


def gather_plane_second(lows, highs, grid):
    first, second = jnp.concatenate(lows), jnp.concatenate(highs)
    return (
        [first] + [grid.along_high(first, -h) for h in range(1, grid.nh)],
        [second] + [grid.along_low(second, -l) for l in range(1, grid.nl)],
    )


def gather_core(first, second, grid):
    pieces = first + second
    return [pieces] + [[grid.along_core(piece, -c) for piece in pieces] for c in range(1, grid.nz)]


def gather_places(grid):
    half = grid.ny // 2
    places = []
    for c in range(grid.nz):
        for h in range(grid.nh):
            places += [(c, h, l, y) for l in range(grid.nl) for y in range(half)]
        for l in range(grid.nl):
            places += [(c, h, l, y) for h in range(grid.nh) for y in range(half, grid.ny)]
    return places


def after(value, *others):
    return lax.optimization_barrier((value, *others))[0]


def assemble(firsts_ref, gathered_refs, flat_ref, windows):
    rows = windows.rows
    inner = max(windows.shard // UNIT - 1, 0) * TILE
    after = TILE + inner

    def clear(place, carry):
        first = pl.multiple_of(firsts_ref[place], TILE)
        flat_ref[pl.ds(first, TILE), :] = jnp.zeros((TILE, LANES), f32)
        flat_ref[pl.ds(first + after, rows - after), :] = jnp.zeros((rows - after, LANES), f32)
        return carry

    lax.fori_loop(0, windows.devices, clear, 0)
    place = 0
    for gathered_ref in gathered_refs:
        blocks = gathered_ref.shape[0] // rows

        def visit(block, carry, gathered_ref=gathered_ref, place=place):
            first = pl.multiple_of(firsts_ref[place + block], TILE)
            value = gathered_ref[pl.ds(pl.multiple_of(block * rows, TILE), rows), :].astype(f32)
            flat_ref[pl.ds(first, TILE), :] += value[:TILE]
            if inner:
                flat_ref[pl.ds(first + TILE, inner), :] = value[TILE:after]
            flat_ref[pl.ds(first + after, rows - after), :] += value[after:]
            return carry

        lax.fori_loop(0, blocks, visit, 0)
        place += blocks


def relay(flat_ref, place, out_ref):
    first, (rows, columns) = place
    chunks = columns // LANES
    step = 64

    def body(index, carry):
        begin = pl.multiple_of(index * step, step)
        for chunk in range(chunks):
            part = flat_ref[pl.ds(first + begin * chunks + chunk, step, stride=chunks), :]
            out_ref[pl.ds(begin, step), chunk * LANES : (chunk + 1) * LANES] = part.astype(out_ref.dtype)
        return carry

    lax.fori_loop(0, rows // step, body, 0)


def relay_vectors(flat_ref, table, out_ref):
    for index, (first, dims) in enumerate(vectors_of(table)):
        for chunk in range(dims[0] // LANES):
            out_ref[index : index + 1, chunk * LANES : (chunk + 1) * LANES] = flat_ref[
                first + chunk : first + chunk + 1, :
            ]


def unpack_cross_kernel(windows, count, firsts_ref, task_ref, *refs):
    vectors_ref, start_ref, query_ref, key_ref, value_ref, output_ref, up_ref, down_ref, flat_ref = refs[count:]
    assemble(firsts_ref, refs[:count], flat_ref, windows)
    relay_vectors(flat_ref, CROSS, vectors_ref)
    chunks = D // LANES
    first, unused = CROSS.task_table
    base = first + task_ref[0] * chunks
    relay(flat_ref, CROSS.latents, start_ref)
    for chunk in range(chunks):
        row = flat_ref[pl.ds(base + chunk, 1), :]
        start_ref[:, chunk * LANES : (chunk + 1) * LANES] += row
    relay(flat_ref, CROSS.query_weight, query_ref)
    relay(flat_ref, CROSS.key_weight, key_ref)
    relay(flat_ref, CROSS.value_weight, value_ref)
    relay(flat_ref, CROSS.output_weight, output_ref)
    relay(flat_ref, CROSS.up_weight, up_ref)
    relay(flat_ref, CROSS.down_weight, down_ref)


def unpack_cross(firsts, gathered, task, windows):
    outs = [
        shape((16, FF), f32), shape((LAT, D), f32), shape((D, D), bf16), shape((C, D), bf16),
        shape((C, D), bf16), shape((D, D), bf16), shape((D, FF), bf16), shape((FF, D), bf16),
    ]
    return call(
        functools.partial(unpack_cross_kernel, windows, len(gathered)), "unpack_cross", outs,
        [firsts, task, *gathered], scratch=[pltpu.VMEM((windows.padded, LANES), f32)], smem=2,
    )


def unpack_latent_kernel(windows, count, firsts_ref, *refs):
    vectors_ref, joint_ref, merge_ref, up_ref, down_ref, flat_ref = refs[count:]
    assemble(firsts_ref, refs[:count], flat_ref, windows)
    relay_vectors(flat_ref, LATENT, vectors_ref)
    relay(flat_ref, LATENT.joint_weight, joint_ref)
    relay(flat_ref, LATENT.merge_weight, merge_ref)
    relay(flat_ref, LATENT.up_weight, up_ref)
    relay(flat_ref, LATENT.down_weight, down_ref)


def unpack_latent(firsts, gathered, windows):
    outs = [
        shape((8, FF), f32), shape((D, 3 * D), bf16), shape((D, D), bf16), shape((D, FF), bf16),
        shape((FF, D), bf16),
    ]
    return call(
        functools.partial(unpack_latent_kernel, windows, len(gathered)), "unpack_latent", outs,
        [firsts, *gathered], scratch=[pltpu.VMEM((windows.padded, LANES), f32)], smem=1,
    )


def put(flat_ref, first, columns, row, value, column=0):
    chunks = columns // LANES
    rows = value.shape[0]
    for chunk in range(value.shape[1] // LANES):
        begin = first + row * chunks + column // LANES + chunk
        flat_ref[pl.ds(begin, rows, stride=chunks), :] = value[:, chunk * LANES : (chunk + 1) * LANES]


def put_vector(flat_ref, first, value, column=0):
    for chunk in range(value.shape[1] // LANES):
        row = first + column // LANES + chunk
        flat_ref[row : row + 1, :] = value[:, chunk * LANES : (chunk + 1) * LANES]


def to_windows(flat_ref, firsts_ref, out_refs, rows, count):
    begin = 0
    for out_ref in out_refs:
        blocks = out_ref.shape[0] // rows

        def visit(place, carry, out_ref=out_ref, begin=begin):
            first = pl.multiple_of(firsts_ref[begin + place], TILE)
            slot = pl.multiple_of(place * rows, TILE)
            out_ref[pl.ds(slot, rows), :] = flat_ref[pl.ds(first, rows), :].astype(bf16)
            return carry

        lax.fori_loop(0, blocks, visit, 0)
        begin += blocks


def clear_tail(flat_ref, used):
    total = flat_ref.shape[0]
    flat_ref[used:total, :] = jnp.zeros((total - used, LANES), f32)


def gelu_and_slope(value):
    half = 0.5 + 0.5 * lax.erf(value * math.sqrt(0.5))
    density = jnp.exp2(value * value * (-0.5 * LOG2E)) * (1.0 / math.sqrt(2.0 * math.pi))
    return value * half, half + value * density


def feed_forward(hidden, gain, bias, up_ref, up_bias, down_ref, down_bias, normed_ref, active_ref, slope_ref):
    unit, rstd = normalise(hidden)
    normed_ref[...] = (unit * gain + bias).astype(bf16)
    step = 256
    for begin in range(0, FF, step):
        inner = dot(normed_ref[...], up_ref[:, begin : begin + step]) + up_bias[:, begin : begin + step]
        active, slope = gelu_and_slope(inner)
        active_ref[:, begin : begin + step] = active.astype(bf16)
        slope_ref[:, begin : begin + step] = slope.astype(bf16)
    return hidden + (dot(active_ref[...], down_ref[...]) + down_bias)


def feed_backward(grad, hidden, gain, up_ref, down_ref, normed_ref, active_ref, slope_ref, flat_ref, table,
                  base=0):
    unit, rstd = normalise(hidden)
    branch = grad.astype(bf16)
    put_vector(flat_ref, table.down_bias[0] - base, column_sum(branch.astype(f32)))
    step = 256
    total = None
    normed = normed_ref[...]
    for begin in range(0, FF, step):
        put(flat_ref, table.down_weight[0] - base, D, begin, dot_tn(active_ref[:, begin : begin + step], branch))
        active_grad = dot_nt(branch, down_ref[begin : begin + step, :])
        inner = (active_grad * slope_ref[:, begin : begin + step].astype(f32)).astype(bf16)
        slope_ref[:, begin : begin + step] = inner
        put_vector(flat_ref, table.up_bias[0] - base, column_sum(inner.astype(f32)), begin)
        put(flat_ref, table.up_weight[0] - base, FF, 0, dot_tn(normed, inner), begin)
    normed_grad = dot_nt(slope_ref[...], up_ref[...])
    put_vector(flat_ref, table.feed_gain[0] - base, column_sum(normed_grad * unit))
    put_vector(flat_ref, table.feed_bias[0] - base, column_sum(normed_grad))
    return grad + normalise_back(normed_grad, unit, rstd, gain)


def vector(vectors_ref, table, place):
    index = vectors_of(table).index(place)
    return vectors_ref[index : index + 1, : place[1][0]]


def block_kinds(count, begin, block, total):
    language = total - LANG
    end = begin + block
    some = (begin < count) | (end > language)
    full = (end <= count) | (count >= language) | (begin >= language)
    return some, full


def masked(scores, count, begin, total):
    place = begin + lax.broadcasted_iota(jnp.int32, (scores.shape[0], 1), 0)
    valid = (place < count) | (place >= total - LANG)
    return jnp.where(valid, scores, negative)


def cross_forward_kernel(count_ref, tokens_ref, start_ref, vectors_ref, wq_ref, wk_ref, wv_ref, wo_ref,
                         up_ref, down_ref,
                         normedq_ref, query_ref, keyed_ref, mixture_ref, lse_ref, hidden_ref, normed_ref,
                         active_ref, slope_ref, out_ref,
                         scores_ref, acc_ref, max_ref, sum_ref):
    total = tokens_ref.shape[0]
    count = count_ref[0]
    start = start_ref[...]
    unit, rstd = normalise(start)
    normedq_ref[...] = (
        unit * vector(vectors_ref, CROSS, CROSS.query_gain) + vector(vectors_ref, CROSS, CROSS.query_bias)
    ).astype(bf16)
    query_ref[...] = dot(normedq_ref[...], wq_ref[...]).astype(bf16)
    keyed_ref[...] = dot_nt(query_ref[...], wk_ref[...]) * D ** (-0.5)
    keyed = split(keyed_ref[...] * LOG2E, 1)
    gain = vector(vectors_ref, CROSS, CROSS.context_gain)
    bias = vector(vectors_ref, CROSS, CROSS.context_bias)
    max_ref[...] = jnp.full(max_ref.shape, negative, f32)
    sum_ref[...] = jnp.zeros(sum_ref.shape, f32)
    acc_ref[...] = jnp.zeros(acc_ref.shape, f32)
    block = scores_ref.shape[0]

    def visit(index, carry):
        begin = pl.multiple_of(index * block, block)
        some, full = block_kinds(count, begin, block, total)

        @pl.when(some)
        def _():
            unit, rstd = normalise(tokens_ref[pl.ds(begin, block), :].astype(f32))
            context = (unit * gain + bias).astype(bf16)
            scores_ref[...] = dot_nt(jnp.concatenate([context, context], axis=1), keyed)

            @pl.when(jnp.logical_not(full))
            def _():
                scores_ref[...] = masked(scores_ref[...], count, begin, total)

            old = max_ref[...]
            newest = jnp.maximum(old, jnp.max(scores_ref[...], axis=0, keepdims=True))
            weights = jnp.exp2(scores_ref[...] - newest)
            fade = jnp.exp2(old - newest)
            max_ref[...] = newest
            sum_ref[...] = sum_ref[...] * fade + column_sum(weights)
            acc_ref[...] = acc_ref[...] * fade + dot_tn(context, weights.astype(bf16))

        return carry

    lax.fori_loop(0, total // block, visit, 0)
    totals = sum_ref[...]
    lse_ref[...] = max_ref[...] + jnp.log2(totals)
    mixture_ref[...] = acc_ref[...] * (1.0 / totals)
    values = jnp.concatenate([wv_ref[...], wv_ref[...]], axis=0)
    attended = dot_tn(split(mixture_ref[...], 0), values)
    hidden_ref[...] = start + (
        dot(attended.astype(bf16), wo_ref[...]) + vector(vectors_ref, CROSS, CROSS.output_bias)
    )
    out_ref[...] = feed_forward(
        hidden_ref[...], vector(vectors_ref, CROSS, CROSS.feed_gain), vector(vectors_ref, CROSS, CROSS.feed_bias),
        up_ref, vector(vectors_ref, CROSS, CROSS.up_bias), down_ref, vector(vectors_ref, CROSS, CROSS.down_bias),
        normed_ref, active_ref, slope_ref,
    )


def cross_forward(count, tokens, start, vectors, wq, wk, wv, wo, up, down):
    block = min(BLOCK, tokens.shape[0])
    outs = [
        shape((LAT, D), bf16), shape((LAT, D), bf16), shape((LAT, C), f32), shape((C, LAT), f32),
        shape((1, LAT), f32), shape((LAT, D), f32), shape((LAT, D), bf16), shape((LAT, FF), bf16),
        shape((LAT, FF), bf16), shape((LAT, D), f32),
    ]
    scratch = [
        pltpu.VMEM((block, LAT), f32), pltpu.VMEM((C, LAT), f32), pltpu.VMEM((1, LAT), f32),
        pltpu.VMEM((1, LAT), f32),
    ]
    return call(
        cross_forward_kernel, "cross_forward", outs,
        [count, tokens, start, vectors, wq, wk, wv, wo, up, down], scratch=scratch, smem=1,
        flops=15_000_000_000, moved=16_000_000,
    )


def pair_mask(value, side):
    lane = lax.broadcasted_iota(jnp.int32, (1, LANES), 1)
    keep = (lane < HEAD) if side == 0 else (lane >= HEAD)
    return jnp.where(keep, value, jnp.zeros_like(value))


def latent_kernel(windows, parts, firsts_ref, hidden_ref, cotangent_ref, vectors_ref, joint_w_ref, merge_ref,
                  up_ref, down_ref, out_ref, grad_ref, *rest):
    windows_refs, rest = rest[:parts], rest[parts:]
    (flat_ref, probs_ref, joint_ref, mixed_ref, after_ref, normedl_ref, normed_ref, active_ref, slope_ref, query_grad_ref, joint_grad_ref) = rest
    gain = vector(vectors_ref, LATENT, LATENT.attend_gain)
    unit, rstd = normalise(hidden_ref[...])
    normedl_ref[...] = (unit * gain + vector(vectors_ref, LATENT, LATENT.attend_bias)).astype(bf16)
    joint_ref[...] = dot(normedl_ref[...], joint_w_ref[...]).astype(bf16)
    scale = HEAD ** (-0.5)
    for pair in range(HEADS // 2):
        lanes = slice(pair * LANES, (pair + 1) * LANES)
        query = joint_ref[:, lanes]
        keys = joint_ref[:, D + pair * LANES : D + (pair + 1) * LANES]
        values = joint_ref[:, 2 * D + pair * LANES : 2 * D + (pair + 1) * LANES]
        mixed = None
        for side in range(2):
            scores = dot_nt(pair_mask(keys, side), query) * (scale * LOG2E)
            weights = jnp.exp2(scores - jnp.max(scores, axis=0, keepdims=True))
            weights = weights * (1.0 / column_sum(weights))
            probs_ref[2 * pair + side] = weights
            part = dot_tn(pair_mask(values, side), weights.astype(bf16))
            mixed = part if mixed is None else mixed + part
        mixed_ref[lanes, :] = mixed.astype(bf16)
    after_ref[...] = hidden_ref[...] + (
        dot_tn(mixed_ref[...], merge_ref[...]) + vector(vectors_ref, LATENT, LATENT.merge_bias)
    )
    feed_gain = vector(vectors_ref, LATENT, LATENT.feed_gain)
    out_ref[...] = feed_forward(
        after_ref[...], feed_gain, vector(vectors_ref, LATENT, LATENT.feed_bias), up_ref,
        vector(vectors_ref, LATENT, LATENT.up_bias), down_ref, vector(vectors_ref, LATENT, LATENT.down_bias),
        normed_ref, active_ref, slope_ref,
    ).astype(bf16)

    clear_tail(flat_ref, LATENT_ROWS)
    after_grad = feed_backward(
        cotangent_ref[...].astype(f32), after_ref[...], feed_gain, up_ref, down_ref, normed_ref, active_ref,
        slope_ref, flat_ref, LATENT,
    )
    branch = after_grad.astype(bf16)
    put(flat_ref, LATENT.merge_weight[0], D, 0, dot(mixed_ref[...], branch))
    put_vector(flat_ref, LATENT.merge_bias[0], column_sum(branch.astype(f32)))
    mixed_grad = dot_nt(branch, merge_ref[...]).astype(bf16)
    for pair in range(HEADS // 2):
        lanes = slice(pair * LANES, (pair + 1) * LANES)
        query = joint_ref[:, lanes]
        keys = joint_ref[:, D + pair * LANES : D + (pair + 1) * LANES]
        values = joint_ref[:, 2 * D + pair * LANES : 2 * D + (pair + 1) * LANES]
        grads = mixed_grad[:, lanes]
        query_part = key_part = value_part = None
        for side in range(2):
            probs = probs_ref[2 * pair + side]
            part = dot(probs.astype(bf16), pair_mask(grads, side))
            value_part = part if side == 0 else value_part + part
            probs_grad = dot_nt(pair_mask(values, side), grads)
            delta = column_sum(probs * probs_grad)
            scores_grad = (probs * (probs_grad - delta)).astype(bf16)
            part = dot(scores_grad, pair_mask(query, side))
            key_part = part if side == 0 else key_part + part
            part = dot_tn(pair_mask(keys, side), scores_grad)
            query_part = part if side == 0 else query_part + part
        query_grad_ref[lanes, :] = query_part * scale
        joint_grad_ref[:, D + pair * LANES : D + (pair + 1) * LANES] = (key_part * scale).astype(bf16)
        joint_grad_ref[:, 2 * D + pair * LANES : 2 * D + (pair + 1) * LANES] = value_part.astype(bf16)
    joint_grad_ref[:, :D] = query_grad_ref[...].T.astype(bf16)
    put(flat_ref, LATENT.joint_weight[0], 3 * D, 0, dot_tn(normedl_ref[...], joint_grad_ref[...]))
    normed_grad = dot_nt(joint_grad_ref[...], joint_w_ref[...])
    put_vector(flat_ref, LATENT.attend_gain[0], column_sum(normed_grad * unit))
    put_vector(flat_ref, LATENT.attend_bias[0], column_sum(normed_grad))
    grad_ref[...] = after_grad + normalise_back(normed_grad, unit, rstd, gain)
    to_windows(flat_ref, firsts_ref, windows_refs, windows.rows, windows.devices)


def latent_layer(firsts, hidden, cotangent, vectors, joint, merge, up, down, windows, grid):
    outs = [shape((LAT, D), bf16), shape((LAT, D), f32)] + windows.outs(grid.nz)
    scratch = [
        pltpu.VMEM((windows.padded, LANES), f32), pltpu.VMEM((HEADS, LAT, LAT), f32),
        pltpu.VMEM((LAT, 3 * D), bf16), pltpu.VMEM((D, LAT), bf16), pltpu.VMEM((LAT, D), f32),
        pltpu.VMEM((LAT, D), bf16), pltpu.VMEM((LAT, D), bf16), pltpu.VMEM((LAT, FF), bf16),
        pltpu.VMEM((LAT, FF), bf16), pltpu.VMEM((D, LAT), f32), pltpu.VMEM((LAT, 3 * D), bf16),
    ]
    return call(
        functools.partial(latent_kernel, windows, grid.nz), "latent_layer", outs,
        [firsts, hidden, cotangent, vectors, joint, merge, up, down], scratch=scratch, smem=1,
        flops=20_000_000_000, moved=16_000_000,
    )


SPLIT = CROSS.output_weight[0] // TILE * TILE


def cross_feed_kernel(windows, parts, firsts_ref, grad_ref, vectors_ref, wv_ref, wo_ref, up_ref, down_ref,
                      mixture_ref, hidden_ref, normed_ref, active_ref, saved_slope_ref,
                      hidden_grad_ref, valued_ref, delta_ref, value_grad_ref, *rest):
    windows_refs = rest[:parts]
    flat_ref, slope_ref = rest[parts:]
    clear_tail(flat_ref, CROSS_ROWS)
    slope_ref[...] = saved_slope_ref[...]
    hidden_grad = feed_backward(
        grad_ref[...], hidden_ref[...], vector(vectors_ref, CROSS, CROSS.feed_gain), up_ref, down_ref, normed_ref,
        active_ref, slope_ref, flat_ref, CROSS,
    )
    hidden_grad_ref[...] = hidden_grad
    branch = hidden_grad.astype(bf16)
    values = jnp.concatenate([wv_ref[...], wv_ref[...]], axis=0)
    mixture = split(mixture_ref[...], 0)
    attended = dot_tn(mixture, values)
    put(flat_ref, CROSS.output_weight[0], D, 0, dot_tn(attended.astype(bf16), branch))
    put_vector(flat_ref, CROSS.output_bias[0], column_sum(branch.astype(f32)))
    attended_grad = dot_nt(branch, wo_ref[...]).astype(bf16)
    both = dot(mixture, attended_grad)
    value_grad_ref[...] = both[:C] + both[C:]
    put(flat_ref, CROSS.value_weight[0], D, 0, value_grad_ref[...])
    valued = dot_nt(attended_grad, wv_ref[...])
    valued_ref[...] = split(valued, 1)
    delta_ref[...] = column_sum((attended_grad.astype(f32) * attended).T)
    flat_ref[:SPLIT, :] = jnp.zeros((SPLIT, LANES), f32)
    to_windows(flat_ref, firsts_ref, windows_refs, windows.rows, windows.devices)


def cross_feed(firsts, grad, vectors, wv, wo, up, down, mixture, hidden, normed, active, slope, windows, grid):
    outs = [
        shape((LAT, D), f32), shape((LAT, 2 * C), bf16), shape((1, LAT), f32), shape((C, D), f32),
    ] + windows.outs(grid.nz)
    return call(
        functools.partial(cross_feed_kernel, windows, grid.nz), "cross_feed", outs,
        [firsts, grad, vectors, wv, wo, up, down, mixture, hidden, normed, active, slope],
        scratch=[pltpu.VMEM((windows.padded, LANES), f32), pltpu.VMEM((LAT, FF), bf16)], smem=1,
        flops=80_000_000_000, moved=1,
    )


def attend_block(offset, blocks, count_ref, tokens_ref, valued_ref, delta_ref, vectors_ref, keyed_ref, lse_ref,
                 token_grad_ref, scores_ref, acc_ref, gains_ref, doubled_ref, paired_ref):
    block = tokens_ref.shape[0]
    begin = (pl.program_id(0) + offset) * block
    total = blocks * block
    count = count_ref[0]
    some, full = block_kinds(count, begin, block, total)

    @pl.when(pl.program_id(0) == 0)
    def _():
        doubled_ref[...] = split(keyed_ref[...] * LOG2E, 1)
        paired_ref[...] = split(keyed_ref[...], 1)

    @pl.when(some)
    def _():
        gain = vector(vectors_ref, CROSS, CROSS.context_gain)
        bias = vector(vectors_ref, CROSS, CROSS.context_bias)
        unit, rstd = normalise(tokens_ref[...].astype(f32))
        context = (unit * gain + bias).astype(bf16)
        twice = jnp.concatenate([context, context], axis=1)
        scores_ref[...] = dot_nt(twice, doubled_ref[...])

        @pl.when(jnp.logical_not(full))
        def _():
            scores_ref[...] = masked(scores_ref[...], count, begin, total)

        probs = jnp.exp2(scores_ref[...] - lse_ref[...])
        scores_grad = (probs * (dot_nt(twice, valued_ref[...]) - delta_ref[...])).astype(bf16)
        acc_ref[...] += dot_tn(context, scores_grad)
        wide = dot(probs.astype(bf16), valued_ref[...]) + dot(scores_grad, paired_ref[...])
        context_grad = wide[:, :C] + wide[:, C:]
        gains_ref[0:1, :] += column_sum(context_grad * unit)
        gains_ref[1:2, :] += column_sum(context_grad)
        token_grad_ref[...] = normalise_back(context_grad, unit, rstd, gain)

    @pl.when(jnp.logical_not(some))
    def _():
        token_grad_ref[...] = jnp.zeros(token_grad_ref.shape, f32)


def attend_first_kernel(blocks, count_ref, tokens_ref, valued_ref, delta_ref, vectors_ref, keyed_ref, lse_ref,
                        token_grad_ref, acc_ref, gains_ref, scores_ref, doubled_ref, paired_ref):
    @pl.when(pl.program_id(0) == 0)
    def _():
        acc_ref[...] = jnp.zeros(acc_ref.shape, f32)
        gains_ref[...] = jnp.zeros(gains_ref.shape, f32)

    attend_block(0, blocks, count_ref, tokens_ref, valued_ref, delta_ref, vectors_ref, keyed_ref, lse_ref,
                 token_grad_ref, scores_ref, acc_ref, gains_ref, doubled_ref, paired_ref)


def attend_second_kernel(offset, blocks, rows, parts, devices, firsts_ref, count_ref, task_ref, tokens_ref, valued_ref,
                         delta_ref, vectors_ref, keyed_ref, lse_ref, acc_before_ref, gains_before_ref, hidden_grad_ref,
                         value_grad_ref, start_ref, wq_ref, wk_ref, normedq_ref, query_ref, kept_ref,
                         token_grad_ref, *rest):
    windows_refs = rest[:parts]
    flat_ref, scores_ref, acc_ref, gains_ref, doubled_ref, paired_ref = rest[parts:]

    @pl.when(pl.program_id(0) == 0)
    def _():
        acc_ref[...] = acc_before_ref[...]
        gains_ref[...] = gains_before_ref[...]

    attend_block(offset, blocks, count_ref, tokens_ref, valued_ref, delta_ref, vectors_ref, keyed_ref, lse_ref,
                 token_grad_ref, scores_ref, acc_ref, gains_ref, doubled_ref, paired_ref)

    @pl.when(pl.program_id(0) == pl.num_programs(0) - 1)
    def _():
        pulled = split(acc_ref[...] * D ** (-0.5), 0)
        both = dot(pulled, query_ref[...])
        put(flat_ref, CROSS.key_weight[0], D, 0, both[:C] + both[C:])
        put(flat_ref, CROSS.value_weight[0], D, 0, value_grad_ref[...])
        put_vector(flat_ref, CROSS.context_gain[0], gains_ref[0:1, :])
        put_vector(flat_ref, CROSS.context_bias[0], gains_ref[1:2, :])
        query_grad = dot_tn(pulled, jnp.concatenate([wk_ref[...], wk_ref[...]], axis=0)).astype(bf16)
        put(flat_ref, CROSS.query_weight[0], D, 0, dot_tn(normedq_ref[...], query_grad))
        normed_grad = dot_nt(query_grad, wq_ref[...])
        unit, rstd = normalise(start_ref[...])
        put_vector(flat_ref, CROSS.query_gain[0], column_sum(normed_grad * unit))
        put_vector(flat_ref, CROSS.query_bias[0], column_sum(normed_grad))
        gain = vector(vectors_ref, CROSS, CROSS.query_gain)
        start_grad = hidden_grad_ref[...] + normalise_back(normed_grad, unit, rstd, gain)
        put(flat_ref, CROSS.latents[0], D, 0, start_grad)
        first, unused = CROSS.task_table
        chunks = D // LANES
        flat_ref[first : first + NTASK * chunks, :] = jnp.zeros((NTASK * chunks, LANES), f32)
        sums = column_sum(start_grad)
        base = first + task_ref[0] * chunks
        for chunk in range(chunks):
            flat_ref[pl.ds(base + chunk, 1), :] = sums[:, chunk * LANES : (chunk + 1) * LANES]
        clear_tail(flat_ref, SPLIT)
        to_windows(flat_ref, firsts_ref, windows_refs, rows, devices)


def attend_scratch(block):
    return [pltpu.VMEM((block, LAT), f32), pltpu.VMEM((LAT, 2 * C), bf16), pltpu.VMEM((LAT, 2 * C), bf16)]


def attend_first(count, tokens, valued, delta, vectors, keyed, lse):
    total = tokens.shape[0]
    block = min(BLOCK, total)
    blocks = total // block
    whole = [valued, delta, vectors, keyed, lse]
    row = lambda i: (i, 0)
    outs = [shape((total, C), f32), shape((C, LAT), f32), shape((8, C), f32)]
    scratch = attend_scratch(block)
    return pl.pallas_call(
        functools.partial(attend_first_kernel, blocks),
        name="attend_first",
        grid=(max(blocks // 2, 1),),
        out_shape=outs,
        in_specs=[pl.BlockSpec(memory_space=pltpu.SMEM), pl.BlockSpec((block, C), row)] + vmem_specs(len(whole)),
        out_specs=[pl.BlockSpec((block, C), row)] + vmem_specs(2),
        scratch_shapes=scratch,
        compiler_params=pltpu.CompilerParams(vmem_limit_bytes=vmem_limit(*whole, *scratch)),
        cost_estimate=pl.CostEstimate(flops=100_000_000_000, bytes_accessed=1, transcendentals=0),
    )(count, tokens, *whole)


def attend_second(firsts, count, task, tokens, valued, delta, vectors, keyed, lse, acc, gains, hidden_grad, value_grad,
                  start, wq, wk, normedq, query, token_grad, windows, grid):
    total = tokens.shape[0]
    block = min(BLOCK, total)
    blocks = total // block
    offset = max(blocks // 2, 1)
    rows = windows.quarter(grid.nx)
    last = grid.ny * grid.nz - 1
    assert SPLIT <= windows.first[last + 1] and blocks > offset
    flat_rows = max(windows.first[last] + rows * grid.nx, SPLIT + TILE)
    whole = [valued, delta, vectors, keyed, lse, acc, gains, hidden_grad, value_grad, start, wq, wk, normedq, query]
    half = windows.devices // grid.nz // grid.ny * rows
    small = [shape((half * depths, LANES), bf16) for c in range(grid.nz) for depths in halves(grid)]
    row = lambda i: (i + offset, 0)
    scratch = [
        pltpu.VMEM((flat_rows, LANES), f32), *attend_scratch(block)[:1], pltpu.VMEM((C, LAT), f32),
        pltpu.VMEM((8, C), f32), *attend_scratch(block)[1:],
    ]
    return pl.pallas_call(
        functools.partial(attend_second_kernel, offset, blocks, rows, len(small), windows.devices),
        name="attend_second",
        grid=(blocks - offset,),
        out_shape=[shape((total, C), f32)] + small,
        in_specs=[pl.BlockSpec(memory_space=pltpu.SMEM)] * 3
        + [pl.BlockSpec((block, C), row)]
        + vmem_specs(len(whole))
        + [pl.BlockSpec(memory_space=pl.ANY)],
        out_specs=[pl.BlockSpec((block, C), row)] + vmem_specs(len(small)),
        scratch_shapes=scratch,
        input_output_aliases={4 + len(whole): 0},
        compiler_params=pltpu.CompilerParams(vmem_limit_bytes=vmem_limit(*whole, *small, *scratch)),
        cost_estimate=pl.CostEstimate(flops=100_000_000_000, bytes_accessed=1, transcendentals=0),
    )(firsts, count, task, tokens, *whole, token_grad)


def body(tokens, task_id, valid_count, cross_params, latent_params, out_grad):
    grid = Grid()
    devices = grid.nx * grid.ny * grid.nz
    cw = Windows(cross_params.shape[0] * devices, devices)
    lw = Windows(latent_params.shape[0] * devices, devices)
    gathered_from = grid.owners(gather_places(grid))
    scattered_to = grid.owners(grid.order())
    tokens = tokens[0]

    cross_window, latent_window = place([cross_params, latent_params], [cw, lw], grid.index)
    latent_all = lax.all_gather(latent_window, AXES, axis=0, tiled=True)
    cross_column = gather_depth(cross_window, grid)
    pieces = gather_plane_second(*gather_plane_first(cross_column, grid), grid)
    cross_all = sum(gather_core(*pieces, grid), [])
    vectors, start, wq, wk, wv, wo, up, down = unpack_cross(cw.firsts(gathered_from), cross_all, task_id, cw)
    normedq, query, keyed, mixture, lse, hidden, normed, active, slope, result = cross_forward(
        valid_count, tokens, start, vectors, wq, wk, wv, wo, up, down
    )
    latent_weights = unpack_latent(jnp.array(lw.first, jnp.int32), [latent_all], lw)
    latents_out, result_grad, *latent_parts = latent_layer(
        lw.firsts(scattered_to), result, out_grad[0], *latent_weights, lw, grid
    )

    latent_lows, latent_highs = reduce_first(reduce_core(latent_parts, grid), lw.rows, grid)
    hidden_grad, valued, delta, value_grad, *later_parts = cross_feed(
        cw.firsts(scattered_to), after(result_grad, latent_lows[0][0]), vectors, wv, wo, up, down, mixture, hidden,
        normed, active, slope, cw, grid,
    )
    latent_lows[0] = (after(latent_lows[0][0], delta), 0)
    latent_first, latent_second = reduce_second(latent_lows, latent_highs, lw.rows, grid)
    later_group = reduce_core(later_parts, grid)
    token_grad, acc, gains = attend_first(
        valid_count, tokens, valued, after(delta, latent_first[0][0]), vectors, keyed, lse
    )
    latent_first[0] = (after(latent_first[0][0], acc), 0)
    latent_column = reduce_depth(latent_first, latent_second, lw.rows, grid)
    later_group[0] = (after(later_group[0][0], latent_column[0]), 0)
    later_lows, later_highs = reduce_first(later_group, cw.rows, grid)
    owner, quarter = quarter_owners(grid)
    small_rows = cw.quarter(grid.nx)
    token_grad, *early_parts = attend_second(
        cw.firsts(owner) + quarter * small_rows, valid_count, task_id, tokens, valued, delta, vectors, keyed, lse,
        after(acc, later_lows[0][0]), gains, hidden_grad, value_grad, start, wq, wk, normedq, query, token_grad, cw,
        grid,
    )
    latent_column[0] = after(latent_column[0], early_parts[0])
    latent_share = extract(latent_column, [], lw, grid)
    later_lows[0] = (after(later_lows[0][0], latent_share), 0)
    early_groups = [reduce_core(early_parts[half::2], grid) for half in range(2)]
    later_first, later_second, early_lows, early_highs = reduce_second_and_first(
        later_lows, later_highs, cw.rows, early_groups, small_rows, grid
    )
    early_first, early_second = reduce_second(early_lows, early_highs, small_rows, grid)
    column = reduce_depth_both(later_first, later_second, cw.rows, early_first, early_second, small_rows, grid)
    quarters = collect_quarters(column, cw.rows, small_rows, grid)
    return (latents_out[None], token_grad[None], extract(column, quarters, cw, grid), latent_share)


def solution(mesh):
    return jax.shard_map(
        body,
        mesh=mesh,
        in_specs=(
            P(AXES, None, None),
            P(AXES),
            P(AXES),
            P(AXES),
            P(AXES),
            P(AXES, None, None),
        ),
        out_specs=(
            P(AXES, None, None),
            P(AXES, None, None),
            P(AXES),
            P(AXES),
        ),
        check_vma=False,
    )
```

```python
import functools
import math
import types

import jax
import jax.numpy as jnp
from jax import lax
from jax.experimental import pallas as pl
from jax.experimental.pallas import tpu as pltpu
from jax.sharding import PartitionSpec as P

D = 512
FF = 2048
C = 128
LAT = 512
HEADS = 8
HEAD = 64
NTASK = 18
LANG = 77
LANES = 128
TILE = 16
UNIT = TILE * LANES
BLOCK = 1024
AXES = ("gx", "gy", "gz")

epsilon = 1e-05
negative = -1e30
LOG2E = math.log2(math.e)
bf16 = jnp.bfloat16
f32 = jnp.float32
VMEM_LIMIT = 60 * 1024 * 1024
ROOM = 6 * 1024 * 1024


def layout_of(**shapes):
    table = {}
    row = 0
    for name, dims in shapes.items():
        table[name] = (row, dims)
        row += math.prod(dims) // LANES
    return types.SimpleNamespace(**table), row


CROSS, CROSS_ROWS = layout_of(
    latents=(LAT, D),
    task_table=(NTASK, D),
    query_gain=(D,),
    query_bias=(D,),
    context_gain=(C,),
    context_bias=(C,),
    query_weight=(D, D),
    key_weight=(C, D),
    value_weight=(C, D),
    output_weight=(D, D),
    output_bias=(D,),
    feed_gain=(D,),
    feed_bias=(D,),
    up_weight=(D, FF),
    up_bias=(FF,),
    down_weight=(FF, D),
    down_bias=(D,),
)
LATENT, LATENT_ROWS = layout_of(
    attend_gain=(D,),
    attend_bias=(D,),
    joint_weight=(D, 3 * D),
    merge_weight=(D, D),
    merge_bias=(D,),
    feed_gain=(D,),
    feed_bias=(D,),
    up_weight=(D, FF),
    up_bias=(FF,),
    down_weight=(FF, D),
    down_bias=(D,),
)


def vectors_of(table):
    return [place for place in vars(table).values() if len(place[1]) == 1]


class Windows:
    def __init__(self, total, devices):
        self.total = total
        self.devices = devices
        self.shard = total // devices
        starts = [self.shard * d for d in range(devices)]
        self.first = [s // UNIT * TILE for s in starts]
        self.phase = [s % UNIT for s in starts]
        self.rows = max(-(-(p + self.shard) // UNIT) * TILE for p in self.phase)
        self.padded = max(f + self.rows for f in self.first)
        self.full = -(-total // UNIT) * TILE
        self.shard_rows = -(-self.shard // (8 * LANES)) * 8

    def outs(self, parts):
        return [shape((self.devices // parts * self.rows, LANES), bf16)] * parts

    def firsts(self, owners):
        return self.shard * owners // UNIT * TILE

    def quarter(self, parts):
        return -(-self.rows // (parts * TILE)) * TILE


def dot(left, right):
    return jnp.dot(left, right, preferred_element_type=f32)


def dot_nt(left, right):
    return lax.dot_general(left, right, (((1,), (1,)), ((), ())), preferred_element_type=f32)


def dot_tn(left, right):
    return lax.dot_general(left, right, (((0,), (0,)), ((), ())), preferred_element_type=f32)


def split(value, axis):
    high = value.astype(bf16)
    low = (value - high.astype(f32)).astype(bf16)
    return jnp.concatenate([high, low], axis=axis)


def normalise(value):
    centred = value - jnp.mean(value, axis=-1, keepdims=True)
    rstd = lax.rsqrt(jnp.mean(centred * centred, axis=-1, keepdims=True) + epsilon)
    return centred * rstd, rstd


def normalise_back(grad, unit, rstd, gain):
    inner = grad * gain
    return rstd * (
        inner
        - jnp.mean(inner, axis=-1, keepdims=True)
        - unit * jnp.mean(inner * unit, axis=-1, keepdims=True)
    )


def column_sum(value):
    return jnp.sum(value, axis=0, keepdims=True)


def vmem_specs(count):
    return [pl.BlockSpec(memory_space=pltpu.VMEM)] * count


def shape(dims, dtype):
    return jax.ShapeDtypeStruct(dims, dtype)


def bytes_of(value):
    return math.prod(value.shape) * jnp.dtype(value.dtype).itemsize


def vmem_limit(*values):
    return min(sum(map(bytes_of, values)) + 16 * 2**20, VMEM_LIMIT)


def call(kernel, name, outs, inputs, scratch=(), smem=0, flops=0, moved=0, alone=True):
    specs = [pl.BlockSpec(memory_space=pltpu.SMEM)] * smem + vmem_specs(len(inputs) - smem)
    limit = VMEM_LIMIT if alone else vmem_limit(*inputs, *jax.tree.leaves(outs), *scratch)
    return pl.pallas_call(
        kernel,
        name=name,
        out_shape=outs,
        in_specs=specs,
        out_specs=jax.tree.map(lambda _: pl.BlockSpec(memory_space=pltpu.VMEM), outs),
        scratch_shapes=list(scratch),
        compiler_params=pltpu.CompilerParams(vmem_limit_bytes=limit),
        cost_estimate=pl.CostEstimate(flops=flops, bytes_accessed=moved, transcendentals=0),
    )(*inputs)


class Traffic:
    def __init__(self):
        self.loads, self.stores, self.blocks, self.begun = {}, {}, {}, []

    def need(self, *refs):
        for ref in refs:
            copy = self.loads.pop(id(ref), None)
            if copy is not None:
                copy.wait()

    def ship(self, *refs):
        for ref in refs:
            copy = self.stores.pop(id(ref), None)
            if copy is not None:
                copy.start()
                self.begun.append(copy)

    def block(self, ref, part, number):
        target, sem = self.blocks[id(ref)]
        return pltpu.make_async_copy(ref.at[part], target.at[part], sem.at[number])


def streamed(kernel, name, outs, inputs, late=(), early=(), blocks=None, scratch=(), smem=0, flops=0, room=0):
    blocks = blocks or {}
    shipped = list(early) + list(blocks)
    vmem, hbm = pl.BlockSpec(memory_space=pltpu.VMEM), pl.BlockSpec(memory_space=pltpu.HBM)
    held = [pltpu.VMEM(inputs[i].shape, inputs[i].dtype) for i in late]
    held += [pltpu.VMEM(outs[i].shape, outs[i].dtype) for i in shipped]
    sems = [pltpu.SemaphoreType.DMA((max(len(late), 1),)), pltpu.SemaphoreType.DMA((max(len(early), 1),))]
    sems += [pltpu.SemaphoreType.DMA((number,)) for number in blocks.values()]

    def body(*refs):
        takes, gives = list(refs[: len(inputs)]), list(refs[len(inputs) : len(inputs) + len(outs)])
        rest = refs[len(inputs) + len(outs) :]
        buffers, rest = rest[: len(held)], rest[len(held) :]
        load_sem, store_sem = rest[:2]
        block_sems, rest = rest[2 : len(sems)], rest[len(sems) :]
        traffic = Traffic()
        for k, i in enumerate(late):
            copy = pltpu.make_async_copy(takes[i], buffers[k], load_sem.at[k])
            copy.start()
            traffic.loads[id(buffers[k])] = copy
            takes[i] = buffers[k]
        for k, i in enumerate(shipped):
            buffer = buffers[len(late) + k]
            if k < len(early):
                traffic.stores[id(buffer)] = pltpu.make_async_copy(buffer, gives[i], store_sem.at[k])
            else:
                traffic.blocks[id(buffer)] = (gives[i], block_sems[k - len(early)])
            gives[i] = buffer
        kernel(traffic, *takes, *gives, *rest)
        assert not traffic.loads and not traffic.stores
        for copy in traffic.begun:
            copy.wait()

    return pl.pallas_call(
        body,
        name=name,
        out_shape=outs,
        in_specs=[pl.BlockSpec(memory_space=pltpu.SMEM)] * smem
        + [hbm if i in late else vmem for i in range(smem, len(inputs))],
        out_specs=[hbm if i in shipped else vmem for i in range(len(outs))],
        scratch_shapes=held + sems + list(scratch),
        compiler_params=pltpu.CompilerParams(vmem_limit_bytes=VMEM_LIMIT - room),
        cost_estimate=pl.CostEstimate(flops=flops, bytes_accessed=1, transcendentals=0),
    )(*inputs)


def shifted(value, shift):
    down, across = shift // LANES, shift % LANES
    turned = pltpu.roll(value, across, axis=1)
    above = pltpu.roll(turned, 1, axis=0)
    lane = lax.broadcasted_iota(jnp.int32, value.shape, 1)
    return pltpu.roll(jnp.where(lane < across, above, turned), down, axis=0)


def place_kernel(shifts_ref, shards_ref, *out_refs):
    begin = 0
    for number, out_ref in enumerate(out_refs):
        rows = out_ref.shape[0]
        value = shards_ref[begin : begin + rows, :].astype(f32)
        out_ref[...] = shifted(value, shifts_ref[number]).astype(bf16)
        begin += rows


def place(shards, windows, index):
    padded = [
        jnp.pad(shard, (0, w.rows * LANES - w.shard)) for shard, w in zip(shards, windows)
    ]
    together = jnp.concatenate(padded).reshape(-1, LANES)
    shifts = jnp.stack([(w.shard * index) % UNIT for w in windows])
    outs = [shape((w.rows, LANES), bf16) for w in windows]
    return call(place_kernel, "place", outs, [shifts, together], smem=1, alone=False)


def extract_kernel(count, shift_ref, *refs):
    out_ref, total_ref = refs[-2:]
    rows = total_ref.shape[0]
    value = refs[0][:rows, :].astype(f32)
    for ref in refs[1:count]:
        value += ref[:rows, :].astype(f32)
    total_ref[...] = value
    begin = 0
    for ref in refs[count:-2]:
        size = min(ref.shape[0], rows - begin)
        if size > 0:
            total_ref[begin : begin + size, :] += ref[:size, :].astype(f32)
        begin += ref.shape[0]
    down, across = shift_ref[0] // LANES, shift_ref[0] % LANES
    turned = pltpu.roll(total_ref[...], lax.rem(LANES - across, LANES), axis=1)
    below = pltpu.roll(turned, rows - 1, axis=0)
    lane = lax.broadcasted_iota(jnp.int32, (rows, LANES), 1)
    merged = pltpu.roll(
        jnp.where(lane < LANES - across, turned, below), lax.rem(rows - down, rows), axis=0
    )
    out_ref[...] = merged[: out_ref.shape[0]]


def extract(parts, quarters, windows, grid):
    shift = (windows.shard * grid.index) % UNIT
    rows = min(windows.shard_rows, windows.rows)
    found = call(
        functools.partial(extract_kernel, len(parts)), "extract", shape((rows, LANES), f32),
        [shift.reshape(1), *parts, *quarters], scratch=[pltpu.VMEM((windows.rows, LANES), f32)], smem=1,
        alone=False,
    )
    return found.reshape(-1)[: windows.shard]


class Grid:
    def __init__(self):
        self.nx, self.ny, self.nz = (lax.axis_size(axis) for axis in AXES)
        self.nl = 2 if self.nx % 2 == 0 else 1
        self.nh = self.nx // self.nl
        self.index = lax.axis_index(AXES)

    def order(self):
        return [
            (c, h, l, y)
            for c in range(self.nz)
            for h in range(self.nh)
            for l in range(self.nl)
            for y in range(self.ny)
        ]

    def owners(self, places):
        gx, gy, gz = (lax.axis_index(axis) for axis in AXES)
        c, h, l, y = (jnp.array(column, jnp.int32) for column in zip(*places))
        high = (gx // self.nl + h) % self.nh
        low = (gx % self.nl + l) % self.nl
        return ((high * self.nl + low) * self.ny + (gy + y) % self.ny) * self.nz + (gz + c) % self.nz

    def along_core(self, value, step):
        return lax.ppermute(value, AXES[2], [(i, (i + step) % self.nz) for i in range(self.nz)])

    def along_depth(self, value, step):
        return lax.ppermute(value, AXES[1], [(i, (i + step) % self.ny) for i in range(self.ny)])

    def along_low(self, value, step):
        nl = self.nl
        return lax.ppermute(
            value, AXES[0], [(i, i // nl * nl + (i + step) % nl) for i in range(self.nx)]
        )

    def along_high(self, value, step):
        nl = self.nl
        return lax.ppermute(value, AXES[0], [(i, (i + step * nl) % self.nx) for i in range(self.nx)])


def combine_kernel(groups, picks, *refs):
    starts = [sum(len(bases) for rows, bases in groups[:g]) for g in range(len(groups))]
    outputs = refs[sum(len(bases) for rows, bases in groups) :]
    for output, pick in zip(outputs, picks):
        row = 0
        for g, block in pick:
            rows, bases = groups[g]
            total = None
            for i, base in enumerate(bases):
                begin = base + block * rows
                part = refs[starts[g] + i][begin : begin + rows, :].astype(f32)
                total = part if total is None else total + part
            output[row : row + rows, :] = total.astype(bf16)
            row += rows


def combine(name, groups, picks):
    inputs = [array for rows, sources in groups for array, base in sources]
    kinds = tuple((rows, tuple(base for array, base in sources)) for rows, sources in groups)
    sizes = [sum(groups[g][0] for g, block in pick) for pick in picks]
    outs = [shape((size, LANES), bf16) for size in sizes]
    moved = 6 * LANES * sum(sizes)
    return call(
        functools.partial(combine_kernel, kinds, picks), name, outs, inputs, flops=moved, moved=moved, alone=False
    )


def reduce_core(parts, grid):
    return [(parts[0], 0)] + [(grid.along_core(parts[c], c), 0) for c in range(1, grid.nz)]


def first_picks(grid, g):
    nh, nl, ny = grid.nh, grid.nl, grid.ny
    half = ny // 2
    block = lambda h, l, y: (g, (h * nl + l) * ny + y)
    lows = [[block(h, l, y) for h in range(nh) for y in range(half)] for l in range(nl)]
    highs = [[block(h, l, y) for l in range(nl) for y in range(half, ny)] for h in range(nh)]
    return lows, highs


def halves(grid):
    return [grid.ny // 2, grid.ny - grid.ny // 2]


def half_order(grid):
    half = grid.ny // 2
    places = []
    for c in range(grid.nz):
        for depths in (range(half), range(half, grid.ny)):
            places += [(c, h, l, y) for h in range(grid.nh) for l in range(grid.nl) for y in depths]
    return places


def half_first_picks(grid, first_group, second_group):
    nh, nl = grid.nh, grid.nl
    half, rest = halves(grid)
    lows = [[(first_group, (h * nl + l) * half + y) for h in range(nh) for y in range(half)] for l in range(nl)]
    highs = [[(second_group, (h * nl + l) * rest + y) for l in range(nl) for y in range(rest)] for h in range(nh)]
    return lows, highs


def second_picks(grid, low_group, high_group):
    half = grid.ny // 2
    rest = grid.ny - half
    highs = [[(low_group, h * half + y) for y in range(half)] for h in range(grid.nh)]
    lows = [[(high_group, l * rest + y) for y in range(rest)] for l in range(grid.nl)]
    return highs, lows


def depth_picks(grid, first_group, second_group):
    half = grid.ny // 2
    return [(first_group, y) for y in range(half)] + [(second_group, y) for y in range(grid.ny - half)]


def send_low(arrays, grid):
    return [grid.along_low(array, l + 1) for l, array in enumerate(arrays)]


def send_high(arrays, grid):
    return [grid.along_high(array, h + 1) for h, array in enumerate(arrays)]


def send_depth(arrays, grid):
    return [grid.along_depth(array, y + 1) for y, array in enumerate(arrays)]


def at(arrays, base=0):
    return [(array, base) for array in arrays]


def reduce_first(group, rows, grid):
    lows, highs = first_picks(grid, 0)
    outs = combine("plane_first", [(rows, group)], lows + highs)
    keep_low, keep_high = outs[0], outs[grid.nl]
    return (
        at([keep_low] + send_low(outs[1 : grid.nl], grid)),
        at([keep_high] + send_high(outs[grid.nl + 1 :], grid)),
    )


def reduce_second(lows, highs, rows, grid):
    to_high, to_low = second_picks(grid, 0, 1)
    outs = combine("plane_second", [(rows, lows), (rows, highs)], to_high + to_low)
    keep_first, keep_second = outs[0], outs[grid.nh]
    return (
        at([keep_first] + send_high(outs[1 : grid.nh], grid)),
        at([keep_second] + send_low(outs[grid.nh + 1 :], grid)),
    )


def reduce_depth(first, second, rows, grid):
    outs = combine("depth", [(rows, first), (rows, second)], [[pick] for pick in depth_picks(grid, 0, 1)])
    return [outs[0]] + send_depth(outs[1:], grid)


def reduce_second_and_first(lows, highs, rows, small_groups, small_rows, grid):
    to_high, to_low = second_picks(grid, 0, 1)
    small_low, small_high = half_first_picks(grid, 2, 3)
    nh, nl, half = grid.nh, grid.nl, grid.ny // 2
    picks = [to_high[0], to_low[0], small_low[0], small_high[0]]
    picks += [to_high[h] + small_high[h] for h in range(1, nh)]
    picks += [to_low[l] + small_low[l] for l in range(1, nl)]
    outs = combine("second_and_first", [(rows, lows), (rows, highs)] + [(small_rows, group) for group in small_groups], picks)
    keep_first, keep_second, keep_low, keep_high = outs[:4]
    high = send_high(outs[4 : 3 + nh], grid)
    low = send_low(outs[3 + nh :], grid)
    first, second = at([keep_first]) + at(high), at([keep_second]) + at(low)
    lows = at([keep_low]) + at(low, (grid.ny - half) * rows)
    highs = at([keep_high]) + at(high, half * rows)
    return first, second, lows, highs


def reduce_depth_both(first, second, rows, small_first, small_second, small_rows, grid):
    groups = [(rows, first), (rows, second), (small_rows, small_first), (small_rows, small_second)]
    picks = [list(pair) for pair in zip(depth_picks(grid, 0, 1), depth_picks(grid, 2, 3))]
    outs = combine("depth_both", groups, picks)
    return [outs[0]] + send_depth(outs[1:], grid)


def quarter_owners(grid):
    gx, gy, gz = (lax.axis_index(axis) for axis in AXES)
    c, h, l, y = (jnp.array(column, jnp.int32) for column in zip(*half_order(grid)))
    quarter = (gx // grid.nl + h) % grid.nh * grid.nl + (gx % grid.nl + l) % grid.nl
    return (gy + y) % grid.ny * grid.nz + (gz + c) % grid.nz, quarter


def collect_quarters(parts, base, rows, grid):
    (own,) = combine("quarter", [(rows, at(parts, base))], [[(0, 0)]])
    zero = jnp.zeros_like(own)
    first = jnp.where(lax.axis_index(AXES[0]) == 0, own, zero)
    return [first] + [lax.ppermute(own, AXES[0], [(x, 0)]) for x in range(1, grid.nx)]


def gather_depth(window, grid):
    return [window] + [grid.along_depth(window, -y) for y in range(1, grid.ny)]


def gather_plane_first(column, grid):
    half = grid.ny // 2
    first, second = jnp.concatenate(column[:half]), jnp.concatenate(column[half:])
    lows = [first] + [grid.along_low(first, -l) for l in range(1, grid.nl)]
    highs = [second] + [grid.along_high(second, -h) for h in range(1, grid.nh)]
    return lows, highs


def gather_plane_second(lows, highs, grid):
    first, second = jnp.concatenate(lows), jnp.concatenate(highs)
    return (
        [first] + [grid.along_high(first, -h) for h in range(1, grid.nh)],
        [second] + [grid.along_low(second, -l) for l in range(1, grid.nl)],
    )


def gather_core(first, second, grid):
    pieces = first + second
    return [pieces] + [[grid.along_core(piece, -c) for piece in pieces] for c in range(1, grid.nz)]


def gather_places(grid):
    half = grid.ny // 2
    places = []
    for c in range(grid.nz):
        for h in range(grid.nh):
            places += [(c, h, l, y) for l in range(grid.nl) for y in range(half)]
        for l in range(grid.nl):
            places += [(c, h, l, y) for h in range(grid.nh) for y in range(half, grid.ny)]
    return places


def after(value, *others):
    return lax.optimization_barrier((value, *others))[0]


def assemble(firsts_ref, gathered_refs, flat_ref, windows):
    rows = windows.rows
    inner = max(windows.shard // UNIT - 1, 0) * TILE
    after = TILE + inner

    def clear(place, carry):
        first = pl.multiple_of(firsts_ref[place], TILE)
        flat_ref[pl.ds(first, TILE), :] = jnp.zeros((TILE, LANES), f32)
        flat_ref[pl.ds(first + after, rows - after), :] = jnp.zeros((rows - after, LANES), f32)
        return carry

    lax.fori_loop(0, windows.devices, clear, 0)
    place = 0
    for gathered_ref in gathered_refs:
        blocks = gathered_ref.shape[0] // rows

        def visit(block, carry, gathered_ref=gathered_ref, place=place):
            first = pl.multiple_of(firsts_ref[place + block], TILE)
            value = gathered_ref[pl.ds(pl.multiple_of(block * rows, TILE), rows), :].astype(f32)
            flat_ref[pl.ds(first, TILE), :] += value[:TILE]
            if inner:
                flat_ref[pl.ds(first + TILE, inner), :] = value[TILE:after]
            flat_ref[pl.ds(first + after, rows - after), :] += value[after:]
            return carry

        lax.fori_loop(0, blocks, visit, 0)
        place += blocks


def relay(flat_ref, place, out_ref):
    first, (rows, columns) = place
    chunks = columns // LANES
    step = 64

    def body(index, carry):
        begin = pl.multiple_of(index * step, step)
        for chunk in range(chunks):
            part = flat_ref[pl.ds(first + begin * chunks + chunk, step, stride=chunks), :]
            out_ref[pl.ds(begin, step), chunk * LANES : (chunk + 1) * LANES] = part.astype(out_ref.dtype)
        return carry

    lax.fori_loop(0, rows // step, body, 0)


def relay_vectors(flat_ref, table, out_ref):
    for index, (first, dims) in enumerate(vectors_of(table)):
        for chunk in range(dims[0] // LANES):
            out_ref[index : index + 1, chunk * LANES : (chunk + 1) * LANES] = flat_ref[
                first + chunk : first + chunk + 1, :
            ]


def unpack_cross_kernel(windows, count, traffic, firsts_ref, task_ref, *refs):
    vectors_ref, start_ref, query_ref, key_ref, value_ref, output_ref, up_ref, down_ref, flat_ref = refs[count:]
    assemble(firsts_ref, refs[:count], flat_ref, windows)
    relay_vectors(flat_ref, CROSS, vectors_ref)
    traffic.ship(vectors_ref)
    chunks = D // LANES
    first, unused = CROSS.task_table
    base = first + task_ref[0] * chunks
    relay(flat_ref, CROSS.latents, start_ref)
    for chunk in range(chunks):
        row = flat_ref[pl.ds(base + chunk, 1), :]
        start_ref[:, chunk * LANES : (chunk + 1) * LANES] += row
    traffic.ship(start_ref)
    relay(flat_ref, CROSS.query_weight, query_ref)
    traffic.ship(query_ref)
    relay(flat_ref, CROSS.key_weight, key_ref)
    traffic.ship(key_ref)
    relay(flat_ref, CROSS.value_weight, value_ref)
    traffic.ship(value_ref)
    relay(flat_ref, CROSS.output_weight, output_ref)
    traffic.ship(output_ref)
    relay(flat_ref, CROSS.up_weight, up_ref)
    traffic.ship(up_ref)
    relay(flat_ref, CROSS.down_weight, down_ref)
    traffic.ship(down_ref)


def unpack_cross(firsts, gathered, task, windows):
    outs = [
        shape((16, FF), f32), shape((LAT, D), f32), shape((D, D), bf16), shape((C, D), bf16),
        shape((C, D), bf16), shape((D, D), bf16), shape((D, FF), bf16), shape((FF, D), bf16),
    ]
    return streamed(
        functools.partial(unpack_cross_kernel, windows, len(gathered)), "unpack_cross", outs,
        [firsts, task, *gathered], early=range(len(outs)), scratch=[pltpu.VMEM((windows.padded, LANES), f32)], smem=2,
        flops=20_000_000_000, room=ROOM,
    )


def unpack_latent_kernel(windows, count, traffic, firsts_ref, *refs):
    vectors_ref, joint_ref, merge_ref, up_ref, down_ref, flat_ref = refs[count:]
    assemble(firsts_ref, refs[:count], flat_ref, windows)
    relay_vectors(flat_ref, LATENT, vectors_ref)
    traffic.ship(vectors_ref)
    relay(flat_ref, LATENT.joint_weight, joint_ref)
    traffic.ship(joint_ref)
    relay(flat_ref, LATENT.merge_weight, merge_ref)
    traffic.ship(merge_ref)
    relay(flat_ref, LATENT.up_weight, up_ref)
    traffic.ship(up_ref)
    relay(flat_ref, LATENT.down_weight, down_ref)
    traffic.ship(down_ref)


def unpack_latent(firsts, gathered, windows):
    outs = [
        shape((8, FF), f32), shape((D, 3 * D), bf16), shape((D, D), bf16), shape((D, FF), bf16),
        shape((FF, D), bf16),
    ]
    return streamed(
        functools.partial(unpack_latent_kernel, windows, len(gathered)), "unpack_latent", outs,
        [firsts, *gathered], early=range(len(outs)), scratch=[pltpu.VMEM((windows.padded, LANES), f32)], smem=1,
        room=ROOM,
    )


def put(flat_ref, first, columns, row, value, column=0):
    chunks = columns // LANES
    rows = value.shape[0]
    for chunk in range(value.shape[1] // LANES):
        begin = first + row * chunks + column // LANES + chunk
        flat_ref[pl.ds(begin, rows, stride=chunks), :] = value[:, chunk * LANES : (chunk + 1) * LANES]


def put_vector(flat_ref, first, value, column=0):
    for chunk in range(value.shape[1] // LANES):
        row = first + column // LANES + chunk
        flat_ref[row : row + 1, :] = value[:, chunk * LANES : (chunk + 1) * LANES]


def to_windows(flat_ref, firsts_ref, out_refs, rows, traffic=None):
    begin = 0
    for out_ref in out_refs:
        blocks = out_ref.shape[0] // rows

        def visit(place, carry, out_ref=out_ref, begin=begin):
            first = pl.multiple_of(firsts_ref[begin + place], TILE)
            part = pl.ds(pl.multiple_of(place * rows, TILE), rows)
            out_ref[part, :] = flat_ref[pl.ds(first, rows), :].astype(bf16)
            if traffic:
                traffic.block(out_ref, part, place).start()
            return carry

        lax.fori_loop(0, blocks, visit, 0)
        begin += blocks
    if not traffic:
        return
    for out_ref in out_refs:

        def finish(place, carry, out_ref=out_ref):
            part = pl.ds(pl.multiple_of(place * rows, TILE), rows)
            traffic.block(out_ref, part, place).wait()
            return carry

        lax.fori_loop(0, out_ref.shape[0] // rows, finish, 0)


def clear_tail(flat_ref, used):
    total = flat_ref.shape[0]
    flat_ref[used:total, :] = jnp.zeros((total - used, LANES), f32)


def gelu_and_slope(value):
    half = 0.5 + 0.5 * lax.erf(value * math.sqrt(0.5))
    density = jnp.exp2(value * value * (-0.5 * LOG2E)) * (1.0 / math.sqrt(2.0 * math.pi))
    return value * half, half + value * density


def feed_forward(traffic, hidden, gain, bias, up_ref, up_bias, down_ref, down_bias, normed_ref, active_ref, slope_ref):
    unit, rstd = normalise(hidden)
    normed_ref[...] = (unit * gain + bias).astype(bf16)
    traffic.ship(normed_ref)
    traffic.need(up_ref)
    step = 256
    for begin in range(0, FF, step):
        inner = dot(normed_ref[...], up_ref[:, begin : begin + step]) + up_bias[:, begin : begin + step]
        active, slope = gelu_and_slope(inner)
        active_ref[:, begin : begin + step] = active.astype(bf16)
        slope_ref[:, begin : begin + step] = slope.astype(bf16)
    traffic.ship(active_ref, slope_ref)
    traffic.need(down_ref)
    return hidden + (dot(active_ref[...], down_ref[...]) + down_bias)


def feed_backward(traffic, grad, hidden, gain, up_ref, down_ref, normed_ref, active_ref, slope_ref, flat_ref, table,
                  base=0):
    unit, rstd = normalise(hidden)
    branch = grad.astype(bf16)
    put_vector(flat_ref, table.down_bias[0] - base, column_sum(branch.astype(f32)))
    step = 256
    total = None
    normed = normed_ref[...]
    for begin in range(0, FF, step):
        put(flat_ref, table.down_weight[0] - base, D, begin, dot_tn(active_ref[:, begin : begin + step], branch))
        active_grad = dot_nt(branch, down_ref[begin : begin + step, :])
        inner = (active_grad * slope_ref[:, begin : begin + step].astype(f32)).astype(bf16)
        slope_ref[:, begin : begin + step] = inner
        put_vector(flat_ref, table.up_bias[0] - base, column_sum(inner.astype(f32)), begin)
        put(flat_ref, table.up_weight[0] - base, FF, 0, dot_tn(normed, inner), begin)
    traffic.need(up_ref)
    normed_grad = dot_nt(slope_ref[...], up_ref[...])
    put_vector(flat_ref, table.feed_gain[0] - base, column_sum(normed_grad * unit))
    put_vector(flat_ref, table.feed_bias[0] - base, column_sum(normed_grad))
    return grad + normalise_back(normed_grad, unit, rstd, gain)


def vector(vectors_ref, table, place):
    index = vectors_of(table).index(place)
    return vectors_ref[index : index + 1, : place[1][0]]


def block_kinds(count, begin, block, total):
    language = total - LANG
    end = begin + block
    some = (begin < count) | (end > language)
    full = (end <= count) | (count >= language) | (begin >= language)
    return some, full


def masked(scores, count, begin, total):
    place = begin + lax.broadcasted_iota(jnp.int32, (scores.shape[0], 1), 0)
    valid = (place < count) | (place >= total - LANG)
    return jnp.where(valid, scores, negative)


def cross_forward_kernel(traffic, count_ref, tokens_ref, start_ref, vectors_ref, wq_ref, wk_ref, wv_ref, wo_ref,
                         up_ref, down_ref,
                         normedq_ref, query_ref, keyed_ref, mixture_ref, lse_ref, hidden_ref, normed_ref,
                         active_ref, slope_ref, out_ref,
                         scores_ref, acc_ref, max_ref, sum_ref):
    total = tokens_ref.shape[0]
    count = count_ref[0]
    start = start_ref[...]
    unit, rstd = normalise(start)
    normedq_ref[...] = (
        unit * vector(vectors_ref, CROSS, CROSS.query_gain) + vector(vectors_ref, CROSS, CROSS.query_bias)
    ).astype(bf16)
    traffic.ship(normedq_ref)
    query_ref[...] = dot(normedq_ref[...], wq_ref[...]).astype(bf16)
    traffic.ship(query_ref)
    keyed_ref[...] = dot_nt(query_ref[...], wk_ref[...]) * D ** (-0.5)
    traffic.ship(keyed_ref)
    keyed = split(keyed_ref[...] * LOG2E, 1)
    gain = vector(vectors_ref, CROSS, CROSS.context_gain)
    bias = vector(vectors_ref, CROSS, CROSS.context_bias)
    max_ref[...] = jnp.full(max_ref.shape, negative, f32)
    sum_ref[...] = jnp.zeros(sum_ref.shape, f32)
    acc_ref[...] = jnp.zeros(acc_ref.shape, f32)
    block = scores_ref.shape[0]

    def visit(index, carry):
        begin = pl.multiple_of(index * block, block)
        some, full = block_kinds(count, begin, block, total)

        @pl.when(some)
        def _():
            unit, rstd = normalise(tokens_ref[pl.ds(begin, block), :].astype(f32))
            context = (unit * gain + bias).astype(bf16)
            scores_ref[...] = dot_nt(jnp.concatenate([context, context], axis=1), keyed)

            @pl.when(jnp.logical_not(full))
            def _():
                scores_ref[...] = masked(scores_ref[...], count, begin, total)

            old = max_ref[...]
            newest = jnp.maximum(old, jnp.max(scores_ref[...], axis=0, keepdims=True))
            weights = jnp.exp2(scores_ref[...] - newest)
            fade = jnp.exp2(old - newest)
            max_ref[...] = newest
            sum_ref[...] = sum_ref[...] * fade + column_sum(weights)
            acc_ref[...] = acc_ref[...] * fade + dot_tn(context, weights.astype(bf16))

        return carry

    lax.fori_loop(0, total // block, visit, 0)
    totals = sum_ref[...]
    lse_ref[...] = max_ref[...] + jnp.log2(totals)
    mixture_ref[...] = acc_ref[...] * (1.0 / totals)
    traffic.ship(lse_ref, mixture_ref)
    traffic.need(wv_ref, wo_ref)
    values = jnp.concatenate([wv_ref[...], wv_ref[...]], axis=0)
    attended = dot_tn(split(mixture_ref[...], 0), values)
    hidden_ref[...] = start + (
        dot(attended.astype(bf16), wo_ref[...]) + vector(vectors_ref, CROSS, CROSS.output_bias)
    )
    traffic.ship(hidden_ref)
    out_ref[...] = feed_forward(
        traffic, hidden_ref[...], vector(vectors_ref, CROSS, CROSS.feed_gain), vector(vectors_ref, CROSS, CROSS.feed_bias),
        up_ref, vector(vectors_ref, CROSS, CROSS.up_bias), down_ref, vector(vectors_ref, CROSS, CROSS.down_bias),
        normed_ref, active_ref, slope_ref,
    )


def cross_forward(count, tokens, start, vectors, wq, wk, wv, wo, up, down):
    block = min(BLOCK, tokens.shape[0])
    outs = [
        shape((LAT, D), bf16), shape((LAT, D), bf16), shape((LAT, C), f32), shape((C, LAT), f32),
        shape((1, LAT), f32), shape((LAT, D), f32), shape((LAT, D), bf16), shape((LAT, FF), bf16),
        shape((LAT, FF), bf16), shape((LAT, D), f32),
    ]
    scratch = [
        pltpu.VMEM((block, LAT), f32), pltpu.VMEM((C, LAT), f32), pltpu.VMEM((1, LAT), f32),
        pltpu.VMEM((1, LAT), f32),
    ]
    return streamed(
        cross_forward_kernel, "cross_forward", outs,
        [count, tokens, start, vectors, wq, wk, wv, wo, up, down], late=range(6, 10), early=range(9), scratch=scratch,
        smem=1, flops=100_000_000_000,
    )


def pair_mask(value, side):
    lane = lax.broadcasted_iota(jnp.int32, (1, LANES), 1)
    keep = (lane < HEAD) if side == 0 else (lane >= HEAD)
    return jnp.where(keep, value, jnp.zeros_like(value))


def latent_kernel(windows, parts, traffic, firsts_ref, hidden_ref, cotangent_ref, vectors_ref, joint_w_ref, merge_ref,
                  up_ref, down_ref, out_ref, grad_ref, *rest):
    windows_refs, rest = rest[:parts], rest[parts:]
    (flat_ref, probs_ref, joint_ref, mixed_ref, after_ref, normedl_ref, normed_ref, active_ref, slope_ref, query_grad_ref, joint_grad_ref) = rest
    gain = vector(vectors_ref, LATENT, LATENT.attend_gain)
    unit, rstd = normalise(hidden_ref[...])
    normedl_ref[...] = (unit * gain + vector(vectors_ref, LATENT, LATENT.attend_bias)).astype(bf16)
    joint_ref[...] = dot(normedl_ref[...], joint_w_ref[...]).astype(bf16)
    scale = HEAD ** (-0.5)
    for pair in range(HEADS // 2):
        lanes = slice(pair * LANES, (pair + 1) * LANES)
        query = joint_ref[:, lanes]
        keys = joint_ref[:, D + pair * LANES : D + (pair + 1) * LANES]
        values = joint_ref[:, 2 * D + pair * LANES : 2 * D + (pair + 1) * LANES]
        mixed = None
        for side in range(2):
            scores = dot_nt(pair_mask(keys, side), query) * (scale * LOG2E)
            weights = jnp.exp2(scores - jnp.max(scores, axis=0, keepdims=True))
            weights = weights * (1.0 / column_sum(weights))
            probs_ref[2 * pair + side] = weights
            part = dot_tn(pair_mask(values, side), weights.astype(bf16))
            mixed = part if mixed is None else mixed + part
        mixed_ref[lanes, :] = mixed.astype(bf16)
    traffic.need(merge_ref)
    after_ref[...] = hidden_ref[...] + (
        dot_tn(mixed_ref[...], merge_ref[...]) + vector(vectors_ref, LATENT, LATENT.merge_bias)
    )
    feed_gain = vector(vectors_ref, LATENT, LATENT.feed_gain)
    out_ref[...] = feed_forward(
        traffic, after_ref[...], feed_gain, vector(vectors_ref, LATENT, LATENT.feed_bias), up_ref,
        vector(vectors_ref, LATENT, LATENT.up_bias), down_ref, vector(vectors_ref, LATENT, LATENT.down_bias),
        normed_ref, active_ref, slope_ref,
    ).astype(bf16)

    traffic.ship(out_ref)
    traffic.need(cotangent_ref)
    clear_tail(flat_ref, LATENT_ROWS)
    after_grad = feed_backward(
        traffic, cotangent_ref[...].astype(f32), after_ref[...], feed_gain, up_ref, down_ref, normed_ref, active_ref,
        slope_ref, flat_ref, LATENT,
    )
    branch = after_grad.astype(bf16)
    put(flat_ref, LATENT.merge_weight[0], D, 0, dot(mixed_ref[...], branch))
    put_vector(flat_ref, LATENT.merge_bias[0], column_sum(branch.astype(f32)))
    mixed_grad = dot_nt(branch, merge_ref[...]).astype(bf16)
    for pair in range(HEADS // 2):
        lanes = slice(pair * LANES, (pair + 1) * LANES)
        query = joint_ref[:, lanes]
        keys = joint_ref[:, D + pair * LANES : D + (pair + 1) * LANES]
        values = joint_ref[:, 2 * D + pair * LANES : 2 * D + (pair + 1) * LANES]
        grads = mixed_grad[:, lanes]
        query_part = key_part = value_part = None
        for side in range(2):
            probs = probs_ref[2 * pair + side]
            part = dot(probs.astype(bf16), pair_mask(grads, side))
            value_part = part if side == 0 else value_part + part
            probs_grad = dot_nt(pair_mask(values, side), grads)
            delta = column_sum(probs * probs_grad)
            scores_grad = (probs * (probs_grad - delta)).astype(bf16)
            part = dot(scores_grad, pair_mask(query, side))
            key_part = part if side == 0 else key_part + part
            part = dot_tn(pair_mask(keys, side), scores_grad)
            query_part = part if side == 0 else query_part + part
        query_grad_ref[lanes, :] = query_part * scale
        joint_grad_ref[:, D + pair * LANES : D + (pair + 1) * LANES] = (key_part * scale).astype(bf16)
        joint_grad_ref[:, 2 * D + pair * LANES : 2 * D + (pair + 1) * LANES] = value_part.astype(bf16)
    joint_grad_ref[:, :D] = query_grad_ref[...].T.astype(bf16)
    put(flat_ref, LATENT.joint_weight[0], 3 * D, 0, dot_tn(normedl_ref[...], joint_grad_ref[...]))
    normed_grad = dot_nt(joint_grad_ref[...], joint_w_ref[...])
    put_vector(flat_ref, LATENT.attend_gain[0], column_sum(normed_grad * unit))
    put_vector(flat_ref, LATENT.attend_bias[0], column_sum(normed_grad))
    grad_ref[...] = after_grad + normalise_back(normed_grad, unit, rstd, gain)
    to_windows(flat_ref, firsts_ref, windows_refs, windows.rows, traffic)


def latent_layer(firsts, hidden, cotangent, vectors, joint, merge, up, down, windows, grid):
    outs = [shape((LAT, D), bf16), shape((LAT, D), f32)] + windows.outs(grid.nz)
    scratch = [
        pltpu.VMEM((windows.padded, LANES), f32), pltpu.VMEM((HEADS, LAT, LAT), f32),
        pltpu.VMEM((LAT, 3 * D), bf16), pltpu.VMEM((D, LAT), bf16), pltpu.VMEM((LAT, D), f32),
        pltpu.VMEM((LAT, D), bf16), pltpu.VMEM((LAT, D), bf16), pltpu.VMEM((LAT, FF), bf16),
        pltpu.VMEM((LAT, FF), bf16), pltpu.VMEM((D, LAT), f32), pltpu.VMEM((LAT, 3 * D), bf16),
    ]
    return streamed(
        functools.partial(latent_kernel, windows, grid.nz), "latent_layer", outs,
        [firsts, hidden, cotangent, vectors, joint, merge, up, down], late=[5, 6, 7, 2], early=[0],
        blocks={2 + c: windows.devices // grid.nz for c in range(grid.nz)}, scratch=scratch, smem=1,
        flops=20_000_000_000,
    )


SPLIT = CROSS.output_weight[0] // TILE * TILE


def cross_feed_kernel(windows, parts, traffic, firsts_ref, grad_ref, vectors_ref, wv_ref, wo_ref, up_ref, down_ref,
                      mixture_ref, hidden_ref, normed_ref, active_ref, saved_slope_ref,
                      hidden_grad_ref, valued_ref, delta_ref, value_grad_ref, *rest):
    windows_refs = rest[:parts]
    flat_ref, slope_ref = rest[parts:]
    clear_tail(flat_ref, CROSS_ROWS)
    slope_ref[...] = saved_slope_ref[...]
    hidden_grad = feed_backward(
        traffic, grad_ref[...], hidden_ref[...], vector(vectors_ref, CROSS, CROSS.feed_gain), up_ref, down_ref, normed_ref,
        active_ref, slope_ref, flat_ref, CROSS,
    )
    hidden_grad_ref[...] = hidden_grad
    traffic.ship(hidden_grad_ref)
    traffic.need(wv_ref, wo_ref, mixture_ref)
    branch = hidden_grad.astype(bf16)
    values = jnp.concatenate([wv_ref[...], wv_ref[...]], axis=0)
    mixture = split(mixture_ref[...], 0)
    attended = dot_tn(mixture, values)
    put(flat_ref, CROSS.output_weight[0], D, 0, dot_tn(attended.astype(bf16), branch))
    put_vector(flat_ref, CROSS.output_bias[0], column_sum(branch.astype(f32)))
    attended_grad = dot_nt(branch, wo_ref[...]).astype(bf16)
    both = dot(mixture, attended_grad)
    value_grad_ref[...] = both[:C] + both[C:]
    put(flat_ref, CROSS.value_weight[0], D, 0, value_grad_ref[...])
    valued = dot_nt(attended_grad, wv_ref[...])
    valued_ref[...] = split(valued, 1)
    delta_ref[...] = column_sum((attended_grad.astype(f32) * attended).T)
    flat_ref[:SPLIT, :] = jnp.zeros((SPLIT, LANES), f32)
    to_windows(flat_ref, firsts_ref, windows_refs, windows.rows, traffic)


def cross_feed(firsts, grad, vectors, wv, wo, up, down, mixture, hidden, normed, active, slope, windows, grid):
    outs = [
        shape((LAT, D), f32), shape((LAT, 2 * C), bf16), shape((1, LAT), f32), shape((C, D), f32),
    ] + windows.outs(grid.nz)
    return streamed(
        functools.partial(cross_feed_kernel, windows, grid.nz), "cross_feed", outs,
        [firsts, grad, vectors, wv, wo, up, down, mixture, hidden, normed, active, slope], late=[5, 3, 4, 7],
        early=[0], blocks={4 + c: windows.devices // grid.nz for c in range(grid.nz)},
        scratch=[pltpu.VMEM((windows.padded, LANES), f32), pltpu.VMEM((LAT, FF), bf16)], smem=1,
        flops=80_000_000_000,
    )


def attend_block(offset, blocks, count_ref, tokens_ref, valued_ref, delta_ref, vectors_ref, keyed_ref, lse_ref,
                 token_grad_ref, scores_ref, acc_ref, gains_ref, doubled_ref, paired_ref):
    block = tokens_ref.shape[0]
    begin = (pl.program_id(0) + offset) * block
    total = blocks * block
    count = count_ref[0]
    some, full = block_kinds(count, begin, block, total)

    @pl.when(pl.program_id(0) == 0)
    def _():
        doubled_ref[...] = split(keyed_ref[...] * LOG2E, 1)
        paired_ref[...] = split(keyed_ref[...], 1)

    @pl.when(some)
    def _():
        gain = vector(vectors_ref, CROSS, CROSS.context_gain)
        bias = vector(vectors_ref, CROSS, CROSS.context_bias)
        unit, rstd = normalise(tokens_ref[...].astype(f32))
        context = (unit * gain + bias).astype(bf16)
        twice = jnp.concatenate([context, context], axis=1)
        scores_ref[...] = dot_nt(twice, doubled_ref[...])

        @pl.when(jnp.logical_not(full))
        def _():
            scores_ref[...] = masked(scores_ref[...], count, begin, total)

        probs = jnp.exp2(scores_ref[...] - lse_ref[...])
        scores_grad = (probs * (dot_nt(twice, valued_ref[...]) - delta_ref[...])).astype(bf16)
        acc_ref[...] += dot_tn(context, scores_grad)
        wide = dot(probs.astype(bf16), valued_ref[...]) + dot(scores_grad, paired_ref[...])
        context_grad = wide[:, :C] + wide[:, C:]
        gains_ref[0:1, :] += column_sum(context_grad * unit)
        gains_ref[1:2, :] += column_sum(context_grad)
        token_grad_ref[...] = normalise_back(context_grad, unit, rstd, gain)

    @pl.when(jnp.logical_not(some))
    def _():
        token_grad_ref[...] = jnp.zeros(token_grad_ref.shape, f32)


def attend_first_kernel(blocks, count_ref, tokens_ref, valued_ref, delta_ref, vectors_ref, keyed_ref, lse_ref,
                        token_grad_ref, acc_ref, gains_ref, scores_ref, doubled_ref, paired_ref):
    @pl.when(pl.program_id(0) == 0)
    def _():
        acc_ref[...] = jnp.zeros(acc_ref.shape, f32)
        gains_ref[...] = jnp.zeros(gains_ref.shape, f32)

    attend_block(0, blocks, count_ref, tokens_ref, valued_ref, delta_ref, vectors_ref, keyed_ref, lse_ref,
                 token_grad_ref, scores_ref, acc_ref, gains_ref, doubled_ref, paired_ref)


def attend_second_kernel(offset, blocks, rows, parts, firsts_ref, count_ref, task_ref, tokens_ref, valued_ref,
                         delta_ref, vectors_ref, keyed_ref, lse_ref, acc_before_ref, gains_before_ref, hidden_grad_ref,
                         value_grad_ref, start_ref, wq_ref, wk_ref, normedq_ref, query_ref, kept_ref,
                         token_grad_ref, *rest):
    windows_refs = rest[:parts]
    flat_ref, scores_ref, acc_ref, gains_ref, doubled_ref, paired_ref = rest[parts:]

    @pl.when(pl.program_id(0) == 0)
    def _():
        acc_ref[...] = acc_before_ref[...]
        gains_ref[...] = gains_before_ref[...]

    attend_block(offset, blocks, count_ref, tokens_ref, valued_ref, delta_ref, vectors_ref, keyed_ref, lse_ref,
                 token_grad_ref, scores_ref, acc_ref, gains_ref, doubled_ref, paired_ref)

    @pl.when(pl.program_id(0) == pl.num_programs(0) - 1)
    def _():
        pulled = split(acc_ref[...] * D ** (-0.5), 0)
        both = dot(pulled, query_ref[...])
        put(flat_ref, CROSS.key_weight[0], D, 0, both[:C] + both[C:])
        put(flat_ref, CROSS.value_weight[0], D, 0, value_grad_ref[...])
        put_vector(flat_ref, CROSS.context_gain[0], gains_ref[0:1, :])
        put_vector(flat_ref, CROSS.context_bias[0], gains_ref[1:2, :])
        query_grad = dot_tn(pulled, jnp.concatenate([wk_ref[...], wk_ref[...]], axis=0)).astype(bf16)
        put(flat_ref, CROSS.query_weight[0], D, 0, dot_tn(normedq_ref[...], query_grad))
        normed_grad = dot_nt(query_grad, wq_ref[...])
        unit, rstd = normalise(start_ref[...])
        put_vector(flat_ref, CROSS.query_gain[0], column_sum(normed_grad * unit))
        put_vector(flat_ref, CROSS.query_bias[0], column_sum(normed_grad))
        gain = vector(vectors_ref, CROSS, CROSS.query_gain)
        start_grad = hidden_grad_ref[...] + normalise_back(normed_grad, unit, rstd, gain)
        put(flat_ref, CROSS.latents[0], D, 0, start_grad)
        first, unused = CROSS.task_table
        chunks = D // LANES
        flat_ref[first : first + NTASK * chunks, :] = jnp.zeros((NTASK * chunks, LANES), f32)
        sums = column_sum(start_grad)
        base = first + task_ref[0] * chunks
        for chunk in range(chunks):
            flat_ref[pl.ds(base + chunk, 1), :] = sums[:, chunk * LANES : (chunk + 1) * LANES]
        clear_tail(flat_ref, SPLIT)
        to_windows(flat_ref, firsts_ref, windows_refs, rows)


def attend_scratch(block):
    return [pltpu.VMEM((block, LAT), f32), pltpu.VMEM((LAT, 2 * C), bf16), pltpu.VMEM((LAT, 2 * C), bf16)]


def attend_first(count, tokens, valued, delta, vectors, keyed, lse):
    total = tokens.shape[0]
    block = min(BLOCK, total)
    blocks = total // block
    whole = [valued, delta, vectors, keyed, lse]
    row = lambda i: (i, 0)
    outs = [shape((total, C), f32), shape((C, LAT), f32), shape((8, C), f32)]
    scratch = attend_scratch(block)
    return pl.pallas_call(
        functools.partial(attend_first_kernel, blocks),
        name="attend_first",
        grid=(max(blocks // 2, 1),),
        out_shape=outs,
        in_specs=[pl.BlockSpec(memory_space=pltpu.SMEM), pl.BlockSpec((block, C), row)] + vmem_specs(len(whole)),
        out_specs=[pl.BlockSpec((block, C), row)] + vmem_specs(2),
        scratch_shapes=scratch,
        compiler_params=pltpu.CompilerParams(vmem_limit_bytes=vmem_limit(*whole, *scratch)),
        cost_estimate=pl.CostEstimate(flops=100_000_000_000, bytes_accessed=1, transcendentals=0),
    )(count, tokens, *whole)


def attend_second(firsts, count, task, tokens, valued, delta, vectors, keyed, lse, acc, gains, hidden_grad, value_grad,
                  start, wq, wk, normedq, query, token_grad, windows, grid):
    total = tokens.shape[0]
    block = min(BLOCK, total)
    blocks = total // block
    offset = max(blocks // 2, 1)
    rows = windows.quarter(grid.nx)
    last = grid.ny * grid.nz - 1
    assert SPLIT <= windows.first[last + 1] and blocks > offset
    flat_rows = max(windows.first[last] + rows * grid.nx, SPLIT + TILE)
    whole = [valued, delta, vectors, keyed, lse, acc, gains, hidden_grad, value_grad, start, wq, wk, normedq, query]
    half = windows.devices // grid.nz // grid.ny * rows
    small = [shape((half * depths, LANES), bf16) for c in range(grid.nz) for depths in halves(grid)]
    row = lambda i: (i + offset, 0)
    scratch = [
        pltpu.VMEM((flat_rows, LANES), f32), *attend_scratch(block)[:1], pltpu.VMEM((C, LAT), f32),
        pltpu.VMEM((8, C), f32), *attend_scratch(block)[1:],
    ]
    return pl.pallas_call(
        functools.partial(attend_second_kernel, offset, blocks, rows, len(small)),
        name="attend_second",
        grid=(blocks - offset,),
        out_shape=[shape((total, C), f32)] + small,
        in_specs=[pl.BlockSpec(memory_space=pltpu.SMEM)] * 3
        + [pl.BlockSpec((block, C), row)]
        + vmem_specs(len(whole))
        + [pl.BlockSpec(memory_space=pl.ANY)],
        out_specs=[pl.BlockSpec((block, C), row)] + vmem_specs(len(small)),
        scratch_shapes=scratch,
        input_output_aliases={4 + len(whole): 0},
        compiler_params=pltpu.CompilerParams(vmem_limit_bytes=vmem_limit(*whole, *small, *scratch)),
        cost_estimate=pl.CostEstimate(flops=100_000_000_000, bytes_accessed=1, transcendentals=0),
    )(firsts, count, task, tokens, *whole, token_grad)


def body(tokens, task_id, valid_count, cross_params, latent_params, out_grad):
    grid = Grid()
    devices = grid.nx * grid.ny * grid.nz
    cw = Windows(cross_params.shape[0] * devices, devices)
    lw = Windows(latent_params.shape[0] * devices, devices)
    gathered_from = grid.owners(gather_places(grid))
    scattered_to = grid.owners(grid.order())
    tokens = tokens[0]

    cross_window, latent_window = place([cross_params, latent_params], [cw, lw], grid.index)
    cross_column = gather_depth(cross_window, grid)
    latent_column = gather_depth(after(latent_window, *cross_column[1:]), grid)
    pieces = gather_plane_second(*gather_plane_first(cross_column, grid), grid)
    for piece in pieces:
        piece[0] = after(piece[0], *latent_column[1:])
        piece[1:] = [after(value, *latent_column[1:]) for value in piece[1:]]
    cross_all = sum(gather_core(*pieces, grid), [])
    latent_column = [after(value, pieces[0][-1], pieces[1][-1]) for value in latent_column]
    lows, highs = gather_plane_first(latent_column, grid)
    vectors, start, wq, wk, wv, wo, up, down = unpack_cross(cw.firsts(gathered_from), cross_all, task_id, cw)
    lows[0], highs[0] = after(lows[0], vectors), after(highs[0], vectors)
    first, second = gather_plane_second(lows, highs, grid)
    normedq, query, keyed, mixture, lse, hidden, normed, active, slope, result = cross_forward(
        valid_count, tokens, after(start, first[0], second[0]), vectors, wq, wk, wv, wo, up, down
    )
    first[1:] = [after(value, result) for value in first[1:]]
    second[1:] = [after(value, result) for value in second[1:]]
    latent_all = sum(gather_core(first, second, grid), [])
    latent_weights = unpack_latent(lw.firsts(gathered_from), latent_all, lw)
    latents_out, result_grad, *latent_parts = latent_layer(
        lw.firsts(scattered_to), result, out_grad[0], *latent_weights, lw, grid
    )

    latent_lows, latent_highs = reduce_first(reduce_core(latent_parts, grid), lw.rows, grid)
    hidden_grad, valued, delta, value_grad, *later_parts = cross_feed(
        cw.firsts(scattered_to), after(result_grad, latent_lows[0][0]), vectors, wv, wo, up, down, mixture, hidden,
        normed, active, slope, cw, grid,
    )
    latent_lows[0] = (after(latent_lows[0][0], delta), 0)
    latent_first, latent_second = reduce_second(latent_lows, latent_highs, lw.rows, grid)
    later_group = reduce_core(later_parts, grid)
    token_grad, acc, gains = attend_first(
        valid_count, tokens, valued, after(delta, latent_first[0][0]), vectors, keyed, lse
    )
    latent_first[0] = (after(latent_first[0][0], acc), 0)
    latent_column = reduce_depth(latent_first, latent_second, lw.rows, grid)
    later_group[0] = (after(later_group[0][0], latent_column[0]), 0)
    later_lows, later_highs = reduce_first(later_group, cw.rows, grid)
    owner, quarter = quarter_owners(grid)
    small_rows = cw.quarter(grid.nx)
    token_grad, *early_parts = attend_second(
        cw.firsts(owner) + quarter * small_rows, valid_count, task_id, tokens, valued, delta, vectors, keyed, lse,
        after(acc, later_lows[0][0]), gains, hidden_grad, value_grad, start, wq, wk, normedq, query, token_grad, cw,
        grid,
    )
    latent_column[0] = after(latent_column[0], early_parts[0])
    latent_share = extract(latent_column, [], lw, grid)
    later_lows[0] = (after(later_lows[0][0], latent_share), 0)
    early_groups = [reduce_core(early_parts[half::2], grid) for half in range(2)]
    later_first, later_second, early_lows, early_highs = reduce_second_and_first(
        later_lows, later_highs, cw.rows, early_groups, small_rows, grid
    )
    early_first, early_second = reduce_second(early_lows, early_highs, small_rows, grid)
    column = reduce_depth_both(later_first, later_second, cw.rows, early_first, early_second, small_rows, grid)
    quarters = collect_quarters(column, cw.rows, small_rows, grid)
    return (latents_out[None], token_grad[None], extract(column, quarters, cw, grid), latent_share)


def solution(mesh):
    return jax.shard_map(
        body,
        mesh=mesh,
        in_specs=(
            P(AXES, None, None),
            P(AXES),
            P(AXES),
            P(AXES),
            P(AXES),
            P(AXES, None, None),
        ),
        out_specs=(
            P(AXES, None, None),
            P(AXES, None, None),
            P(AXES),
            P(AXES),
        ),
        check_vma=False,
    )
```

```python
import functools
import math
import types

import jax
import jax.numpy as jnp
from jax import lax
from jax.experimental import pallas as pl
from jax.experimental.pallas import tpu as pltpu
from jax.sharding import PartitionSpec as P

D = 512
FF = 2048
C = 128
LAT = 512
HEADS = 8
HEAD = 64
NTASK = 18
LANG = 77
LANES = 128
TILE = 16
UNIT = TILE * LANES
BLOCK = 2048
PART = 512
AXES = ("gx", "gy", "gz")

epsilon = 1e-05
negative = -1e30
LOG2E = math.log2(math.e)
bf16 = jnp.bfloat16
f32 = jnp.float32
VMEM_LIMIT = 60 * 1024 * 1024
ROOM = 6 * 1024 * 1024


def layout_of(**shapes):
    table = {}
    row = 0
    for name, dims in shapes.items():
        table[name] = (row, dims)
        row += math.prod(dims) // LANES
    return types.SimpleNamespace(**table), row


CROSS, CROSS_ROWS = layout_of(
    latents=(LAT, D),
    task_table=(NTASK, D),
    query_gain=(D,),
    query_bias=(D,),
    context_gain=(C,),
    context_bias=(C,),
    query_weight=(D, D),
    key_weight=(C, D),
    value_weight=(C, D),
    output_weight=(D, D),
    output_bias=(D,),
    feed_gain=(D,),
    feed_bias=(D,),
    up_weight=(D, FF),
    up_bias=(FF,),
    down_weight=(FF, D),
    down_bias=(D,),
)
LATENT, LATENT_ROWS = layout_of(
    attend_gain=(D,),
    attend_bias=(D,),
    joint_weight=(D, 3 * D),
    merge_weight=(D, D),
    merge_bias=(D,),
    feed_gain=(D,),
    feed_bias=(D,),
    up_weight=(D, FF),
    up_bias=(FF,),
    down_weight=(FF, D),
    down_bias=(D,),
)


def vectors_of(table):
    return [place for place in vars(table).values() if len(place[1]) == 1]


class Windows:
    def __init__(self, total, devices):
        self.total = total
        self.devices = devices
        self.shard = total // devices
        starts = [self.shard * d for d in range(devices)]
        self.first = [s // UNIT * TILE for s in starts]
        self.phase = [s % UNIT for s in starts]
        self.rows = max(-(-(p + self.shard) // UNIT) * TILE for p in self.phase)
        self.padded = max(f + self.rows for f in self.first)
        self.full = -(-total // UNIT) * TILE
        self.shard_rows = -(-self.shard // (8 * LANES)) * 8

    def outs(self, parts):
        return [shape((self.devices // parts * self.rows, LANES), bf16)] * parts

    def firsts(self, owners):
        return self.shard * owners // UNIT * TILE

    def quarter(self, parts):
        return -(-self.rows // (parts * TILE)) * TILE


def dot(left, right):
    return jnp.dot(left, right, preferred_element_type=f32)


def dot_nt(left, right):
    return lax.dot_general(left, right, (((1,), (1,)), ((), ())), preferred_element_type=f32)


def dot_tn(left, right):
    return lax.dot_general(left, right, (((0,), (0,)), ((), ())), preferred_element_type=f32)


def split(value, axis):
    high = value.astype(bf16)
    low = (value - high.astype(f32)).astype(bf16)
    return jnp.concatenate([high, low], axis=axis)


def normalise(value):
    centred = value - jnp.mean(value, axis=-1, keepdims=True)
    rstd = lax.rsqrt(jnp.mean(centred * centred, axis=-1, keepdims=True) + epsilon)
    return centred * rstd, rstd


def normalise_back(grad, unit, rstd, gain):
    inner = grad * gain
    return rstd * (
        inner
        - jnp.mean(inner, axis=-1, keepdims=True)
        - unit * jnp.mean(inner * unit, axis=-1, keepdims=True)
    )


def column_sum(value):
    return jnp.sum(value, axis=0, keepdims=True)


def vmem_specs(count):
    return [pl.BlockSpec(memory_space=pltpu.VMEM)] * count


def shape(dims, dtype):
    return jax.ShapeDtypeStruct(dims, dtype)


def bytes_of(value):
    return math.prod(value.shape) * jnp.dtype(value.dtype).itemsize


def vmem_limit(*values):
    return min(sum(map(bytes_of, values)) + 16 * 2**20, VMEM_LIMIT)


def call(kernel, name, outs, inputs, scratch=(), smem=0, flops=0, moved=0, alone=True):
    specs = [pl.BlockSpec(memory_space=pltpu.SMEM)] * smem + vmem_specs(len(inputs) - smem)
    limit = VMEM_LIMIT if alone else vmem_limit(*inputs, *jax.tree.leaves(outs), *scratch)
    return pl.pallas_call(
        kernel,
        name=name,
        out_shape=outs,
        in_specs=specs,
        out_specs=jax.tree.map(lambda _: pl.BlockSpec(memory_space=pltpu.VMEM), outs),
        scratch_shapes=list(scratch),
        compiler_params=pltpu.CompilerParams(vmem_limit_bytes=limit),
        cost_estimate=pl.CostEstimate(flops=flops, bytes_accessed=moved, transcendentals=0),
    )(*inputs)


class Traffic:
    def __init__(self):
        self.loads, self.stores, self.blocks, self.begun = {}, {}, {}, []

    def need(self, *refs):
        for ref in refs:
            copy = self.loads.pop(id(ref), None)
            if copy is not None:
                copy.wait()

    def ship(self, *refs):
        for ref in refs:
            copy = self.stores.pop(id(ref), None)
            if copy is not None:
                copy.start()
                self.begun.append(copy)

    def block(self, ref, part, number):
        target, sem = self.blocks[id(ref)]
        return pltpu.make_async_copy(ref.at[part], target.at[part], sem.at[number])


def streamed(kernel, name, outs, inputs, late=(), early=(), blocks=None, scratch=(), smem=0, flops=0, room=0):
    blocks = blocks or {}
    shipped = list(early) + list(blocks)
    vmem, hbm = pl.BlockSpec(memory_space=pltpu.VMEM), pl.BlockSpec(memory_space=pltpu.HBM)
    held = [pltpu.VMEM(inputs[i].shape, inputs[i].dtype) for i in late]
    held += [pltpu.VMEM(outs[i].shape, outs[i].dtype) for i in shipped]
    sems = [pltpu.SemaphoreType.DMA((max(len(late), 1),)), pltpu.SemaphoreType.DMA((max(len(early), 1),))]
    sems += [pltpu.SemaphoreType.DMA((number,)) for number in blocks.values()]

    def body(*refs):
        takes, gives = list(refs[: len(inputs)]), list(refs[len(inputs) : len(inputs) + len(outs)])
        rest = refs[len(inputs) + len(outs) :]
        buffers, rest = rest[: len(held)], rest[len(held) :]
        load_sem, store_sem = rest[:2]
        block_sems, rest = rest[2 : len(sems)], rest[len(sems) :]
        traffic = Traffic()
        for k, i in enumerate(late):
            copy = pltpu.make_async_copy(takes[i], buffers[k], load_sem.at[k])
            copy.start()
            traffic.loads[id(buffers[k])] = copy
            takes[i] = buffers[k]
        for k, i in enumerate(shipped):
            buffer = buffers[len(late) + k]
            if k < len(early):
                traffic.stores[id(buffer)] = pltpu.make_async_copy(buffer, gives[i], store_sem.at[k])
            else:
                traffic.blocks[id(buffer)] = (gives[i], block_sems[k - len(early)])
            gives[i] = buffer
        kernel(traffic, *takes, *gives, *rest)
        assert not traffic.loads and not traffic.stores
        for copy in traffic.begun:
            copy.wait()

    return pl.pallas_call(
        body,
        name=name,
        out_shape=outs,
        in_specs=[pl.BlockSpec(memory_space=pltpu.SMEM)] * smem
        + [hbm if i in late else vmem for i in range(smem, len(inputs))],
        out_specs=[hbm if i in shipped else vmem for i in range(len(outs))],
        scratch_shapes=held + sems + list(scratch),
        compiler_params=pltpu.CompilerParams(vmem_limit_bytes=VMEM_LIMIT - room),
        cost_estimate=pl.CostEstimate(flops=flops, bytes_accessed=1, transcendentals=0),
    )(*inputs)


def shifted(value, shift):
    down, across = shift // LANES, shift % LANES
    turned = pltpu.roll(value, across, axis=1)
    above = pltpu.roll(turned, 1, axis=0)
    lane = lax.broadcasted_iota(jnp.int32, value.shape, 1)
    return pltpu.roll(jnp.where(lane < across, above, turned), down, axis=0)


def place_kernel(shifts_ref, shards_ref, *out_refs):
    begin = 0
    for number, out_ref in enumerate(out_refs):
        rows = out_ref.shape[0]
        value = shards_ref[begin : begin + rows, :].astype(f32)
        out_ref[...] = shifted(value, shifts_ref[number]).astype(bf16)
        begin += rows


def place(shards, windows, index):
    padded = [
        jnp.pad(shard, (0, w.rows * LANES - w.shard)) for shard, w in zip(shards, windows)
    ]
    together = jnp.concatenate(padded).reshape(-1, LANES)
    shifts = jnp.stack([(w.shard * index) % UNIT for w in windows])
    outs = [shape((w.rows, LANES), bf16) for w in windows]
    return call(place_kernel, "place", outs, [shifts, together], smem=1, alone=False)


def extract_kernel(count, shift_ref, *refs):
    out_ref, total_ref = refs[-2:]
    rows = total_ref.shape[0]
    value = refs[0][:rows, :].astype(f32)
    for ref in refs[1:count]:
        value += ref[:rows, :].astype(f32)
    total_ref[...] = value
    begin = 0
    for ref in refs[count:-2]:
        size = min(ref.shape[0], rows - begin)
        if size > 0:
            total_ref[begin : begin + size, :] += ref[:size, :].astype(f32)
        begin += ref.shape[0]
    down, across = shift_ref[0] // LANES, shift_ref[0] % LANES
    turned = pltpu.roll(total_ref[...], lax.rem(LANES - across, LANES), axis=1)
    below = pltpu.roll(turned, rows - 1, axis=0)
    lane = lax.broadcasted_iota(jnp.int32, (rows, LANES), 1)
    merged = pltpu.roll(
        jnp.where(lane < LANES - across, turned, below), lax.rem(rows - down, rows), axis=0
    )
    out_ref[...] = merged[: out_ref.shape[0]]


def extract(parts, quarters, windows, grid):
    shift = (windows.shard * grid.index) % UNIT
    rows = min(windows.shard_rows, windows.rows)
    found = call(
        functools.partial(extract_kernel, len(parts)), "extract", shape((rows, LANES), f32),
        [shift.reshape(1), *parts, *quarters], scratch=[pltpu.VMEM((windows.rows, LANES), f32)], smem=1,
        alone=False,
    )
    return found.reshape(-1)[: windows.shard]


class Grid:
    def __init__(self):
        self.nx, self.ny, self.nz = (lax.axis_size(axis) for axis in AXES)
        self.nl = 2 if self.nx % 2 == 0 else 1
        self.nh = self.nx // self.nl
        self.index = lax.axis_index(AXES)

    def order(self):
        return [
            (c, h, l, y)
            for c in range(self.nz)
            for h in range(self.nh)
            for l in range(self.nl)
            for y in range(self.ny)
        ]

    def owners(self, places):
        gx, gy, gz = (lax.axis_index(axis) for axis in AXES)
        c, h, l, y = (jnp.array(column, jnp.int32) for column in zip(*places))
        high = (gx // self.nl + h) % self.nh
        low = (gx % self.nl + l) % self.nl
        return ((high * self.nl + low) * self.ny + (gy + y) % self.ny) * self.nz + (gz + c) % self.nz

    def along_core(self, value, step):
        return lax.ppermute(value, AXES[2], [(i, (i + step) % self.nz) for i in range(self.nz)])

    def along_depth(self, value, step):
        return lax.ppermute(value, AXES[1], [(i, (i + step) % self.ny) for i in range(self.ny)])

    def along_low(self, value, step):
        nl = self.nl
        return lax.ppermute(
            value, AXES[0], [(i, i // nl * nl + (i + step) % nl) for i in range(self.nx)]
        )

    def along_high(self, value, step):
        nl = self.nl
        return lax.ppermute(value, AXES[0], [(i, (i + step * nl) % self.nx) for i in range(self.nx)])


def combine_kernel(groups, picks, *refs):
    starts = [sum(len(bases) for rows, bases in groups[:g]) for g in range(len(groups))]
    outputs = refs[sum(len(bases) for rows, bases in groups) :]
    for output, pick in zip(outputs, picks):
        row = 0
        for g, block in pick:
            rows, bases = groups[g]
            total = None
            for i, base in enumerate(bases):
                begin = base + block * rows
                part = refs[starts[g] + i][begin : begin + rows, :].astype(f32)
                total = part if total is None else total + part
            output[row : row + rows, :] = total.astype(bf16)
            row += rows


def combine(name, groups, picks):
    inputs = [array for rows, sources in groups for array, base in sources]
    kinds = tuple((rows, tuple(base for array, base in sources)) for rows, sources in groups)
    sizes = [sum(groups[g][0] for g, block in pick) for pick in picks]
    outs = [shape((size, LANES), bf16) for size in sizes]
    moved = 6 * LANES * sum(sizes)
    return call(
        functools.partial(combine_kernel, kinds, picks), name, outs, inputs, flops=moved, moved=moved, alone=False
    )


def reduce_core(parts, grid):
    return [(parts[0], 0)] + [(grid.along_core(parts[c], c), 0) for c in range(1, grid.nz)]


def first_picks(grid, g):
    nh, nl, ny = grid.nh, grid.nl, grid.ny
    half = ny // 2
    block = lambda h, l, y: (g, (h * nl + l) * ny + y)
    lows = [[block(h, l, y) for h in range(nh) for y in range(half)] for l in range(nl)]
    highs = [[block(h, l, y) for l in range(nl) for y in range(half, ny)] for h in range(nh)]
    return lows, highs


def halves(grid):
    return [grid.ny // 2, grid.ny - grid.ny // 2]


def half_order(grid):
    half = grid.ny // 2
    places = []
    for c in range(grid.nz):
        for depths in (range(half), range(half, grid.ny)):
            places += [(c, h, l, y) for h in range(grid.nh) for l in range(grid.nl) for y in depths]
    return places


def half_first_picks(grid, first_group, second_group):
    nh, nl = grid.nh, grid.nl
    half, rest = halves(grid)
    lows = [[(first_group, (h * nl + l) * half + y) for h in range(nh) for y in range(half)] for l in range(nl)]
    highs = [[(second_group, (h * nl + l) * rest + y) for l in range(nl) for y in range(rest)] for h in range(nh)]
    return lows, highs


def second_picks(grid, low_group, high_group):
    half = grid.ny // 2
    rest = grid.ny - half
    highs = [[(low_group, h * half + y) for y in range(half)] for h in range(grid.nh)]
    lows = [[(high_group, l * rest + y) for y in range(rest)] for l in range(grid.nl)]
    return highs, lows


def depth_picks(grid, first_group, second_group):
    half = grid.ny // 2
    return [(first_group, y) for y in range(half)] + [(second_group, y) for y in range(grid.ny - half)]


def send_low(arrays, grid):
    return [grid.along_low(array, l + 1) for l, array in enumerate(arrays)]


def send_high(arrays, grid):
    return [grid.along_high(array, h + 1) for h, array in enumerate(arrays)]


def send_depth(arrays, grid):
    return [grid.along_depth(array, y + 1) for y, array in enumerate(arrays)]


def at(arrays, base=0):
    return [(array, base) for array in arrays]


def reduce_first(group, rows, grid):
    lows, highs = first_picks(grid, 0)
    outs = combine("plane_first", [(rows, group)], lows + highs)
    keep_low, keep_high = outs[0], outs[grid.nl]
    return (
        at([keep_low] + send_low(outs[1 : grid.nl], grid)),
        at([keep_high] + send_high(outs[grid.nl + 1 :], grid)),
    )


def reduce_second(lows, highs, rows, grid):
    to_high, to_low = second_picks(grid, 0, 1)
    outs = combine("plane_second", [(rows, lows), (rows, highs)], to_high + to_low)
    keep_first, keep_second = outs[0], outs[grid.nh]
    return (
        at([keep_first] + send_high(outs[1 : grid.nh], grid)),
        at([keep_second] + send_low(outs[grid.nh + 1 :], grid)),
    )


def reduce_depth(first, second, rows, grid):
    outs = combine("depth", [(rows, first), (rows, second)], [[pick] for pick in depth_picks(grid, 0, 1)])
    return [outs[0]] + send_depth(outs[1:], grid)


def reduce_second_and_first(lows, highs, rows, small_groups, small_rows, grid):
    to_high, to_low = second_picks(grid, 0, 1)
    small_low, small_high = half_first_picks(grid, 2, 3)
    nh, nl, half = grid.nh, grid.nl, grid.ny // 2
    picks = [to_high[0], to_low[0], small_low[0], small_high[0]]
    picks += [to_high[h] + small_high[h] for h in range(1, nh)]
    picks += [to_low[l] + small_low[l] for l in range(1, nl)]
    outs = combine("second_and_first", [(rows, lows), (rows, highs)] + [(small_rows, group) for group in small_groups], picks)
    keep_first, keep_second, keep_low, keep_high = outs[:4]
    high = send_high(outs[4 : 3 + nh], grid)
    low = send_low(outs[3 + nh :], grid)
    first, second = at([keep_first]) + at(high), at([keep_second]) + at(low)
    lows = at([keep_low]) + at(low, (grid.ny - half) * rows)
    highs = at([keep_high]) + at(high, half * rows)
    return first, second, lows, highs


def reduce_depth_both(first, second, rows, small_first, small_second, small_rows, grid):
    groups = [(rows, first), (rows, second), (small_rows, small_first), (small_rows, small_second)]
    picks = [list(pair) for pair in zip(depth_picks(grid, 0, 1), depth_picks(grid, 2, 3))]
    outs = combine("depth_both", groups, picks)
    return [outs[0]] + send_depth(outs[1:], grid)


def quarter_owners(grid):
    gx, gy, gz = (lax.axis_index(axis) for axis in AXES)
    c, h, l, y = (jnp.array(column, jnp.int32) for column in zip(*half_order(grid)))
    quarter = (gx // grid.nl + h) % grid.nh * grid.nl + (gx % grid.nl + l) % grid.nl
    return (gy + y) % grid.ny * grid.nz + (gz + c) % grid.nz, quarter


def collect_quarters(parts, base, rows, grid):
    (own,) = combine("quarter", [(rows, at(parts, base))], [[(0, 0)]])
    zero = jnp.zeros_like(own)
    first = jnp.where(lax.axis_index(AXES[0]) == 0, own, zero)
    return [first] + [lax.ppermute(own, AXES[0], [(x, 0)]) for x in range(1, grid.nx)]


def gather_depth(window, grid):
    return [window] + [grid.along_depth(window, -y) for y in range(1, grid.ny)]


def gather_plane_first(column, grid):
    half = grid.ny // 2
    first, second = jnp.concatenate(column[:half]), jnp.concatenate(column[half:])
    lows = [first] + [grid.along_low(first, -l) for l in range(1, grid.nl)]
    highs = [second] + [grid.along_high(second, -h) for h in range(1, grid.nh)]
    return lows, highs


def gather_plane_second(lows, highs, grid):
    first, second = jnp.concatenate(lows), jnp.concatenate(highs)
    return (
        [first] + [grid.along_high(first, -h) for h in range(1, grid.nh)],
        [second] + [grid.along_low(second, -l) for l in range(1, grid.nl)],
    )


def gather_core(first, second, grid):
    pieces = first + second
    return [pieces] + [[grid.along_core(piece, -c) for piece in pieces] for c in range(1, grid.nz)]


def gather_places(grid):
    half = grid.ny // 2
    places = []
    for c in range(grid.nz):
        for h in range(grid.nh):
            places += [(c, h, l, y) for l in range(grid.nl) for y in range(half)]
        for l in range(grid.nl):
            places += [(c, h, l, y) for h in range(grid.nh) for y in range(half, grid.ny)]
    return places


def after(value, *others):
    return lax.optimization_barrier((value, *others))[0]


def assemble(firsts_ref, gathered_refs, flat_ref, windows):
    rows = windows.rows
    inner = max(windows.shard // UNIT - 1, 0) * TILE
    after = TILE + inner

    def clear(place, carry):
        first = pl.multiple_of(firsts_ref[place], TILE)
        flat_ref[pl.ds(first, TILE), :] = jnp.zeros((TILE, LANES), f32)
        flat_ref[pl.ds(first + after, rows - after), :] = jnp.zeros((rows - after, LANES), f32)
        return carry

    lax.fori_loop(0, windows.devices, clear, 0)
    place = 0
    for gathered_ref in gathered_refs:
        blocks = gathered_ref.shape[0] // rows

        def visit(block, carry, gathered_ref=gathered_ref, place=place):
            first = pl.multiple_of(firsts_ref[place + block], TILE)
            value = gathered_ref[pl.ds(pl.multiple_of(block * rows, TILE), rows), :].astype(f32)
            flat_ref[pl.ds(first, TILE), :] += value[:TILE]
            if inner:
                flat_ref[pl.ds(first + TILE, inner), :] = value[TILE:after]
            flat_ref[pl.ds(first + after, rows - after), :] += value[after:]
            return carry

        lax.fori_loop(0, blocks, visit, 0)
        place += blocks


def relay(flat_ref, place, out_ref):
    first, (rows, columns) = place
    chunks = columns // LANES
    step = 64

    def body(index, carry):
        begin = pl.multiple_of(index * step, step)
        for chunk in range(chunks):
            part = flat_ref[pl.ds(first + begin * chunks + chunk, step, stride=chunks), :]
            out_ref[pl.ds(begin, step), chunk * LANES : (chunk + 1) * LANES] = part.astype(out_ref.dtype)
        return carry

    lax.fori_loop(0, rows // step, body, 0)


def relay_vectors(flat_ref, table, out_ref):
    for index, (first, dims) in enumerate(vectors_of(table)):
        for chunk in range(dims[0] // LANES):
            out_ref[index : index + 1, chunk * LANES : (chunk + 1) * LANES] = flat_ref[
                first + chunk : first + chunk + 1, :
            ]


def unpack_cross_kernel(windows, count, traffic, firsts_ref, task_ref, *refs):
    vectors_ref, start_ref, query_ref, key_ref, value_ref, output_ref, up_ref, down_ref, flat_ref = refs[count:]
    assemble(firsts_ref, refs[:count], flat_ref, windows)
    relay_vectors(flat_ref, CROSS, vectors_ref)
    traffic.ship(vectors_ref)
    chunks = D // LANES
    first, unused = CROSS.task_table
    base = first + task_ref[0] * chunks
    relay(flat_ref, CROSS.latents, start_ref)
    for chunk in range(chunks):
        row = flat_ref[pl.ds(base + chunk, 1), :]
        start_ref[:, chunk * LANES : (chunk + 1) * LANES] += row
    traffic.ship(start_ref)
    relay(flat_ref, CROSS.query_weight, query_ref)
    traffic.ship(query_ref)
    relay(flat_ref, CROSS.key_weight, key_ref)
    traffic.ship(key_ref)
    relay(flat_ref, CROSS.value_weight, value_ref)
    traffic.ship(value_ref)
    relay(flat_ref, CROSS.output_weight, output_ref)
    traffic.ship(output_ref)
    relay(flat_ref, CROSS.up_weight, up_ref)
    traffic.ship(up_ref)
    relay(flat_ref, CROSS.down_weight, down_ref)
    traffic.ship(down_ref)


def unpack_cross(firsts, gathered, task, windows):
    outs = [
        shape((16, FF), f32), shape((LAT, D), f32), shape((D, D), bf16), shape((C, D), bf16),
        shape((C, D), bf16), shape((D, D), bf16), shape((D, FF), bf16), shape((FF, D), bf16),
    ]
    return streamed(
        functools.partial(unpack_cross_kernel, windows, len(gathered)), "unpack_cross", outs,
        [firsts, task, *gathered], early=range(len(outs)), scratch=[pltpu.VMEM((windows.padded, LANES), f32)], smem=2,
        flops=20_000_000_000, room=ROOM,
    )


def unpack_latent_kernel(windows, count, traffic, firsts_ref, *refs):
    vectors_ref, joint_ref, merge_ref, up_ref, down_ref, flat_ref = refs[count:]
    assemble(firsts_ref, refs[:count], flat_ref, windows)
    relay_vectors(flat_ref, LATENT, vectors_ref)
    traffic.ship(vectors_ref)
    relay(flat_ref, LATENT.joint_weight, joint_ref)
    traffic.ship(joint_ref)
    relay(flat_ref, LATENT.merge_weight, merge_ref)
    traffic.ship(merge_ref)
    relay(flat_ref, LATENT.up_weight, up_ref)
    traffic.ship(up_ref)
    relay(flat_ref, LATENT.down_weight, down_ref)
    traffic.ship(down_ref)


def unpack_latent(firsts, gathered, windows):
    outs = [
        shape((8, FF), f32), shape((D, 3 * D), bf16), shape((D, D), bf16), shape((D, FF), bf16),
        shape((FF, D), bf16),
    ]
    return streamed(
        functools.partial(unpack_latent_kernel, windows, len(gathered)), "unpack_latent", outs,
        [firsts, *gathered], early=range(len(outs)), scratch=[pltpu.VMEM((windows.padded, LANES), f32)], smem=1,
        room=ROOM,
    )


def put(flat_ref, first, columns, row, value, column=0):
    chunks = columns // LANES
    rows = value.shape[0]
    for chunk in range(value.shape[1] // LANES):
        begin = first + row * chunks + column // LANES + chunk
        flat_ref[pl.ds(begin, rows, stride=chunks), :] = value[:, chunk * LANES : (chunk + 1) * LANES]


def put_vector(flat_ref, first, value, column=0):
    for chunk in range(value.shape[1] // LANES):
        row = first + column // LANES + chunk
        flat_ref[row : row + 1, :] = value[:, chunk * LANES : (chunk + 1) * LANES]


def to_windows(flat_ref, firsts_ref, out_refs, rows, traffic=None):
    begin = 0
    for out_ref in out_refs:
        blocks = out_ref.shape[0] // rows

        def visit(place, carry, out_ref=out_ref, begin=begin):
            first = pl.multiple_of(firsts_ref[begin + place], TILE)
            part = pl.ds(pl.multiple_of(place * rows, TILE), rows)
            out_ref[part, :] = flat_ref[pl.ds(first, rows), :].astype(bf16)
            if traffic:
                traffic.block(out_ref, part, place).start()
            return carry

        lax.fori_loop(0, blocks, visit, 0)
        begin += blocks
    if not traffic:
        return
    for out_ref in out_refs:

        def finish(place, carry, out_ref=out_ref):
            part = pl.ds(pl.multiple_of(place * rows, TILE), rows)
            traffic.block(out_ref, part, place).wait()
            return carry

        lax.fori_loop(0, out_ref.shape[0] // rows, finish, 0)


def clear_tail(flat_ref, used):
    total = flat_ref.shape[0]
    flat_ref[used:total, :] = jnp.zeros((total - used, LANES), f32)


def gelu_and_slope(value):
    half = 0.5 + 0.5 * lax.erf(value * math.sqrt(0.5))
    density = jnp.exp2(value * value * (-0.5 * LOG2E)) * (1.0 / math.sqrt(2.0 * math.pi))
    return value * half, half + value * density


def feed_forward(traffic, hidden, gain, bias, up_ref, up_bias, down_ref, down_bias, normed_ref, active_ref, slope_ref):
    unit, rstd = normalise(hidden)
    normed_ref[...] = (unit * gain + bias).astype(bf16)
    traffic.ship(normed_ref)
    traffic.need(up_ref)
    step = 256
    for begin in range(0, FF, step):
        inner = dot(normed_ref[...], up_ref[:, begin : begin + step]) + up_bias[:, begin : begin + step]
        active, slope = gelu_and_slope(inner)
        active_ref[:, begin : begin + step] = active.astype(bf16)
        slope_ref[:, begin : begin + step] = slope.astype(bf16)
    traffic.ship(active_ref, slope_ref)
    traffic.need(down_ref)
    return hidden + (dot(active_ref[...], down_ref[...]) + down_bias)


def feed_backward(traffic, grad, hidden, gain, up_ref, down_ref, normed_ref, active_ref, slope_ref, flat_ref, table,
                  base=0):
    unit, rstd = normalise(hidden)
    branch = grad.astype(bf16)
    put_vector(flat_ref, table.down_bias[0] - base, column_sum(branch.astype(f32)))
    step = 256
    total = None
    normed = normed_ref[...]
    for begin in range(0, FF, step):
        put(flat_ref, table.down_weight[0] - base, D, begin, dot_tn(active_ref[:, begin : begin + step], branch))
        active_grad = dot_nt(branch, down_ref[begin : begin + step, :])
        inner = (active_grad * slope_ref[:, begin : begin + step].astype(f32)).astype(bf16)
        slope_ref[:, begin : begin + step] = inner
        put_vector(flat_ref, table.up_bias[0] - base, column_sum(inner.astype(f32)), begin)
        put(flat_ref, table.up_weight[0] - base, FF, 0, dot_tn(normed, inner), begin)
    traffic.need(up_ref)
    normed_grad = dot_nt(slope_ref[...], up_ref[...])
    put_vector(flat_ref, table.feed_gain[0] - base, column_sum(normed_grad * unit))
    put_vector(flat_ref, table.feed_bias[0] - base, column_sum(normed_grad))
    return grad + normalise_back(normed_grad, unit, rstd, gain)


def vector(vectors_ref, table, place):
    index = vectors_of(table).index(place)
    return vectors_ref[index : index + 1, : place[1][0]]


def block_kinds(count, begin, block, total):
    language = total - LANG
    end = begin + block
    some = (begin < count) | (end > language)
    full = (end <= count) | (count >= language) | (begin >= language)
    return some, full


def masked(scores, count, begin, total):
    place = begin + lax.broadcasted_iota(jnp.int32, (scores.shape[0], 1), 0)
    valid = (place < count) | (place >= total - LANG)
    return jnp.where(valid, scores, negative)


def cross_forward_kernel(traffic, count_ref, tokens_ref, start_ref, vectors_ref, wq_ref, wk_ref, wv_ref, wo_ref,
                         up_ref, down_ref,
                         normedq_ref, query_ref, keyed_ref, mixture_ref, lse_ref, hidden_ref, normed_ref,
                         active_ref, slope_ref, out_ref,
                         acc_ref, max_ref, sum_ref):
    total = tokens_ref.shape[0]
    count = count_ref[0]
    start = start_ref[...]
    unit, rstd = normalise(start)
    normedq_ref[...] = (
        unit * vector(vectors_ref, CROSS, CROSS.query_gain) + vector(vectors_ref, CROSS, CROSS.query_bias)
    ).astype(bf16)
    traffic.ship(normedq_ref)
    query_ref[...] = dot(normedq_ref[...], wq_ref[...]).astype(bf16)
    traffic.ship(query_ref)
    keyed_ref[...] = dot_nt(query_ref[...], wk_ref[...]) * D ** (-0.5)
    traffic.ship(keyed_ref)
    keyed = split(keyed_ref[...] * LOG2E, 1)
    gain = vector(vectors_ref, CROSS, CROSS.context_gain)
    bias = vector(vectors_ref, CROSS, CROSS.context_bias)
    max_ref[...] = jnp.full(max_ref.shape, negative, f32)
    sum_ref[...] = jnp.zeros(sum_ref.shape, f32)
    acc_ref[...] = jnp.zeros(acc_ref.shape, f32)
    block = min(BLOCK, total)

    def visit(index, carry):
        begin = pl.multiple_of(index * block, block)
        some, full = block_kinds(count, begin, block, total)

        @pl.when(some)
        def _():
            contexts, scores = [], []
            for part in range(0, block, PART):
                unit, rstd = normalise(tokens_ref[pl.ds(begin + part, PART), :].astype(f32))
                context = (unit * gain + bias).astype(bf16)
                contexts.append(context)
                raw = dot_nt(jnp.concatenate([context, context], axis=1), keyed)
                scores.append(masked(raw, count, begin + part, total))
            old = max_ref[...]
            newest = old
            for score in scores:
                newest = jnp.maximum(newest, jnp.max(score, axis=0, keepdims=True))
            fade = jnp.exp2(old - newest)
            max_ref[...] = newest
            added, mixed = sum_ref[...] * fade, acc_ref[...] * fade
            for context, score in zip(contexts, scores):
                weights = jnp.exp2(score - newest)
                added += column_sum(weights)
                mixed += dot_tn(context, weights.astype(bf16))
            sum_ref[...] = added
            acc_ref[...] = mixed

        return carry

    lax.fori_loop(0, total // block, visit, 0)
    totals = sum_ref[...]
    lse_ref[...] = max_ref[...] + jnp.log2(totals)
    mixture_ref[...] = acc_ref[...] * (1.0 / totals)
    traffic.ship(lse_ref, mixture_ref)
    traffic.need(wv_ref, wo_ref)
    values = jnp.concatenate([wv_ref[...], wv_ref[...]], axis=0)
    attended = dot_tn(split(mixture_ref[...], 0), values)
    hidden_ref[...] = start + (
        dot(attended.astype(bf16), wo_ref[...]) + vector(vectors_ref, CROSS, CROSS.output_bias)
    )
    traffic.ship(hidden_ref)
    out_ref[...] = feed_forward(
        traffic, hidden_ref[...], vector(vectors_ref, CROSS, CROSS.feed_gain), vector(vectors_ref, CROSS, CROSS.feed_bias),
        up_ref, vector(vectors_ref, CROSS, CROSS.up_bias), down_ref, vector(vectors_ref, CROSS, CROSS.down_bias),
        normed_ref, active_ref, slope_ref,
    )


def cross_forward(count, tokens, start, vectors, wq, wk, wv, wo, up, down):
    outs = [
        shape((LAT, D), bf16), shape((LAT, D), bf16), shape((LAT, C), f32), shape((C, LAT), f32),
        shape((1, LAT), f32), shape((LAT, D), f32), shape((LAT, D), bf16), shape((LAT, FF), bf16),
        shape((LAT, FF), bf16), shape((LAT, D), f32),
    ]
    scratch = [
        pltpu.VMEM((C, LAT), f32), pltpu.VMEM((1, LAT), f32), pltpu.VMEM((1, LAT), f32),
    ]
    return streamed(
        cross_forward_kernel, "cross_forward", outs,
        [count, tokens, start, vectors, wq, wk, wv, wo, up, down], late=range(6, 10), early=range(9), scratch=scratch,
        smem=1, flops=100_000_000_000,
    )


def pair_mask(value, side):
    lane = lax.broadcasted_iota(jnp.int32, (1, LANES), 1)
    keep = (lane < HEAD) if side == 0 else (lane >= HEAD)
    return jnp.where(keep, value, jnp.zeros_like(value))


def latent_kernel(windows, parts, traffic, firsts_ref, hidden_ref, cotangent_ref, vectors_ref, joint_w_ref, merge_ref,
                  up_ref, down_ref, out_ref, grad_ref, *rest):
    windows_refs, rest = rest[:parts], rest[parts:]
    (flat_ref, probs_ref, joint_ref, mixed_ref, after_ref, normedl_ref, normed_ref, active_ref, slope_ref, query_grad_ref, joint_grad_ref) = rest
    gain = vector(vectors_ref, LATENT, LATENT.attend_gain)
    unit, rstd = normalise(hidden_ref[...])
    normedl_ref[...] = (unit * gain + vector(vectors_ref, LATENT, LATENT.attend_bias)).astype(bf16)
    joint_ref[...] = dot(normedl_ref[...], joint_w_ref[...]).astype(bf16)
    scale = HEAD ** (-0.5)
    for pair in range(HEADS // 2):
        lanes = slice(pair * LANES, (pair + 1) * LANES)
        query = joint_ref[:, lanes]
        keys = joint_ref[:, D + pair * LANES : D + (pair + 1) * LANES]
        values = joint_ref[:, 2 * D + pair * LANES : 2 * D + (pair + 1) * LANES]
        mixed = None
        for side in range(2):
            scores = dot_nt(pair_mask(keys, side), query) * (scale * LOG2E)
            weights = jnp.exp2(scores - jnp.max(scores, axis=0, keepdims=True))
            weights = weights * (1.0 / column_sum(weights))
            probs_ref[2 * pair + side] = weights
            part = dot_tn(pair_mask(values, side), weights.astype(bf16))
            mixed = part if mixed is None else mixed + part
        mixed_ref[lanes, :] = mixed.astype(bf16)
    traffic.need(merge_ref)
    after_ref[...] = hidden_ref[...] + (
        dot_tn(mixed_ref[...], merge_ref[...]) + vector(vectors_ref, LATENT, LATENT.merge_bias)
    )
    feed_gain = vector(vectors_ref, LATENT, LATENT.feed_gain)
    out_ref[...] = feed_forward(
        traffic, after_ref[...], feed_gain, vector(vectors_ref, LATENT, LATENT.feed_bias), up_ref,
        vector(vectors_ref, LATENT, LATENT.up_bias), down_ref, vector(vectors_ref, LATENT, LATENT.down_bias),
        normed_ref, active_ref, slope_ref,
    ).astype(bf16)

    traffic.ship(out_ref)
    traffic.need(cotangent_ref)
    clear_tail(flat_ref, LATENT_ROWS)
    after_grad = feed_backward(
        traffic, cotangent_ref[...].astype(f32), after_ref[...], feed_gain, up_ref, down_ref, normed_ref, active_ref,
        slope_ref, flat_ref, LATENT,
    )
    branch = after_grad.astype(bf16)
    put(flat_ref, LATENT.merge_weight[0], D, 0, dot(mixed_ref[...], branch))
    put_vector(flat_ref, LATENT.merge_bias[0], column_sum(branch.astype(f32)))
    mixed_grad = dot_nt(branch, merge_ref[...]).astype(bf16)
    for pair in range(HEADS // 2):
        lanes = slice(pair * LANES, (pair + 1) * LANES)
        query = joint_ref[:, lanes]
        keys = joint_ref[:, D + pair * LANES : D + (pair + 1) * LANES]
        values = joint_ref[:, 2 * D + pair * LANES : 2 * D + (pair + 1) * LANES]
        grads = mixed_grad[:, lanes]
        query_part = key_part = value_part = None
        for side in range(2):
            probs = probs_ref[2 * pair + side]
            part = dot(probs.astype(bf16), pair_mask(grads, side))
            value_part = part if side == 0 else value_part + part
            probs_grad = dot_nt(pair_mask(values, side), grads)
            delta = column_sum(probs * probs_grad)
            scores_grad = (probs * (probs_grad - delta)).astype(bf16)
            part = dot(scores_grad, pair_mask(query, side))
            key_part = part if side == 0 else key_part + part
            part = dot_tn(pair_mask(keys, side), scores_grad)
            query_part = part if side == 0 else query_part + part
        query_grad_ref[lanes, :] = query_part * scale
        joint_grad_ref[:, D + pair * LANES : D + (pair + 1) * LANES] = (key_part * scale).astype(bf16)
        joint_grad_ref[:, 2 * D + pair * LANES : 2 * D + (pair + 1) * LANES] = value_part.astype(bf16)
    joint_grad_ref[:, :D] = query_grad_ref[...].T.astype(bf16)
    put(flat_ref, LATENT.joint_weight[0], 3 * D, 0, dot_tn(normedl_ref[...], joint_grad_ref[...]))
    normed_grad = dot_nt(joint_grad_ref[...], joint_w_ref[...])
    put_vector(flat_ref, LATENT.attend_gain[0], column_sum(normed_grad * unit))
    put_vector(flat_ref, LATENT.attend_bias[0], column_sum(normed_grad))
    grad_ref[...] = after_grad + normalise_back(normed_grad, unit, rstd, gain)
    to_windows(flat_ref, firsts_ref, windows_refs, windows.rows, traffic)


def latent_layer(firsts, hidden, cotangent, vectors, joint, merge, up, down, windows, grid):
    outs = [shape((LAT, D), bf16), shape((LAT, D), f32)] + windows.outs(grid.nz)
    scratch = [
        pltpu.VMEM((windows.padded, LANES), f32), pltpu.VMEM((HEADS, LAT, LAT), f32),
        pltpu.VMEM((LAT, 3 * D), bf16), pltpu.VMEM((D, LAT), bf16), pltpu.VMEM((LAT, D), f32),
        pltpu.VMEM((LAT, D), bf16), pltpu.VMEM((LAT, D), bf16), pltpu.VMEM((LAT, FF), bf16),
        pltpu.VMEM((LAT, FF), bf16), pltpu.VMEM((D, LAT), f32), pltpu.VMEM((LAT, 3 * D), bf16),
    ]
    return streamed(
        functools.partial(latent_kernel, windows, grid.nz), "latent_layer", outs,
        [firsts, hidden, cotangent, vectors, joint, merge, up, down], late=[5, 6, 7, 2], early=[0],
        blocks={2 + c: windows.devices // grid.nz for c in range(grid.nz)}, scratch=scratch, smem=1,
        flops=20_000_000_000,
    )


SPLIT = CROSS.output_weight[0] // TILE * TILE


def cross_feed_kernel(windows, parts, traffic, firsts_ref, grad_ref, vectors_ref, wv_ref, wo_ref, up_ref, down_ref,
                      mixture_ref, hidden_ref, normed_ref, active_ref, saved_slope_ref,
                      hidden_grad_ref, valued_ref, delta_ref, value_grad_ref, *rest):
    windows_refs = rest[:parts]
    flat_ref, slope_ref = rest[parts:]
    clear_tail(flat_ref, CROSS_ROWS)
    slope_ref[...] = saved_slope_ref[...]
    hidden_grad = feed_backward(
        traffic, grad_ref[...], hidden_ref[...], vector(vectors_ref, CROSS, CROSS.feed_gain), up_ref, down_ref, normed_ref,
        active_ref, slope_ref, flat_ref, CROSS,
    )
    hidden_grad_ref[...] = hidden_grad
    traffic.ship(hidden_grad_ref)
    traffic.need(wv_ref, wo_ref, mixture_ref)
    branch = hidden_grad.astype(bf16)
    values = jnp.concatenate([wv_ref[...], wv_ref[...]], axis=0)
    mixture = split(mixture_ref[...], 0)
    attended = dot_tn(mixture, values)
    put(flat_ref, CROSS.output_weight[0], D, 0, dot_tn(attended.astype(bf16), branch))
    put_vector(flat_ref, CROSS.output_bias[0], column_sum(branch.astype(f32)))
    attended_grad = dot_nt(branch, wo_ref[...]).astype(bf16)
    both = dot(mixture, attended_grad)
    value_grad_ref[...] = both[:C] + both[C:]
    put(flat_ref, CROSS.value_weight[0], D, 0, value_grad_ref[...])
    valued = dot_nt(attended_grad, wv_ref[...])
    valued_ref[...] = split(valued, 1)
    delta_ref[...] = column_sum((attended_grad.astype(f32) * attended).T)
    flat_ref[:SPLIT, :] = jnp.zeros((SPLIT, LANES), f32)
    to_windows(flat_ref, firsts_ref, windows_refs, windows.rows, traffic)


def cross_feed(firsts, grad, vectors, wv, wo, up, down, mixture, hidden, normed, active, slope, windows, grid):
    outs = [
        shape((LAT, D), f32), shape((LAT, 2 * C), bf16), shape((1, LAT), f32), shape((C, D), f32),
    ] + windows.outs(grid.nz)
    return streamed(
        functools.partial(cross_feed_kernel, windows, grid.nz), "cross_feed", outs,
        [firsts, grad, vectors, wv, wo, up, down, mixture, hidden, normed, active, slope], late=[5, 3, 4, 7],
        early=[0], blocks={4 + c: windows.devices // grid.nz for c in range(grid.nz)},
        scratch=[pltpu.VMEM((windows.padded, LANES), f32), pltpu.VMEM((LAT, FF), bf16)], smem=1,
        flops=80_000_000_000,
    )


def attend_block(offset, blocks, count_ref, tokens_ref, valued_ref, delta_ref, vectors_ref, keyed_ref, lse_ref,
                 token_grad_ref, acc_ref, gains_ref, doubled_ref, paired_ref):
    block = tokens_ref.shape[0]
    begin = (pl.program_id(0) + offset) * block
    total = blocks * block
    count = count_ref[0]
    some, full = block_kinds(count, begin, block, total)

    @pl.when(pl.program_id(0) == 0)
    def _():
        doubled_ref[...] = split(keyed_ref[...] * LOG2E, 1)
        paired_ref[...] = split(keyed_ref[...], 1)

    @pl.when(some)
    def _():
        gain = vector(vectors_ref, CROSS, CROSS.context_gain)
        bias = vector(vectors_ref, CROSS, CROSS.context_bias)
        for part in range(0, block, PART):
            rows = slice(part, part + PART)
            unit, rstd = normalise(tokens_ref[rows, :].astype(f32))
            context = (unit * gain + bias).astype(bf16)
            twice = jnp.concatenate([context, context], axis=1)
            scores = masked(dot_nt(twice, doubled_ref[...]), count, begin + part, total)
            probs = jnp.exp2(scores - lse_ref[...])
            scores_grad = (probs * (dot_nt(twice, valued_ref[...]) - delta_ref[...])).astype(bf16)
            acc_ref[...] += dot_tn(context, scores_grad)
            wide = dot(probs.astype(bf16), valued_ref[...]) + dot(scores_grad, paired_ref[...])
            context_grad = wide[:, :C] + wide[:, C:]
            gains_ref[0:1, :] += column_sum(context_grad * unit)
            gains_ref[1:2, :] += column_sum(context_grad)
            token_grad_ref[rows, :] = normalise_back(context_grad, unit, rstd, gain)

    @pl.when(jnp.logical_not(some))
    def _():
        token_grad_ref[...] = jnp.zeros(token_grad_ref.shape, f32)


def attend_first_kernel(blocks, count_ref, tokens_ref, valued_ref, delta_ref, vectors_ref, keyed_ref, lse_ref,
                        token_grad_ref, acc_ref, gains_ref, doubled_ref, paired_ref):
    @pl.when(pl.program_id(0) == 0)
    def _():
        acc_ref[...] = jnp.zeros(acc_ref.shape, f32)
        gains_ref[...] = jnp.zeros(gains_ref.shape, f32)

    attend_block(0, blocks, count_ref, tokens_ref, valued_ref, delta_ref, vectors_ref, keyed_ref, lse_ref,
                 token_grad_ref, acc_ref, gains_ref, doubled_ref, paired_ref)


def attend_second_kernel(offset, blocks, rows, parts, firsts_ref, count_ref, task_ref, tokens_ref, valued_ref,
                         delta_ref, vectors_ref, keyed_ref, lse_ref, acc_before_ref, gains_before_ref, hidden_grad_ref,
                         value_grad_ref, start_ref, wq_ref, wk_ref, normedq_ref, query_ref, kept_ref,
                         token_grad_ref, *rest):
    windows_refs = rest[:parts]
    flat_ref, acc_ref, gains_ref, doubled_ref, paired_ref = rest[parts:]

    @pl.when(pl.program_id(0) == 0)
    def _():
        acc_ref[...] = acc_before_ref[...]
        gains_ref[...] = gains_before_ref[...]

    attend_block(offset, blocks, count_ref, tokens_ref, valued_ref, delta_ref, vectors_ref, keyed_ref, lse_ref,
                 token_grad_ref, acc_ref, gains_ref, doubled_ref, paired_ref)

    @pl.when(pl.program_id(0) == pl.num_programs(0) - 1)
    def _():
        pulled = split(acc_ref[...] * D ** (-0.5), 0)
        both = dot(pulled, query_ref[...])
        put(flat_ref, CROSS.key_weight[0], D, 0, both[:C] + both[C:])
        put(flat_ref, CROSS.value_weight[0], D, 0, value_grad_ref[...])
        put_vector(flat_ref, CROSS.context_gain[0], gains_ref[0:1, :])
        put_vector(flat_ref, CROSS.context_bias[0], gains_ref[1:2, :])
        query_grad = dot_tn(pulled, jnp.concatenate([wk_ref[...], wk_ref[...]], axis=0)).astype(bf16)
        put(flat_ref, CROSS.query_weight[0], D, 0, dot_tn(normedq_ref[...], query_grad))
        normed_grad = dot_nt(query_grad, wq_ref[...])
        unit, rstd = normalise(start_ref[...])
        put_vector(flat_ref, CROSS.query_gain[0], column_sum(normed_grad * unit))
        put_vector(flat_ref, CROSS.query_bias[0], column_sum(normed_grad))
        gain = vector(vectors_ref, CROSS, CROSS.query_gain)
        start_grad = hidden_grad_ref[...] + normalise_back(normed_grad, unit, rstd, gain)
        put(flat_ref, CROSS.latents[0], D, 0, start_grad)
        first, unused = CROSS.task_table
        chunks = D // LANES
        flat_ref[first : first + NTASK * chunks, :] = jnp.zeros((NTASK * chunks, LANES), f32)
        sums = column_sum(start_grad)
        base = first + task_ref[0] * chunks
        for chunk in range(chunks):
            flat_ref[pl.ds(base + chunk, 1), :] = sums[:, chunk * LANES : (chunk + 1) * LANES]
        clear_tail(flat_ref, SPLIT)
        to_windows(flat_ref, firsts_ref, windows_refs, rows)


def attend_scratch():
    return [pltpu.VMEM((LAT, 2 * C), bf16), pltpu.VMEM((LAT, 2 * C), bf16)]


def attend_first(count, tokens, valued, delta, vectors, keyed, lse):
    total = tokens.shape[0]
    block = min(BLOCK, total)
    blocks = total // block
    whole = [valued, delta, vectors, keyed, lse]
    row = lambda i: (i, 0)
    outs = [shape((total, C), f32), shape((C, LAT), f32), shape((8, C), f32)]
    scratch = attend_scratch()
    return pl.pallas_call(
        functools.partial(attend_first_kernel, blocks),
        name="attend_first",
        grid=(max(blocks // 2, 1),),
        out_shape=outs,
        in_specs=[pl.BlockSpec(memory_space=pltpu.SMEM), pl.BlockSpec((block, C), row)] + vmem_specs(len(whole)),
        out_specs=[pl.BlockSpec((block, C), row)] + vmem_specs(2),
        scratch_shapes=scratch,
        compiler_params=pltpu.CompilerParams(vmem_limit_bytes=vmem_limit(*whole, *scratch)),
        cost_estimate=pl.CostEstimate(flops=100_000_000_000, bytes_accessed=1, transcendentals=0),
    )(count, tokens, *whole)


def attend_second(firsts, count, task, tokens, valued, delta, vectors, keyed, lse, acc, gains, hidden_grad, value_grad,
                  start, wq, wk, normedq, query, token_grad, windows, grid):
    total = tokens.shape[0]
    block = min(BLOCK, total)
    blocks = total // block
    offset = max(blocks // 2, 1)
    rows = windows.quarter(grid.nx)
    last = grid.ny * grid.nz - 1
    assert SPLIT <= windows.first[last + 1] and blocks > offset
    flat_rows = max(windows.first[last] + rows * grid.nx, SPLIT + TILE)
    whole = [valued, delta, vectors, keyed, lse, acc, gains, hidden_grad, value_grad, start, wq, wk, normedq, query]
    half = windows.devices // grid.nz // grid.ny * rows
    small = [shape((half * depths, LANES), bf16) for c in range(grid.nz) for depths in halves(grid)]
    row = lambda i: (i + offset, 0)
    scratch = [
        pltpu.VMEM((flat_rows, LANES), f32), pltpu.VMEM((C, LAT), f32),
        pltpu.VMEM((8, C), f32), *attend_scratch(),
    ]
    return pl.pallas_call(
        functools.partial(attend_second_kernel, offset, blocks, rows, len(small)),
        name="attend_second",
        grid=(blocks - offset,),
        out_shape=[shape((total, C), f32)] + small,
        in_specs=[pl.BlockSpec(memory_space=pltpu.SMEM)] * 3
        + [pl.BlockSpec((block, C), row)]
        + vmem_specs(len(whole))
        + [pl.BlockSpec(memory_space=pl.ANY)],
        out_specs=[pl.BlockSpec((block, C), row)] + vmem_specs(len(small)),
        scratch_shapes=scratch,
        input_output_aliases={4 + len(whole): 0},
        compiler_params=pltpu.CompilerParams(vmem_limit_bytes=vmem_limit(*whole, *small, *scratch)),
        cost_estimate=pl.CostEstimate(flops=100_000_000_000, bytes_accessed=1, transcendentals=0),
    )(firsts, count, task, tokens, *whole, token_grad)


def body(tokens, task_id, valid_count, cross_params, latent_params, out_grad):
    grid = Grid()
    devices = grid.nx * grid.ny * grid.nz
    cw = Windows(cross_params.shape[0] * devices, devices)
    lw = Windows(latent_params.shape[0] * devices, devices)
    gathered_from = grid.owners(gather_places(grid))
    scattered_to = grid.owners(grid.order())
    tokens = tokens[0]

    cross_window, latent_window = place([cross_params, latent_params], [cw, lw], grid.index)
    cross_column = gather_depth(cross_window, grid)
    latent_column = gather_depth(after(latent_window, *cross_column[1:]), grid)
    pieces = gather_plane_second(*gather_plane_first(cross_column, grid), grid)
    for piece in pieces:
        piece[0] = after(piece[0], *latent_column[1:])
        piece[1:] = [after(value, *latent_column[1:]) for value in piece[1:]]
    cross_all = sum(gather_core(*pieces, grid), [])
    latent_column = [after(value, pieces[0][-1], pieces[1][-1]) for value in latent_column]
    lows, highs = gather_plane_first(latent_column, grid)
    vectors, start, wq, wk, wv, wo, up, down = unpack_cross(cw.firsts(gathered_from), cross_all, task_id, cw)
    lows[0], highs[0] = after(lows[0], vectors), after(highs[0], vectors)
    first, second = gather_plane_second(lows, highs, grid)
    normedq, query, keyed, mixture, lse, hidden, normed, active, slope, result = cross_forward(
        valid_count, tokens, after(start, first[0], second[0]), vectors, wq, wk, wv, wo, up, down
    )
    first[1:] = [after(value, result) for value in first[1:]]
    second[1:] = [after(value, result) for value in second[1:]]
    latent_all = sum(gather_core(first, second, grid), [])
    latent_weights = unpack_latent(lw.firsts(gathered_from), latent_all, lw)
    latents_out, result_grad, *latent_parts = latent_layer(
        lw.firsts(scattered_to), result, out_grad[0], *latent_weights, lw, grid
    )

    latent_lows, latent_highs = reduce_first(reduce_core(latent_parts, grid), lw.rows, grid)
    hidden_grad, valued, delta, value_grad, *later_parts = cross_feed(
        cw.firsts(scattered_to), after(result_grad, latent_lows[0][0]), vectors, wv, wo, up, down, mixture, hidden,
        normed, active, slope, cw, grid,
    )
    latent_lows[0] = (after(latent_lows[0][0], delta), 0)
    latent_first, latent_second = reduce_second(latent_lows, latent_highs, lw.rows, grid)
    later_group = reduce_core(later_parts, grid)
    token_grad, acc, gains = attend_first(
        valid_count, tokens, valued, after(delta, latent_first[0][0]), vectors, keyed, lse
    )
    latent_first[0] = (after(latent_first[0][0], acc), 0)
    latent_column = reduce_depth(latent_first, latent_second, lw.rows, grid)
    later_group[0] = (after(later_group[0][0], latent_column[0]), 0)
    later_lows, later_highs = reduce_first(later_group, cw.rows, grid)
    owner, quarter = quarter_owners(grid)
    small_rows = cw.quarter(grid.nx)
    token_grad, *early_parts = attend_second(
        cw.firsts(owner) + quarter * small_rows, valid_count, task_id, tokens, valued, delta, vectors, keyed, lse,
        after(acc, later_lows[0][0]), gains, hidden_grad, value_grad, start, wq, wk, normedq, query, token_grad, cw,
        grid,
    )
    latent_column[0] = after(latent_column[0], early_parts[0])
    latent_share = extract(latent_column, [], lw, grid)
    later_lows[0] = (after(later_lows[0][0], latent_share), 0)
    early_parts = [after(part, latent_share) for part in early_parts]
    early_groups = [reduce_core(early_parts[half::2], grid) for half in range(2)]
    later_first, later_second, early_lows, early_highs = reduce_second_and_first(
        later_lows, later_highs, cw.rows, early_groups, small_rows, grid
    )
    early_first, early_second = reduce_second(early_lows, early_highs, small_rows, grid)
    column = reduce_depth_both(later_first, later_second, cw.rows, early_first, early_second, small_rows, grid)
    quarters = collect_quarters(column, cw.rows, small_rows, grid)
    return (latents_out[None], token_grad[None], extract(column, quarters, cw, grid), latent_share)


def solution(mesh):
    return jax.shard_map(
        body,
        mesh=mesh,
        in_specs=(
            P(AXES, None, None),
            P(AXES),
            P(AXES),
            P(AXES),
            P(AXES),
            P(AXES, None, None),
        ),
        out_specs=(
            P(AXES, None, None),
            P(AXES, None, None),
            P(AXES),
            P(AXES),
        ),
        check_vma=False,
    )
```

```python
import functools
import math
import types

import jax
import jax.numpy as jnp
from jax import lax
from jax.experimental import pallas as pl
from jax.experimental.pallas import tpu as pltpu
from jax.sharding import PartitionSpec as P

D = 512
FF = 2048
C = 128
LAT = 512
HEADS = 8
HEAD = 64
NTASK = 18
LANG = 77
LANES = 128
TILE = 16
UNIT = TILE * LANES
BLOCK = 2048
PART = 512
AXES = ("gx", "gy", "gz")

epsilon = 1e-05
negative = -1e30
LOG2E = math.log2(math.e)
bf16 = jnp.bfloat16
f32 = jnp.float32
VMEM_LIMIT = 60 * 1024 * 1024
ROOM = 6 * 1024 * 1024
SLOTS = 2


def layout_of(**shapes):
    table = {}
    row = 0
    for name, dims in shapes.items():
        table[name] = (row, dims)
        row += math.prod(dims) // LANES
    return types.SimpleNamespace(**table), row


CROSS, CROSS_ROWS = layout_of(
    latents=(LAT, D),
    task_table=(NTASK, D),
    query_gain=(D,),
    query_bias=(D,),
    context_gain=(C,),
    context_bias=(C,),
    query_weight=(D, D),
    key_weight=(C, D),
    value_weight=(C, D),
    output_weight=(D, D),
    output_bias=(D,),
    feed_gain=(D,),
    feed_bias=(D,),
    up_weight=(D, FF),
    up_bias=(FF,),
    down_weight=(FF, D),
    down_bias=(D,),
)
LATENT, LATENT_ROWS = layout_of(
    attend_gain=(D,),
    attend_bias=(D,),
    joint_weight=(D, 3 * D),
    merge_weight=(D, D),
    merge_bias=(D,),
    feed_gain=(D,),
    feed_bias=(D,),
    up_weight=(D, FF),
    up_bias=(FF,),
    down_weight=(FF, D),
    down_bias=(D,),
)


def vectors_of(table):
    return [place for place in vars(table).values() if len(place[1]) == 1]


class Windows:
    def __init__(self, total, devices):
        self.total = total
        self.devices = devices
        self.shard = total // devices
        starts = [self.shard * d for d in range(devices)]
        self.first = [s // UNIT * TILE for s in starts]
        self.phase = [s % UNIT for s in starts]
        self.rows = max(-(-(p + self.shard) // UNIT) * TILE for p in self.phase)
        self.padded = max(f + self.rows for f in self.first)
        self.full = -(-total // UNIT) * TILE
        self.shard_rows = -(-self.shard // (8 * LANES)) * 8

    def outs(self, parts):
        return [shape((self.devices // parts * self.rows, LANES), bf16)] * parts

    def firsts(self, owners):
        return self.shard * owners // UNIT * TILE

    def quarter(self, parts):
        return -(-self.rows // (parts * TILE)) * TILE


def dot(left, right):
    return jnp.dot(left, right, preferred_element_type=f32)


def dot_nt(left, right):
    return lax.dot_general(left, right, (((1,), (1,)), ((), ())), preferred_element_type=f32)


def dot_tn(left, right):
    return lax.dot_general(left, right, (((0,), (0,)), ((), ())), preferred_element_type=f32)


def split(value, axis):
    high = value.astype(bf16)
    low = (value - high.astype(f32)).astype(bf16)
    return jnp.concatenate([high, low], axis=axis)


def normalise(value):
    centred = value - jnp.mean(value, axis=-1, keepdims=True)
    rstd = lax.rsqrt(jnp.mean(centred * centred, axis=-1, keepdims=True) + epsilon)
    return centred * rstd, rstd


def normalise_back(grad, unit, rstd, gain):
    inner = grad * gain
    return rstd * (
        inner
        - jnp.mean(inner, axis=-1, keepdims=True)
        - unit * jnp.mean(inner * unit, axis=-1, keepdims=True)
    )


def column_sum(value):
    return jnp.sum(value, axis=0, keepdims=True)


def vmem_specs(count):
    return [pl.BlockSpec(memory_space=pltpu.VMEM)] * count


def shape(dims, dtype):
    return jax.ShapeDtypeStruct(dims, dtype)


def bytes_of(value):
    return math.prod(value.shape) * jnp.dtype(value.dtype).itemsize


def vmem_limit(*values):
    return min(sum(map(bytes_of, values)) + 16 * 2**20, VMEM_LIMIT)


def call(kernel, name, outs, inputs, scratch=(), smem=0, flops=0, moved=0, alone=True):
    specs = [pl.BlockSpec(memory_space=pltpu.SMEM)] * smem + vmem_specs(len(inputs) - smem)
    limit = VMEM_LIMIT if alone else vmem_limit(*inputs, *jax.tree.leaves(outs), *scratch)
    return pl.pallas_call(
        kernel,
        name=name,
        out_shape=outs,
        in_specs=specs,
        out_specs=jax.tree.map(lambda _: pl.BlockSpec(memory_space=pltpu.VMEM), outs),
        scratch_shapes=list(scratch),
        compiler_params=pltpu.CompilerParams(vmem_limit_bytes=limit),
        cost_estimate=pl.CostEstimate(flops=flops, bytes_accessed=moved, transcendentals=0),
    )(*inputs)


class Traffic:
    def __init__(self):
        self.loads, self.stores, self.blocks, self.begun = {}, {}, {}, []

    def need(self, *refs):
        for ref in refs:
            copy = self.loads.pop(id(ref), None)
            if copy is not None:
                copy.wait()

    def ship(self, *refs):
        for ref in refs:
            copy = self.stores.pop(id(ref), None)
            if copy is not None:
                copy.start()
                self.begun.append(copy)

    def block(self, ref, number, rows):
        target, sem = self.blocks[id(ref)]
        slot = pl.multiple_of(number % SLOTS * rows, TILE)
        part = pl.multiple_of(number * rows, TILE)
        return pltpu.make_async_copy(ref.at[pl.ds(slot, rows)], target.at[pl.ds(part, rows)], sem.at[number])


def streamed(kernel, name, outs, inputs, late=(), early=(), blocks=None, scratch=(), smem=0, flops=0, room=0):
    blocks = blocks or {}
    shipped = list(early) + list(blocks)
    vmem, hbm = pl.BlockSpec(memory_space=pltpu.VMEM), pl.BlockSpec(memory_space=pltpu.HBM)
    held = [pltpu.VMEM(inputs[i].shape, inputs[i].dtype) for i in late]
    held += [pltpu.VMEM(outs[i].shape, outs[i].dtype) for i in early]
    held += [pltpu.VMEM((SLOTS * outs[i].shape[0] // number, LANES), outs[i].dtype) for i, number in blocks.items()]
    sems = [pltpu.SemaphoreType.DMA((max(len(late), 1),)), pltpu.SemaphoreType.DMA((max(len(early), 1),))]
    sems += [pltpu.SemaphoreType.DMA((number,)) for number in blocks.values()]

    def body(*refs):
        takes, gives = list(refs[: len(inputs)]), list(refs[len(inputs) : len(inputs) + len(outs)])
        rest = refs[len(inputs) + len(outs) :]
        buffers, rest = rest[: len(held)], rest[len(held) :]
        load_sem, store_sem = rest[:2]
        block_sems, rest = rest[2 : len(sems)], rest[len(sems) :]
        traffic = Traffic()
        for k, i in enumerate(late):
            copy = pltpu.make_async_copy(takes[i], buffers[k], load_sem.at[k])
            copy.start()
            traffic.loads[id(buffers[k])] = copy
            takes[i] = buffers[k]
        for k, i in enumerate(shipped):
            buffer = buffers[len(late) + k]
            if k < len(early):
                traffic.stores[id(buffer)] = pltpu.make_async_copy(buffer, gives[i], store_sem.at[k])
            else:
                traffic.blocks[id(buffer)] = (gives[i], block_sems[k - len(early)])
            gives[i] = buffer
        kernel(traffic, *takes, *gives, *rest)
        assert not traffic.loads and not traffic.stores
        for copy in traffic.begun:
            copy.wait()

    return pl.pallas_call(
        body,
        name=name,
        out_shape=outs,
        in_specs=[pl.BlockSpec(memory_space=pltpu.SMEM)] * smem
        + [hbm if i in late else vmem for i in range(smem, len(inputs))],
        out_specs=[hbm if i in shipped else vmem for i in range(len(outs))],
        scratch_shapes=held + sems + list(scratch),
        compiler_params=pltpu.CompilerParams(vmem_limit_bytes=VMEM_LIMIT - room),
        cost_estimate=pl.CostEstimate(flops=flops, bytes_accessed=1, transcendentals=0),
    )(*inputs)


def shifted(value, shift):
    down, across = shift // LANES, shift % LANES
    turned = pltpu.roll(value, across, axis=1)
    above = pltpu.roll(turned, 1, axis=0)
    lane = lax.broadcasted_iota(jnp.int32, value.shape, 1)
    return pltpu.roll(jnp.where(lane < across, above, turned), down, axis=0)


def place_kernel(shifts_ref, shards_ref, *out_refs):
    begin = 0
    for number, out_ref in enumerate(out_refs):
        rows = out_ref.shape[0]
        value = shards_ref[begin : begin + rows, :].astype(f32)
        out_ref[...] = shifted(value, shifts_ref[number]).astype(bf16)
        begin += rows


def place(shards, windows, index):
    padded = [
        jnp.pad(shard, (0, w.rows * LANES - w.shard)) for shard, w in zip(shards, windows)
    ]
    together = jnp.concatenate(padded).reshape(-1, LANES)
    shifts = jnp.stack([(w.shard * index) % UNIT for w in windows])
    outs = [shape((w.rows, LANES), bf16) for w in windows]
    return call(place_kernel, "place", outs, [shifts, together], smem=1, alone=False)


def extract_kernel(count, shift_ref, *refs):
    out_ref, total_ref = refs[-2:]
    rows = total_ref.shape[0]
    value = refs[0][:rows, :].astype(f32)
    for ref in refs[1:count]:
        value += ref[:rows, :].astype(f32)
    total_ref[...] = value
    begin = 0
    for ref in refs[count:-2]:
        size = min(ref.shape[0], rows - begin)
        if size > 0:
            total_ref[begin : begin + size, :] += ref[:size, :].astype(f32)
        begin += ref.shape[0]
    down, across = shift_ref[0] // LANES, shift_ref[0] % LANES
    turned = pltpu.roll(total_ref[...], lax.rem(LANES - across, LANES), axis=1)
    below = pltpu.roll(turned, rows - 1, axis=0)
    lane = lax.broadcasted_iota(jnp.int32, (rows, LANES), 1)
    merged = pltpu.roll(
        jnp.where(lane < LANES - across, turned, below), lax.rem(rows - down, rows), axis=0
    )
    out_ref[...] = merged[: out_ref.shape[0]]


def extract(parts, quarters, windows, grid):
    shift = (windows.shard * grid.index) % UNIT
    rows = min(windows.shard_rows, windows.rows)
    found = call(
        functools.partial(extract_kernel, len(parts)), "extract", shape((rows, LANES), f32),
        [shift.reshape(1), *parts, *quarters], scratch=[pltpu.VMEM((windows.rows, LANES), f32)], smem=1,
        alone=False,
    )
    return found.reshape(-1)[: windows.shard]


class Grid:
    def __init__(self):
        self.nx, self.ny, self.nz = (lax.axis_size(axis) for axis in AXES)
        self.nl = 2 if self.nx % 2 == 0 else 1
        self.nh = self.nx // self.nl
        self.index = lax.axis_index(AXES)

    def order(self):
        return [
            (c, h, l, y)
            for c in range(self.nz)
            for h in range(self.nh)
            for l in range(self.nl)
            for y in range(self.ny)
        ]

    def owners(self, places):
        gx, gy, gz = (lax.axis_index(axis) for axis in AXES)
        c, h, l, y = (jnp.array(column, jnp.int32) for column in zip(*places))
        high = (gx // self.nl + h) % self.nh
        low = (gx % self.nl + l) % self.nl
        return ((high * self.nl + low) * self.ny + (gy + y) % self.ny) * self.nz + (gz + c) % self.nz

    def along_core(self, value, step):
        return lax.ppermute(value, AXES[2], [(i, (i + step) % self.nz) for i in range(self.nz)])

    def along_depth(self, value, step):
        return lax.ppermute(value, AXES[1], [(i, (i + step) % self.ny) for i in range(self.ny)])

    def along_low(self, value, step):
        nl = self.nl
        return lax.ppermute(
            value, AXES[0], [(i, i // nl * nl + (i + step) % nl) for i in range(self.nx)]
        )

    def along_high(self, value, step):
        nl = self.nl
        return lax.ppermute(value, AXES[0], [(i, (i + step * nl) % self.nx) for i in range(self.nx)])


def combine_kernel(groups, picks, *refs):
    starts = [sum(len(bases) for rows, bases in groups[:g]) for g in range(len(groups))]
    outputs = refs[sum(len(bases) for rows, bases in groups) :]
    for output, pick in zip(outputs, picks):
        row = 0
        for g, block in pick:
            rows, bases = groups[g]
            total = None
            for i, base in enumerate(bases):
                begin = base + block * rows
                part = refs[starts[g] + i][begin : begin + rows, :].astype(f32)
                total = part if total is None else total + part
            output[row : row + rows, :] = total.astype(bf16)
            row += rows


def combine(name, groups, picks):
    inputs = [array for rows, sources in groups for array, base in sources]
    kinds = tuple((rows, tuple(base for array, base in sources)) for rows, sources in groups)
    sizes = [sum(groups[g][0] for g, block in pick) for pick in picks]
    outs = [shape((size, LANES), bf16) for size in sizes]
    moved = 6 * LANES * sum(sizes)
    return call(
        functools.partial(combine_kernel, kinds, picks), name, outs, inputs, flops=moved, moved=moved, alone=False
    )


def reduce_core(parts, grid):
    return [(parts[0], 0)] + [(grid.along_core(parts[c], c), 0) for c in range(1, grid.nz)]


def first_picks(grid, g):
    nh, nl, ny = grid.nh, grid.nl, grid.ny
    half = ny // 2
    block = lambda h, l, y: (g, (h * nl + l) * ny + y)
    lows = [[block(h, l, y) for h in range(nh) for y in range(half)] for l in range(nl)]
    highs = [[block(h, l, y) for l in range(nl) for y in range(half, ny)] for h in range(nh)]
    return lows, highs


def halves(grid):
    return [grid.ny // 2, grid.ny - grid.ny // 2]


def half_order(grid):
    half = grid.ny // 2
    places = []
    for c in range(grid.nz):
        for depths in (range(half), range(half, grid.ny)):
            places += [(c, h, l, y) for h in range(grid.nh) for l in range(grid.nl) for y in depths]
    return places


def half_first_picks(grid, first_group, second_group):
    nh, nl = grid.nh, grid.nl
    half, rest = halves(grid)
    lows = [[(first_group, (h * nl + l) * half + y) for h in range(nh) for y in range(half)] for l in range(nl)]
    highs = [[(second_group, (h * nl + l) * rest + y) for l in range(nl) for y in range(rest)] for h in range(nh)]
    return lows, highs


def second_picks(grid, low_group, high_group):
    half = grid.ny // 2
    rest = grid.ny - half
    highs = [[(low_group, h * half + y) for y in range(half)] for h in range(grid.nh)]
    lows = [[(high_group, l * rest + y) for y in range(rest)] for l in range(grid.nl)]
    return highs, lows


def depth_picks(grid, first_group, second_group):
    half = grid.ny // 2
    return [(first_group, y) for y in range(half)] + [(second_group, y) for y in range(grid.ny - half)]


def send_low(arrays, grid):
    return [grid.along_low(array, l + 1) for l, array in enumerate(arrays)]


def send_high(arrays, grid):
    return [grid.along_high(array, h + 1) for h, array in enumerate(arrays)]


def send_depth(arrays, grid):
    return [grid.along_depth(array, y + 1) for y, array in enumerate(arrays)]


def at(arrays, base=0):
    return [(array, base) for array in arrays]


def reduce_first(group, rows, grid):
    lows, highs = first_picks(grid, 0)
    outs = combine("plane_first", [(rows, group)], lows + highs)
    keep_low, keep_high = outs[0], outs[grid.nl]
    return (
        at([keep_low] + send_low(outs[1 : grid.nl], grid)),
        at([keep_high] + send_high(outs[grid.nl + 1 :], grid)),
    )


def reduce_second(lows, highs, rows, grid):
    to_high, to_low = second_picks(grid, 0, 1)
    outs = combine("plane_second", [(rows, lows), (rows, highs)], to_high + to_low)
    keep_first, keep_second = outs[0], outs[grid.nh]
    return (
        at([keep_first] + send_high(outs[1 : grid.nh], grid)),
        at([keep_second] + send_low(outs[grid.nh + 1 :], grid)),
    )


def reduce_depth(first, second, rows, grid):
    outs = combine("depth", [(rows, first), (rows, second)], [[pick] for pick in depth_picks(grid, 0, 1)])
    return [outs[0]] + send_depth(outs[1:], grid)


def reduce_second_and_first(lows, highs, rows, small_groups, small_rows, grid):
    to_high, to_low = second_picks(grid, 0, 1)
    small_low, small_high = half_first_picks(grid, 2, 3)
    nh, nl, half = grid.nh, grid.nl, grid.ny // 2
    picks = [to_high[0], to_low[0], small_low[0], small_high[0]]
    picks += [to_high[h] + small_high[h] for h in range(1, nh)]
    picks += [to_low[l] + small_low[l] for l in range(1, nl)]
    outs = combine("second_and_first", [(rows, lows), (rows, highs)] + [(small_rows, group) for group in small_groups], picks)
    keep_first, keep_second, keep_low, keep_high = outs[:4]
    high = send_high(outs[4 : 3 + nh], grid)
    low = send_low(outs[3 + nh :], grid)
    first, second = at([keep_first]) + at(high), at([keep_second]) + at(low)
    lows = at([keep_low]) + at(low, (grid.ny - half) * rows)
    highs = at([keep_high]) + at(high, half * rows)
    return first, second, lows, highs


def reduce_depth_both(first, second, rows, small_first, small_second, small_rows, grid):
    groups = [(rows, first), (rows, second), (small_rows, small_first), (small_rows, small_second)]
    picks = [list(pair) for pair in zip(depth_picks(grid, 0, 1), depth_picks(grid, 2, 3))]
    outs = combine("depth_both", groups, picks)
    return [outs[0]] + send_depth(outs[1:], grid)


def quarter_owners(grid):
    gx, gy, gz = (lax.axis_index(axis) for axis in AXES)
    c, h, l, y = (jnp.array(column, jnp.int32) for column in zip(*half_order(grid)))
    quarter = (gx // grid.nl + h) % grid.nh * grid.nl + (gx % grid.nl + l) % grid.nl
    return (gy + y) % grid.ny * grid.nz + (gz + c) % grid.nz, quarter


def collect_quarters(parts, base, rows, grid):
    (own,) = combine("quarter", [(rows, at(parts, base))], [[(0, 0)]])
    zero = jnp.zeros_like(own)
    first = jnp.where(lax.axis_index(AXES[0]) == 0, own, zero)
    return [first] + [lax.ppermute(own, AXES[0], [(x, 0)]) for x in range(1, grid.nx)]


def gather_depth(window, grid):
    return [window] + [grid.along_depth(window, -y) for y in range(1, grid.ny)]


def gather_plane_first(column, grid):
    half = grid.ny // 2
    first, second = jnp.concatenate(column[:half]), jnp.concatenate(column[half:])
    lows = [first] + [grid.along_low(first, -l) for l in range(1, grid.nl)]
    highs = [second] + [grid.along_high(second, -h) for h in range(1, grid.nh)]
    return lows, highs


def gather_plane_second(lows, highs, grid):
    first, second = jnp.concatenate(lows), jnp.concatenate(highs)
    return (
        [first] + [grid.along_high(first, -h) for h in range(1, grid.nh)],
        [second] + [grid.along_low(second, -l) for l in range(1, grid.nl)],
    )


def gather_core(first, second, grid):
    pieces = first + second
    return [pieces] + [[grid.along_core(piece, -c) for piece in pieces] for c in range(1, grid.nz)]


def gather_places(grid):
    half = grid.ny // 2
    places = []
    for c in range(grid.nz):
        for h in range(grid.nh):
            places += [(c, h, l, y) for l in range(grid.nl) for y in range(half)]
        for l in range(grid.nl):
            places += [(c, h, l, y) for h in range(grid.nh) for y in range(half, grid.ny)]
    return places


def after(value, *others):
    return lax.optimization_barrier((value, *others))[0]


def assemble(firsts_ref, gathered_refs, flat_ref, windows):
    rows = windows.rows
    inner = max(windows.shard // UNIT - 1, 0) * TILE
    after = TILE + inner

    def clear(place, carry):
        first = pl.multiple_of(firsts_ref[place], TILE)
        flat_ref[pl.ds(first, TILE), :] = jnp.zeros((TILE, LANES), f32)
        flat_ref[pl.ds(first + after, rows - after), :] = jnp.zeros((rows - after, LANES), f32)
        return carry

    lax.fori_loop(0, windows.devices, clear, 0)
    place = 0
    for gathered_ref in gathered_refs:
        blocks = gathered_ref.shape[0] // rows

        def visit(block, carry, gathered_ref=gathered_ref, place=place):
            first = pl.multiple_of(firsts_ref[place + block], TILE)
            value = gathered_ref[pl.ds(pl.multiple_of(block * rows, TILE), rows), :].astype(f32)
            flat_ref[pl.ds(first, TILE), :] += value[:TILE]
            if inner:
                flat_ref[pl.ds(first + TILE, inner), :] = value[TILE:after]
            flat_ref[pl.ds(first + after, rows - after), :] += value[after:]
            return carry

        lax.fori_loop(0, blocks, visit, 0)
        place += blocks


def relay(flat_ref, place, out_ref):
    first, (rows, columns) = place
    chunks = columns // LANES
    step = 64

    def body(index, carry):
        begin = pl.multiple_of(index * step, step)
        for chunk in range(chunks):
            part = flat_ref[pl.ds(first + begin * chunks + chunk, step, stride=chunks), :]
            out_ref[pl.ds(begin, step), chunk * LANES : (chunk + 1) * LANES] = part.astype(out_ref.dtype)
        return carry

    lax.fori_loop(0, rows // step, body, 0)


def relay_vectors(flat_ref, table, out_ref):
    for index, (first, dims) in enumerate(vectors_of(table)):
        for chunk in range(dims[0] // LANES):
            out_ref[index : index + 1, chunk * LANES : (chunk + 1) * LANES] = flat_ref[
                first + chunk : first + chunk + 1, :
            ]


def unpack_cross_kernel(windows, count, traffic, firsts_ref, task_ref, *refs):
    vectors_ref, start_ref, query_ref, key_ref, value_ref, output_ref, up_ref, down_ref, flat_ref = refs[count:]
    assemble(firsts_ref, refs[:count], flat_ref, windows)
    relay_vectors(flat_ref, CROSS, vectors_ref)
    traffic.ship(vectors_ref)
    chunks = D // LANES
    first, unused = CROSS.task_table
    base = first + task_ref[0] * chunks
    relay(flat_ref, CROSS.latents, start_ref)
    for chunk in range(chunks):
        row = flat_ref[pl.ds(base + chunk, 1), :]
        start_ref[:, chunk * LANES : (chunk + 1) * LANES] += row
    traffic.ship(start_ref)
    relay(flat_ref, CROSS.query_weight, query_ref)
    traffic.ship(query_ref)
    relay(flat_ref, CROSS.key_weight, key_ref)
    traffic.ship(key_ref)
    relay(flat_ref, CROSS.value_weight, value_ref)
    traffic.ship(value_ref)
    relay(flat_ref, CROSS.output_weight, output_ref)
    traffic.ship(output_ref)
    relay(flat_ref, CROSS.up_weight, up_ref)
    traffic.ship(up_ref)
    relay(flat_ref, CROSS.down_weight, down_ref)
    traffic.ship(down_ref)


def unpack_cross(firsts, gathered, task, windows):
    outs = [
        shape((16, FF), f32), shape((LAT, D), f32), shape((D, D), bf16), shape((C, D), bf16),
        shape((C, D), bf16), shape((D, D), bf16), shape((D, FF), bf16), shape((FF, D), bf16),
    ]
    return streamed(
        functools.partial(unpack_cross_kernel, windows, len(gathered)), "unpack_cross", outs,
        [firsts, task, *gathered], early=range(len(outs)), scratch=[pltpu.VMEM((windows.padded, LANES), f32)], smem=2,
        flops=20_000_000_000, room=ROOM,
    )


def unpack_latent_kernel(windows, count, traffic, firsts_ref, *refs):
    vectors_ref, joint_ref, merge_ref, up_ref, down_ref, flat_ref = refs[count:]
    assemble(firsts_ref, refs[:count], flat_ref, windows)
    relay_vectors(flat_ref, LATENT, vectors_ref)
    traffic.ship(vectors_ref)
    relay(flat_ref, LATENT.joint_weight, joint_ref)
    traffic.ship(joint_ref)
    relay(flat_ref, LATENT.merge_weight, merge_ref)
    traffic.ship(merge_ref)
    relay(flat_ref, LATENT.up_weight, up_ref)
    traffic.ship(up_ref)
    relay(flat_ref, LATENT.down_weight, down_ref)
    traffic.ship(down_ref)


def unpack_latent(firsts, gathered, windows):
    outs = [
        shape((8, FF), f32), shape((D, 3 * D), bf16), shape((D, D), bf16), shape((D, FF), bf16),
        shape((FF, D), bf16),
    ]
    return streamed(
        functools.partial(unpack_latent_kernel, windows, len(gathered)), "unpack_latent", outs,
        [firsts, *gathered], scratch=[pltpu.VMEM((windows.padded, LANES), f32)], smem=1, room=20 * 2**20,
    )


def put(flat_ref, first, columns, row, value, column=0):
    chunks = columns // LANES
    rows = value.shape[0]
    for chunk in range(value.shape[1] // LANES):
        begin = first + row * chunks + column // LANES + chunk
        flat_ref[pl.ds(begin, rows, stride=chunks), :] = value[:, chunk * LANES : (chunk + 1) * LANES]


def put_vector(flat_ref, first, value, column=0):
    for chunk in range(value.shape[1] // LANES):
        row = first + column // LANES + chunk
        flat_ref[row : row + 1, :] = value[:, chunk * LANES : (chunk + 1) * LANES]


def to_windows(flat_ref, firsts_ref, out_refs, rows, traffic=None):
    begin = 0
    for out_ref in out_refs:
        held = out_ref.shape[0] // rows
        blocks = traffic.blocks[id(out_ref)][0].shape[0] // rows if traffic else held

        def visit(place, carry, out_ref=out_ref, begin=begin, held=held):
            if traffic:

                @pl.when(place >= held)
                def _():
                    traffic.block(out_ref, place - held, rows).wait()

            first = pl.multiple_of(firsts_ref[begin + place], TILE)
            slot = pl.multiple_of(place % held * rows, TILE)
            out_ref[pl.ds(slot, rows), :] = flat_ref[pl.ds(first, rows), :].astype(bf16)
            if traffic:
                traffic.block(out_ref, place, rows).start()
            return carry

        def finish(place, carry, out_ref=out_ref):
            traffic.block(out_ref, place, rows).wait()
            return carry

        lax.fori_loop(0, blocks, visit, 0)
        if traffic:
            lax.fori_loop(blocks - held, blocks, finish, 0)
        begin += blocks


def clear_tail(flat_ref, used):
    total = flat_ref.shape[0]
    flat_ref[used:total, :] = jnp.zeros((total - used, LANES), f32)


def gelu_and_slope(value):
    half = 0.5 + 0.5 * lax.erf(value * math.sqrt(0.5))
    density = jnp.exp2(value * value * (-0.5 * LOG2E)) * (1.0 / math.sqrt(2.0 * math.pi))
    return value * half, half + value * density


def feed_forward(traffic, hidden, gain, bias, up_ref, up_bias, down_ref, down_bias, normed_ref, active_ref, slope_ref):
    unit, rstd = normalise(hidden)
    normed_ref[...] = (unit * gain + bias).astype(bf16)
    traffic.ship(normed_ref)
    traffic.need(up_ref)
    step = 256
    for begin in range(0, FF, step):
        inner = dot(normed_ref[...], up_ref[:, begin : begin + step]) + up_bias[:, begin : begin + step]
        active, slope = gelu_and_slope(inner)
        active_ref[:, begin : begin + step] = active.astype(bf16)
        slope_ref[:, begin : begin + step] = slope.astype(bf16)
    traffic.ship(active_ref, slope_ref)
    traffic.need(down_ref)
    return hidden + (dot(active_ref[...], down_ref[...]) + down_bias)


def feed_backward(traffic, grad, hidden, gain, up_ref, down_ref, normed_ref, active_ref, slope_ref, flat_ref, table,
                  base=0):
    unit, rstd = normalise(hidden)
    branch = grad.astype(bf16)
    put_vector(flat_ref, table.down_bias[0] - base, column_sum(branch.astype(f32)))
    step = 256
    total = None
    normed = normed_ref[...]
    for begin in range(0, FF, step):
        put(flat_ref, table.down_weight[0] - base, D, begin, dot_tn(active_ref[:, begin : begin + step], branch))
        active_grad = dot_nt(branch, down_ref[begin : begin + step, :])
        inner = (active_grad * slope_ref[:, begin : begin + step].astype(f32)).astype(bf16)
        slope_ref[:, begin : begin + step] = inner
        put_vector(flat_ref, table.up_bias[0] - base, column_sum(inner.astype(f32)), begin)
        put(flat_ref, table.up_weight[0] - base, FF, 0, dot_tn(normed, inner), begin)
    traffic.need(up_ref)
    normed_grad = dot_nt(slope_ref[...], up_ref[...])
    put_vector(flat_ref, table.feed_gain[0] - base, column_sum(normed_grad * unit))
    put_vector(flat_ref, table.feed_bias[0] - base, column_sum(normed_grad))
    return grad + normalise_back(normed_grad, unit, rstd, gain)


def vector(vectors_ref, table, place):
    index = vectors_of(table).index(place)
    return vectors_ref[index : index + 1, : place[1][0]]


def block_kinds(count, begin, block, total):
    language = total - LANG
    end = begin + block
    some = (begin < count) | (end > language)
    full = (end <= count) | (count >= language) | (begin >= language)
    return some, full


def masked(scores, count, begin, total):
    place = begin + lax.broadcasted_iota(jnp.int32, (scores.shape[0], 1), 0)
    valid = (place < count) | (place >= total - LANG)
    return jnp.where(valid, scores, negative)


def cross_forward_kernel(traffic, count_ref, tokens_ref, start_ref, vectors_ref, wq_ref, wk_ref, wv_ref, wo_ref,
                         up_ref, down_ref,
                         normedq_ref, query_ref, keyed_ref, mixture_ref, lse_ref, hidden_ref, normed_ref,
                         active_ref, slope_ref, out_ref,
                         acc_ref, max_ref, sum_ref):
    total = tokens_ref.shape[0]
    count = count_ref[0]
    start = start_ref[...]
    unit, rstd = normalise(start)
    normedq_ref[...] = (
        unit * vector(vectors_ref, CROSS, CROSS.query_gain) + vector(vectors_ref, CROSS, CROSS.query_bias)
    ).astype(bf16)
    traffic.ship(normedq_ref)
    query_ref[...] = dot(normedq_ref[...], wq_ref[...]).astype(bf16)
    traffic.ship(query_ref)
    keyed_ref[...] = dot_nt(query_ref[...], wk_ref[...]) * D ** (-0.5)
    traffic.ship(keyed_ref)
    keyed = split(keyed_ref[...] * LOG2E, 1)
    gain = vector(vectors_ref, CROSS, CROSS.context_gain)
    bias = vector(vectors_ref, CROSS, CROSS.context_bias)
    max_ref[...] = jnp.full(max_ref.shape, negative, f32)
    sum_ref[...] = jnp.zeros(sum_ref.shape, f32)
    acc_ref[...] = jnp.zeros(acc_ref.shape, f32)
    block = min(BLOCK, total)

    def visit(index, carry):
        begin = pl.multiple_of(index * block, block)
        some, full = block_kinds(count, begin, block, total)

        @pl.when(some)
        def _():
            contexts, scores = [], []
            for part in range(0, block, PART):
                unit, rstd = normalise(tokens_ref[pl.ds(begin + part, PART), :].astype(f32))
                context = (unit * gain + bias).astype(bf16)
                contexts.append(context)
                raw = dot_nt(jnp.concatenate([context, context], axis=1), keyed)
                scores.append(masked(raw, count, begin + part, total))
            old = max_ref[...]
            newest = old
            for score in scores:
                newest = jnp.maximum(newest, jnp.max(score, axis=0, keepdims=True))
            fade = jnp.exp2(old - newest)
            max_ref[...] = newest
            added, mixed = sum_ref[...] * fade, acc_ref[...] * fade
            for context, score in zip(contexts, scores):
                weights = jnp.exp2(score - newest)
                added += column_sum(weights)
                mixed += dot_tn(context, weights.astype(bf16))
            sum_ref[...] = added
            acc_ref[...] = mixed

        return carry

    lax.fori_loop(0, total // block, visit, 0)
    totals = sum_ref[...]
    lse_ref[...] = max_ref[...] + jnp.log2(totals)
    mixture_ref[...] = acc_ref[...] * (1.0 / totals)
    traffic.ship(lse_ref, mixture_ref)
    traffic.need(wv_ref, wo_ref)
    values = jnp.concatenate([wv_ref[...], wv_ref[...]], axis=0)
    attended = dot_tn(split(mixture_ref[...], 0), values)
    hidden_ref[...] = start + (
        dot(attended.astype(bf16), wo_ref[...]) + vector(vectors_ref, CROSS, CROSS.output_bias)
    )
    traffic.ship(hidden_ref)
    out_ref[...] = feed_forward(
        traffic, hidden_ref[...], vector(vectors_ref, CROSS, CROSS.feed_gain), vector(vectors_ref, CROSS, CROSS.feed_bias),
        up_ref, vector(vectors_ref, CROSS, CROSS.up_bias), down_ref, vector(vectors_ref, CROSS, CROSS.down_bias),
        normed_ref, active_ref, slope_ref,
    )


def cross_forward(count, tokens, start, vectors, wq, wk, wv, wo, up, down):
    outs = [
        shape((LAT, D), bf16), shape((LAT, D), bf16), shape((LAT, C), f32), shape((C, LAT), f32),
        shape((1, LAT), f32), shape((LAT, D), f32), shape((LAT, D), bf16), shape((LAT, FF), bf16),
        shape((LAT, FF), bf16), shape((LAT, D), f32),
    ]
    scratch = [
        pltpu.VMEM((C, LAT), f32), pltpu.VMEM((1, LAT), f32), pltpu.VMEM((1, LAT), f32),
    ]
    return streamed(
        cross_forward_kernel, "cross_forward", outs,
        [count, tokens, start, vectors, wq, wk, wv, wo, up, down], late=range(6, 10), early=range(9), scratch=scratch,
        smem=1, flops=100_000_000_000,
    )


def pair_mask(value, side):
    lane = lax.broadcasted_iota(jnp.int32, (1, LANES), 1)
    keep = (lane < HEAD) if side == 0 else (lane >= HEAD)
    return jnp.where(keep, value, jnp.zeros_like(value))


def latent_kernel(windows, parts, traffic, firsts_ref, hidden_ref, cotangent_ref, vectors_ref, joint_w_ref, merge_ref,
                  up_ref, down_ref, out_ref, grad_ref, *rest):
    windows_refs, rest = rest[:parts], rest[parts:]
    (flat_ref, probs_ref, joint_ref, mixed_ref, after_ref, normedl_ref, normed_ref, active_ref, slope_ref, query_grad_ref, joint_grad_ref) = rest
    gain = vector(vectors_ref, LATENT, LATENT.attend_gain)
    unit, rstd = normalise(hidden_ref[...])
    normedl_ref[...] = (unit * gain + vector(vectors_ref, LATENT, LATENT.attend_bias)).astype(bf16)
    joint_ref[...] = dot(normedl_ref[...], joint_w_ref[...]).astype(bf16)
    scale = HEAD ** (-0.5)
    for pair in range(HEADS // 2):
        lanes = slice(pair * LANES, (pair + 1) * LANES)
        query = joint_ref[:, lanes]
        keys = joint_ref[:, D + pair * LANES : D + (pair + 1) * LANES]
        values = joint_ref[:, 2 * D + pair * LANES : 2 * D + (pair + 1) * LANES]
        mixed = None
        for side in range(2):
            scores = dot_nt(pair_mask(keys, side), query) * (scale * LOG2E)
            weights = jnp.exp2(scores - jnp.max(scores, axis=0, keepdims=True))
            weights = weights * (1.0 / column_sum(weights))
            probs_ref[2 * pair + side] = weights
            part = dot_tn(pair_mask(values, side), weights.astype(bf16))
            mixed = part if mixed is None else mixed + part
        mixed_ref[lanes, :] = mixed.astype(bf16)
    traffic.need(merge_ref)
    after_ref[...] = hidden_ref[...] + (
        dot_tn(mixed_ref[...], merge_ref[...]) + vector(vectors_ref, LATENT, LATENT.merge_bias)
    )
    feed_gain = vector(vectors_ref, LATENT, LATENT.feed_gain)
    out_ref[...] = feed_forward(
        traffic, after_ref[...], feed_gain, vector(vectors_ref, LATENT, LATENT.feed_bias), up_ref,
        vector(vectors_ref, LATENT, LATENT.up_bias), down_ref, vector(vectors_ref, LATENT, LATENT.down_bias),
        normed_ref, active_ref, slope_ref,
    ).astype(bf16)

    traffic.ship(out_ref)
    traffic.need(cotangent_ref)
    clear_tail(flat_ref, LATENT_ROWS)
    after_grad = feed_backward(
        traffic, cotangent_ref[...].astype(f32), after_ref[...], feed_gain, up_ref, down_ref, normed_ref, active_ref,
        slope_ref, flat_ref, LATENT,
    )
    branch = after_grad.astype(bf16)
    put(flat_ref, LATENT.merge_weight[0], D, 0, dot(mixed_ref[...], branch))
    put_vector(flat_ref, LATENT.merge_bias[0], column_sum(branch.astype(f32)))
    mixed_grad = dot_nt(branch, merge_ref[...]).astype(bf16)
    for pair in range(HEADS // 2):
        lanes = slice(pair * LANES, (pair + 1) * LANES)
        query = joint_ref[:, lanes]
        keys = joint_ref[:, D + pair * LANES : D + (pair + 1) * LANES]
        values = joint_ref[:, 2 * D + pair * LANES : 2 * D + (pair + 1) * LANES]
        grads = mixed_grad[:, lanes]
        query_part = key_part = value_part = None
        for side in range(2):
            probs = probs_ref[2 * pair + side]
            part = dot(probs.astype(bf16), pair_mask(grads, side))
            value_part = part if side == 0 else value_part + part
            probs_grad = dot_nt(pair_mask(values, side), grads)
            delta = column_sum(probs * probs_grad)
            scores_grad = (probs * (probs_grad - delta)).astype(bf16)
            part = dot(scores_grad, pair_mask(query, side))
            key_part = part if side == 0 else key_part + part
            part = dot_tn(pair_mask(keys, side), scores_grad)
            query_part = part if side == 0 else query_part + part
        query_grad_ref[lanes, :] = query_part * scale
        joint_grad_ref[:, D + pair * LANES : D + (pair + 1) * LANES] = (key_part * scale).astype(bf16)
        joint_grad_ref[:, 2 * D + pair * LANES : 2 * D + (pair + 1) * LANES] = value_part.astype(bf16)
    joint_grad_ref[:, :D] = query_grad_ref[...].T.astype(bf16)
    put(flat_ref, LATENT.joint_weight[0], 3 * D, 0, dot_tn(normedl_ref[...], joint_grad_ref[...]))
    normed_grad = dot_nt(joint_grad_ref[...], joint_w_ref[...])
    put_vector(flat_ref, LATENT.attend_gain[0], column_sum(normed_grad * unit))
    put_vector(flat_ref, LATENT.attend_bias[0], column_sum(normed_grad))
    grad_ref[...] = after_grad + normalise_back(normed_grad, unit, rstd, gain)
    to_windows(flat_ref, firsts_ref, windows_refs, windows.rows, traffic)


def latent_layer(firsts, hidden, cotangent, vectors, joint, merge, up, down, windows, grid):
    outs = [shape((LAT, D), bf16), shape((LAT, D), f32)] + windows.outs(grid.nz)
    scratch = [
        pltpu.VMEM((windows.padded, LANES), f32), pltpu.VMEM((HEADS, LAT, LAT), f32),
        pltpu.VMEM((LAT, 3 * D), bf16), pltpu.VMEM((D, LAT), bf16), pltpu.VMEM((LAT, D), f32),
        pltpu.VMEM((LAT, D), bf16), pltpu.VMEM((LAT, D), bf16), pltpu.VMEM((LAT, FF), bf16),
        pltpu.VMEM((LAT, FF), bf16), pltpu.VMEM((D, LAT), f32), pltpu.VMEM((LAT, 3 * D), bf16),
    ]
    return streamed(
        functools.partial(latent_kernel, windows, grid.nz), "latent_layer", outs,
        [firsts, hidden, cotangent, vectors, joint, merge, up, down], late=[2], early=[0],
        blocks={2 + c: windows.devices // grid.nz for c in range(grid.nz)}, scratch=scratch, smem=1,
        flops=20_000_000_000, room=14 * 2**20,
    )


SPLIT = CROSS.output_weight[0] // TILE * TILE


def cross_feed_kernel(windows, parts, traffic, firsts_ref, grad_ref, vectors_ref, wv_ref, wo_ref, up_ref, down_ref,
                      mixture_ref, hidden_ref, normed_ref, active_ref, saved_slope_ref,
                      hidden_grad_ref, valued_ref, delta_ref, value_grad_ref, *rest):
    windows_refs = rest[:parts]
    flat_ref, slope_ref = rest[parts:]
    clear_tail(flat_ref, CROSS_ROWS)
    slope_ref[...] = saved_slope_ref[...]
    hidden_grad = feed_backward(
        traffic, grad_ref[...], hidden_ref[...], vector(vectors_ref, CROSS, CROSS.feed_gain), up_ref, down_ref, normed_ref,
        active_ref, slope_ref, flat_ref, CROSS,
    )
    hidden_grad_ref[...] = hidden_grad
    traffic.ship(hidden_grad_ref)
    traffic.need(wv_ref, wo_ref, mixture_ref)
    branch = hidden_grad.astype(bf16)
    values = jnp.concatenate([wv_ref[...], wv_ref[...]], axis=0)
    mixture = split(mixture_ref[...], 0)
    attended = dot_tn(mixture, values)
    put(flat_ref, CROSS.output_weight[0], D, 0, dot_tn(attended.astype(bf16), branch))
    put_vector(flat_ref, CROSS.output_bias[0], column_sum(branch.astype(f32)))
    attended_grad = dot_nt(branch, wo_ref[...]).astype(bf16)
    both = dot(mixture, attended_grad)
    value_grad_ref[...] = both[:C] + both[C:]
    put(flat_ref, CROSS.value_weight[0], D, 0, value_grad_ref[...])
    valued = dot_nt(attended_grad, wv_ref[...])
    valued_ref[...] = split(valued, 1)
    delta_ref[...] = column_sum((attended_grad.astype(f32) * attended).T)
    flat_ref[:SPLIT, :] = jnp.zeros((SPLIT, LANES), f32)
    to_windows(flat_ref, firsts_ref, windows_refs, windows.rows, traffic)


def cross_feed(firsts, grad, vectors, wv, wo, up, down, mixture, hidden, normed, active, slope, windows, grid):
    outs = [
        shape((LAT, D), f32), shape((LAT, 2 * C), bf16), shape((1, LAT), f32), shape((C, D), f32),
    ] + windows.outs(grid.nz)
    return streamed(
        functools.partial(cross_feed_kernel, windows, grid.nz), "cross_feed", outs,
        [firsts, grad, vectors, wv, wo, up, down, mixture, hidden, normed, active, slope], late=[5, 3, 4, 7],
        early=[0], blocks={4 + c: windows.devices // grid.nz for c in range(grid.nz)},
        scratch=[pltpu.VMEM((windows.padded, LANES), f32), pltpu.VMEM((LAT, FF), bf16)], smem=1,
        flops=80_000_000_000,
    )


def attend_block(offset, blocks, count_ref, tokens_ref, valued_ref, delta_ref, vectors_ref, keyed_ref, lse_ref,
                 token_grad_ref, acc_ref, gains_ref, doubled_ref, paired_ref):
    block = tokens_ref.shape[0]
    begin = (pl.program_id(0) + offset) * block
    total = blocks * block
    count = count_ref[0]
    some, full = block_kinds(count, begin, block, total)

    @pl.when(pl.program_id(0) == 0)
    def _():
        doubled_ref[...] = split(keyed_ref[...] * LOG2E, 1)
        paired_ref[...] = split(keyed_ref[...], 1)

    @pl.when(some)
    def _():
        gain = vector(vectors_ref, CROSS, CROSS.context_gain)
        bias = vector(vectors_ref, CROSS, CROSS.context_bias)
        for part in range(0, block, PART):
            rows = slice(part, part + PART)
            unit, rstd = normalise(tokens_ref[rows, :].astype(f32))
            context = (unit * gain + bias).astype(bf16)
            twice = jnp.concatenate([context, context], axis=1)
            scores = masked(dot_nt(twice, doubled_ref[...]), count, begin + part, total)
            probs = jnp.exp2(scores - lse_ref[...])
            scores_grad = (probs * (dot_nt(twice, valued_ref[...]) - delta_ref[...])).astype(bf16)
            acc_ref[...] += dot_tn(context, scores_grad)
            wide = dot(probs.astype(bf16), valued_ref[...]) + dot(scores_grad, paired_ref[...])
            context_grad = wide[:, :C] + wide[:, C:]
            gains_ref[0:1, :] += column_sum(context_grad * unit)
            gains_ref[1:2, :] += column_sum(context_grad)
            token_grad_ref[rows, :] = normalise_back(context_grad, unit, rstd, gain)

    @pl.when(jnp.logical_not(some))
    def _():
        token_grad_ref[...] = jnp.zeros(token_grad_ref.shape, f32)


def attend_first_kernel(blocks, count_ref, tokens_ref, valued_ref, delta_ref, vectors_ref, keyed_ref, lse_ref,
                        token_grad_ref, acc_ref, gains_ref, doubled_ref, paired_ref):
    @pl.when(pl.program_id(0) == 0)
    def _():
        acc_ref[...] = jnp.zeros(acc_ref.shape, f32)
        gains_ref[...] = jnp.zeros(gains_ref.shape, f32)

    attend_block(0, blocks, count_ref, tokens_ref, valued_ref, delta_ref, vectors_ref, keyed_ref, lse_ref,
                 token_grad_ref, acc_ref, gains_ref, doubled_ref, paired_ref)


def attend_second_kernel(offset, blocks, rows, parts, firsts_ref, count_ref, task_ref, tokens_ref, valued_ref,
                         delta_ref, vectors_ref, keyed_ref, lse_ref, acc_before_ref, gains_before_ref, hidden_grad_ref,
                         value_grad_ref, start_ref, wq_ref, wk_ref, normedq_ref, query_ref, kept_ref,
                         token_grad_ref, *rest):
    windows_refs = rest[:parts]
    flat_ref, acc_ref, gains_ref, doubled_ref, paired_ref = rest[parts:]

    @pl.when(pl.program_id(0) == 0)
    def _():
        acc_ref[...] = acc_before_ref[...]
        gains_ref[...] = gains_before_ref[...]

    attend_block(offset, blocks, count_ref, tokens_ref, valued_ref, delta_ref, vectors_ref, keyed_ref, lse_ref,
                 token_grad_ref, acc_ref, gains_ref, doubled_ref, paired_ref)

    @pl.when(pl.program_id(0) == pl.num_programs(0) - 1)
    def _():
        pulled = split(acc_ref[...] * D ** (-0.5), 0)
        both = dot(pulled, query_ref[...])
        put(flat_ref, CROSS.key_weight[0], D, 0, both[:C] + both[C:])
        put(flat_ref, CROSS.value_weight[0], D, 0, value_grad_ref[...])
        put_vector(flat_ref, CROSS.context_gain[0], gains_ref[0:1, :])
        put_vector(flat_ref, CROSS.context_bias[0], gains_ref[1:2, :])
        query_grad = dot_tn(pulled, jnp.concatenate([wk_ref[...], wk_ref[...]], axis=0)).astype(bf16)
        put(flat_ref, CROSS.query_weight[0], D, 0, dot_tn(normedq_ref[...], query_grad))
        normed_grad = dot_nt(query_grad, wq_ref[...])
        unit, rstd = normalise(start_ref[...])
        put_vector(flat_ref, CROSS.query_gain[0], column_sum(normed_grad * unit))
        put_vector(flat_ref, CROSS.query_bias[0], column_sum(normed_grad))
        gain = vector(vectors_ref, CROSS, CROSS.query_gain)
        start_grad = hidden_grad_ref[...] + normalise_back(normed_grad, unit, rstd, gain)
        put(flat_ref, CROSS.latents[0], D, 0, start_grad)
        first, unused = CROSS.task_table
        chunks = D // LANES
        flat_ref[first : first + NTASK * chunks, :] = jnp.zeros((NTASK * chunks, LANES), f32)
        sums = column_sum(start_grad)
        base = first + task_ref[0] * chunks
        for chunk in range(chunks):
            flat_ref[pl.ds(base + chunk, 1), :] = sums[:, chunk * LANES : (chunk + 1) * LANES]
        clear_tail(flat_ref, SPLIT)
        to_windows(flat_ref, firsts_ref, windows_refs, rows)


def attend_scratch():
    return [pltpu.VMEM((LAT, 2 * C), bf16), pltpu.VMEM((LAT, 2 * C), bf16)]


def attend_first(count, tokens, valued, delta, vectors, keyed, lse):
    total = tokens.shape[0]
    block = min(BLOCK, total)
    blocks = total // block
    whole = [valued, delta, vectors, keyed, lse]
    row = lambda i: (i, 0)
    outs = [shape((total, C), f32), shape((C, LAT), f32), shape((8, C), f32)]
    scratch = attend_scratch()
    return pl.pallas_call(
        functools.partial(attend_first_kernel, blocks),
        name="attend_first",
        grid=(max(blocks // 2, 1),),
        out_shape=outs,
        in_specs=[pl.BlockSpec(memory_space=pltpu.SMEM), pl.BlockSpec((block, C), row)] + vmem_specs(len(whole)),
        out_specs=[pl.BlockSpec((block, C), row)] + vmem_specs(2),
        scratch_shapes=scratch,
        compiler_params=pltpu.CompilerParams(vmem_limit_bytes=vmem_limit(*whole, *scratch)),
        cost_estimate=pl.CostEstimate(flops=100_000_000_000, bytes_accessed=1, transcendentals=0),
    )(count, tokens, *whole)


def attend_second(firsts, count, task, tokens, valued, delta, vectors, keyed, lse, acc, gains, hidden_grad, value_grad,
                  start, wq, wk, normedq, query, token_grad, windows, grid):
    total = tokens.shape[0]
    block = min(BLOCK, total)
    blocks = total // block
    offset = max(blocks // 2, 1)
    rows = windows.quarter(grid.nx)
    last = grid.ny * grid.nz - 1
    assert SPLIT <= windows.first[last + 1] and blocks > offset
    flat_rows = max(windows.first[last] + rows * grid.nx, SPLIT + TILE)
    whole = [valued, delta, vectors, keyed, lse, acc, gains, hidden_grad, value_grad, start, wq, wk, normedq, query]
    half = windows.devices // grid.nz // grid.ny * rows
    small = [shape((half * depths, LANES), bf16) for c in range(grid.nz) for depths in halves(grid)]
    row = lambda i: (i + offset, 0)
    scratch = [
        pltpu.VMEM((flat_rows, LANES), f32), pltpu.VMEM((C, LAT), f32),
        pltpu.VMEM((8, C), f32), *attend_scratch(),
    ]
    return pl.pallas_call(
        functools.partial(attend_second_kernel, offset, blocks, rows, len(small)),
        name="attend_second",
        grid=(blocks - offset,),
        out_shape=[shape((total, C), f32)] + small,
        in_specs=[pl.BlockSpec(memory_space=pltpu.SMEM)] * 3
        + [pl.BlockSpec((block, C), row)]
        + vmem_specs(len(whole))
        + [pl.BlockSpec(memory_space=pl.ANY)],
        out_specs=[pl.BlockSpec((block, C), row)] + vmem_specs(len(small)),
        scratch_shapes=scratch,
        input_output_aliases={4 + len(whole): 0},
        compiler_params=pltpu.CompilerParams(vmem_limit_bytes=vmem_limit(*whole, *small, *scratch)),
        cost_estimate=pl.CostEstimate(flops=100_000_000_000, bytes_accessed=1, transcendentals=0),
    )(firsts, count, task, tokens, *whole, token_grad)


def body(tokens, task_id, valid_count, cross_params, latent_params, out_grad):
    grid = Grid()
    devices = grid.nx * grid.ny * grid.nz
    cw = Windows(cross_params.shape[0] * devices, devices)
    lw = Windows(latent_params.shape[0] * devices, devices)
    gathered_from = grid.owners(gather_places(grid))
    scattered_to = grid.owners(grid.order())
    tokens = tokens[0]

    cross_window, latent_window = place([cross_params, latent_params], [cw, lw], grid.index)
    cross_column = gather_depth(cross_window, grid)
    latent_column = gather_depth(after(latent_window, *cross_column[1:]), grid)
    pieces = gather_plane_second(*gather_plane_first(cross_column, grid), grid)
    for piece in pieces:
        piece[0] = after(piece[0], *latent_column[1:])
        piece[1:] = [after(value, *latent_column[1:]) for value in piece[1:]]
    cross_all = sum(gather_core(*pieces, grid), [])
    latent_column = [after(value, pieces[0][-1], pieces[1][-1]) for value in latent_column]
    lows, highs = gather_plane_first(latent_column, grid)
    vectors, start, wq, wk, wv, wo, up, down = unpack_cross(cw.firsts(gathered_from), cross_all, task_id, cw)
    lows[0], highs[0] = after(lows[0], vectors), after(highs[0], vectors)
    first, second = gather_plane_second(lows, highs, grid)
    normedq, query, keyed, mixture, lse, hidden, normed, active, slope, result = cross_forward(
        valid_count, tokens, after(start, first[0], second[0]), vectors, wq, wk, wv, wo, up, down
    )
    first[1:] = [after(value, result) for value in first[1:]]
    second[1:] = [after(value, result) for value in second[1:]]
    latent_all = sum(gather_core(first, second, grid), [])
    latent_weights = unpack_latent(lw.firsts(gathered_from), latent_all, lw)
    latents_out, result_grad, *latent_parts = latent_layer(
        lw.firsts(scattered_to), result, out_grad[0], *latent_weights, lw, grid
    )

    latent_lows, latent_highs = reduce_first(reduce_core(latent_parts, grid), lw.rows, grid)
    hidden_grad, valued, delta, value_grad, *later_parts = cross_feed(
        cw.firsts(scattered_to), after(result_grad, latent_lows[0][0]), vectors, wv, wo, up, down, mixture, hidden,
        normed, active, slope, cw, grid,
    )
    latent_lows[0] = (after(latent_lows[0][0], delta), 0)
    latent_first, latent_second = reduce_second(latent_lows, latent_highs, lw.rows, grid)
    later_group = reduce_core(later_parts, grid)
    token_grad, acc, gains = attend_first(
        valid_count, tokens, valued, after(delta, latent_first[0][0]), vectors, keyed, lse
    )
    latent_first[0] = (after(latent_first[0][0], acc), 0)
    latent_column = reduce_depth(latent_first, latent_second, lw.rows, grid)
    later_group[0] = (after(later_group[0][0], latent_column[0]), 0)
    later_lows, later_highs = reduce_first(later_group, cw.rows, grid)
    owner, quarter = quarter_owners(grid)
    small_rows = cw.quarter(grid.nx)
    token_grad, *early_parts = attend_second(
        cw.firsts(owner) + quarter * small_rows, valid_count, task_id, tokens, valued, delta, vectors, keyed, lse,
        after(acc, later_lows[0][0]), gains, hidden_grad, value_grad, start, wq, wk, normedq, query, token_grad, cw,
        grid,
    )
    latent_column[0] = after(latent_column[0], early_parts[0])
    latent_share = extract(latent_column, [], lw, grid)
    later_lows[0] = (after(later_lows[0][0], latent_share), 0)
    early_parts = [after(part, latent_share) for part in early_parts]
    early_groups = [reduce_core(early_parts[half::2], grid) for half in range(2)]
    later_first, later_second, early_lows, early_highs = reduce_second_and_first(
        later_lows, later_highs, cw.rows, early_groups, small_rows, grid
    )
    early_first, early_second = reduce_second(early_lows, early_highs, small_rows, grid)
    column = reduce_depth_both(later_first, later_second, cw.rows, early_first, early_second, small_rows, grid)
    quarters = collect_quarters(column, cw.rows, small_rows, grid)
    return (latents_out[None], token_grad[None], extract(column, quarters, cw, grid), latent_share)


def solution(mesh):
    return jax.shard_map(
        body,
        mesh=mesh,
        in_specs=(
            P(AXES, None, None),
            P(AXES),
            P(AXES),
            P(AXES),
            P(AXES),
            P(AXES, None, None),
        ),
        out_specs=(
            P(AXES, None, None),
            P(AXES, None, None),
            P(AXES),
            P(AXES),
        ),
        check_vma=False,
    )
```

```python
import functools
import math
import types

import jax
import jax.numpy as jnp
from jax import lax
from jax.experimental import pallas as pl
from jax.experimental.pallas import tpu as pltpu
from jax.sharding import PartitionSpec as P

D = 512
FF = 2048
C = 128
LAT = 512
HEADS = 8
HEAD = 64
NTASK = 18
LANG = 77
LANES = 128
TILE = 16
UNIT = TILE * LANES
BLOCK = 2048
PART = 512
AXES = ("gx", "gy", "gz")

epsilon = 1e-05
negative = -1e30
LOG2E = math.log2(math.e)
bf16 = jnp.bfloat16
f32 = jnp.float32
VMEM_LIMIT = 60 * 1024 * 1024
ROOM = 6 * 1024 * 1024
SLOTS = 8


def layout_of(**shapes):
    table = {}
    row = 0
    for name, dims in shapes.items():
        table[name] = (row, dims)
        row += math.prod(dims) // LANES
    return types.SimpleNamespace(**table), row


CROSS, CROSS_ROWS = layout_of(
    latents=(LAT, D),
    task_table=(NTASK, D),
    query_gain=(D,),
    query_bias=(D,),
    context_gain=(C,),
    context_bias=(C,),
    query_weight=(D, D),
    key_weight=(C, D),
    value_weight=(C, D),
    output_weight=(D, D),
    output_bias=(D,),
    feed_gain=(D,),
    feed_bias=(D,),
    up_weight=(D, FF),
    up_bias=(FF,),
    down_weight=(FF, D),
    down_bias=(D,),
)
LATENT, LATENT_ROWS = layout_of(
    attend_gain=(D,),
    attend_bias=(D,),
    joint_weight=(D, 3 * D),
    merge_weight=(D, D),
    merge_bias=(D,),
    feed_gain=(D,),
    feed_bias=(D,),
    up_weight=(D, FF),
    up_bias=(FF,),
    down_weight=(FF, D),
    down_bias=(D,),
)


def vectors_of(table):
    return [place for place in vars(table).values() if len(place[1]) == 1]


class Windows:
    def __init__(self, total, devices):
        self.total = total
        self.devices = devices
        self.shard = total // devices
        starts = [self.shard * d for d in range(devices)]
        self.first = [s // UNIT * TILE for s in starts]
        self.phase = [s % UNIT for s in starts]
        self.rows = max(-(-(p + self.shard) // UNIT) * TILE for p in self.phase)
        self.padded = max(f + self.rows for f in self.first)
        self.full = -(-total // UNIT) * TILE
        self.shard_rows = -(-self.shard // (8 * LANES)) * 8

    def outs(self, parts):
        return [shape((self.devices // parts * self.rows, LANES), bf16)] * parts

    def firsts(self, owners):
        return self.shard * owners // UNIT * TILE

    def quarter(self, parts):
        return -(-self.rows // (parts * TILE)) * TILE


def dot(left, right):
    return jnp.dot(left, right, preferred_element_type=f32)


def dot_nt(left, right):
    return lax.dot_general(left, right, (((1,), (1,)), ((), ())), preferred_element_type=f32)


def dot_tn(left, right):
    return lax.dot_general(left, right, (((0,), (0,)), ((), ())), preferred_element_type=f32)


def split(value, axis):
    high = value.astype(bf16)
    low = (value - high.astype(f32)).astype(bf16)
    return jnp.concatenate([high, low], axis=axis)


def normalise(value):
    centred = value - jnp.mean(value, axis=-1, keepdims=True)
    rstd = lax.rsqrt(jnp.mean(centred * centred, axis=-1, keepdims=True) + epsilon)
    return centred * rstd, rstd


def normalise_back(grad, unit, rstd, gain):
    inner = grad * gain
    return rstd * (
        inner
        - jnp.mean(inner, axis=-1, keepdims=True)
        - unit * jnp.mean(inner * unit, axis=-1, keepdims=True)
    )


def column_sum(value):
    return jnp.sum(value, axis=0, keepdims=True)


def vmem_specs(count):
    return [pl.BlockSpec(memory_space=pltpu.VMEM)] * count


def shape(dims, dtype):
    return jax.ShapeDtypeStruct(dims, dtype)


def bytes_of(value):
    return math.prod(value.shape) * jnp.dtype(value.dtype).itemsize


def vmem_limit(*values):
    return min(sum(map(bytes_of, values)) + 16 * 2**20, VMEM_LIMIT)


def call(kernel, name, outs, inputs, scratch=(), smem=0, flops=0, moved=0, alone=True):
    specs = [pl.BlockSpec(memory_space=pltpu.SMEM)] * smem + vmem_specs(len(inputs) - smem)
    limit = VMEM_LIMIT if alone else vmem_limit(*inputs, *jax.tree.leaves(outs), *scratch)
    return pl.pallas_call(
        kernel,
        name=name,
        out_shape=outs,
        in_specs=specs,
        out_specs=jax.tree.map(lambda _: pl.BlockSpec(memory_space=pltpu.VMEM), outs),
        scratch_shapes=list(scratch),
        compiler_params=pltpu.CompilerParams(vmem_limit_bytes=limit),
        cost_estimate=pl.CostEstimate(flops=flops, bytes_accessed=moved, transcendentals=0),
    )(*inputs)


class Traffic:
    def __init__(self):
        self.loads, self.stores, self.blocks, self.begun = {}, {}, {}, []

    def need(self, *refs):
        for ref in refs:
            copy = self.loads.pop(id(ref), None)
            if copy is not None:
                copy.wait()

    def ship(self, *refs):
        for ref in refs:
            copy = self.stores.pop(id(ref), None)
            if copy is not None:
                copy.start()
                self.begun.append(copy)

    def block(self, ref, number, rows):
        target, sem = self.blocks[id(ref)]
        slot = pl.multiple_of(number % (ref.shape[0] // rows) * rows, TILE)
        part = pl.multiple_of(number * rows, TILE)
        return pltpu.make_async_copy(ref.at[pl.ds(slot, rows)], target.at[pl.ds(part, rows)], sem.at[number])


def streamed(kernel, name, outs, inputs, late=(), early=(), blocks=None, scratch=(), smem=0, flops=0, room=0, slots=None):
    blocks = blocks or {}
    shipped = list(early) + list(blocks)
    vmem, hbm = pl.BlockSpec(memory_space=pltpu.VMEM), pl.BlockSpec(memory_space=pltpu.HBM)
    held = [pltpu.VMEM(inputs[i].shape, inputs[i].dtype) for i in late]
    held += [pltpu.VMEM(outs[i].shape, outs[i].dtype) for i in early]
    held += [pltpu.VMEM((min(slots or number, number) * outs[i].shape[0] // number, LANES), bf16) for i, number in blocks.items()]
    sems = [pltpu.SemaphoreType.DMA((max(len(late), 1),)), pltpu.SemaphoreType.DMA((max(len(early), 1),))]
    sems += [pltpu.SemaphoreType.DMA((number,)) for number in blocks.values()]

    def body(*refs):
        takes, gives = list(refs[: len(inputs)]), list(refs[len(inputs) : len(inputs) + len(outs)])
        rest = refs[len(inputs) + len(outs) :]
        buffers, rest = rest[: len(held)], rest[len(held) :]
        load_sem, store_sem = rest[:2]
        block_sems, rest = rest[2 : len(sems)], rest[len(sems) :]
        traffic = Traffic()
        for k, i in enumerate(late):
            copy = pltpu.make_async_copy(takes[i], buffers[k], load_sem.at[k])
            copy.start()
            traffic.loads[id(buffers[k])] = copy
            takes[i] = buffers[k]
        for k, i in enumerate(shipped):
            buffer = buffers[len(late) + k]
            if k < len(early):
                traffic.stores[id(buffer)] = pltpu.make_async_copy(buffer, gives[i], store_sem.at[k])
            else:
                traffic.blocks[id(buffer)] = (gives[i], block_sems[k - len(early)])
            gives[i] = buffer
        kernel(traffic, *takes, *gives, *rest)
        assert not traffic.loads and not traffic.stores
        for copy in traffic.begun:
            copy.wait()

    return pl.pallas_call(
        body,
        name=name,
        out_shape=outs,
        in_specs=[pl.BlockSpec(memory_space=pltpu.SMEM)] * smem
        + [hbm if i in late else vmem for i in range(smem, len(inputs))],
        out_specs=[hbm if i in shipped else vmem for i in range(len(outs))],
        scratch_shapes=held + sems + list(scratch),
        compiler_params=pltpu.CompilerParams(vmem_limit_bytes=VMEM_LIMIT - room),
        cost_estimate=pl.CostEstimate(flops=flops, bytes_accessed=1, transcendentals=0),
    )(*inputs)


def shifted(value, shift):
    down, across = shift // LANES, shift % LANES
    turned = pltpu.roll(value, across, axis=1)
    above = pltpu.roll(turned, 1, axis=0)
    lane = lax.broadcasted_iota(jnp.int32, value.shape, 1)
    return pltpu.roll(jnp.where(lane < across, above, turned), down, axis=0)


def place_kernel(shifts_ref, shards_ref, *out_refs):
    begin = 0
    for number, out_ref in enumerate(out_refs):
        rows = out_ref.shape[0]
        value = shards_ref[begin : begin + rows, :].astype(f32)
        out_ref[...] = shifted(value, shifts_ref[number]).astype(bf16)
        begin += rows


def place(shards, windows, index):
    padded = [
        jnp.pad(shard, (0, w.rows * LANES - w.shard)) for shard, w in zip(shards, windows)
    ]
    together = jnp.concatenate(padded).reshape(-1, LANES)
    shifts = jnp.stack([(w.shard * index) % UNIT for w in windows])
    outs = [shape((w.rows, LANES), bf16) for w in windows]
    return call(place_kernel, "place", outs, [shifts, together], smem=1, alone=False)


def extract_kernel(count, shift_ref, *refs):
    out_ref, total_ref = refs[-2:]
    rows = total_ref.shape[0]
    value = refs[0][:rows, :].astype(f32)
    for ref in refs[1:count]:
        value += ref[:rows, :].astype(f32)
    total_ref[...] = value
    begin = 0
    for ref in refs[count:-2]:
        size = min(ref.shape[0], rows - begin)
        if size > 0:
            total_ref[begin : begin + size, :] += ref[:size, :].astype(f32)
        begin += ref.shape[0]
    down, across = shift_ref[0] // LANES, shift_ref[0] % LANES
    turned = pltpu.roll(total_ref[...], lax.rem(LANES - across, LANES), axis=1)
    below = pltpu.roll(turned, rows - 1, axis=0)
    lane = lax.broadcasted_iota(jnp.int32, (rows, LANES), 1)
    merged = pltpu.roll(
        jnp.where(lane < LANES - across, turned, below), lax.rem(rows - down, rows), axis=0
    )
    out_ref[...] = merged[: out_ref.shape[0]]


def extract(parts, quarters, windows, grid):
    shift = (windows.shard * grid.index) % UNIT
    rows = min(windows.shard_rows, windows.rows)
    found = call(
        functools.partial(extract_kernel, len(parts)), "extract", shape((rows, LANES), f32),
        [shift.reshape(1), *parts, *quarters], scratch=[pltpu.VMEM((windows.rows, LANES), f32)], smem=1,
        alone=False,
    )
    return found.reshape(-1)[: windows.shard]


class Grid:
    def __init__(self):
        self.nx, self.ny, self.nz = (lax.axis_size(axis) for axis in AXES)
        self.nl = 2 if self.nx % 2 == 0 else 1
        self.nh = self.nx // self.nl
        self.index = lax.axis_index(AXES)

    def order(self):
        return [
            (c, h, l, y)
            for c in range(self.nz)
            for h in range(self.nh)
            for l in range(self.nl)
            for y in range(self.ny)
        ]

    def owners(self, places):
        gx, gy, gz = (lax.axis_index(axis) for axis in AXES)
        c, h, l, y = (jnp.array(column, jnp.int32) for column in zip(*places))
        high = (gx // self.nl + h) % self.nh
        low = (gx % self.nl + l) % self.nl
        return ((high * self.nl + low) * self.ny + (gy + y) % self.ny) * self.nz + (gz + c) % self.nz

    def along_core(self, value, step):
        return lax.ppermute(value, AXES[2], [(i, (i + step) % self.nz) for i in range(self.nz)])

    def along_depth(self, value, step):
        return lax.ppermute(value, AXES[1], [(i, (i + step) % self.ny) for i in range(self.ny)])

    def along_low(self, value, step):
        nl = self.nl
        return lax.ppermute(
            value, AXES[0], [(i, i // nl * nl + (i + step) % nl) for i in range(self.nx)]
        )

    def along_high(self, value, step):
        nl = self.nl
        return lax.ppermute(value, AXES[0], [(i, (i + step * nl) % self.nx) for i in range(self.nx)])


def combine_kernel(groups, picks, *refs):
    starts = [sum(len(bases) for rows, bases in groups[:g]) for g in range(len(groups))]
    outputs = refs[sum(len(bases) for rows, bases in groups) :]
    for output, pick in zip(outputs, picks):
        row = 0
        for g, block in pick:
            rows, bases = groups[g]
            total = None
            for i, base in enumerate(bases):
                begin = base + block * rows
                part = refs[starts[g] + i][begin : begin + rows, :].astype(f32)
                total = part if total is None else total + part
            output[row : row + rows, :] = total.astype(bf16)
            row += rows


def combine(name, groups, picks):
    inputs = [array for rows, sources in groups for array, base in sources]
    kinds = tuple((rows, tuple(base for array, base in sources)) for rows, sources in groups)
    sizes = [sum(groups[g][0] for g, block in pick) for pick in picks]
    outs = [shape((size, LANES), bf16) for size in sizes]
    moved = 6 * LANES * sum(sizes)
    return call(
        functools.partial(combine_kernel, kinds, picks), name, outs, inputs, flops=moved, moved=moved, alone=False
    )


def reduce_core(parts, grid):
    return [(parts[0], 0)] + [(grid.along_core(parts[c], c), 0) for c in range(1, grid.nz)]


def first_picks(grid, g):
    nh, nl, ny = grid.nh, grid.nl, grid.ny
    half = ny // 2
    block = lambda h, l, y: (g, (h * nl + l) * ny + y)
    lows = [[block(h, l, y) for h in range(nh) for y in range(half)] for l in range(nl)]
    highs = [[block(h, l, y) for l in range(nl) for y in range(half, ny)] for h in range(nh)]
    return lows, highs


def halves(grid):
    return [grid.ny // 2, grid.ny - grid.ny // 2]


def half_order(grid):
    half = grid.ny // 2
    places = []
    for c in range(grid.nz):
        for depths in (range(half), range(half, grid.ny)):
            places += [(c, h, l, y) for h in range(grid.nh) for l in range(grid.nl) for y in depths]
    return places


def half_first_picks(grid, first_group, second_group):
    nh, nl = grid.nh, grid.nl
    half, rest = halves(grid)
    lows = [[(first_group, (h * nl + l) * half + y) for h in range(nh) for y in range(half)] for l in range(nl)]
    highs = [[(second_group, (h * nl + l) * rest + y) for l in range(nl) for y in range(rest)] for h in range(nh)]
    return lows, highs


def second_picks(grid, low_group, high_group):
    half = grid.ny // 2
    rest = grid.ny - half
    highs = [[(low_group, h * half + y) for y in range(half)] for h in range(grid.nh)]
    lows = [[(high_group, l * rest + y) for y in range(rest)] for l in range(grid.nl)]
    return highs, lows


def depth_picks(grid, first_group, second_group):
    half = grid.ny // 2
    return [(first_group, y) for y in range(half)] + [(second_group, y) for y in range(grid.ny - half)]


def send_low(arrays, grid):
    return [grid.along_low(array, l + 1) for l, array in enumerate(arrays)]


def send_high(arrays, grid):
    return [grid.along_high(array, h + 1) for h, array in enumerate(arrays)]


def send_depth(arrays, grid):
    return [grid.along_depth(array, y + 1) for y, array in enumerate(arrays)]


def at(arrays, base=0):
    return [(array, base) for array in arrays]


def reduce_first(group, rows, grid):
    lows, highs = first_picks(grid, 0)
    outs = combine("plane_first", [(rows, group)], lows + highs)
    keep_low, keep_high = outs[0], outs[grid.nl]
    return (
        at([keep_low] + send_low(outs[1 : grid.nl], grid)),
        at([keep_high] + send_high(outs[grid.nl + 1 :], grid)),
    )


def reduce_second(lows, highs, rows, grid):
    to_high, to_low = second_picks(grid, 0, 1)
    outs = combine("plane_second", [(rows, lows), (rows, highs)], to_high + to_low)
    keep_first, keep_second = outs[0], outs[grid.nh]
    return (
        at([keep_first] + send_high(outs[1 : grid.nh], grid)),
        at([keep_second] + send_low(outs[grid.nh + 1 :], grid)),
    )


def reduce_depth(first, second, rows, grid):
    outs = combine("depth", [(rows, first), (rows, second)], [[pick] for pick in depth_picks(grid, 0, 1)])
    return [outs[0]] + send_depth(outs[1:], grid)


def reduce_second_and_first(lows, highs, rows, small_groups, small_rows, grid):
    to_high, to_low = second_picks(grid, 0, 1)
    small_low, small_high = half_first_picks(grid, 2, 3)
    nh, nl, half = grid.nh, grid.nl, grid.ny // 2
    picks = [to_high[0], to_low[0], small_low[0], small_high[0]]
    picks += [to_high[h] + small_high[h] for h in range(1, nh)]
    picks += [to_low[l] + small_low[l] for l in range(1, nl)]
    outs = combine("second_and_first", [(rows, lows), (rows, highs)] + [(small_rows, group) for group in small_groups], picks)
    keep_first, keep_second, keep_low, keep_high = outs[:4]
    high = send_high(outs[4 : 3 + nh], grid)
    low = send_low(outs[3 + nh :], grid)
    first, second = at([keep_first]) + at(high), at([keep_second]) + at(low)
    lows = at([keep_low]) + at(low, (grid.ny - half) * rows)
    highs = at([keep_high]) + at(high, half * rows)
    return first, second, lows, highs


def reduce_depth_both(first, second, rows, small_first, small_second, small_rows, grid):
    groups = [(rows, first), (rows, second), (small_rows, small_first), (small_rows, small_second)]
    picks = [list(pair) for pair in zip(depth_picks(grid, 0, 1), depth_picks(grid, 2, 3))]
    outs = combine("depth_both", groups, picks)
    return [outs[0]] + send_depth(outs[1:], grid)


def quarter_owners(grid):
    gx, gy, gz = (lax.axis_index(axis) for axis in AXES)
    c, h, l, y = (jnp.array(column, jnp.int32) for column in zip(*half_order(grid)))
    quarter = (gx // grid.nl + h) % grid.nh * grid.nl + (gx % grid.nl + l) % grid.nl
    return (gy + y) % grid.ny * grid.nz + (gz + c) % grid.nz, quarter


def collect_quarters(parts, base, rows, grid):
    (own,) = combine("quarter", [(rows, at(parts, base))], [[(0, 0)]])
    zero = jnp.zeros_like(own)
    first = jnp.where(lax.axis_index(AXES[0]) == 0, own, zero)
    return [first] + [lax.ppermute(own, AXES[0], [(x, 0)]) for x in range(1, grid.nx)]


def gather_depth(window, grid):
    return [window] + [grid.along_depth(window, -y) for y in range(1, grid.ny)]


def gather_plane_first(column, grid):
    half = grid.ny // 2
    first, second = jnp.concatenate(column[:half]), jnp.concatenate(column[half:])
    lows = [first] + [grid.along_low(first, -l) for l in range(1, grid.nl)]
    highs = [second] + [grid.along_high(second, -h) for h in range(1, grid.nh)]
    return lows, highs


def gather_plane_second(lows, highs, grid):
    first, second = jnp.concatenate(lows), jnp.concatenate(highs)
    return (
        [first] + [grid.along_high(first, -h) for h in range(1, grid.nh)],
        [second] + [grid.along_low(second, -l) for l in range(1, grid.nl)],
    )


def gather_core(first, second, grid):
    pieces = first + second
    return [pieces] + [[grid.along_core(piece, -c) for piece in pieces] for c in range(1, grid.nz)]


def gather_places(grid):
    half = grid.ny // 2
    places = []
    for c in range(grid.nz):
        for h in range(grid.nh):
            places += [(c, h, l, y) for l in range(grid.nl) for y in range(half)]
        for l in range(grid.nl):
            places += [(c, h, l, y) for h in range(grid.nh) for y in range(half, grid.ny)]
    return places


def after(value, *others):
    return lax.optimization_barrier((value, *others))[0]


def assemble(firsts_ref, gathered_refs, flat_ref, windows):
    rows = windows.rows
    inner = max(windows.shard // UNIT - 1, 0) * TILE
    after = TILE + inner

    def clear(place, carry):
        first = pl.multiple_of(firsts_ref[place], TILE)
        flat_ref[pl.ds(first, TILE), :] = jnp.zeros((TILE, LANES), f32)
        flat_ref[pl.ds(first + after, rows - after), :] = jnp.zeros((rows - after, LANES), f32)
        return carry

    lax.fori_loop(0, windows.devices, clear, 0)
    place = 0
    for gathered_ref in gathered_refs:
        blocks = gathered_ref.shape[0] // rows

        def visit(block, carry, gathered_ref=gathered_ref, place=place):
            first = pl.multiple_of(firsts_ref[place + block], TILE)
            value = gathered_ref[pl.ds(pl.multiple_of(block * rows, TILE), rows), :].astype(f32)
            flat_ref[pl.ds(first, TILE), :] += value[:TILE]
            if inner:
                flat_ref[pl.ds(first + TILE, inner), :] = value[TILE:after]
            flat_ref[pl.ds(first + after, rows - after), :] += value[after:]
            return carry

        lax.fori_loop(0, blocks, visit, 0)
        place += blocks


def relay(flat_ref, place, out_ref):
    first, (rows, columns) = place
    chunks = columns // LANES
    step = 64

    def body(index, carry):
        begin = pl.multiple_of(index * step, step)
        for chunk in range(chunks):
            part = flat_ref[pl.ds(first + begin * chunks + chunk, step, stride=chunks), :]
            out_ref[pl.ds(begin, step), chunk * LANES : (chunk + 1) * LANES] = part.astype(out_ref.dtype)
        return carry

    lax.fori_loop(0, rows // step, body, 0)


def relay_vectors(flat_ref, table, out_ref):
    for index, (first, dims) in enumerate(vectors_of(table)):
        for chunk in range(dims[0] // LANES):
            out_ref[index : index + 1, chunk * LANES : (chunk + 1) * LANES] = flat_ref[
                first + chunk : first + chunk + 1, :
            ]


def unpack_cross_kernel(windows, count, traffic, firsts_ref, task_ref, *refs):
    vectors_ref, start_ref, query_ref, key_ref, value_ref, output_ref, up_ref, down_ref, flat_ref = refs[count:]
    assemble(firsts_ref, refs[:count], flat_ref, windows)
    relay_vectors(flat_ref, CROSS, vectors_ref)
    traffic.ship(vectors_ref)
    chunks = D // LANES
    first, unused = CROSS.task_table
    base = first + task_ref[0] * chunks
    relay(flat_ref, CROSS.latents, start_ref)
    for chunk in range(chunks):
        row = flat_ref[pl.ds(base + chunk, 1), :]
        start_ref[:, chunk * LANES : (chunk + 1) * LANES] += row
    traffic.ship(start_ref)
    relay(flat_ref, CROSS.query_weight, query_ref)
    traffic.ship(query_ref)
    relay(flat_ref, CROSS.key_weight, key_ref)
    traffic.ship(key_ref)
    relay(flat_ref, CROSS.value_weight, value_ref)
    traffic.ship(value_ref)
    relay(flat_ref, CROSS.output_weight, output_ref)
    traffic.ship(output_ref)
    relay(flat_ref, CROSS.up_weight, up_ref)
    traffic.ship(up_ref)
    relay(flat_ref, CROSS.down_weight, down_ref)
    traffic.ship(down_ref)


def unpack_cross(firsts, gathered, task, windows):
    outs = [
        shape((16, FF), f32), shape((LAT, D), f32), shape((D, D), bf16), shape((C, D), bf16),
        shape((C, D), bf16), shape((D, D), bf16), shape((D, FF), bf16), shape((FF, D), bf16),
    ]
    return streamed(
        functools.partial(unpack_cross_kernel, windows, len(gathered)), "unpack_cross", outs,
        [firsts, task, *gathered], early=range(len(outs)), scratch=[pltpu.VMEM((windows.padded, LANES), f32)], smem=2,
        flops=20_000_000_000, room=ROOM,
    )


def unpack_latent_kernel(windows, count, traffic, firsts_ref, *refs):
    vectors_ref, joint_ref, merge_ref, up_ref, down_ref, flat_ref = refs[count:]
    assemble(firsts_ref, refs[:count], flat_ref, windows)
    relay_vectors(flat_ref, LATENT, vectors_ref)
    traffic.ship(vectors_ref)
    relay(flat_ref, LATENT.joint_weight, joint_ref)
    traffic.ship(joint_ref)
    relay(flat_ref, LATENT.merge_weight, merge_ref)
    traffic.ship(merge_ref)
    relay(flat_ref, LATENT.up_weight, up_ref)
    traffic.ship(up_ref)
    relay(flat_ref, LATENT.down_weight, down_ref)
    traffic.ship(down_ref)


def unpack_latent(firsts, gathered, windows):
    outs = [
        shape((8, FF), f32), shape((D, 3 * D), bf16), shape((D, D), bf16), shape((D, FF), bf16),
        shape((FF, D), bf16),
    ]
    return streamed(
        functools.partial(unpack_latent_kernel, windows, len(gathered)), "unpack_latent", outs,
        [firsts, *gathered], scratch=[pltpu.VMEM((windows.padded, LANES), f32)], smem=1, room=20 * 2**20,
    )


def put(flat_ref, first, columns, row, value, column=0):
    chunks = columns // LANES
    rows = value.shape[0]
    for chunk in range(value.shape[1] // LANES):
        begin = first + row * chunks + column // LANES + chunk
        flat_ref[pl.ds(begin, rows, stride=chunks), :] = value[:, chunk * LANES : (chunk + 1) * LANES]


def put_vector(flat_ref, first, value, column=0):
    for chunk in range(value.shape[1] // LANES):
        row = first + column // LANES + chunk
        flat_ref[row : row + 1, :] = value[:, chunk * LANES : (chunk + 1) * LANES]


def to_windows(flat_ref, firsts_ref, out_refs, rows, traffic=None):
    begin = 0
    for out_ref in out_refs:
        held = out_ref.shape[0] // rows
        blocks = traffic.blocks[id(out_ref)][0].shape[0] // rows if traffic else held

        def visit(place, carry, out_ref=out_ref, begin=begin, held=held):
            if traffic:

                @pl.when(place >= held)
                def _():
                    traffic.block(out_ref, place - held, rows).wait()

            first = pl.multiple_of(firsts_ref[begin + place], TILE)
            slot = pl.multiple_of(place % held * rows, TILE)
            out_ref[pl.ds(slot, rows), :] = flat_ref[pl.ds(first, rows), :].astype(bf16)
            if traffic:
                traffic.block(out_ref, place, rows).start()
            return carry

        def finish(place, carry, out_ref=out_ref):
            traffic.block(out_ref, place, rows).wait()
            return carry

        lax.fori_loop(0, blocks, visit, 0)
        if traffic:
            lax.fori_loop(blocks - held, blocks, finish, 0)
        begin += blocks


def clear_tail(flat_ref, used):
    total = flat_ref.shape[0]
    flat_ref[used:total, :] = jnp.zeros((total - used, LANES), f32)


def gelu_and_slope(value):
    half = 0.5 + 0.5 * lax.erf(value * math.sqrt(0.5))
    density = jnp.exp2(value * value * (-0.5 * LOG2E)) * (1.0 / math.sqrt(2.0 * math.pi))
    return value * half, half + value * density


def feed_forward(traffic, hidden, gain, bias, up_ref, up_bias, down_ref, down_bias, normed_ref, active_ref, slope_ref):
    unit, rstd = normalise(hidden)
    normed_ref[...] = (unit * gain + bias).astype(bf16)
    traffic.ship(normed_ref)
    traffic.need(up_ref)
    step = 256
    for begin in range(0, FF, step):
        inner = dot(normed_ref[...], up_ref[:, begin : begin + step]) + up_bias[:, begin : begin + step]
        active, slope = gelu_and_slope(inner)
        active_ref[:, begin : begin + step] = active.astype(bf16)
        slope_ref[:, begin : begin + step] = slope.astype(bf16)
    traffic.ship(active_ref, slope_ref)
    traffic.need(down_ref)
    return hidden + (dot(active_ref[...], down_ref[...]) + down_bias)


def feed_backward(traffic, grad, hidden, gain, up_ref, down_ref, normed_ref, active_ref, slope_ref, flat_ref, table,
                  base=0):
    unit, rstd = normalise(hidden)
    branch = grad.astype(bf16)
    put_vector(flat_ref, table.down_bias[0] - base, column_sum(branch.astype(f32)))
    step = 256
    total = None
    normed = normed_ref[...]
    for begin in range(0, FF, step):
        put(flat_ref, table.down_weight[0] - base, D, begin, dot_tn(active_ref[:, begin : begin + step], branch))
        active_grad = dot_nt(branch, down_ref[begin : begin + step, :])
        inner = (active_grad * slope_ref[:, begin : begin + step].astype(f32)).astype(bf16)
        slope_ref[:, begin : begin + step] = inner
        put_vector(flat_ref, table.up_bias[0] - base, column_sum(inner.astype(f32)), begin)
        put(flat_ref, table.up_weight[0] - base, FF, 0, dot_tn(normed, inner), begin)
    traffic.need(up_ref)
    normed_grad = dot_nt(slope_ref[...], up_ref[...])
    put_vector(flat_ref, table.feed_gain[0] - base, column_sum(normed_grad * unit))
    put_vector(flat_ref, table.feed_bias[0] - base, column_sum(normed_grad))
    return grad + normalise_back(normed_grad, unit, rstd, gain)


def vector(vectors_ref, table, place):
    index = vectors_of(table).index(place)
    return vectors_ref[index : index + 1, : place[1][0]]


def block_kinds(count, begin, block, total):
    language = total - LANG
    end = begin + block
    some = (begin < count) | (end > language)
    full = (end <= count) | (count >= language) | (begin >= language)
    return some, full


def masked(scores, count, begin, total):
    place = begin + lax.broadcasted_iota(jnp.int32, (scores.shape[0], 1), 0)
    valid = (place < count) | (place >= total - LANG)
    return jnp.where(valid, scores, negative)


def cross_forward_kernel(traffic, count_ref, tokens_ref, start_ref, vectors_ref, wq_ref, wk_ref, wv_ref, wo_ref,
                         up_ref, down_ref,
                         normedq_ref, query_ref, keyed_ref, mixture_ref, lse_ref, hidden_ref, normed_ref,
                         active_ref, slope_ref, out_ref,
                         acc_ref, max_ref, sum_ref):
    total = tokens_ref.shape[0]
    count = count_ref[0]
    start = start_ref[...]
    unit, rstd = normalise(start)
    normedq_ref[...] = (
        unit * vector(vectors_ref, CROSS, CROSS.query_gain) + vector(vectors_ref, CROSS, CROSS.query_bias)
    ).astype(bf16)
    traffic.ship(normedq_ref)
    query_ref[...] = dot(normedq_ref[...], wq_ref[...]).astype(bf16)
    traffic.ship(query_ref)
    keyed_ref[...] = dot_nt(query_ref[...], wk_ref[...]) * D ** (-0.5)
    traffic.ship(keyed_ref)
    keyed = split(keyed_ref[...] * LOG2E, 1)
    gain = vector(vectors_ref, CROSS, CROSS.context_gain)
    bias = vector(vectors_ref, CROSS, CROSS.context_bias)
    max_ref[...] = jnp.full(max_ref.shape, negative, f32)
    sum_ref[...] = jnp.zeros(sum_ref.shape, f32)
    acc_ref[...] = jnp.zeros(acc_ref.shape, f32)
    block = min(BLOCK, total)

    def visit(index, carry):
        begin = pl.multiple_of(index * block, block)
        some, full = block_kinds(count, begin, block, total)

        @pl.when(some)
        def _():
            contexts, scores = [], []
            for part in range(0, block, PART):
                unit, rstd = normalise(tokens_ref[pl.ds(begin + part, PART), :].astype(f32))
                context = (unit * gain + bias).astype(bf16)
                contexts.append(context)
                raw = dot_nt(jnp.concatenate([context, context], axis=1), keyed)
                scores.append(masked(raw, count, begin + part, total))
            old = max_ref[...]
            newest = old
            for score in scores:
                newest = jnp.maximum(newest, jnp.max(score, axis=0, keepdims=True))
            fade = jnp.exp2(old - newest)
            max_ref[...] = newest
            added, mixed = sum_ref[...] * fade, acc_ref[...] * fade
            for context, score in zip(contexts, scores):
                weights = jnp.exp2(score - newest)
                added += column_sum(weights)
                mixed += dot_tn(context, weights.astype(bf16))
            sum_ref[...] = added
            acc_ref[...] = mixed

        return carry

    lax.fori_loop(0, total // block, visit, 0)
    totals = sum_ref[...]
    lse_ref[...] = max_ref[...] + jnp.log2(totals)
    mixture_ref[...] = acc_ref[...] * (1.0 / totals)
    traffic.ship(lse_ref, mixture_ref)
    traffic.need(wv_ref, wo_ref)
    values = jnp.concatenate([wv_ref[...], wv_ref[...]], axis=0)
    attended = dot_tn(split(mixture_ref[...], 0), values)
    hidden_ref[...] = start + (
        dot(attended.astype(bf16), wo_ref[...]) + vector(vectors_ref, CROSS, CROSS.output_bias)
    )
    traffic.ship(hidden_ref)
    out_ref[...] = feed_forward(
        traffic, hidden_ref[...], vector(vectors_ref, CROSS, CROSS.feed_gain), vector(vectors_ref, CROSS, CROSS.feed_bias),
        up_ref, vector(vectors_ref, CROSS, CROSS.up_bias), down_ref, vector(vectors_ref, CROSS, CROSS.down_bias),
        normed_ref, active_ref, slope_ref,
    )


def cross_forward(count, tokens, start, vectors, wq, wk, wv, wo, up, down):
    outs = [
        shape((LAT, D), bf16), shape((LAT, D), bf16), shape((LAT, C), f32), shape((C, LAT), f32),
        shape((1, LAT), f32), shape((LAT, D), f32), shape((LAT, D), bf16), shape((LAT, FF), bf16),
        shape((LAT, FF), bf16), shape((LAT, D), f32),
    ]
    scratch = [
        pltpu.VMEM((C, LAT), f32), pltpu.VMEM((1, LAT), f32), pltpu.VMEM((1, LAT), f32),
    ]
    return streamed(
        cross_forward_kernel, "cross_forward", outs,
        [count, tokens, start, vectors, wq, wk, wv, wo, up, down], late=range(6, 10), early=range(9), scratch=scratch,
        smem=1, flops=100_000_000_000,
    )


def pair_mask(value, side):
    lane = lax.broadcasted_iota(jnp.int32, (1, LANES), 1)
    keep = (lane < HEAD) if side == 0 else (lane >= HEAD)
    return jnp.where(keep, value, jnp.zeros_like(value))


def latent_kernel(windows, parts, traffic, firsts_ref, hidden_ref, cotangent_ref, vectors_ref, joint_w_ref, merge_ref,
                  up_ref, down_ref, out_ref, grad_ref, *rest):
    windows_refs, rest = rest[:parts], rest[parts:]
    (flat_ref, probs_ref, joint_ref, mixed_ref, after_ref, normedl_ref, normed_ref, active_ref, slope_ref, query_grad_ref, joint_grad_ref) = rest
    gain = vector(vectors_ref, LATENT, LATENT.attend_gain)
    unit, rstd = normalise(hidden_ref[...])
    normedl_ref[...] = (unit * gain + vector(vectors_ref, LATENT, LATENT.attend_bias)).astype(bf16)
    joint_ref[...] = dot(normedl_ref[...], joint_w_ref[...]).astype(bf16)
    scale = HEAD ** (-0.5)
    for pair in range(HEADS // 2):
        lanes = slice(pair * LANES, (pair + 1) * LANES)
        query = joint_ref[:, lanes]
        keys = joint_ref[:, D + pair * LANES : D + (pair + 1) * LANES]
        values = joint_ref[:, 2 * D + pair * LANES : 2 * D + (pair + 1) * LANES]
        mixed = None
        for side in range(2):
            scores = dot_nt(pair_mask(keys, side), query) * (scale * LOG2E)
            weights = jnp.exp2(scores - jnp.max(scores, axis=0, keepdims=True))
            weights = weights * (1.0 / column_sum(weights))
            weights = weights.astype(bf16)
            probs_ref[2 * pair + side] = weights
            part = dot_tn(pair_mask(values, side), weights)
            mixed = part if mixed is None else mixed + part
        mixed_ref[lanes, :] = mixed.astype(bf16)
    traffic.need(merge_ref)
    after_ref[...] = hidden_ref[...] + (
        dot_tn(mixed_ref[...], merge_ref[...]) + vector(vectors_ref, LATENT, LATENT.merge_bias)
    )
    feed_gain = vector(vectors_ref, LATENT, LATENT.feed_gain)
    out_ref[...] = feed_forward(
        traffic, after_ref[...], feed_gain, vector(vectors_ref, LATENT, LATENT.feed_bias), up_ref,
        vector(vectors_ref, LATENT, LATENT.up_bias), down_ref, vector(vectors_ref, LATENT, LATENT.down_bias),
        normed_ref, active_ref, slope_ref,
    ).astype(bf16)

    traffic.ship(out_ref)
    traffic.need(cotangent_ref)
    clear_tail(flat_ref, LATENT_ROWS)
    after_grad = feed_backward(
        traffic, cotangent_ref[...].astype(f32), after_ref[...], feed_gain, up_ref, down_ref, normed_ref, active_ref,
        slope_ref, flat_ref, LATENT,
    )
    branch = after_grad.astype(bf16)
    put(flat_ref, LATENT.merge_weight[0], D, 0, dot(mixed_ref[...], branch))
    put_vector(flat_ref, LATENT.merge_bias[0], column_sum(branch.astype(f32)))
    mixed_grad = dot_nt(branch, merge_ref[...]).astype(bf16)
    for pair in range(HEADS // 2):
        lanes = slice(pair * LANES, (pair + 1) * LANES)
        query = joint_ref[:, lanes]
        keys = joint_ref[:, D + pair * LANES : D + (pair + 1) * LANES]
        values = joint_ref[:, 2 * D + pair * LANES : 2 * D + (pair + 1) * LANES]
        grads = mixed_grad[:, lanes]
        query_part = key_part = value_part = None
        for side in range(2):
            probs = probs_ref[2 * pair + side].astype(f32)
            part = dot(probs.astype(bf16), pair_mask(grads, side))
            value_part = part if side == 0 else value_part + part
            probs_grad = dot_nt(pair_mask(values, side), grads)
            delta = column_sum(probs * probs_grad)
            scores_grad = (probs * (probs_grad - delta)).astype(bf16)
            part = dot(scores_grad, pair_mask(query, side))
            key_part = part if side == 0 else key_part + part
            part = dot_tn(pair_mask(keys, side), scores_grad)
            query_part = part if side == 0 else query_part + part
        query_grad_ref[lanes, :] = query_part * scale
        joint_grad_ref[:, D + pair * LANES : D + (pair + 1) * LANES] = (key_part * scale).astype(bf16)
        joint_grad_ref[:, 2 * D + pair * LANES : 2 * D + (pair + 1) * LANES] = value_part.astype(bf16)
    joint_grad_ref[:, :D] = query_grad_ref[...].T.astype(bf16)
    put(flat_ref, LATENT.joint_weight[0], 3 * D, 0, dot_tn(normedl_ref[...], joint_grad_ref[...]))
    normed_grad = dot_nt(joint_grad_ref[...], joint_w_ref[...])
    put_vector(flat_ref, LATENT.attend_gain[0], column_sum(normed_grad * unit))
    put_vector(flat_ref, LATENT.attend_bias[0], column_sum(normed_grad))
    grad_ref[...] = after_grad + normalise_back(normed_grad, unit, rstd, gain)
    to_windows(flat_ref, firsts_ref, windows_refs, windows.rows, traffic)


def latent_layer(firsts, hidden, cotangent, vectors, joint, merge, up, down, windows, grid):
    outs = [shape((LAT, D), bf16), shape((LAT, D), f32)] + windows.outs(grid.nz)
    scratch = [
        pltpu.VMEM((windows.padded, LANES), f32), pltpu.VMEM((HEADS, LAT, LAT), bf16),
        pltpu.VMEM((LAT, 3 * D), bf16), pltpu.VMEM((D, LAT), bf16), pltpu.VMEM((LAT, D), f32),
        pltpu.VMEM((LAT, D), bf16), pltpu.VMEM((LAT, D), bf16), pltpu.VMEM((LAT, FF), bf16),
        pltpu.VMEM((LAT, FF), bf16), pltpu.VMEM((D, LAT), f32), pltpu.VMEM((LAT, 3 * D), bf16),
    ]
    return streamed(
        functools.partial(latent_kernel, windows, grid.nz), "latent_layer", outs,
        [firsts, hidden, cotangent, vectors, joint, merge, up, down], late=[2], early=[0],
        blocks={2 + c: windows.devices // grid.nz for c in range(grid.nz)}, scratch=scratch, smem=1,
        flops=20_000_000_000, room=14 * 2**20, slots=SLOTS,
    )


SPLIT = CROSS.output_weight[0] // TILE * TILE


def cross_feed_kernel(windows, parts, traffic, firsts_ref, grad_ref, vectors_ref, wv_ref, wo_ref, up_ref, down_ref,
                      mixture_ref, hidden_ref, normed_ref, active_ref, saved_slope_ref,
                      hidden_grad_ref, valued_ref, delta_ref, value_grad_ref, *rest):
    windows_refs = rest[:parts]
    flat_ref, slope_ref = rest[parts:]
    clear_tail(flat_ref, CROSS_ROWS)
    slope_ref[...] = saved_slope_ref[...]
    hidden_grad = feed_backward(
        traffic, grad_ref[...], hidden_ref[...], vector(vectors_ref, CROSS, CROSS.feed_gain), up_ref, down_ref, normed_ref,
        active_ref, slope_ref, flat_ref, CROSS,
    )
    hidden_grad_ref[...] = hidden_grad
    traffic.ship(hidden_grad_ref)
    traffic.need(wv_ref, wo_ref, mixture_ref)
    branch = hidden_grad.astype(bf16)
    values = jnp.concatenate([wv_ref[...], wv_ref[...]], axis=0)
    mixture = split(mixture_ref[...], 0)
    attended = dot_tn(mixture, values)
    put(flat_ref, CROSS.output_weight[0], D, 0, dot_tn(attended.astype(bf16), branch))
    put_vector(flat_ref, CROSS.output_bias[0], column_sum(branch.astype(f32)))
    attended_grad = dot_nt(branch, wo_ref[...]).astype(bf16)
    both = dot(mixture, attended_grad)
    value_grad_ref[...] = both[:C] + both[C:]
    put(flat_ref, CROSS.value_weight[0], D, 0, value_grad_ref[...])
    valued = dot_nt(attended_grad, wv_ref[...])
    valued_ref[...] = split(valued, 1)
    delta_ref[...] = column_sum((attended_grad.astype(f32) * attended).T)
    flat_ref[:SPLIT, :] = jnp.zeros((SPLIT, LANES), f32)
    to_windows(flat_ref, firsts_ref, windows_refs, windows.rows, traffic)


def cross_feed(firsts, grad, vectors, wv, wo, up, down, mixture, hidden, normed, active, slope, windows, grid):
    outs = [
        shape((LAT, D), f32), shape((LAT, 2 * C), bf16), shape((1, LAT), f32), shape((C, D), f32),
    ] + windows.outs(grid.nz)
    return streamed(
        functools.partial(cross_feed_kernel, windows, grid.nz), "cross_feed", outs,
        [firsts, grad, vectors, wv, wo, up, down, mixture, hidden, normed, active, slope], late=[5, 3, 4, 7],
        early=[0], blocks={4 + c: windows.devices // grid.nz for c in range(grid.nz)},
        scratch=[pltpu.VMEM((windows.padded, LANES), f32), pltpu.VMEM((LAT, FF), bf16)], smem=1,
        flops=80_000_000_000,
    )


def attend_block(offset, blocks, count_ref, tokens_ref, valued_ref, delta_ref, vectors_ref, keyed_ref, lse_ref,
                 token_grad_ref, acc_ref, gains_ref, doubled_ref, paired_ref):
    block = tokens_ref.shape[0]
    begin = (pl.program_id(0) + offset) * block
    total = blocks * block
    count = count_ref[0]
    some, full = block_kinds(count, begin, block, total)

    @pl.when(pl.program_id(0) == 0)
    def _():
        doubled_ref[...] = split(keyed_ref[...] * LOG2E, 1)
        paired_ref[...] = split(keyed_ref[...], 1)

    @pl.when(some)
    def _():
        gain = vector(vectors_ref, CROSS, CROSS.context_gain)
        bias = vector(vectors_ref, CROSS, CROSS.context_bias)
        for part in range(0, block, PART):
            rows = slice(part, part + PART)
            unit, rstd = normalise(tokens_ref[rows, :].astype(f32))
            context = (unit * gain + bias).astype(bf16)
            twice = jnp.concatenate([context, context], axis=1)
            scores = masked(dot_nt(twice, doubled_ref[...]), count, begin + part, total)
            probs = jnp.exp2(scores - lse_ref[...])
            scores_grad = (probs * (dot_nt(twice, valued_ref[...]) - delta_ref[...])).astype(bf16)
            acc_ref[...] += dot_tn(context, scores_grad)
            wide = dot(probs.astype(bf16), valued_ref[...]) + dot(scores_grad, paired_ref[...])
            context_grad = wide[:, :C] + wide[:, C:]
            gains_ref[0:1, :] += column_sum(context_grad * unit)
            gains_ref[1:2, :] += column_sum(context_grad)
            token_grad_ref[rows, :] = normalise_back(context_grad, unit, rstd, gain)

    @pl.when(jnp.logical_not(some))
    def _():
        token_grad_ref[...] = jnp.zeros(token_grad_ref.shape, f32)


def attend_first_kernel(blocks, count_ref, tokens_ref, valued_ref, delta_ref, vectors_ref, keyed_ref, lse_ref,
                        token_grad_ref, acc_ref, gains_ref, doubled_ref, paired_ref):
    @pl.when(pl.program_id(0) == 0)
    def _():
        acc_ref[...] = jnp.zeros(acc_ref.shape, f32)
        gains_ref[...] = jnp.zeros(gains_ref.shape, f32)

    attend_block(0, blocks, count_ref, tokens_ref, valued_ref, delta_ref, vectors_ref, keyed_ref, lse_ref,
                 token_grad_ref, acc_ref, gains_ref, doubled_ref, paired_ref)


def attend_second_kernel(offset, blocks, rows, parts, firsts_ref, count_ref, task_ref, tokens_ref, valued_ref,
                         delta_ref, vectors_ref, keyed_ref, lse_ref, acc_before_ref, gains_before_ref, hidden_grad_ref,
                         value_grad_ref, start_ref, wq_ref, wk_ref, normedq_ref, query_ref, kept_ref,
                         token_grad_ref, *rest):
    windows_refs = rest[:parts]
    flat_ref, acc_ref, gains_ref, doubled_ref, paired_ref = rest[parts:]

    @pl.when(pl.program_id(0) == 0)
    def _():
        acc_ref[...] = acc_before_ref[...]
        gains_ref[...] = gains_before_ref[...]

    attend_block(offset, blocks, count_ref, tokens_ref, valued_ref, delta_ref, vectors_ref, keyed_ref, lse_ref,
                 token_grad_ref, acc_ref, gains_ref, doubled_ref, paired_ref)

    @pl.when(pl.program_id(0) == pl.num_programs(0) - 1)
    def _():
        pulled = split(acc_ref[...] * D ** (-0.5), 0)
        both = dot(pulled, query_ref[...])
        put(flat_ref, CROSS.key_weight[0], D, 0, both[:C] + both[C:])
        put(flat_ref, CROSS.value_weight[0], D, 0, value_grad_ref[...])
        put_vector(flat_ref, CROSS.context_gain[0], gains_ref[0:1, :])
        put_vector(flat_ref, CROSS.context_bias[0], gains_ref[1:2, :])
        query_grad = dot_tn(pulled, jnp.concatenate([wk_ref[...], wk_ref[...]], axis=0)).astype(bf16)
        put(flat_ref, CROSS.query_weight[0], D, 0, dot_tn(normedq_ref[...], query_grad))
        normed_grad = dot_nt(query_grad, wq_ref[...])
        unit, rstd = normalise(start_ref[...])
        put_vector(flat_ref, CROSS.query_gain[0], column_sum(normed_grad * unit))
        put_vector(flat_ref, CROSS.query_bias[0], column_sum(normed_grad))
        gain = vector(vectors_ref, CROSS, CROSS.query_gain)
        start_grad = hidden_grad_ref[...] + normalise_back(normed_grad, unit, rstd, gain)
        put(flat_ref, CROSS.latents[0], D, 0, start_grad)
        first, unused = CROSS.task_table
        chunks = D // LANES
        flat_ref[first : first + NTASK * chunks, :] = jnp.zeros((NTASK * chunks, LANES), f32)
        sums = column_sum(start_grad)
        base = first + task_ref[0] * chunks
        for chunk in range(chunks):
            flat_ref[pl.ds(base + chunk, 1), :] = sums[:, chunk * LANES : (chunk + 1) * LANES]
        clear_tail(flat_ref, SPLIT)
        to_windows(flat_ref, firsts_ref, windows_refs, rows)


def attend_scratch():
    return [pltpu.VMEM((LAT, 2 * C), bf16), pltpu.VMEM((LAT, 2 * C), bf16)]


def attend_first(count, tokens, valued, delta, vectors, keyed, lse):
    total = tokens.shape[0]
    block = min(BLOCK, total)
    blocks = total // block
    whole = [valued, delta, vectors, keyed, lse]
    row = lambda i: (i, 0)
    outs = [shape((total, C), f32), shape((C, LAT), f32), shape((8, C), f32)]
    scratch = attend_scratch()
    return pl.pallas_call(
        functools.partial(attend_first_kernel, blocks),
        name="attend_first",
        grid=(max(blocks // 2, 1),),
        out_shape=outs,
        in_specs=[pl.BlockSpec(memory_space=pltpu.SMEM), pl.BlockSpec((block, C), row)] + vmem_specs(len(whole)),
        out_specs=[pl.BlockSpec((block, C), row)] + vmem_specs(2),
        scratch_shapes=scratch,
        compiler_params=pltpu.CompilerParams(vmem_limit_bytes=vmem_limit(*whole, *scratch)),
        cost_estimate=pl.CostEstimate(flops=100_000_000_000, bytes_accessed=1, transcendentals=0),
    )(count, tokens, *whole)


def attend_second(firsts, count, task, tokens, valued, delta, vectors, keyed, lse, acc, gains, hidden_grad, value_grad,
                  start, wq, wk, normedq, query, token_grad, windows, grid):
    total = tokens.shape[0]
    block = min(BLOCK, total)
    blocks = total // block
    offset = max(blocks // 2, 1)
    rows = windows.quarter(grid.nx)
    last = grid.ny * grid.nz - 1
    assert SPLIT <= windows.first[last + 1] and blocks > offset
    flat_rows = max(windows.first[last] + rows * grid.nx, SPLIT + TILE)
    whole = [valued, delta, vectors, keyed, lse, acc, gains, hidden_grad, value_grad, start, wq, wk, normedq, query]
    half = windows.devices // grid.nz // grid.ny * rows
    small = [shape((half * depths, LANES), bf16) for c in range(grid.nz) for depths in halves(grid)]
    row = lambda i: (i + offset, 0)
    scratch = [
        pltpu.VMEM((flat_rows, LANES), f32), pltpu.VMEM((C, LAT), f32),
        pltpu.VMEM((8, C), f32), *attend_scratch(),
    ]
    return pl.pallas_call(
        functools.partial(attend_second_kernel, offset, blocks, rows, len(small)),
        name="attend_second",
        grid=(blocks - offset,),
        out_shape=[shape((total, C), f32)] + small,
        in_specs=[pl.BlockSpec(memory_space=pltpu.SMEM)] * 3
        + [pl.BlockSpec((block, C), row)]
        + vmem_specs(len(whole))
        + [pl.BlockSpec(memory_space=pl.ANY)],
        out_specs=[pl.BlockSpec((block, C), row)] + vmem_specs(len(small)),
        scratch_shapes=scratch,
        input_output_aliases={4 + len(whole): 0},
        compiler_params=pltpu.CompilerParams(vmem_limit_bytes=vmem_limit(*whole, *small, *scratch)),
        cost_estimate=pl.CostEstimate(flops=100_000_000_000, bytes_accessed=1, transcendentals=0),
    )(firsts, count, task, tokens, *whole, token_grad)


def body(tokens, task_id, valid_count, cross_params, latent_params, out_grad):
    grid = Grid()
    devices = grid.nx * grid.ny * grid.nz
    cw = Windows(cross_params.shape[0] * devices, devices)
    lw = Windows(latent_params.shape[0] * devices, devices)
    gathered_from = grid.owners(gather_places(grid))
    scattered_to = grid.owners(grid.order())
    tokens = tokens[0]

    cross_window, latent_window = place([cross_params, latent_params], [cw, lw], grid.index)
    cross_column = gather_depth(cross_window, grid)
    latent_column = gather_depth(after(latent_window, *cross_column[1:]), grid)
    pieces = gather_plane_second(*gather_plane_first(cross_column, grid), grid)
    for piece in pieces:
        piece[0] = after(piece[0], *latent_column[1:])
        piece[1:] = [after(value, *latent_column[1:]) for value in piece[1:]]
    cross_all = sum(gather_core(*pieces, grid), [])
    latent_column = [after(value, pieces[0][-1], pieces[1][-1]) for value in latent_column]
    lows, highs = gather_plane_first(latent_column, grid)
    vectors, start, wq, wk, wv, wo, up, down = unpack_cross(cw.firsts(gathered_from), cross_all, task_id, cw)
    lows[0], highs[0] = after(lows[0], vectors), after(highs[0], vectors)
    first, second = gather_plane_second(lows, highs, grid)
    normedq, query, keyed, mixture, lse, hidden, normed, active, slope, result = cross_forward(
        valid_count, tokens, after(start, first[0], second[0]), vectors, wq, wk, wv, wo, up, down
    )
    first[1:] = [after(value, result) for value in first[1:]]
    second[1:] = [after(value, result) for value in second[1:]]
    latent_all = sum(gather_core(first, second, grid), [])
    latent_weights = unpack_latent(lw.firsts(gathered_from), latent_all, lw)
    latents_out, result_grad, *latent_parts = latent_layer(
        lw.firsts(scattered_to), result, out_grad[0], *latent_weights, lw, grid
    )

    latent_lows, latent_highs = reduce_first(reduce_core(latent_parts, grid), lw.rows, grid)
    hidden_grad, valued, delta, value_grad, *later_parts = cross_feed(
        cw.firsts(scattered_to), after(result_grad, latent_lows[0][0]), vectors, wv, wo, up, down, mixture, hidden,
        normed, active, slope, cw, grid,
    )
    latent_lows[0] = (after(latent_lows[0][0], delta), 0)
    latent_first, latent_second = reduce_second(latent_lows, latent_highs, lw.rows, grid)
    later_group = reduce_core(later_parts, grid)
    token_grad, acc, gains = attend_first(
        valid_count, tokens, valued, after(delta, latent_first[0][0]), vectors, keyed, lse
    )
    latent_first[0] = (after(latent_first[0][0], acc), 0)
    latent_column = reduce_depth(latent_first, latent_second, lw.rows, grid)
    later_group[0] = (after(later_group[0][0], latent_column[0]), 0)
    later_lows, later_highs = reduce_first(later_group, cw.rows, grid)
    owner, quarter = quarter_owners(grid)
    small_rows = cw.quarter(grid.nx)
    token_grad, *early_parts = attend_second(
        cw.firsts(owner) + quarter * small_rows, valid_count, task_id, tokens, valued, delta, vectors, keyed, lse,
        after(acc, later_lows[0][0]), gains, hidden_grad, value_grad, start, wq, wk, normedq, query, token_grad, cw,
        grid,
    )
    latent_column[0] = after(latent_column[0], early_parts[0])
    latent_share = extract(latent_column, [], lw, grid)
    later_lows[0] = (after(later_lows[0][0], latent_share), 0)
    early_parts = [after(part, latent_share) for part in early_parts]
    early_groups = [reduce_core(early_parts[half::2], grid) for half in range(2)]
    later_first, later_second, early_lows, early_highs = reduce_second_and_first(
        later_lows, later_highs, cw.rows, early_groups, small_rows, grid
    )
    early_first, early_second = reduce_second(early_lows, early_highs, small_rows, grid)
    column = reduce_depth_both(later_first, later_second, cw.rows, early_first, early_second, small_rows, grid)
    quarters = collect_quarters(column, cw.rows, small_rows, grid)
    return (latents_out[None], token_grad[None], extract(column, quarters, cw, grid), latent_share)


def solution(mesh):
    return jax.shard_map(
        body,
        mesh=mesh,
        in_specs=(
            P(AXES, None, None),
            P(AXES),
            P(AXES),
            P(AXES),
            P(AXES),
            P(AXES, None, None),
        ),
        out_specs=(
            P(AXES, None, None),
            P(AXES, None, None),
            P(AXES),
            P(AXES),
        ),
        check_vma=False,
    )
```

```python
import functools
import math
import types

import jax
import jax.numpy as jnp
from jax import lax
from jax.experimental import pallas as pl
from jax.experimental.pallas import tpu as pltpu
from jax.sharding import PartitionSpec as P

D = 512
FF = 2048
C = 128
LAT = 512
HEADS = 8
HEAD = 64
NTASK = 18
LANG = 77
LANES = 128
TILE = 16
UNIT = TILE * LANES
BLOCK = 2048
PART = 512
AXES = ("gx", "gy", "gz")

epsilon = 1e-05
negative = -1e30
LOG2E = math.log2(math.e)
bf16 = jnp.bfloat16
f32 = jnp.float32
VMEM_LIMIT = 60 * 1024 * 1024
ROOM = 6 * 1024 * 1024
SLOTS = 8


def layout_of(**shapes):
    table = {}
    row = 0
    for name, dims in shapes.items():
        table[name] = (row, dims)
        row += math.prod(dims) // LANES
    return types.SimpleNamespace(**table), row


CROSS, CROSS_ROWS = layout_of(
    latents=(LAT, D),
    task_table=(NTASK, D),
    query_gain=(D,),
    query_bias=(D,),
    context_gain=(C,),
    context_bias=(C,),
    query_weight=(D, D),
    key_weight=(C, D),
    value_weight=(C, D),
    output_weight=(D, D),
    output_bias=(D,),
    feed_gain=(D,),
    feed_bias=(D,),
    up_weight=(D, FF),
    up_bias=(FF,),
    down_weight=(FF, D),
    down_bias=(D,),
)
LATENT, LATENT_ROWS = layout_of(
    attend_gain=(D,),
    attend_bias=(D,),
    joint_weight=(D, 3 * D),
    merge_weight=(D, D),
    merge_bias=(D,),
    feed_gain=(D,),
    feed_bias=(D,),
    up_weight=(D, FF),
    up_bias=(FF,),
    down_weight=(FF, D),
    down_bias=(D,),
)


def vectors_of(table):
    return [place for place in vars(table).values() if len(place[1]) == 1]


class Windows:
    def __init__(self, total, devices):
        self.total = total
        self.devices = devices
        self.shard = total // devices
        starts = [self.shard * d for d in range(devices)]
        self.first = [s // UNIT * TILE for s in starts]
        self.phase = [s % UNIT for s in starts]
        self.rows = max(-(-(p + self.shard) // UNIT) * TILE for p in self.phase)
        self.padded = max(f + self.rows for f in self.first)
        self.full = -(-total // UNIT) * TILE
        self.shard_rows = -(-self.shard // (8 * LANES)) * 8

    def outs(self, parts):
        return [shape((self.devices // parts * self.rows, LANES), bf16)] * parts

    def firsts(self, owners):
        return self.shard * owners // UNIT * TILE

    def quarter(self, parts):
        return -(-self.rows // (parts * TILE)) * TILE


def dot(left, right):
    return jnp.dot(left, right, preferred_element_type=f32)


def dot_nt(left, right):
    return lax.dot_general(left, right, (((1,), (1,)), ((), ())), preferred_element_type=f32)


def dot_tn(left, right):
    return lax.dot_general(left, right, (((0,), (0,)), ((), ())), preferred_element_type=f32)


def split(value, axis):
    high = value.astype(bf16)
    low = (value - high.astype(f32)).astype(bf16)
    return jnp.concatenate([high, low], axis=axis)


def normalise(value):
    centred = value - jnp.mean(value, axis=-1, keepdims=True)
    rstd = lax.rsqrt(jnp.mean(centred * centred, axis=-1, keepdims=True) + epsilon)
    return centred * rstd, rstd


def normalise_back(grad, unit, rstd, gain):
    inner = grad * gain
    return rstd * (
        inner
        - jnp.mean(inner, axis=-1, keepdims=True)
        - unit * jnp.mean(inner * unit, axis=-1, keepdims=True)
    )


def column_sum(value):
    return jnp.sum(value, axis=0, keepdims=True)


def vmem_specs(count):
    return [pl.BlockSpec(memory_space=pltpu.VMEM)] * count


def shape(dims, dtype):
    return jax.ShapeDtypeStruct(dims, dtype)


def bytes_of(value):
    return math.prod(value.shape) * jnp.dtype(value.dtype).itemsize


def vmem_limit(*values):
    return min(sum(map(bytes_of, values)) + 16 * 2**20, VMEM_LIMIT)


def call(kernel, name, outs, inputs, scratch=(), smem=0, flops=0, moved=0, alone=True):
    specs = [pl.BlockSpec(memory_space=pltpu.SMEM)] * smem + vmem_specs(len(inputs) - smem)
    limit = VMEM_LIMIT if alone else vmem_limit(*inputs, *jax.tree.leaves(outs), *scratch)
    return pl.pallas_call(
        kernel,
        name=name,
        out_shape=outs,
        in_specs=specs,
        out_specs=jax.tree.map(lambda _: pl.BlockSpec(memory_space=pltpu.VMEM), outs),
        scratch_shapes=list(scratch),
        compiler_params=pltpu.CompilerParams(vmem_limit_bytes=limit),
        cost_estimate=pl.CostEstimate(flops=flops, bytes_accessed=moved, transcendentals=0),
    )(*inputs)


class Traffic:
    def __init__(self):
        self.loads, self.stores, self.blocks, self.begun = {}, {}, {}, []

    def need(self, *refs):
        for ref in refs:
            copy = self.loads.pop(id(ref), None)
            if copy is not None:
                copy.wait()

    def ship(self, *refs):
        for ref in refs:
            copy = self.stores.pop(id(ref), None)
            if copy is not None:
                copy.start()
                self.begun.append(copy)

    def block(self, ref, number, rows):
        target, sem = self.blocks[id(ref)]
        slot = pl.multiple_of(number % (ref.shape[0] // rows) * rows, TILE)
        part = pl.multiple_of(number * rows, TILE)
        return pltpu.make_async_copy(ref.at[pl.ds(slot, rows)], target.at[pl.ds(part, rows)], sem.at[number])


def streamed(kernel, name, outs, inputs, late=(), early=(), blocks=None, scratch=(), smem=0, flops=0, room=0, slots=None):
    blocks = blocks or {}
    shipped = list(early) + list(blocks)
    vmem, hbm = pl.BlockSpec(memory_space=pltpu.VMEM), pl.BlockSpec(memory_space=pltpu.HBM)
    held = [pltpu.VMEM(inputs[i].shape, inputs[i].dtype) for i in late]
    held += [pltpu.VMEM(outs[i].shape, outs[i].dtype) for i in early]
    held += [pltpu.VMEM((min(slots or number, number) * outs[i].shape[0] // number, LANES), bf16) for i, number in blocks.items()]
    sems = [pltpu.SemaphoreType.DMA((max(len(late), 1),)), pltpu.SemaphoreType.DMA((max(len(early), 1),))]
    sems += [pltpu.SemaphoreType.DMA((number,)) for number in blocks.values()]

    def body(*refs):
        takes, gives = list(refs[: len(inputs)]), list(refs[len(inputs) : len(inputs) + len(outs)])
        rest = refs[len(inputs) + len(outs) :]
        buffers, rest = rest[: len(held)], rest[len(held) :]
        load_sem, store_sem = rest[:2]
        block_sems, rest = rest[2 : len(sems)], rest[len(sems) :]
        traffic = Traffic()
        for k, i in enumerate(late):
            copy = pltpu.make_async_copy(takes[i], buffers[k], load_sem.at[k])
            copy.start()
            traffic.loads[id(buffers[k])] = copy
            takes[i] = buffers[k]
        for k, i in enumerate(shipped):
            buffer = buffers[len(late) + k]
            if k < len(early):
                traffic.stores[id(buffer)] = pltpu.make_async_copy(buffer, gives[i], store_sem.at[k])
            else:
                traffic.blocks[id(buffer)] = (gives[i], block_sems[k - len(early)])
            gives[i] = buffer
        kernel(traffic, *takes, *gives, *rest)
        assert not traffic.loads and not traffic.stores
        for copy in traffic.begun:
            copy.wait()

    return pl.pallas_call(
        body,
        name=name,
        out_shape=outs,
        in_specs=[pl.BlockSpec(memory_space=pltpu.SMEM)] * smem
        + [hbm if i in late else vmem for i in range(smem, len(inputs))],
        out_specs=[hbm if i in shipped else vmem for i in range(len(outs))],
        scratch_shapes=held + sems + list(scratch),
        compiler_params=pltpu.CompilerParams(vmem_limit_bytes=VMEM_LIMIT - room),
        cost_estimate=pl.CostEstimate(flops=flops, bytes_accessed=1, transcendentals=0),
    )(*inputs)


def shifted(value, shift):
    down, across = shift // LANES, shift % LANES
    turned = pltpu.roll(value, across, axis=1)
    above = pltpu.roll(turned, 1, axis=0)
    lane = lax.broadcasted_iota(jnp.int32, value.shape, 1)
    return pltpu.roll(jnp.where(lane < across, above, turned), down, axis=0)


def place_kernel(shifts_ref, shards_ref, *out_refs):
    begin = 0
    for number, out_ref in enumerate(out_refs):
        rows = out_ref.shape[0]
        value = shards_ref[begin : begin + rows, :].astype(f32)
        out_ref[...] = shifted(value, shifts_ref[number]).astype(bf16)
        begin += rows


def place(shards, windows, index):
    padded = [
        jnp.pad(shard, (0, w.rows * LANES - w.shard)) for shard, w in zip(shards, windows)
    ]
    together = jnp.concatenate(padded).reshape(-1, LANES)
    shifts = jnp.stack([(w.shard * index) % UNIT for w in windows])
    outs = [shape((w.rows, LANES), bf16) for w in windows]
    return call(place_kernel, "place", outs, [shifts, together], smem=1, alone=False)


def extract_kernel(count, shift_ref, *refs):
    out_ref, total_ref = refs[-2:]
    rows = total_ref.shape[0]
    value = refs[0][:rows, :].astype(f32)
    for ref in refs[1:count]:
        value += ref[:rows, :].astype(f32)
    total_ref[...] = value
    begin = 0
    for ref in refs[count:-2]:
        size = min(ref.shape[0], rows - begin)
        if size > 0:
            total_ref[begin : begin + size, :] += ref[:size, :].astype(f32)
        begin += ref.shape[0]
    down, across = shift_ref[0] // LANES, shift_ref[0] % LANES
    turned = pltpu.roll(total_ref[...], lax.rem(LANES - across, LANES), axis=1)
    below = pltpu.roll(turned, rows - 1, axis=0)
    lane = lax.broadcasted_iota(jnp.int32, (rows, LANES), 1)
    merged = pltpu.roll(
        jnp.where(lane < LANES - across, turned, below), lax.rem(rows - down, rows), axis=0
    )
    out_ref[...] = merged[: out_ref.shape[0]]


def extract(parts, quarters, windows, grid):
    shift = (windows.shard * grid.index) % UNIT
    rows = min(windows.shard_rows, windows.rows)
    found = call(
        functools.partial(extract_kernel, len(parts)), "extract", shape((rows, LANES), f32),
        [shift.reshape(1), *parts, *quarters], scratch=[pltpu.VMEM((windows.rows, LANES), f32)], smem=1,
        alone=False,
    )
    return found.reshape(-1)[: windows.shard]


class Grid:
    def __init__(self):
        self.nx, self.ny, self.nz = (lax.axis_size(axis) for axis in AXES)
        self.nl = 2 if self.nx % 2 == 0 else 1
        self.nh = self.nx // self.nl
        self.index = lax.axis_index(AXES)

    def order(self):
        return [
            (c, h, l, y)
            for c in range(self.nz)
            for h in range(self.nh)
            for l in range(self.nl)
            for y in range(self.ny)
        ]

    def owners(self, places):
        gx, gy, gz = (lax.axis_index(axis) for axis in AXES)
        c, h, l, y = (jnp.array(column, jnp.int32) for column in zip(*places))
        high = (gx // self.nl + h) % self.nh
        low = (gx % self.nl + l) % self.nl
        return ((high * self.nl + low) * self.ny + (gy + y) % self.ny) * self.nz + (gz + c) % self.nz

    def along_core(self, value, step):
        return lax.ppermute(value, AXES[2], [(i, (i + step) % self.nz) for i in range(self.nz)])

    def along_depth(self, value, step):
        return lax.ppermute(value, AXES[1], [(i, (i + step) % self.ny) for i in range(self.ny)])

    def along_low(self, value, step):
        nl = self.nl
        return lax.ppermute(
            value, AXES[0], [(i, i // nl * nl + (i + step) % nl) for i in range(self.nx)]
        )

    def along_high(self, value, step):
        nl = self.nl
        return lax.ppermute(value, AXES[0], [(i, (i + step * nl) % self.nx) for i in range(self.nx)])


def combine_kernel(groups, picks, *refs):
    starts = [sum(len(bases) for rows, bases in groups[:g]) for g in range(len(groups))]
    outputs = refs[sum(len(bases) for rows, bases in groups) :]
    for output, pick in zip(outputs, picks):
        row = 0
        for g, block in pick:
            rows, bases = groups[g]
            total = None
            for i, base in enumerate(bases):
                begin = base + block * rows
                part = refs[starts[g] + i][begin : begin + rows, :].astype(f32)
                total = part if total is None else total + part
            output[row : row + rows, :] = total.astype(bf16)
            row += rows


def combine(name, groups, picks):
    inputs = [array for rows, sources in groups for array, base in sources]
    kinds = tuple((rows, tuple(base for array, base in sources)) for rows, sources in groups)
    sizes = [sum(groups[g][0] for g, block in pick) for pick in picks]
    outs = [shape((size, LANES), bf16) for size in sizes]
    moved = 6 * LANES * sum(sizes)
    return call(
        functools.partial(combine_kernel, kinds, picks), name, outs, inputs, flops=moved, moved=moved, alone=False
    )


def reduce_core(parts, grid):
    return [(parts[0], 0)] + [(grid.along_core(parts[c], c), 0) for c in range(1, grid.nz)]


def first_picks(grid, g):
    nh, nl, ny = grid.nh, grid.nl, grid.ny
    half = ny // 2
    block = lambda h, l, y: (g, (h * nl + l) * ny + y)
    lows = [[block(h, l, y) for h in range(nh) for y in range(half)] for l in range(nl)]
    highs = [[block(h, l, y) for l in range(nl) for y in range(half, ny)] for h in range(nh)]
    return lows, highs


def halves(grid):
    return [grid.ny // 2, grid.ny - grid.ny // 2]


def half_order(grid):
    half = grid.ny // 2
    places = []
    for c in range(grid.nz):
        for depths in (range(half), range(half, grid.ny)):
            places += [(c, h, l, y) for h in range(grid.nh) for l in range(grid.nl) for y in depths]
    return places


def half_first_picks(grid, first_group, second_group):
    nh, nl = grid.nh, grid.nl
    half, rest = halves(grid)
    lows = [[(first_group, (h * nl + l) * half + y) for h in range(nh) for y in range(half)] for l in range(nl)]
    highs = [[(second_group, (h * nl + l) * rest + y) for l in range(nl) for y in range(rest)] for h in range(nh)]
    return lows, highs


def second_picks(grid, low_group, high_group):
    half = grid.ny // 2
    rest = grid.ny - half
    highs = [[(low_group, h * half + y) for y in range(half)] for h in range(grid.nh)]
    lows = [[(high_group, l * rest + y) for y in range(rest)] for l in range(grid.nl)]
    return highs, lows


def depth_picks(grid, first_group, second_group):
    half = grid.ny // 2
    return [(first_group, y) for y in range(half)] + [(second_group, y) for y in range(grid.ny - half)]


def send_low(arrays, grid):
    return [grid.along_low(array, l + 1) for l, array in enumerate(arrays)]


def send_high(arrays, grid):
    return [grid.along_high(array, h + 1) for h, array in enumerate(arrays)]


def send_depth(arrays, grid):
    return [grid.along_depth(array, y + 1) for y, array in enumerate(arrays)]


def at(arrays, base=0):
    return [(array, base) for array in arrays]


def reduce_first(group, rows, grid):
    lows, highs = first_picks(grid, 0)
    outs = combine("plane_first", [(rows, group)], lows + highs)
    keep_low, keep_high = outs[0], outs[grid.nl]
    return (
        at([keep_low] + send_low(outs[1 : grid.nl], grid)),
        at([keep_high] + send_high(outs[grid.nl + 1 :], grid)),
    )


def reduce_second(lows, highs, rows, grid):
    to_high, to_low = second_picks(grid, 0, 1)
    outs = combine("plane_second", [(rows, lows), (rows, highs)], to_high + to_low)
    keep_first, keep_second = outs[0], outs[grid.nh]
    return (
        at([keep_first] + send_high(outs[1 : grid.nh], grid)),
        at([keep_second] + send_low(outs[grid.nh + 1 :], grid)),
    )


def reduce_depth(first, second, rows, grid):
    outs = combine("depth", [(rows, first), (rows, second)], [[pick] for pick in depth_picks(grid, 0, 1)])
    return [outs[0]] + send_depth(outs[1:], grid)


def reduce_second_and_first(lows, highs, rows, small_groups, small_rows, grid):
    to_high, to_low = second_picks(grid, 0, 1)
    small_low, small_high = half_first_picks(grid, 2, 3)
    nh, nl, half = grid.nh, grid.nl, grid.ny // 2
    picks = [to_high[0], to_low[0], small_low[0], small_high[0]]
    picks += [to_high[h] + small_high[h] for h in range(1, nh)]
    picks += [to_low[l] + small_low[l] for l in range(1, nl)]
    outs = combine("second_and_first", [(rows, lows), (rows, highs)] + [(small_rows, group) for group in small_groups], picks)
    keep_first, keep_second, keep_low, keep_high = outs[:4]
    high = send_high(outs[4 : 3 + nh], grid)
    low = send_low(outs[3 + nh :], grid)
    first, second = at([keep_first]) + at(high), at([keep_second]) + at(low)
    lows = at([keep_low]) + at(low, (grid.ny - half) * rows)
    highs = at([keep_high]) + at(high, half * rows)
    return first, second, lows, highs


def reduce_depth_both(first, second, rows, small_first, small_second, small_rows, grid):
    groups = [(rows, first), (rows, second), (small_rows, small_first), (small_rows, small_second)]
    picks = [list(pair) for pair in zip(depth_picks(grid, 0, 1), depth_picks(grid, 2, 3))]
    outs = combine("depth_both", groups, picks)
    return [outs[0]] + send_depth(outs[1:], grid)


def quarter_owners(grid):
    gx, gy, gz = (lax.axis_index(axis) for axis in AXES)
    c, h, l, y = (jnp.array(column, jnp.int32) for column in zip(*half_order(grid)))
    quarter = (gx // grid.nl + h) % grid.nh * grid.nl + (gx % grid.nl + l) % grid.nl
    return (gy + y) % grid.ny * grid.nz + (gz + c) % grid.nz, quarter


def collect_quarters(parts, base, rows, grid):
    (own,) = combine("quarter", [(rows, at(parts, base))], [[(0, 0)]])
    zero = jnp.zeros_like(own)
    first = jnp.where(lax.axis_index(AXES[0]) == 0, own, zero)
    return [first] + [lax.ppermute(own, AXES[0], [(x, 0)]) for x in range(1, grid.nx)]


def gather_depth(window, grid):
    return [window] + [grid.along_depth(window, -y) for y in range(1, grid.ny)]


def gather_plane_first(column, grid):
    half = grid.ny // 2
    first, second = jnp.concatenate(column[:half]), jnp.concatenate(column[half:])
    lows = [first] + [grid.along_low(first, -l) for l in range(1, grid.nl)]
    highs = [second] + [grid.along_high(second, -h) for h in range(1, grid.nh)]
    return lows, highs


def gather_plane_second(lows, highs, grid):
    first, second = jnp.concatenate(lows), jnp.concatenate(highs)
    return (
        [first] + [grid.along_high(first, -h) for h in range(1, grid.nh)],
        [second] + [grid.along_low(second, -l) for l in range(1, grid.nl)],
    )


def gather_core(first, second, grid):
    pieces = first + second
    return [pieces] + [[grid.along_core(piece, -c) for piece in pieces] for c in range(1, grid.nz)]


def gather_places(grid):
    half = grid.ny // 2
    places = []
    for c in range(grid.nz):
        for h in range(grid.nh):
            places += [(c, h, l, y) for l in range(grid.nl) for y in range(half)]
        for l in range(grid.nl):
            places += [(c, h, l, y) for h in range(grid.nh) for y in range(half, grid.ny)]
    return places


def after(value, *others):
    return lax.optimization_barrier((value, *others))[0]


def assemble(firsts_ref, gathered_refs, flat_ref, windows):
    rows = windows.rows
    inner = max(windows.shard // UNIT - 1, 0) * TILE
    after = TILE + inner

    def clear(place, carry):
        first = pl.multiple_of(firsts_ref[place], TILE)
        flat_ref[pl.ds(first, TILE), :] = jnp.zeros((TILE, LANES), f32)
        flat_ref[pl.ds(first + after, rows - after), :] = jnp.zeros((rows - after, LANES), f32)
        return carry

    lax.fori_loop(0, windows.devices, clear, 0)
    place = 0
    for gathered_ref in gathered_refs:
        blocks = gathered_ref.shape[0] // rows

        def visit(block, carry, gathered_ref=gathered_ref, place=place):
            first = pl.multiple_of(firsts_ref[place + block], TILE)
            value = gathered_ref[pl.ds(pl.multiple_of(block * rows, TILE), rows), :].astype(f32)
            flat_ref[pl.ds(first, TILE), :] += value[:TILE]
            if inner:
                flat_ref[pl.ds(first + TILE, inner), :] = value[TILE:after]
            flat_ref[pl.ds(first + after, rows - after), :] += value[after:]
            return carry

        lax.fori_loop(0, blocks, visit, 0)
        place += blocks


def relay(flat_ref, place, out_ref):
    first, (rows, columns) = place
    chunks = columns // LANES
    step = 64

    def body(index, carry):
        begin = pl.multiple_of(index * step, step)
        for chunk in range(chunks):
            part = flat_ref[pl.ds(first + begin * chunks + chunk, step, stride=chunks), :]
            out_ref[pl.ds(begin, step), chunk * LANES : (chunk + 1) * LANES] = part.astype(out_ref.dtype)
        return carry

    lax.fori_loop(0, rows // step, body, 0)


def relay_vectors(flat_ref, table, out_ref):
    for index, (first, dims) in enumerate(vectors_of(table)):
        for chunk in range(dims[0] // LANES):
            out_ref[index : index + 1, chunk * LANES : (chunk + 1) * LANES] = flat_ref[
                first + chunk : first + chunk + 1, :
            ]


def unpack_cross_kernel(windows, count, traffic, firsts_ref, task_ref, *refs):
    vectors_ref, start_ref, query_ref, key_ref, value_ref, output_ref, up_ref, down_ref, flat_ref = refs[count:]
    assemble(firsts_ref, refs[:count], flat_ref, windows)
    relay_vectors(flat_ref, CROSS, vectors_ref)
    traffic.ship(vectors_ref)
    chunks = D // LANES
    first, unused = CROSS.task_table
    base = first + task_ref[0] * chunks
    relay(flat_ref, CROSS.latents, start_ref)
    for chunk in range(chunks):
        row = flat_ref[pl.ds(base + chunk, 1), :]
        start_ref[:, chunk * LANES : (chunk + 1) * LANES] += row
    traffic.ship(start_ref)
    relay(flat_ref, CROSS.query_weight, query_ref)
    traffic.ship(query_ref)
    relay(flat_ref, CROSS.key_weight, key_ref)
    traffic.ship(key_ref)
    relay(flat_ref, CROSS.value_weight, value_ref)
    traffic.ship(value_ref)
    relay(flat_ref, CROSS.output_weight, output_ref)
    traffic.ship(output_ref)
    relay(flat_ref, CROSS.up_weight, up_ref)
    traffic.ship(up_ref)
    relay(flat_ref, CROSS.down_weight, down_ref)
    traffic.ship(down_ref)


def unpack_cross(firsts, gathered, task, windows):
    outs = [
        shape((16, FF), f32), shape((LAT, D), f32), shape((D, D), bf16), shape((C, D), bf16),
        shape((C, D), bf16), shape((D, D), bf16), shape((D, FF), bf16), shape((FF, D), bf16),
    ]
    return streamed(
        functools.partial(unpack_cross_kernel, windows, len(gathered)), "unpack_cross", outs,
        [firsts, task, *gathered], early=range(len(outs)), scratch=[pltpu.VMEM((windows.padded, LANES), f32)], smem=2,
        flops=20_000_000_000, room=ROOM,
    )


def unpack_latent_kernel(windows, count, traffic, firsts_ref, *refs):
    vectors_ref, joint_ref, merge_ref, up_ref, down_ref, flat_ref = refs[count:]
    assemble(firsts_ref, refs[:count], flat_ref, windows)
    relay_vectors(flat_ref, LATENT, vectors_ref)
    traffic.ship(vectors_ref)
    relay(flat_ref, LATENT.joint_weight, joint_ref)
    traffic.ship(joint_ref)
    relay(flat_ref, LATENT.merge_weight, merge_ref)
    traffic.ship(merge_ref)
    relay(flat_ref, LATENT.up_weight, up_ref)
    traffic.ship(up_ref)
    relay(flat_ref, LATENT.down_weight, down_ref)
    traffic.ship(down_ref)


def unpack_latent(firsts, gathered, windows):
    outs = [
        shape((8, FF), f32), shape((D, 3 * D), bf16), shape((D, D), bf16), shape((D, FF), bf16),
        shape((FF, D), bf16),
    ]
    return streamed(
        functools.partial(unpack_latent_kernel, windows, len(gathered)), "unpack_latent", outs,
        [firsts, *gathered], scratch=[pltpu.VMEM((windows.padded, LANES), f32)], smem=1, room=20 * 2**20,
    )


def put(flat_ref, first, columns, row, value, column=0):
    chunks = columns // LANES
    rows = value.shape[0]
    for chunk in range(value.shape[1] // LANES):
        begin = first + row * chunks + column // LANES + chunk
        flat_ref[pl.ds(begin, rows, stride=chunks), :] = value[:, chunk * LANES : (chunk + 1) * LANES]


def put_vector(flat_ref, first, value, column=0):
    for chunk in range(value.shape[1] // LANES):
        row = first + column // LANES + chunk
        flat_ref[row : row + 1, :] = value[:, chunk * LANES : (chunk + 1) * LANES]


def to_windows(flat_ref, firsts_ref, out_refs, rows, traffic=None):
    begin = 0
    for out_ref in out_refs:
        held = out_ref.shape[0] // rows
        blocks = traffic.blocks[id(out_ref)][0].shape[0] // rows if traffic else held

        def visit(place, carry, out_ref=out_ref, begin=begin, held=held):
            if traffic:

                @pl.when(place >= held)
                def _():
                    traffic.block(out_ref, place - held, rows).wait()

            first = pl.multiple_of(firsts_ref[begin + place], TILE)
            slot = pl.multiple_of(place % held * rows, TILE)
            out_ref[pl.ds(slot, rows), :] = flat_ref[pl.ds(first, rows), :].astype(bf16)
            if traffic:
                traffic.block(out_ref, place, rows).start()
            return carry

        def finish(place, carry, out_ref=out_ref):
            traffic.block(out_ref, place, rows).wait()
            return carry

        lax.fori_loop(0, blocks, visit, 0)
        if traffic:
            lax.fori_loop(blocks - held, blocks, finish, 0)
        begin += blocks


def clear_tail(flat_ref, used):
    total = flat_ref.shape[0]
    flat_ref[used:total, :] = jnp.zeros((total - used, LANES), f32)


def gelu_and_slope(value):
    half = 0.5 + 0.5 * lax.erf(value * math.sqrt(0.5))
    density = jnp.exp2(value * value * (-0.5 * LOG2E)) * (1.0 / math.sqrt(2.0 * math.pi))
    return value * half, half + value * density


def feed_forward(traffic, hidden, gain, bias, up_ref, up_bias, down_ref, down_bias, normed_ref, active_ref, slope_ref):
    unit, rstd = normalise(hidden)
    normed_ref[...] = (unit * gain + bias).astype(bf16)
    traffic.ship(normed_ref)
    traffic.need(up_ref)
    step = 256
    for begin in range(0, FF, step):
        inner = dot(normed_ref[...], up_ref[:, begin : begin + step]) + up_bias[:, begin : begin + step]
        active, slope = gelu_and_slope(inner)
        active_ref[:, begin : begin + step] = active.astype(bf16)
        slope_ref[:, begin : begin + step] = slope.astype(bf16)
    traffic.ship(active_ref, slope_ref)
    traffic.need(down_ref)
    return hidden + (dot(active_ref[...], down_ref[...]) + down_bias)


def feed_backward(traffic, grad, hidden, gain, up_ref, down_ref, normed_ref, active_ref, slope_ref, flat_ref, table,
                  base=0):
    unit, rstd = normalise(hidden)
    branch = grad.astype(bf16)
    put_vector(flat_ref, table.down_bias[0] - base, column_sum(branch.astype(f32)))
    step = 256
    total = None
    normed = normed_ref[...]
    for begin in range(0, FF, step):
        put(flat_ref, table.down_weight[0] - base, D, begin, dot_tn(active_ref[:, begin : begin + step], branch))
        active_grad = dot_nt(branch, down_ref[begin : begin + step, :])
        inner = (active_grad * slope_ref[:, begin : begin + step].astype(f32)).astype(bf16)
        slope_ref[:, begin : begin + step] = inner
        put_vector(flat_ref, table.up_bias[0] - base, column_sum(inner.astype(f32)), begin)
        put(flat_ref, table.up_weight[0] - base, FF, 0, dot_tn(normed, inner), begin)
    traffic.need(up_ref)
    normed_grad = dot_nt(slope_ref[...], up_ref[...])
    put_vector(flat_ref, table.feed_gain[0] - base, column_sum(normed_grad * unit))
    put_vector(flat_ref, table.feed_bias[0] - base, column_sum(normed_grad))
    return grad + normalise_back(normed_grad, unit, rstd, gain)


def vector(vectors_ref, table, place):
    index = vectors_of(table).index(place)
    return vectors_ref[index : index + 1, : place[1][0]]


def block_kinds(count, begin, block, total):
    language = total - LANG
    end = begin + block
    some = (begin < count) | (end > language)
    full = (end <= count) | (count >= language) | (begin >= language)
    return some, full


def masked(scores, count, begin, total):
    place = begin + lax.broadcasted_iota(jnp.int32, (scores.shape[0], 1), 0)
    valid = (place < count) | (place >= total - LANG)
    return jnp.where(valid, scores, negative)


def cross_forward_kernel(traffic, count_ref, tokens_ref, start_ref, vectors_ref, wq_ref, wk_ref, wv_ref, wo_ref,
                         up_ref, down_ref,
                         normedq_ref, query_ref, keyed_ref, mixture_ref, lse_ref, hidden_ref, normed_ref,
                         active_ref, slope_ref, out_ref,
                         acc_ref, max_ref, sum_ref):
    total = tokens_ref.shape[0]
    count = count_ref[0]
    start = start_ref[...]
    unit, rstd = normalise(start)
    normedq_ref[...] = (
        unit * vector(vectors_ref, CROSS, CROSS.query_gain) + vector(vectors_ref, CROSS, CROSS.query_bias)
    ).astype(bf16)
    traffic.ship(normedq_ref)
    query_ref[...] = dot(normedq_ref[...], wq_ref[...]).astype(bf16)
    traffic.ship(query_ref)
    keyed_ref[...] = dot_nt(query_ref[...], wk_ref[...]) * D ** (-0.5)
    traffic.ship(keyed_ref)
    keyed = split(keyed_ref[...] * LOG2E, 1)
    gain = vector(vectors_ref, CROSS, CROSS.context_gain)
    bias = vector(vectors_ref, CROSS, CROSS.context_bias)
    max_ref[...] = jnp.full(max_ref.shape, negative, f32)
    sum_ref[...] = jnp.zeros(sum_ref.shape, f32)
    acc_ref[...] = jnp.zeros(acc_ref.shape, f32)
    block = min(BLOCK, total)

    def visit(index, carry):
        begin = pl.multiple_of(index * block, block)
        some, full = block_kinds(count, begin, block, total)

        @pl.when(some)
        def _():
            contexts, scores = [], []
            for part in range(0, block, PART):
                unit, rstd = normalise(tokens_ref[pl.ds(begin + part, PART), :].astype(f32))
                context = (unit * gain + bias).astype(bf16)
                contexts.append(context)
                raw = dot_nt(jnp.concatenate([context, context], axis=1), keyed)
                scores.append(masked(raw, count, begin + part, total))
            old = max_ref[...]
            newest = old
            for score in scores:
                newest = jnp.maximum(newest, jnp.max(score, axis=0, keepdims=True))
            fade = jnp.exp2(old - newest)
            max_ref[...] = newest
            added, mixed = sum_ref[...] * fade, acc_ref[...] * fade
            for context, score in zip(contexts, scores):
                weights = jnp.exp2(score - newest)
                added += column_sum(weights)
                mixed += dot_tn(context, weights.astype(bf16))
            sum_ref[...] = added
            acc_ref[...] = mixed

        return carry

    lax.fori_loop(0, total // block, visit, 0)
    totals = sum_ref[...]
    lse_ref[...] = max_ref[...] + jnp.log2(totals)
    mixture_ref[...] = acc_ref[...] * (1.0 / totals)
    traffic.ship(lse_ref, mixture_ref)
    traffic.need(wv_ref, wo_ref)
    values = jnp.concatenate([wv_ref[...], wv_ref[...]], axis=0)
    attended = dot_tn(split(mixture_ref[...], 0), values)
    hidden_ref[...] = start + (
        dot(attended.astype(bf16), wo_ref[...]) + vector(vectors_ref, CROSS, CROSS.output_bias)
    )
    traffic.ship(hidden_ref)
    out_ref[...] = feed_forward(
        traffic, hidden_ref[...], vector(vectors_ref, CROSS, CROSS.feed_gain), vector(vectors_ref, CROSS, CROSS.feed_bias),
        up_ref, vector(vectors_ref, CROSS, CROSS.up_bias), down_ref, vector(vectors_ref, CROSS, CROSS.down_bias),
        normed_ref, active_ref, slope_ref,
    )


def cross_forward(count, tokens, start, vectors, wq, wk, wv, wo, up, down):
    outs = [
        shape((LAT, D), bf16), shape((LAT, D), bf16), shape((LAT, C), f32), shape((C, LAT), f32),
        shape((1, LAT), f32), shape((LAT, D), f32), shape((LAT, D), bf16), shape((LAT, FF), bf16),
        shape((LAT, FF), bf16), shape((LAT, D), f32),
    ]
    scratch = [
        pltpu.VMEM((C, LAT), f32), pltpu.VMEM((1, LAT), f32), pltpu.VMEM((1, LAT), f32),
    ]
    return streamed(
        cross_forward_kernel, "cross_forward", outs,
        [count, tokens, start, vectors, wq, wk, wv, wo, up, down], late=range(6, 10), early=range(9), scratch=scratch,
        smem=1, flops=100_000_000_000,
    )


def pair_mask(value, side):
    lane = lax.broadcasted_iota(jnp.int32, (1, LANES), 1)
    keep = (lane < HEAD) if side == 0 else (lane >= HEAD)
    return jnp.where(keep, value, jnp.zeros_like(value))


def latent_kernel(windows, parts, traffic, firsts_ref, hidden_ref, cotangent_ref, vectors_ref, joint_w_ref, merge_ref,
                  up_ref, down_ref, out_ref, grad_ref, *rest):
    windows_refs, rest = rest[:parts], rest[parts:]
    (flat_ref, probs_ref, joint_ref, mixed_ref, after_ref, normedl_ref, normed_ref, active_ref, slope_ref, query_grad_ref, joint_grad_ref) = rest
    gain = vector(vectors_ref, LATENT, LATENT.attend_gain)
    unit, rstd = normalise(hidden_ref[...])
    normedl_ref[...] = (unit * gain + vector(vectors_ref, LATENT, LATENT.attend_bias)).astype(bf16)
    joint_ref[...] = dot(normedl_ref[...], joint_w_ref[...]).astype(bf16)
    scale = HEAD ** (-0.5)
    for pair in range(HEADS // 2):
        lanes = slice(pair * LANES, (pair + 1) * LANES)
        query = joint_ref[:, lanes]
        keys = joint_ref[:, D + pair * LANES : D + (pair + 1) * LANES]
        values = joint_ref[:, 2 * D + pair * LANES : 2 * D + (pair + 1) * LANES]
        mixed = None
        for side in range(2):
            scores = dot_nt(pair_mask(keys, side), query) * (scale * LOG2E)
            weights = jnp.exp2(scores - jnp.max(scores, axis=0, keepdims=True))
            weights = weights * (1.0 / column_sum(weights))
            weights = weights.astype(bf16)
            probs_ref[2 * pair + side] = weights
            part = dot_tn(pair_mask(values, side), weights)
            mixed = part if mixed is None else mixed + part
        mixed_ref[lanes, :] = mixed.astype(bf16)
    traffic.need(merge_ref)
    after_ref[...] = hidden_ref[...] + (
        dot_tn(mixed_ref[...], merge_ref[...]) + vector(vectors_ref, LATENT, LATENT.merge_bias)
    )
    feed_gain = vector(vectors_ref, LATENT, LATENT.feed_gain)
    out_ref[...] = feed_forward(
        traffic, after_ref[...], feed_gain, vector(vectors_ref, LATENT, LATENT.feed_bias), up_ref,
        vector(vectors_ref, LATENT, LATENT.up_bias), down_ref, vector(vectors_ref, LATENT, LATENT.down_bias),
        normed_ref, active_ref, slope_ref,
    ).astype(bf16)

    traffic.ship(out_ref)
    traffic.need(cotangent_ref)
    clear_tail(flat_ref, LATENT_ROWS)
    after_grad = feed_backward(
        traffic, cotangent_ref[...].astype(f32), after_ref[...], feed_gain, up_ref, down_ref, normed_ref, active_ref,
        slope_ref, flat_ref, LATENT,
    )
    branch = after_grad.astype(bf16)
    put(flat_ref, LATENT.merge_weight[0], D, 0, dot(mixed_ref[...], branch))
    put_vector(flat_ref, LATENT.merge_bias[0], column_sum(branch.astype(f32)))
    mixed_grad = dot_nt(branch, merge_ref[...]).astype(bf16)
    for pair in range(HEADS // 2):
        lanes = slice(pair * LANES, (pair + 1) * LANES)
        query = joint_ref[:, lanes]
        keys = joint_ref[:, D + pair * LANES : D + (pair + 1) * LANES]
        values = joint_ref[:, 2 * D + pair * LANES : 2 * D + (pair + 1) * LANES]
        grads = mixed_grad[:, lanes]
        query_part = key_part = value_part = None
        for side in range(2):
            probs = probs_ref[2 * pair + side].astype(f32)
            part = dot(probs.astype(bf16), pair_mask(grads, side))
            value_part = part if side == 0 else value_part + part
            probs_grad = dot_nt(pair_mask(values, side), grads)
            delta = column_sum(probs * probs_grad)
            scores_grad = (probs * (probs_grad - delta)).astype(bf16)
            part = dot(scores_grad, pair_mask(query, side))
            key_part = part if side == 0 else key_part + part
            part = dot_tn(pair_mask(keys, side), scores_grad)
            query_part = part if side == 0 else query_part + part
        query_grad_ref[lanes, :] = query_part * scale
        joint_grad_ref[:, D + pair * LANES : D + (pair + 1) * LANES] = (key_part * scale).astype(bf16)
        joint_grad_ref[:, 2 * D + pair * LANES : 2 * D + (pair + 1) * LANES] = value_part.astype(bf16)
    joint_grad_ref[:, :D] = query_grad_ref[...].T.astype(bf16)
    put(flat_ref, LATENT.joint_weight[0], 3 * D, 0, dot_tn(normedl_ref[...], joint_grad_ref[...]))
    normed_grad = dot_nt(joint_grad_ref[...], joint_w_ref[...])
    put_vector(flat_ref, LATENT.attend_gain[0], column_sum(normed_grad * unit))
    put_vector(flat_ref, LATENT.attend_bias[0], column_sum(normed_grad))
    grad_ref[...] = after_grad + normalise_back(normed_grad, unit, rstd, gain)
    to_windows(flat_ref, firsts_ref, windows_refs, windows.rows, traffic)


def latent_layer(firsts, hidden, cotangent, vectors, joint, merge, up, down, windows, grid):
    outs = [shape((LAT, D), bf16), shape((LAT, D), f32)] + windows.outs(grid.nz)
    scratch = [
        pltpu.VMEM((windows.padded, LANES), f32), pltpu.VMEM((HEADS, LAT, LAT), bf16),
        pltpu.VMEM((LAT, 3 * D), bf16), pltpu.VMEM((D, LAT), bf16), pltpu.VMEM((LAT, D), f32),
        pltpu.VMEM((LAT, D), bf16), pltpu.VMEM((LAT, D), bf16), pltpu.VMEM((LAT, FF), bf16),
        pltpu.VMEM((LAT, FF), bf16), pltpu.VMEM((D, LAT), f32), pltpu.VMEM((LAT, 3 * D), bf16),
    ]
    return streamed(
        functools.partial(latent_kernel, windows, grid.nz), "latent_layer", outs,
        [firsts, hidden, cotangent, vectors, joint, merge, up, down], late=[2], early=[0],
        blocks={2 + c: windows.devices // grid.nz for c in range(grid.nz)}, scratch=scratch, smem=1,
        flops=20_000_000_000, room=14 * 2**20, slots=SLOTS,
    )


SPLIT = CROSS.output_weight[0] // TILE * TILE


def cross_feed_kernel(windows, parts, traffic, firsts_ref, grad_ref, vectors_ref, wv_ref, wo_ref, up_ref, down_ref,
                      mixture_ref, hidden_ref, normed_ref, active_ref, saved_slope_ref,
                      hidden_grad_ref, valued_ref, delta_ref, value_grad_ref, *rest):
    windows_refs = rest[:parts]
    flat_ref, slope_ref = rest[parts:]
    clear_tail(flat_ref, CROSS_ROWS)
    slope_ref[...] = saved_slope_ref[...]
    hidden_grad = feed_backward(
        traffic, grad_ref[...], hidden_ref[...], vector(vectors_ref, CROSS, CROSS.feed_gain), up_ref, down_ref, normed_ref,
        active_ref, slope_ref, flat_ref, CROSS,
    )
    hidden_grad_ref[...] = hidden_grad
    traffic.ship(hidden_grad_ref)
    traffic.need(wv_ref, wo_ref, mixture_ref)
    branch = hidden_grad.astype(bf16)
    values = jnp.concatenate([wv_ref[...], wv_ref[...]], axis=0)
    mixture = split(mixture_ref[...], 0)
    attended = dot_tn(mixture, values)
    put(flat_ref, CROSS.output_weight[0], D, 0, dot_tn(attended.astype(bf16), branch))
    put_vector(flat_ref, CROSS.output_bias[0], column_sum(branch.astype(f32)))
    attended_grad = dot_nt(branch, wo_ref[...]).astype(bf16)
    both = dot(mixture, attended_grad)
    value_grad_ref[...] = both[:C] + both[C:]
    put(flat_ref, CROSS.value_weight[0], D, 0, value_grad_ref[...])
    valued = dot_nt(attended_grad, wv_ref[...])
    valued_ref[...] = split(valued, 1)
    delta_ref[...] = column_sum((attended_grad.astype(f32) * attended).T)
    flat_ref[:SPLIT, :] = jnp.zeros((SPLIT, LANES), f32)
    to_windows(flat_ref, firsts_ref, windows_refs, windows.rows, traffic)


def cross_feed(firsts, grad, vectors, wv, wo, up, down, mixture, hidden, normed, active, slope, windows, grid):
    outs = [
        shape((LAT, D), f32), shape((LAT, 2 * C), bf16), shape((1, LAT), f32), shape((C, D), f32),
    ] + windows.outs(grid.nz)
    return streamed(
        functools.partial(cross_feed_kernel, windows, grid.nz), "cross_feed", outs,
        [firsts, grad, vectors, wv, wo, up, down, mixture, hidden, normed, active, slope], late=[5, 3, 4, 7],
        early=[0], blocks={4 + c: windows.devices // grid.nz for c in range(grid.nz)},
        scratch=[pltpu.VMEM((windows.padded, LANES), f32), pltpu.VMEM((LAT, FF), bf16)], smem=1,
        flops=80_000_000_000,
    )


def attend_block(offset, blocks, count_ref, tokens_ref, valued_ref, delta_ref, vectors_ref, keyed_ref, lse_ref,
                 token_grad_ref, acc_ref, gains_ref, doubled_ref, paired_ref):
    block = tokens_ref.shape[0]
    begin = (pl.program_id(0) + offset) * block
    total = blocks * block
    count = count_ref[0]
    some, full = block_kinds(count, begin, block, total)

    @pl.when(pl.program_id(0) == 0)
    def _():
        doubled_ref[...] = split(keyed_ref[...] * LOG2E, 1)
        paired_ref[...] = split(keyed_ref[...], 1)

    @pl.when(some)
    def _():
        gain = vector(vectors_ref, CROSS, CROSS.context_gain)
        bias = vector(vectors_ref, CROSS, CROSS.context_bias)
        for part in range(0, block, PART):
            rows = slice(part, part + PART)
            unit, rstd = normalise(tokens_ref[rows, :].astype(f32))
            context = (unit * gain + bias).astype(bf16)
            twice = jnp.concatenate([context, context], axis=1)
            scores = masked(dot_nt(twice, doubled_ref[...]), count, begin + part, total)
            probs = jnp.exp2(scores - lse_ref[...])
            scores_grad = (probs * (dot_nt(twice, valued_ref[...]) - delta_ref[...])).astype(bf16)
            acc_ref[...] += dot_tn(context, scores_grad)
            wide = dot(probs.astype(bf16), valued_ref[...]) + dot(scores_grad, paired_ref[...])
            context_grad = wide[:, :C] + wide[:, C:]
            gains_ref[0:1, :] += column_sum(context_grad * unit)
            gains_ref[1:2, :] += column_sum(context_grad)
            token_grad_ref[rows, :] = normalise_back(context_grad, unit, rstd, gain)

    @pl.when(jnp.logical_not(some))
    def _():
        token_grad_ref[...] = jnp.zeros(token_grad_ref.shape, f32)


def attend_first_kernel(blocks, count_ref, tokens_ref, valued_ref, delta_ref, vectors_ref, keyed_ref, lse_ref,
                        token_grad_ref, acc_ref, gains_ref, doubled_ref, paired_ref):
    @pl.when(pl.program_id(0) == 0)
    def _():
        acc_ref[...] = jnp.zeros(acc_ref.shape, f32)
        gains_ref[...] = jnp.zeros(gains_ref.shape, f32)

    attend_block(0, blocks, count_ref, tokens_ref, valued_ref, delta_ref, vectors_ref, keyed_ref, lse_ref,
                 token_grad_ref, acc_ref, gains_ref, doubled_ref, paired_ref)


def attend_second_kernel(offset, blocks, rows, parts, firsts_ref, count_ref, task_ref, tokens_ref, valued_ref,
                         delta_ref, vectors_ref, keyed_ref, lse_ref, acc_before_ref, gains_before_ref, hidden_grad_ref,
                         value_grad_ref, start_ref, wq_ref, wk_ref, normedq_ref, query_ref, kept_ref,
                         token_grad_ref, *rest):
    windows_refs = rest[:parts]
    flat_ref, acc_ref, gains_ref, doubled_ref, paired_ref = rest[parts:]

    @pl.when(pl.program_id(0) == 0)
    def _():
        acc_ref[...] = acc_before_ref[...]
        gains_ref[...] = gains_before_ref[...]

    attend_block(offset, blocks, count_ref, tokens_ref, valued_ref, delta_ref, vectors_ref, keyed_ref, lse_ref,
                 token_grad_ref, acc_ref, gains_ref, doubled_ref, paired_ref)

    @pl.when(pl.program_id(0) == pl.num_programs(0) - 1)
    def _():
        pulled = split(acc_ref[...] * D ** (-0.5), 0)
        both = dot(pulled, query_ref[...])
        put(flat_ref, CROSS.key_weight[0], D, 0, both[:C] + both[C:])
        put(flat_ref, CROSS.value_weight[0], D, 0, value_grad_ref[...])
        put_vector(flat_ref, CROSS.context_gain[0], gains_ref[0:1, :])
        put_vector(flat_ref, CROSS.context_bias[0], gains_ref[1:2, :])
        query_grad = dot_tn(pulled, jnp.concatenate([wk_ref[...], wk_ref[...]], axis=0)).astype(bf16)
        put(flat_ref, CROSS.query_weight[0], D, 0, dot_tn(normedq_ref[...], query_grad))
        normed_grad = dot_nt(query_grad, wq_ref[...])
        unit, rstd = normalise(start_ref[...])
        put_vector(flat_ref, CROSS.query_gain[0], column_sum(normed_grad * unit))
        put_vector(flat_ref, CROSS.query_bias[0], column_sum(normed_grad))
        gain = vector(vectors_ref, CROSS, CROSS.query_gain)
        start_grad = hidden_grad_ref[...] + normalise_back(normed_grad, unit, rstd, gain)
        put(flat_ref, CROSS.latents[0], D, 0, start_grad)
        first, unused = CROSS.task_table
        chunks = D // LANES
        flat_ref[first : first + NTASK * chunks, :] = jnp.zeros((NTASK * chunks, LANES), f32)
        sums = column_sum(start_grad)
        base = first + task_ref[0] * chunks
        for chunk in range(chunks):
            flat_ref[pl.ds(base + chunk, 1), :] = sums[:, chunk * LANES : (chunk + 1) * LANES]
        clear_tail(flat_ref, SPLIT)
        to_windows(flat_ref, firsts_ref, windows_refs, rows)


def attend_scratch():
    return [pltpu.VMEM((LAT, 2 * C), bf16), pltpu.VMEM((LAT, 2 * C), bf16)]


def attend_first(count, tokens, valued, delta, vectors, keyed, lse):
    total = tokens.shape[0]
    block = min(BLOCK, total)
    blocks = total // block
    whole = [valued, delta, vectors, keyed, lse]
    row = lambda i: (i, 0)
    outs = [shape((total, C), f32), shape((C, LAT), f32), shape((8, C), f32)]
    scratch = attend_scratch()
    return pl.pallas_call(
        functools.partial(attend_first_kernel, blocks),
        name="attend_first",
        grid=(max(blocks // 2, 1),),
        out_shape=outs,
        in_specs=[pl.BlockSpec(memory_space=pltpu.SMEM), pl.BlockSpec((block, C), row)] + vmem_specs(len(whole)),
        out_specs=[pl.BlockSpec((block, C), row)] + vmem_specs(2),
        scratch_shapes=scratch,
        compiler_params=pltpu.CompilerParams(vmem_limit_bytes=vmem_limit(*whole, *scratch)),
        cost_estimate=pl.CostEstimate(flops=100_000_000_000, bytes_accessed=1, transcendentals=0),
    )(count, tokens, *whole)


def attend_second(firsts, count, task, tokens, valued, delta, vectors, keyed, lse, acc, gains, hidden_grad, value_grad,
                  start, wq, wk, normedq, query, token_grad, windows, grid):
    total = tokens.shape[0]
    block = min(BLOCK, total)
    blocks = total // block
    offset = max(blocks // 2, 1)
    rows = windows.quarter(grid.nx)
    last = grid.ny * grid.nz - 1
    assert SPLIT <= windows.first[last + 1] and blocks > offset
    flat_rows = max(windows.first[last] + rows * grid.nx, SPLIT + TILE)
    whole = [valued, delta, vectors, keyed, lse, acc, gains, hidden_grad, value_grad, start, wq, wk, normedq, query]
    half = windows.devices // grid.nz // grid.ny * rows
    small = [shape((half * depths, LANES), bf16) for c in range(grid.nz) for depths in halves(grid)]
    row = lambda i: (i + offset, 0)
    scratch = [
        pltpu.VMEM((flat_rows, LANES), f32), pltpu.VMEM((C, LAT), f32),
        pltpu.VMEM((8, C), f32), *attend_scratch(),
    ]
    return pl.pallas_call(
        functools.partial(attend_second_kernel, offset, blocks, rows, len(small)),
        name="attend_second",
        grid=(blocks - offset,),
        out_shape=[shape((total, C), f32)] + small,
        in_specs=[pl.BlockSpec(memory_space=pltpu.SMEM)] * 3
        + [pl.BlockSpec((block, C), row)]
        + vmem_specs(len(whole))
        + [pl.BlockSpec(memory_space=pl.ANY)],
        out_specs=[pl.BlockSpec((block, C), row)] + vmem_specs(len(small)),
        scratch_shapes=scratch,
        input_output_aliases={4 + len(whole): 0},
        compiler_params=pltpu.CompilerParams(vmem_limit_bytes=vmem_limit(*whole, *small, *scratch)),
        cost_estimate=pl.CostEstimate(flops=100_000_000_000, bytes_accessed=1, transcendentals=0),
    )(firsts, count, task, tokens, *whole, token_grad)


def body(tokens, task_id, valid_count, cross_params, latent_params, out_grad):
    grid = Grid()
    devices = grid.nx * grid.ny * grid.nz
    cw = Windows(cross_params.shape[0] * devices, devices)
    lw = Windows(latent_params.shape[0] * devices, devices)
    gathered_from = grid.owners(gather_places(grid))
    scattered_to = grid.owners(grid.order())
    tokens = tokens[0]

    cross_window, latent_window = place([cross_params, latent_params], [cw, lw], grid.index)
    cross_column = gather_depth(cross_window, grid)
    latent_column = gather_depth(after(latent_window, *cross_column[1:]), grid)
    pieces = gather_plane_second(*gather_plane_first(cross_column, grid), grid)
    for piece in pieces:
        piece[0] = after(piece[0], *latent_column[1:])
        piece[1:] = [after(value, *latent_column[1:]) for value in piece[1:]]
    cross_all = sum(gather_core(*pieces, grid), [])
    latent_column = [after(value, pieces[0][-1], pieces[1][-1]) for value in latent_column]
    lows, highs = gather_plane_first(latent_column, grid)
    vectors, start, wq, wk, wv, wo, up, down = unpack_cross(cw.firsts(gathered_from), cross_all, task_id, cw)
    lows[0], highs[0] = after(lows[0], vectors), after(highs[0], vectors)
    first, second = gather_plane_second(lows, highs, grid)
    normedq, query, keyed, mixture, lse, hidden, normed, active, slope, result = cross_forward(
        valid_count, tokens, after(start, first[0], second[0]), vectors, wq, wk, wv, wo, up, down
    )
    first[1:] = [after(value, result) for value in first[1:]]
    second[1:] = [after(value, result) for value in second[1:]]
    latent_all = sum(gather_core(first, second, grid), [])
    latent_weights = unpack_latent(lw.firsts(gathered_from), latent_all, lw)
    latents_out, result_grad, *latent_parts = latent_layer(
        lw.firsts(scattered_to), result, out_grad[0], *latent_weights, lw, grid
    )

    latent_lows, latent_highs = reduce_first(reduce_core(latent_parts, grid), lw.rows, grid)
    hidden_grad, valued, delta, value_grad, *later_parts = cross_feed(
        cw.firsts(scattered_to), after(result_grad, latent_lows[0][0]), vectors, wv, wo, up, down, mixture, hidden,
        normed, active, slope, cw, grid,
    )
    latent_lows[0] = (after(latent_lows[0][0], delta), 0)
    latent_first, latent_second = reduce_second(latent_lows, latent_highs, lw.rows, grid)
    later_group = reduce_core(later_parts, grid)
    token_grad, acc, gains = attend_first(
        valid_count, tokens, valued, after(delta, latent_first[0][0]), vectors, keyed, lse
    )
    later_group[0] = (after(later_group[0][0], acc), 0)
    later_lows, later_highs = reduce_first(later_group, cw.rows, grid)
    latent_first[0] = (after(latent_first[0][0], later_lows[0][0]), 0)
    latent_column = reduce_depth(latent_first, latent_second, lw.rows, grid)
    owner, quarter = quarter_owners(grid)
    small_rows = cw.quarter(grid.nx)
    token_grad, *early_parts = attend_second(
        cw.firsts(owner) + quarter * small_rows, valid_count, task_id, tokens, valued, delta, vectors, keyed, lse,
        after(acc, latent_column[0]), gains, hidden_grad, value_grad, start, wq, wk, normedq, query, token_grad, cw,
        grid,
    )
    latent_column[0] = after(latent_column[0], early_parts[0])
    latent_share = extract(latent_column, [], lw, grid)
    later_lows[0] = (after(later_lows[0][0], latent_share), 0)
    early_parts = [after(part, latent_share) for part in early_parts]
    early_groups = [reduce_core(early_parts[half::2], grid) for half in range(2)]
    later_first, later_second, early_lows, early_highs = reduce_second_and_first(
        later_lows, later_highs, cw.rows, early_groups, small_rows, grid
    )
    early_first, early_second = reduce_second(early_lows, early_highs, small_rows, grid)
    column = reduce_depth_both(later_first, later_second, cw.rows, early_first, early_second, small_rows, grid)
    quarters = collect_quarters(column, cw.rows, small_rows, grid)
    return (latents_out[None], token_grad[None], extract(column, quarters, cw, grid), latent_share)


def solution(mesh):
    return jax.shard_map(
        body,
        mesh=mesh,
        in_specs=(
            P(AXES, None, None),
            P(AXES),
            P(AXES),
            P(AXES),
            P(AXES),
            P(AXES, None, None),
        ),
        out_specs=(
            P(AXES, None, None),
            P(AXES, None, None),
            P(AXES),
            P(AXES),
        ),
        check_vma=False,
    )
```
